32 devices in a mesh: dp: 8 (over z, x), blk: 4 (over y, core).
Axes of the slice: x: 2, y: 2, z: 4, core: 2. Of those that a mesh axis runs over, the one named last changes fastest.
Arguments:
- tokens: bfloat16 [8192, 1024], P(('dp', 'blk')), may hold values from -6 to 6
- lengths: int32 [8, 5], P('dp'), may hold values from 0 to 512, as said below
- ln1_gain: float32 [1024], replicated, may hold values from 0.5 to 1.5
- ln1_bias: float32 [1024], replicated, may hold values from -1.75 to 1.75
- w_qkv: bfloat16 [1024, 3072], replicated, may hold values from -0.1875 to 0.1875
- qv_bias: float32 [2048], replicated, may hold values from -1.75 to 1.75
- head_scale: float32 [16], replicated, may hold values from 0.5 to 2
- w_out: bfloat16 [1024, 1024], replicated, may hold values from -0.1875 to 0.1875
- out_bias: float32 [1024], replicated, may hold values from -0.625 to 0.625
- lnpa_gain: float32 [1024], replicated, may hold values from 0.5 to 1.5
- lnpa_bias: float32 [1024], replicated, may hold values from -1.75 to 1.75
- ln2_gain: float32 [1024], replicated, may hold values from 0.5 to 1.5
- ln2_bias: float32 [1024], replicated, may hold values from -1.75 to 1.75
- w_fc1: bfloat16 [1024, 4096], replicated, may hold values from -0.1875 to 0.1875
- fc1_bias: float32 [4096], replicated, may hold values from -1.75 to 1.75
- lnf_gain: float32 [4096], replicated, may hold values from 0.5 to 1.5
- lnf_bias: float32 [4096], replicated, may hold values from -1.75 to 1.75
- w_fc2: bfloat16 [4096, 1024], replicated, may hold values from -0.09375 to 0.09375
- fc2_bias: float32 [1024], replicated, may hold values from -1.75 to 1.75
- cotangent: bfloat16 [8192, 1024], P(('dp', 'blk')), may hold values from -6 to 6
Outputs:
- layer_out: bfloat16 [8192, 1024], P(('dp', 'blk'))
- grad_tokens: float32 [8192, 1024], P(('dp', 'blk'))
- grad_ln1_gain: float32 [1024], replicated
- grad_ln1_bias: float32 [1024], replicated
- grad_w_qkv: float32 [1024, 3072], P(('dp', 'blk'))
- grad_qv_bias: float32 [2048], replicated
- grad_head_scale: float32 [16], replicated
- grad_w_out: float32 [1024, 1024], P(('dp', 'blk'))
- grad_out_bias: float32 [1024], replicated
- grad_lnpa_gain: float32 [1024], replicated
- grad_lnpa_bias: float32 [1024], replicated
- grad_ln2_gain: float32 [1024], replicated
- grad_ln2_bias: float32 [1024], replicated
- grad_w_fc1: float32 [1024, 4096], P(('dp', 'blk'))
- grad_fc1_bias: float32 [4096], replicated
- grad_lnf_gain: float32 [4096], replicated
- grad_lnf_bias: float32 [4096], replicated
- grad_w_fc2: float32 [4096, 1024], P(('dp', 'blk'))
- grad_fc2_bias: float32 [1024], replicated
The draws below stay inside these ranges and needn't reach their ends.
Inputs may be any that keep to these rules, and one draw needn't show every extreme that they name: Each row of lengths sums to 1024 and is a window of a stream of whole sequences of 512 and 256 tokens: its first entry, 1 to 255, is the end of a sequence begun before the bucket; then come whole sequences (two of 512; one of 512 and two of 256 in some order; or four of 256), the last of them cut short by the first entry; trailing entries are 0.
All inputs are finite; a program needn't handle non-finite values.
Results may differ from the reference program's by a relative error of at most 0.018.
Values may be sent and summed in bfloat16 or wider, within the bound.
A program may use at most 256 MiB of HBM per device.

```python
import math
import jax
import jax.numpy as jnp
from jax import lax

D = 1024
HEADS = 16
HEAD_DIM = 64
FF = 4096
TOK_DEV = 256
GROUP = 1024
TOKENS = 8192
N_DP = 8
N_BLK = 4


def draw_lengths(key, part):
    key = jax.random.fold_in(key, 17)
    first_key, second_key, third_key = jax.random.split(key, 3)
    unit = TOK_DEV * N_BLK // 4
    offset = jax.random.randint(first_key, (), 0, 3)
    kinds = ((jnp.arange(N_DP, dtype=jnp.int32) + offset) % 3)[:, None]
    leads = jax.random.randint(second_key, (N_DP, 1), 1, TOK_DEV)
    places = jax.random.randint(third_key, (N_DP, 1), 0, 3)
    slot_index = jnp.arange(4, dtype=jnp.int32)[None, :]
    pattern_two = jnp.where(slot_index < 2, 2, 0)
    pattern_mixed = jnp.where(slot_index < 3, jnp.where(slot_index == places, 2, 1), 0)
    pattern_four = jnp.ones((N_DP, 4), jnp.int32)
    pattern = jnp.where(kinds == 0, pattern_two, jnp.where(kinds == 1, pattern_mixed, pattern_four))
    last_slot = jnp.where(kinds == 0, 1, jnp.where(kinds == 1, 2, 3))
    whole = pattern * unit - leads * (slot_index == last_slot).astype(jnp.int32)
    return jnp.concatenate([leads, whole], axis=1).astype(jnp.int32)


def steps_of(stream_key, dims, cuts, low, high):
    level = 1.0
    for dim, parts in cuts:
        heights = jax.random.uniform(jax.random.fold_in(jax.random.fold_in(stream_key, 6), dim), (parts,), jnp.float32, low / len(cuts), high / len(cuts))
        level = level * jnp.repeat(jnp.exp(heights), dims[dim] // parts).reshape((-1,) + (1,) * (len(dims) - 1 - dim))
    return level


def noise(key, shape, width, limit, shards=(), kind=jnp.bfloat16):
    values = jax.random.normal(key, shape, jnp.float32) * width
    if len(shards) > 0:
        values = steps_of(key, shape, shards, -0.22, 0.18) * values
    return jnp.clip(values, min=-limit, max=limit).astype(kind)


def setup_inputs(seed: int = 0) -> dict:
    seeds = jax.random.split(jax.random.key(seed), 21)
    return {
        "tokens": noise(seeds[0], (TOKENS, D), 1.0, 6.0, ((0, 32),)),
        "lengths": draw_lengths(jax.random.fold_in(seeds[20], 71), 0),
        "ln1_gain": jnp.clip(1.0 + 0.1 * jax.random.normal(seeds[2], (D,), jnp.float32), 0.5, 1.5),
        "ln1_bias": noise(seeds[3], (D,), 0.3, 1.75, (), jnp.float32),
        "w_qkv": noise(seeds[4], (D, 3 * D), D ** -0.5, 0.1875),
        "qv_bias": noise(seeds[5], (2 * D,), 0.3, 1.75, (), jnp.float32),
        "head_scale": jnp.clip(jnp.exp(jax.random.uniform(seeds[6], (HEADS,), jnp.float32, math.log(0.5), math.log(2.0))), 0.5, 2.0),
        "w_out": noise(seeds[7], (D, D), D ** -0.5, 0.1875),
        "out_bias": noise(seeds[8], (D,), 0.1, 0.625, (), jnp.float32),
        "lnpa_gain": jnp.clip(1.0 + 0.1 * jax.random.normal(seeds[9], (D,), jnp.float32), 0.5, 1.5),
        "lnpa_bias": noise(seeds[10], (D,), 0.3, 1.75, (), jnp.float32),
        "ln2_gain": jnp.clip(1.0 + 0.1 * jax.random.normal(seeds[11], (D,), jnp.float32), 0.5, 1.5),
        "ln2_bias": noise(seeds[12], (D,), 0.3, 1.75, (), jnp.float32),
        "w_fc1": noise(seeds[13], (D, FF), D ** -0.5, 0.1875),
        "fc1_bias": noise(seeds[14], (FF,), 0.3, 1.75, (), jnp.float32),
        "lnf_gain": jnp.clip(1.0 + 0.1 * jax.random.normal(seeds[15], (FF,), jnp.float32), 0.5, 1.5),
        "lnf_bias": noise(seeds[16], (FF,), 0.3, 1.75, (), jnp.float32),
        "w_fc2": noise(seeds[17], (FF, D), FF ** -0.5, 0.09375),
        "fc2_bias": noise(seeds[18], (D,), 0.3, 1.75, (), jnp.float32),
        "cotangent": noise(seeds[19], (TOKENS, D), 1.0, 6.0, ((0, 32),)),
    }


@jax.custom_vjp
def low(v):
    return lax.optimization_barrier(v.astype(jnp.bfloat16)).astype(jnp.float32)

@jax.custom_vjp
def low_back(v):
    return v

def low_keep(v):
    return (low(v), None)

def low_pass(kept, grad):
    return (grad,)

def back_keep(v):
    return (v, None)

def back_low(kept, grad):
    return (low(grad),)
low.defvjp(low_keep, low_pass)
low_back.defvjp(back_keep, back_low)

def norm_rows(values_in, gain_vec, bias_vec):
    row_mean = lax.optimization_barrier(jnp.mean(values_in, axis=-1, keepdims=True))
    centered = values_in - row_mean
    variance = lax.optimization_barrier(jnp.mean(centered * centered, axis=-1, keepdims=True))
    return centered * lax.rsqrt(variance + 1e-05) * gain_vec + bias_vec

def gelu_exact(pre_values):
    return 0.5 * pre_values * (1.0 + lax.erf(pre_values * 0.7071067811865476))

def bucket_pass(parameters, bucket_rows, counts):
    ln1_gain, ln1_bias, w_qkv, qv_bias, head_scale, w_out, out_bias, lnpa_gain, lnpa_bias, ln2_gain, ln2_bias, w_fc1, fc1_bias, lnf_gain, lnf_bias, w_fc2, fc2_bias = parameters
    highest = lax.Precision.HIGHEST
    normed_in = low(norm_rows(bucket_rows, ln1_gain, ln1_bias))
    projected = jnp.dot(normed_in, w_qkv, precision=highest)
    queries = low_back(low(projected[:, :D] + qv_bias[:D])).reshape(GROUP, HEADS, HEAD_DIM)
    key_heads = low_back(low(projected[:, D:2 * D])).reshape(GROUP, HEADS, HEAD_DIM)
    values = low_back(low(projected[:, 2 * D:] + qv_bias[D:])).reshape(GROUP, HEADS, HEAD_DIM)
    seq_ends = jnp.cumsum(counts)
    positions = jnp.arange(GROUP, dtype=jnp.int32)
    labels = lax.optimization_barrier(jnp.sum((positions[:, None] >= seq_ends[None, :]).astype(jnp.int32), axis=1))
    query_span = math.gcd(GROUP, 512)

    def attend(block_index):
        row_start = block_index * query_span
        query_part = lax.dynamic_slice_in_dim(queries, row_start, query_span, 0)
        raw_scores = jnp.einsum('qhd,khd->hqk', query_part, key_heads, precision=highest)
        scores = low_back(raw_scores * HEAD_DIM ** (-0.5))
        q_spots = row_start + jnp.arange(query_span, dtype=jnp.int32)
        q_labels = lax.dynamic_slice_in_dim(labels, row_start, query_span, 0)
        visible = (labels[None, :] == q_labels[:, None]) & (positions[None, :] <= q_spots[:, None])
        scores = jnp.where(visible[None], scores, -1e+30)
        top_score = lax.optimization_barrier(jnp.max(scores, axis=-1, keepdims=True))
        weights = jnp.exp(scores - top_score)
        softmax_out = weights / lax.optimization_barrier(jnp.sum(weights, axis=-1, keepdims=True))
        return jnp.einsum('hqk,khd->qhd', low(softmax_out), values, precision=highest).reshape(query_span, D)
    attended = lax.map(jax.checkpoint(attend), jnp.arange(GROUP // query_span, dtype=jnp.int32))
    attended = low_back(attended.reshape(GROUP, D))
    scaled = low(attended * jnp.repeat(head_scale, HEAD_DIM))
    attn_out = low_back(jnp.dot(scaled, w_out, precision=highest) + out_bias)
    first_sum = bucket_rows + norm_rows(attn_out, lnpa_gain, lnpa_bias)
    normed_mid = low(norm_rows(first_sum, ln2_gain, ln2_bias))
    pre_act = low_back(jnp.dot(normed_mid, w_fc1, precision=highest) + fc1_bias)
    ffn_normed = low(norm_rows(gelu_exact(pre_act), lnf_gain, lnf_bias))
    return first_sum + jnp.dot(ffn_normed, w_fc2, precision=highest) + fc2_bias

def reference(tokens, lengths, ln1_gain, ln1_bias, w_qkv, qv_bias, head_scale, w_out, out_bias, lnpa_gain, lnpa_bias, ln2_gain, ln2_bias, w_fc1, fc1_bias, lnf_gain, lnf_bias, w_fc2, fc2_bias, cotangent):
    parameters = tuple((item.astype(jnp.float32) for item in (ln1_gain, ln1_bias, w_qkv, qv_bias, head_scale, w_out, out_bias, lnpa_gain, lnpa_bias, ln2_gain, ln2_bias, w_fc1, fc1_bias, lnf_gain, lnf_bias, w_fc2, fc2_bias)))
    inputs = tokens.astype(jnp.float32)

    def forward(params_in, inputs_in):
        buckets = inputs_in.reshape(N_DP, GROUP, D)

        def one_bucket(bucket_pair):
            return bucket_pass(params_in, bucket_pair[0], bucket_pair[1])
        outputs = lax.map(jax.checkpoint(one_bucket), (buckets, lengths))
        return outputs.reshape(TOKENS, D)
    result, pullback = jax.vjp(forward, parameters, inputs)
    gradients, input_grad = pullback(cotangent.astype(jnp.float32))
    return (result.astype(jnp.bfloat16), input_grad, gradients[0], gradients[1], gradients[2], gradients[3], gradients[4], gradients[5], gradients[6], gradients[7], gradients[8], gradients[9], gradients[10], gradients[11], gradients[12], gradients[13], gradients[14], gradients[15], gradients[16])
```

```python
import functools
import math

import jax
import jax.numpy as jnp
from jax import lax
from jax.experimental import pallas as pl
from jax.experimental.pallas import tpu as pltpu
from jax.sharding import PartitionSpec as P

HEADS = 16
MESH = pl.DeviceIdType.MESH
F32, BF16 = jnp.float32, jnp.bfloat16
WX = 384
WZ = 256
WR = 2 * WX + WZ
ROWS = 16
SLOTS = 8


def norm_rows(values_in, gain_vec, bias_vec):
    row_mean = jnp.mean(values_in, axis=-1, keepdims=True)
    centered = values_in - row_mean
    variance = jnp.mean(centered * centered, axis=-1, keepdims=True)
    return centered * lax.rsqrt(variance + 1e-05) * gain_vec + bias_vec


def gelu_exact(pre_values):
    return 0.5 * pre_values * (1.0 + lax.erf(pre_values * 0.7071067811865476))


def over_rows(left, right):
    return lax.dot_general(
        left, right, (((0,), (0,)), ((), ())), preferred_element_type=jnp.float32
    )


def over_cols(left, right):
    return lax.dot_general(
        left, right, (((1,), (1,)), ((), ())), preferred_element_type=jnp.float32
    )


def dot32(left, right):
    return jnp.dot(left, right, preferred_element_type=F32)


def dot_nt(left, right):
    return lax.dot_general(left, right, (((1,), (1,)), ((), ())), preferred_element_type=F32)


def dot_tn(left, right):
    return lax.dot_general(left, right, (((0,), (0,)), ((), ())), preferred_element_type=F32)


def norm_in(rows, gain, bias):
    mean = jnp.mean(rows, axis=-1, keepdims=True)
    centered = rows - mean
    variance = jnp.mean(centered * centered, axis=-1, keepdims=True)
    return centered * lax.rsqrt(variance + 1e-05) * gain + bias


def sequence_starts(lens, spots):
    start = jnp.zeros_like(spots)
    end = jnp.int32(0)
    for j in range(lens.shape[1]):
        end = end + lens[0, j]
        start = jnp.where(spots >= end, jnp.maximum(start, end), start)
    return start


def attend_kernel(lens, tok, gain, bias, w_hbm, qv_bias, low_in, qw, kw, vw, att, lse,
                  w, tok_y, low_y, mask, acc, w_sem, sends, recvs):
    dp, blk = lax.axis_index("dp"), lax.axis_index("blk")
    y, c = blk // 2, blk % 2
    core_dev, y_dev = (dp, blk + 1 - 2 * c), (dp, blk + 2 - 4 * y)
    rows, width = tok.shape
    dim = width // HEADS
    half = rows // 2

    def remote(src, dst, i, dev):
        return pltpu.make_async_remote_copy(src, dst, sends.at[i], recvs.at[i], device_id=dev, device_id_type=MESH)

    n_w = 6
    wc = 3 * width // n_w
    loads = [pltpu.make_async_copy(w_hbm.at[:, pl.ds(i * wc, wc)], w.at[:, pl.ds(i * wc, wc)], w_sem.at[i]) for i in range(n_w)]
    for cp in loads:
        cp.start()
    bar = pltpu.get_barrier_semaphore()
    for dev in (core_dev, y_dev):
        pl.semaphore_signal(bar, inc=1, device_id=dev, device_id_type=MESH)
    pl.semaphore_wait(bar, 2)
    cross = [remote(tok.at[pl.ds(i * half, half)], tok_y.at[pl.ds(i * half, half)], i, y_dev) for i in range(2)]
    for cp in cross:
        cp.start()

    q_spots = blk * rows + lax.broadcasted_iota(jnp.int32, (1, rows), 1)
    starts = sequence_starts(lens, q_spots)
    k_spots = (blk - 2) * rows + lax.broadcasted_iota(jnp.int32, (3 * rows, 1), 0)
    mask[...] = jnp.where((k_spots >= starts) & (k_spots <= q_spots), 0.0, -1e30)

    low_in[...] = norm_in(tok[...].astype(F32), gain[...], bias[...]).astype(BF16)

    def project(src, r0, n, part):
        res = dot32(src[r0:r0 + n], w[:, part * width:(part + 1) * width])
        if part == 0:
            res = (res + qv_bias[:, 0:width]).astype(BF16).astype(F32) * (dim ** -0.5)
        if part == 2:
            res = res + qv_bias[:, width:]
        return res.astype(BF16)

    own_q = remote(qw.at[0], qw.at[1], 2, core_dev)
    own_k = remote(kw.at[2], kw.at[1], 3, core_dev)
    own_v = remote(vw.at[2], vw.at[1], 4, core_dev)
    relay_q = remote(qw.at[2], qw.at[1], 5, core_dev)
    relay_k = remote(kw.at[0], kw.at[1], 6, core_dev)
    relay_v = remote(vw.at[0], vw.at[1], 7, core_dev)

    for cp in loads[2:4]:
        cp.wait()
    kw[2] = project(low_in, 0, rows, 1)

    @pl.when(c == 0)
    def _():
        own_k.start()

    for cp in loads[4:6]:
        cp.wait()
    vw[2] = project(low_in, 0, rows, 2)

    @pl.when(c == 0)
    def _():
        own_v.start()

    for cp in loads[0:2]:
        cp.wait()
    qw[0] = project(low_in, 0, rows, 0)

    @pl.when(c == 1)
    def _():
        own_q.start()

    for i in range(2):
        cross[i].wait_recv()
        low_y[i * half:(i + 1) * half] = norm_in(tok_y[i * half:(i + 1) * half].astype(F32), gain[...], bias[...]).astype(BF16)

        @pl.when(y == 1)
        def _():
            kw[0, i * half:(i + 1) * half] = project(low_y, i * half, half, 1)
            vw[0, i * half:(i + 1) * half] = project(low_y, i * half, half, 2)

        @pl.when(y == 0)
        def _():
            qw[2, i * half:(i + 1) * half] = project(low_y, i * half, half, 0)

    @pl.when((y == 1) & (c == 1))
    def _():
        relay_k.start()
        relay_v.start()

    @pl.when((y == 0) & (c == 0))
    def _():
        relay_q.start()

    @pl.when(c == 1)
    def _():
        own_k.wait_recv()
        own_v.wait_recv()

    @pl.when((y == 1) & (c == 0))
    def _():
        relay_k.wait_recv()
        relay_v.wait_recv()

    def heads(first):
        def pair(i, carry):
            cols = pl.ds(pl.multiple_of(i * 2 * dim, 2 * dim), 2 * dim)
            q2 = qw[0, :, cols]
            k2 = [kw[j, :, cols] for j in range(first, 3)]
            v2 = [vw[j, :, cols] for j in range(first, 3)]
            for sub in range(2):
                part = slice(sub * dim, (sub + 1) * dim)
                scores = [dot_nt(k[:, part], q2[:, part]) + mask[(first + n) * rows:(first + n + 1) * rows]
                          for n, k in enumerate(k2)]
                top = jnp.max(scores[0], axis=0, keepdims=True)
                for s in scores[1:]:
                    top = jnp.maximum(top, jnp.max(s, axis=0, keepdims=True))
                total, out = None, None
                for s, v in zip(scores, v2):
                    p = jnp.exp(s - top)
                    one = jnp.sum(p, axis=0, keepdims=True)
                    term = dot_tn(v[:, part], p.astype(BF16))
                    total = one if total is None else total + one
                    out = term if out is None else out + term
                acc[part] = out / total
                lse[pl.ds(2 * i + sub, 1)] = top + jnp.log(total)
            att[:, cols] = acc[...].T
            return carry

        lax.fori_loop(0, HEADS // 2, pair, 0)

    @pl.when(blk == 0)
    def _():
        heads(2)

    @pl.when(blk == 1)
    def _():
        heads(1)

    @pl.when(blk >= 2)
    def _():
        heads(0)

    for cp in cross:
        cp.wait_send()

    @pl.when(c == 0)
    def _():
        own_k.wait_send()
        own_v.wait_send()
        own_q.wait_recv()

    @pl.when(c == 1)
    def _():
        own_q.wait_send()

    @pl.when((y == 1) & (c == 1))
    def _():
        relay_k.wait_send()
        relay_v.wait_send()

    @pl.when((y == 0) & (c == 0))
    def _():
        relay_q.wait_send()

    @pl.when((y == 0) & (c == 1))
    def _():
        relay_q.wait_recv()


def attend(lengths, tokens, gain, bias, w_qkv, qv_bias):
    rows, width = tokens.shape
    vmem, hbm = pl.BlockSpec(memory_space=pltpu.VMEM), pl.BlockSpec(memory_space=pl.ANY)
    window = jax.ShapeDtypeStruct((3, rows, width), BF16)
    return pl.pallas_call(
        attend_kernel,
        out_shape=[jax.ShapeDtypeStruct((rows, width), BF16), window, window, window,
                   jax.ShapeDtypeStruct((rows, width), F32), jax.ShapeDtypeStruct((HEADS, rows), F32)],
        in_specs=[pl.BlockSpec(memory_space=pltpu.SMEM), vmem, vmem, vmem, hbm, vmem],
        out_specs=[vmem] * 6,
        scratch_shapes=[pltpu.VMEM((width, 3 * width), BF16), pltpu.VMEM((rows, width), BF16), pltpu.VMEM((rows, width), BF16),
                        pltpu.VMEM((3 * rows, rows), F32), pltpu.VMEM((2 * width // HEADS, rows), F32),
                        pltpu.SemaphoreType.DMA((6,)), pltpu.SemaphoreType.DMA((8,)), pltpu.SemaphoreType.DMA((8,))],
        compiler_params=pltpu.CompilerParams(collective_id=1, has_side_effects=True, vmem_limit_bytes=56 << 20),
        cost_estimate=pl.CostEstimate(flops=8 << 30, bytes_accessed=12 << 20, transcendentals=3 << 20),
    )(lengths, tokens, gain[None], bias[None], w_qkv, qv_bias[None])


RECV = 12
PAIR0 = 4


def back_kernel(tok, a2, a1, ao, aq, b2, b1, bo, lens, qw, kw, vw, d_att, stats, w_hbm, tokens, gain, d_first, vec_in,
                out, vout, grad_tok,
                am, ap, bm, bp, s1x, s1y, s2x, s2y, sr, sl, szr, szl, szx, szy, swx, swy,
                r1x, r1y, r2x, r2y, rr, rl, rzr, rzl, rzx, rzy, rwx, rwy,
                k2x, k2y, t3, kzx, kzy, kwx, kwy, vec, vown, vrecv,
                w, dow, stw, mask, mask_q, dqa, dka, dva, d_in,
                load_sem, peer_send, peer_recv, send, recv, vsend, vrecv_sem, w_sem, asend, arecv):
    dp, blk = lax.axis_index("dp"), lax.axis_index("blk")
    z, x = dp // 2, dp % 2
    y, c = blk // 2, blk % 2
    core_dev, x_dev, y_dev = (dp, blk + 1 - 2 * c), (dp + 1 - 2 * x, blk), (dp, blk + 2 - 4 * y)
    up_dev, down_dev = (dp + 2, blk), (dp - 2, blk)
    rounds = 24
    rows, width = tokens.shape
    dim = width // HEADS

    w_load = pltpu.make_async_copy(w_hbm, w, w_sem.at[0])

    bar = pltpu.get_barrier_semaphore()
    z_devs = [((dp + 2 * k) % 8, blk) for k in range(1, 4)]
    for dev in [core_dev, x_dev, y_dev] + z_devs:
        pl.semaphore_signal(bar, inc=1, device_id=dev, device_id_type=MESH)
    pl.semaphore_wait(bar, 6)

    def remote(src, dst, ssem, rsem, dev):
        return pltpu.make_async_remote_copy(src, dst, ssem, rsem, device_id=dev, device_id_type=MESH)

    def window(kind):
        src, dst, dev = {"cross": (0, 2, y_dev), "own": (0, 1, core_dev), "relay": (2, 1, core_dev)}[kind]
        k = {"cross": 0, "own": 2, "relay": 4}[kind]
        return [remote(d_att if src == 0 else dow.at[src], dow.at[dst], asend.at[k], arecv.at[k], dev),
                remote(stats if src == 0 else stw.at[src], stw.at[dst], asend.at[k + 1], arecv.at[k + 1], dev)]

    @pl.when(y == 1)
    def _():
        for cp in window("cross"):
            cp.start()

    @pl.when(c == 1)
    def _():
        for cp in window("own"):
            cp.start()

    a_src = [(a2, g) for g in range(8)] + [(a1, 0), (a1, 1), (ao, 0), (ao, 1), (aq, 0), (aq, 1)]
    b_src = [(b2, 0)] + [(b1, i) for i in range(4)] + [(bo, 0)]
    n_a = len(a_src)

    def loads(kind, i, own):
        k = i if kind == "a" else n_a + i
        if kind == "a":
            ref, g = a_src[i]
            if own:
                return pltpu.make_async_copy(ref.at[:, :, :, c, g], am.at[i], load_sem.at[k])
            return remote(ref.at[:, :, :, 1 - c, g], ap.at[i], peer_send.at[k], peer_recv.at[k], core_dev)
        ref, g = b_src[i]
        part = ref.at[:, pl.ds(g * WR, WR)]
        if own:
            return pltpu.make_async_copy(part, bm.at[i], load_sem.at[k])
        return remote(part, bp.at[i], peer_send.at[k], peer_recv.at[k], core_dev)

    phases = [([("b", 0)] + [("a", g) for g in range(8)]),
              ([("a", 8), ("a", 9)] + [("b", i) for i in range(1, 5)]),
              ([("a", 10), ("a", 11), ("b", 5), ("a", 12), ("a", 13)])]
    for phase in phases:
        for item in phase:
            loads(*item, True).start()
            loads(*item, False).start()
    w_load.start()

    def peer_b(i):
        k = n_a + i
        return remote(bm.at[i], bp.at[i], peer_send.at[k], peer_recv.at[k], core_dev)

    def arrive(phase):
        for item in phase:
            loads(*item, True).wait()
            loads(*item, False).wait_recv()

    vec[...] = vec_in[...]
    q_spots = blk * rows + lax.broadcasted_iota(jnp.int32, (1, rows), 1)
    k_spots = (blk - 2) * rows + lax.broadcasted_iota(jnp.int32, (3 * rows, 1), 0)
    mask[...] = jnp.where((k_spots >= sequence_starts(lens, q_spots)) & (k_spots <= q_spots), 0.0, -1e30)
    q_spots = (blk + 1) * rows + lax.broadcasted_iota(jnp.int32, (1, 2 * rows), 1)
    k_spots = blk * rows + lax.broadcasted_iota(jnp.int32, (rows, 1), 0)
    mask_q[...] = jnp.where(k_spots >= sequence_starts(lens, q_spots), 0.0, -1e30)

    def place(r):
        g = jnp.where(r < 8, r, jnp.where(r < 16, 8 + r % 2, jnp.where(r < 18, 10 + r % 2, 12 + r % 2)))
        b = jnp.where(r < 8, 0, (r - 8) // 2 + 1)
        return g, b

    def product(r, zs, xs, ys, col, width):
        g, b = place(r)
        cols = pl.ds(col, width)
        la, lp = am[g, zs, xs, ys], ap[g, zs, xs, ys]
        lead = la.shape[:-1]
        m = 1
        for d in lead:
            m *= d
        res = dot32(la.reshape(m, tok), bm[b, :, cols]) + dot32(lp.reshape(m, tok), bp[b, :, cols])
        return res.reshape(lead + (width,))

    ALL = slice(None)
    col_y, col_z = WX, 2 * WX
    S1X, S1Y, S2X, S2Y, SR, SL, SZR, SZL, SZX, SZY, SWX, SWY = range(12)

    def message(src, dst, kind, dev):
        def make(r):
            return remote(src.at[r % SLOTS], dst.at[r % RECV], send.at[kind, r % SLOTS], recv.at[kind, r % RECV], dev)
        return make

    step1x, step1y = message(s1x, r1x, S1X, x_dev), message(s1y, r1y, S1Y, y_dev)
    step2x, step2y = message(s2x, r2x, S2X, y_dev), message(s2y, r2y, S2Y, x_dev)
    stepzx, stepzy = message(szx, rzx, SZX, x_dev), message(szy, rzy, SZY, y_dev)
    stepwx, stepwy = message(swx, rwx, SWX, y_dev), message(swy, rwy, SWY, x_dev)

    def chain(src, dst, kind, r, lo, hi, dev):
        return remote(src.at[r % SLOTS, lo:hi], dst.at[r % RECV, lo:hi], send.at[kind, r % SLOTS], recv.at[kind, r % RECV], dev)

    def chain_hop(hop, r, src, dst, kind_r, kind_l, term):
        slot, rslot = r % SLOTS, r % RECV

        @pl.when(z == hop)
        def _():
            if hop > 0:
                chain(src[0], dst[0], kind_r, r, hop - 1, 3, up_dev).wait_recv()
            for d in range(hop + 1, 4):
                value = term(r, d)
                if hop > 0:
                    value = value + dst[0][rslot, d - 1].astype(F32)
                src[0][slot, d - 1] = value.astype(BF16)
            chain(src[0], dst[0], kind_r, r, hop, 3, up_dev).start()

        @pl.when(z == 3 - hop)
        def _():
            if hop > 0:
                chain(src[1], dst[1], kind_l, r, 0, 4 - hop, down_dev).wait_recv()
            for d in range(0, 3 - hop):
                value = term(r, d)
                if hop > 0:
                    value = value + dst[1][rslot, d].astype(F32)
                src[1][slot, d] = value.astype(BF16)
            chain(src[1], dst[1], kind_l, r, 0, 3 - hop, down_dev).start()

    def chain_last(r, src, dst, kind_r, kind_l, total_ref):
        rslot = r % RECV
        for at in range(4):
            @pl.when(z == at)
            def _():
                if at == 3:
                    chain(src[0], dst[0], kind_r, r, 2, 3, up_dev).wait_recv()
                if at == 0:
                    chain(src[1], dst[1], kind_l, r, 0, 1, down_dev).wait_recv()
                value = None
                if at > 0:
                    value = dst[0][rslot, at - 1].astype(F32)
                if at < 3:
                    down = dst[1][rslot, at].astype(F32)
                    value = down if value is None else value + down
                total_ref[...] = value

    def chain_drain(r, src, dst, kind_r, kind_l):
        for hop in range(3):
            @pl.when(z == hop)
            def _():
                chain(src[0], dst[0], kind_r, r, hop, 3, up_dev).wait_send()

            @pl.when(z == 3 - hop)
            def _():
                chain(src[1], dst[1], kind_l, r, 0, 3 - hop, down_dev).wait_send()

    def z_term(r, d):
        return product(r, d, ALL, ALL, col_z, WZ)

    def t_term(r, d):
        return t3[r % SLOTS, d]

    zsrc, zdst = (szr, szl), (rzr, rzl)
    csrc, cdst = (sr, sl), (rr, rl)

    def p0(r):
        s1x[r % SLOTS] = product(r, ALL, 1 - x, ALL, 0, WX).astype(BF16)
        step1x(r).start()
        s1y[r % SLOTS] = product(r, ALL, ALL, 1 - y, col_y, WX).astype(BF16)
        step1y(r).start()
        chain_hop(0, r, zsrc, zdst, SZR, SZL, z_term)

    def p1(r):
        slot = r % SLOTS
        step1x(r).wait_recv()
        k2x[...] = product(r, ALL, x, ALL, 0, WX) + r1x[r % RECV].astype(F32)
        s2x[slot] = k2x[:, 1 - y].astype(BF16)
        step2x(r).start()
        kwx[slot] = k2x[:, y]
        step1y(r).wait_recv()
        k2y[...] = product(r, ALL, ALL, y, col_y, WX) + r1y[r % RECV].astype(F32)
        s2y[slot] = k2y[:, 1 - x].astype(BF16)
        step2y(r).start()
        kwy[slot] = k2y[:, x]
        chain_hop(1, r, zsrc, zdst, SZR, SZL, z_term)

    def p2(r):
        slot = r % SLOTS
        step2x(r).wait_recv()
        t3[slot, :, :, 0:WX] = kwx[slot] + r2x[r % RECV].astype(F32)
        step2y(r).wait_recv()
        t3[slot, :, :, WX:2 * WX] = kwy[slot] + r2y[r % RECV].astype(F32)
        chain_hop(0, r, csrc, cdst, SR, SL, t_term)
        chain_hop(2, r, zsrc, zdst, SZR, SZL, z_term)

    def p3(r):
        slot = r % SLOTS
        chain_hop(1, r, csrc, cdst, SR, SL, t_term)
        chain_last(r, zsrc, zdst, SZR, SZL, kzx)
        kzx[...] = kzx[...] + product(r, z, ALL, ALL, col_z, WZ)
        szx[slot] = kzx[1 - x, :, :, 0:WZ // 2].astype(BF16)
        stepzx(r).start()
        szy[slot] = kzx[:, 1 - y, :, WZ // 2:WZ].astype(BF16)
        stepzy(r).start()
        kzy[slot, 0] = kzx[x, :, :, 0:WZ // 2]
        kzy[slot, 1] = kzx[:, y, :, WZ // 2:WZ]

    def p4(r):
        slot = r % SLOTS
        chain_hop(2, r, csrc, cdst, SR, SL, t_term)
        stepzx(r).wait_recv()
        kzy[slot, 0] = kzy[slot, 0] + rzx[r % RECV].astype(F32)
        swx[slot] = kzy[slot, 0, 1 - y].astype(BF16)
        stepwx(r).start()
        stepzy(r).wait_recv()
        kzy[slot, 1] = kzy[slot, 1] + rzy[r % RECV].astype(F32)
        swy[slot] = kzy[slot, 1, 1 - x].astype(BF16)
        stepwy(r).start()

    def p5(r):
        slot = r % SLOTS
        chain_last(r, csrc, cdst, SR, SL, out.at[r, :, 0:2 * WX])
        out[r, :, 0:2 * WX] = out[r, :, 0:2 * WX] + t3[slot, z]
        stepwx(r).wait_recv()
        out[r, :, 2 * WX:2 * WX + WZ // 2] = kzy[slot, 0, y] + rwx[r % RECV].astype(F32)
        stepwy(r).wait_recv()
        out[r, :, 2 * WX + WZ // 2:] = kzy[slot, 1, x] + rwy[r % RECV].astype(F32)

    def drain(r):
        for step in (step1x, step1y, step2x, step2y, stepzx, stepzy, stepwx, stepwy):
            step(r).wait_send()
        chain_drain(r, csrc, cdst, SR, SL)
        chain_drain(r, zsrc, zdst, SZR, SZL)

    v = vec.shape[0]
    h1, h2, h3 = v // 2, v // 4, v // 8
    o1 = c * h1
    o2 = o1 + x * h2
    o3 = o2 + y * h3
    base = h1 + h2 + h3

    def vstep(i):
        if i == 0:
            return [remote(vec.at[pl.ds((1 - c) * h1, h1)], vrecv.at[pl.ds(0, h1)], vsend.at[0], vrecv_sem.at[0], core_dev)]
        if i == 1:
            return [remote(vown.at[pl.ds(o1 + (1 - x) * h2, h2)], vrecv.at[pl.ds(h1, h2)], vsend.at[1], vrecv_sem.at[1], x_dev)]
        if i == 2:
            return [remote(vown.at[pl.ds(o2 + (1 - y) * h3, h3)], vrecv.at[pl.ds(h1 + h2, h3)], vsend.at[2], vrecv_sem.at[2], y_dev)]
        if i == 3:
            return [remote(vown.at[pl.ds(o3, h3)], vrecv.at[pl.ds(base + z * h3, h3)], vsend.at[3 + k], vrecv_sem.at[3 + k],
                           z_devs[k - 1]) for k in range(1, 4)]
        if i == 4:
            return [remote(vout.at[pl.ds(o3, h3)], vout.at[pl.ds(o3, h3)], vsend.at[7], vrecv_sem.at[7], y_dev)]
        if i == 5:
            return [remote(vout.at[pl.ds(o2, h2)], vout.at[pl.ds(o2, h2)], vsend.at[8], vrecv_sem.at[8], x_dev)]
        return [remote(vout.at[pl.ds(o1, h1)], vout.at[pl.ds(o1, h1)], vsend.at[9], vrecv_sem.at[9], core_dev)]

    def vector_step(i):
        if i > 0:
            for cp in vstep(i - 1):
                cp.wait_recv()
        if i == 1:
            vown[pl.ds(o1, h1)] = vec[pl.ds(o1, h1)] + vrecv[0:h1]
        if i == 2:
            vown[pl.ds(o2, h2)] = vown[pl.ds(o2, h2)] + vrecv[h1:h1 + h2]
        if i == 3:
            vown[pl.ds(o3, h3)] = vown[pl.ds(o3, h3)] + vrecv[h1 + h2:base]
            vrecv[pl.ds(base + z * h3, h3)] = vown[pl.ds(o3, h3)]
        if i == 4:
            total = vrecv[base:base + h3]
            for k in range(1, 4):
                total = total + vrecv[base + k * h3:base + (k + 1) * h3]
            vout[pl.ds(o3, h3)] = total
        if i < 7:
            for cp in vstep(i):
                cp.start()

    def windows_arrive():
        dow[0] = d_att[...]
        stw[0] = stats[...]

        @pl.when(y == 0)
        def _():
            for cp in window("cross"):
                cp.wait_recv()

        @pl.when((y == 0) & (c == 0))
        def _():
            for cp in window("relay"):
                cp.start()

        @pl.when(c == 0)
        def _():
            for cp in window("own"):
                cp.wait_recv()

        @pl.when((y == 0) & (c == 1))
        def _():
            for cp in window("relay"):
                cp.wait_recv()

    def windows_drain():
        @pl.when(y == 1)
        def _():
            for cp in window("cross"):
                cp.wait_send()

        @pl.when(c == 1)
        def _():
            for cp in window("own"):
                cp.wait_send()

        @pl.when((y == 0) & (c == 0))
        def _():
            for cp in window("relay"):
                cp.wait_send()

    def attend_back(i):
        cols = pl.ds(pl.multiple_of(i * 2 * dim, 2 * dim), 2 * dim)

        def pairs(kj, qj, bias, to_q, to_k, first):
            k2, v2, q2, d2 = kw[kj, :, cols], vw[kj, :, cols], qw[qj, :, cols], dow[qj, :, cols]
            for sub in range(2):
                part = slice(sub * dim, (sub + 1) * dim)
                k1, v1, q1, d1 = k2[:, part], v2[:, part], q2[:, part], d2[:, part]
                log_total = stw[qj, pl.ds(2 * i + sub, 1)]
                delta = stw[qj, pl.ds(HEADS + 2 * i + sub, 1)]
                probs = jnp.exp(dot_nt(k1, q1) + bias[...] - log_total)
                low_s = (probs * (dot_nt(v1, d1) - delta)).astype(BF16)
                if to_q:
                    term = dot_tn(k1, low_s)
                    dqa[part] = term if first else dqa[part] + term
                if to_k:
                    term = dot32(low_s, q1)
                    dka[sub] = term if first else dka[sub] + term
                    term = dot32(probs.astype(BF16), d1)
                    dva[sub] = term if first else dva[sub] + term

        pairs(2, 0, mask.at[2 * rows:3 * rows], True, True, True)

        @pl.when(blk >= 1)
        def _():
            pairs(1, 0, mask.at[rows:2 * rows], True, False, False)

        @pl.when(blk >= 2)
        def _():
            pairs(0, 0, mask.at[0:rows], True, False, False)

        @pl.when(blk <= 2)
        def _():
            pairs(2, 1, mask_q.at[:, 0:rows], False, True, False)

        @pl.when(blk <= 1)
        def _():
            pairs(2, 2, mask_q.at[:, rows:2 * rows], False, True, False)

        bm[6, :, cols] = (dqa[...].T * (dim ** -0.5)).astype(BF16)
        bm[7, :, cols] = jnp.concatenate([dka[0], dka[1]], axis=1).astype(BF16)
        bm[8, :, cols] = jnp.concatenate([dva[0], dva[1]], axis=1).astype(BF16)

    def put_row(first, row):
        for k in range(row.shape[1] // 128):
            vec[first + k:first + k + 1, :] = row[:, k * 128:(k + 1) * 128]

    def input_back():
        for i in range(6, 9):
            peer_b(i).start()
        w_load.wait()
        d_in[...] = dot_nt(bm[6], w[:, 0:width])
        d_in[...] = d_in[...] + dot_nt(bm[7], w[:, width:2 * width])
        grad = d_in[...] + dot_nt(bm[8], w[:, 2 * width:])
        rows_in = tokens[...].astype(F32)
        centered = rows_in - jnp.mean(rows_in, axis=-1, keepdims=True)
        scale = lax.rsqrt(jnp.mean(centered * centered, axis=-1, keepdims=True) + 1e-05)
        normed = centered * scale
        put_row(0, jnp.sum(grad * normed, axis=0, keepdims=True))
        put_row(width // 128, jnp.sum(grad, axis=0, keepdims=True))
        put_row(2 * width // 128, jnp.sum(bm[6].astype(F32), axis=0, keepdims=True))
        put_row(3 * width // 128, jnp.sum(bm[8].astype(F32), axis=0, keepdims=True))
        grad = grad * gain[...]
        grad = grad - jnp.mean(grad, axis=-1, keepdims=True) - normed * jnp.mean(grad * normed, axis=-1, keepdims=True)
        grad_tok[...] = d_first[...] + scale * grad

    phase_list = (p0, p1, p2, p3, p4, p5)
    lags = (0, 2, 4, 5, 6, 7)
    n_pairs = HEADS // 2
    after = PAIR0 + n_pairs

    def slot_step(s, carry):
        for k in (5, 4, 3, 2, 1):
            r = s - lags[k]

            @pl.when((r >= 0) & (r < rounds))
            def _():
                phase_list[k](r)

        for at, phase in ((0, 0), (7, 1), (15, 2)):
            @pl.when(s == at)
            def _():
                arrive(phases[phase])

        @pl.when(s == 17)
        def _():
            for i in range(6, 9):
                peer_b(i).wait_recv()

        @pl.when((s >= SLOTS) & (s < rounds))
        def _():
            drain(s - SLOTS)

        @pl.when(s < rounds)
        def _():
            p0(s)

        @pl.when(s == PAIR0)
        def _():
            windows_arrive()

        @pl.when((s >= PAIR0) & (s < after))
        def _():
            attend_back(s - PAIR0)

        @pl.when(s == after)
        def _():
            input_back()

        for i in range(8):
            @pl.when(s == after + i)
            def _():
                vector_step(i)

        return carry

    lax.fori_loop(0, rounds + lags[5], slot_step, 0)
    lax.fori_loop(rounds - SLOTS, rounds, lambda r, carry: (drain(r), carry)[1], 0)
    windows_drain()
    for phase in phases:
        for item in phase:
            loads(*item, False).wait_send()
    for i in range(6, 9):
        peer_b(i).wait_send()
    for i in range(7):
        for cp in vstep(i):
            cp.wait_send()


def rows_first(act, rows_block):
    tok = act.shape[0]
    return act.T.reshape(4, 2, 2, 2, rows_block // ROWS, ROWS, tok)


def backward(low_ffn, cot, low_mid, low_pre, scaled, low_attn, low_in, lengths, q_win, k_win, v_win, d_att, stats,
             w_qkv, tokens, gain, d_first, vec):
    tok, width = tokens.shape
    rounds = 24
    hbm, vmem = pl.BlockSpec(memory_space=pl.ANY), pl.BlockSpec(memory_space=pltpu.VMEM)
    a_shape = (14, 4, 2, 2, ROWS, tok)
    b_shape = (9, tok, WR)
    msgs = [(4, 2, ROWS, WX), (4, 2, ROWS, WX), (4, ROWS, WX), (4, ROWS, WX), (3, ROWS, 2 * WX), (3, ROWS, 2 * WX),
            (3, 2, 2, ROWS, WZ), (3, 2, 2, ROWS, WZ), (2, ROWS, WZ // 2), (2, ROWS, WZ // 2), (ROWS, WZ // 2), (ROWS, WZ // 2)]
    v = vec.shape[0]
    dma = pltpu.SemaphoreType.DMA
    return pl.pallas_call(
        functools.partial(back_kernel, tok),
        out_shape=[jax.ShapeDtypeStruct((rounds, ROWS, WR), F32), jax.ShapeDtypeStruct(vec.shape, F32),
                   jax.ShapeDtypeStruct(tokens.shape, F32)],
        in_specs=[hbm] * 7 + [pl.BlockSpec(memory_space=pltpu.SMEM)] + [vmem] * 5 + [hbm] + [vmem] * 4,
        out_specs=[vmem] * 3,
        scratch_shapes=[pltpu.VMEM(a_shape, BF16), pltpu.VMEM(a_shape, BF16), pltpu.VMEM(b_shape, BF16), pltpu.VMEM(b_shape, BF16)]
        + [pltpu.VMEM((SLOTS,) + m, BF16) for m in msgs]
        + [pltpu.VMEM((RECV,) + m, BF16) for m in msgs]
        + [pltpu.VMEM((4, 2, ROWS, WX), F32), pltpu.VMEM((4, 2, ROWS, WX), F32), pltpu.VMEM((SLOTS, 4, ROWS, 2 * WX), F32),
           pltpu.VMEM((2, 2, ROWS, WZ), F32), pltpu.VMEM((SLOTS, 2, 2, ROWS, WZ // 2), F32),
           pltpu.VMEM((SLOTS, 4, ROWS, WX), F32), pltpu.VMEM((SLOTS, 4, ROWS, WX), F32),
           pltpu.VMEM((v, 128), F32), pltpu.VMEM((v, 128), F32), pltpu.VMEM((v // 2 + v // 4 + v // 8 * 5, 128), F32),
           pltpu.VMEM((width, 3 * width), BF16), pltpu.VMEM((3, tok, width), BF16), pltpu.VMEM((3, 2 * HEADS, tok), F32),
           pltpu.VMEM((3 * tok, tok), F32), pltpu.VMEM((tok, 2 * tok), F32),
           pltpu.VMEM((2 * width // HEADS, tok), F32), pltpu.VMEM((2, tok, width // HEADS), F32),
           pltpu.VMEM((2, tok, width // HEADS), F32), pltpu.VMEM((tok, width), F32),
           dma((20,)), dma((23,)), dma((23,)), dma((12, SLOTS)), dma((12, RECV)), dma((10,)), dma((10,)), dma((1,)), dma((6,)), dma((6,))],
        compiler_params=pltpu.CompilerParams(collective_id=0, has_side_effects=True, vmem_limit_bytes=62 << 20),
        cost_estimate=pl.CostEstimate(flops=20 << 30, bytes_accessed=30 << 20, transcendentals=4 << 20),
    )(rows_first(low_ffn, 128), rows_first(low_mid, 32), rows_first(scaled, 32), rows_first(low_in, 32),
      cot, low_pre, low_attn, lengths, q_win, k_win, v_win, d_att, stats, w_qkv, tokens, gain[None], d_first, vec)


def fast_shards(
    tokens, lengths, ln1_gain, ln1_bias, w_qkv, qv_bias, head_scale, w_out, out_bias, lnpa_gain, lnpa_bias,
    ln2_gain, ln2_bias, w_fc1, fc1_bias, lnf_gain, lnf_bias, w_fc2, fc2_bias, cotangent,
):
    row_count, width = tokens.shape
    head_dim = width // HEADS
    inputs = tokens.astype(F32)
    low_in, q_win, k_win, v_win, attended, log_total = attend(lengths, tokens, ln1_gain, ln1_bias, w_qkv, qv_bias)
    head_gain = jnp.repeat(head_scale, head_dim)
    scaled = (attended * head_gain).astype(BF16)
    attn_out = dot32(scaled, w_out) + out_bias
    branch, pa_back = jax.vjp(norm_rows, attn_out, lnpa_gain, lnpa_bias)
    first_sum = inputs + branch
    normed_mid, ln2_back = jax.vjp(norm_rows, first_sum, ln2_gain, ln2_bias)
    low_mid = normed_mid.astype(BF16)
    pre_act = dot32(low_mid, w_fc1) + fc1_bias
    activated, gelu_back = jax.vjp(gelu_exact, pre_act)
    ffn_normed, lnf_back = jax.vjp(norm_rows, activated, lnf_gain, lnf_bias)
    low_ffn = ffn_normed.astype(BF16)
    layer_out = (first_sum + dot32(low_ffn, w_fc2) + fc2_bias).astype(BF16)
    d_output = cotangent.astype(F32)
    grad_c2 = jnp.sum(d_output, axis=0)
    d_ffn = over_cols(cotangent, w_fc2)
    d_active, grad_lnf_gain, grad_lnf_bias = lnf_back(d_ffn)
    (d_pre,) = gelu_back(d_active)
    low_pre = d_pre.astype(BF16)
    grad_c1 = jnp.sum(low_pre.astype(F32), axis=0)
    d_mid = over_cols(low_pre, w_fc1)
    d_first_norm, grad_ln2_gain, grad_ln2_bias = ln2_back(d_mid)
    d_first = d_output + d_first_norm
    d_attn, grad_pa_gain, grad_pa_bias = pa_back(d_first)
    low_attn = d_attn.astype(BF16)
    grad_bo = jnp.sum(low_attn.astype(F32), axis=0)
    d_scaled = over_cols(low_attn, w_out)
    grad_hs = jnp.sum((d_scaled * attended).reshape(row_count, HEADS, head_dim), axis=(0, 2))
    d_attended = (d_scaled * head_gain).astype(BF16)
    delta = jnp.sum((d_attended.astype(F32) * attended).reshape(row_count, HEADS, head_dim), axis=-1).T
    stats = jnp.concatenate([log_total, delta], axis=0)
    vectors = (grad_bo, grad_pa_gain, grad_pa_bias, grad_ln2_gain, grad_ln2_bias, grad_c1, grad_lnf_gain, grad_lnf_bias,
               grad_c2, grad_hs)
    flat = jnp.concatenate((jnp.zeros((4 * width,), F32),) + vectors)
    flat = jnp.pad(flat, (0, 192 * 128 - flat.shape[0])).reshape(192, 128)
    out, flat, grad_tokens = backward(
        low_ffn, cotangent, low_mid, low_pre, scaled, low_attn, low_in, lengths, q_win, k_win, v_win, d_attended, stats,
        w_qkv, tokens, ln1_gain, d_first, flat)
    share_w2 = out[:8].reshape(128, WR)
    share_w1 = out[8:16].reshape(4, 32, WR).transpose(1, 0, 2).reshape(32, 4 * WR)
    share_wo = out[16:18].reshape(32, WR)
    share_wqkv = out[18:24].reshape(3, 32, WR).transpose(1, 0, 2).reshape(32, 3 * WR)
    flat = flat.reshape(-1)
    sizes = (width, width, 2 * width) + tuple(item.shape[0] for item in vectors)
    starts = [sum(sizes[:i]) for i in range(len(sizes))]
    ln1g, ln1b, qv, bo, pag, pab, ln2g, ln2b, c1, lnfg, lnfb, c2, hs = (
        lax.slice(flat, (start,), (start + size,)) for start, size in zip(starts, sizes))
    return (layer_out, grad_tokens, ln1g, ln1b, share_wqkv, qv, hs, share_wo, bo, pag, pab, ln2g, ln2b, share_w1, c1,
            lnfg, lnfb, share_w2, c2)


def shards(
    tokens,
    lengths,
    ln1_gain,
    ln1_bias,
    w_qkv,
    qv_bias,
    head_scale,
    w_out,
    out_bias,
    lnpa_gain,
    lnpa_bias,
    ln2_gain,
    ln2_bias,
    w_fc1,
    fc1_bias,
    lnf_gain,
    lnf_bias,
    w_fc2,
    fc2_bias,
    cotangent,
):
    row_count, width = tokens.shape
    head_dim = width // HEADS
    factor = head_dim ** (-0.5)
    group = row_count * lax.axis_size("blk")
    own_start = lax.axis_index("blk") * row_count
    seq_ends = jnp.cumsum(lengths[0])
    positions = jnp.arange(group, dtype=jnp.int32)
    labels = jnp.sum((positions[:, None] >= seq_ends[None, :]).astype(jnp.int32), axis=1)
    q_labels = lax.dynamic_slice_in_dim(labels, own_start, row_count, 0)
    q_spots = own_start + jnp.arange(row_count, dtype=jnp.int32)
    inputs = tokens.astype(jnp.float32)
    normed_in, ln1_back = jax.vjp(norm_rows, inputs, ln1_gain, ln1_bias)
    low_in = normed_in.astype(jnp.bfloat16)
    projected = jnp.dot(low_in, w_qkv, preferred_element_type=jnp.float32)
    queries = (projected[:, :width] + qv_bias[:width]).astype(jnp.bfloat16)
    key_rows = projected[:, width : 2 * width].astype(jnp.bfloat16)
    value_rows = (projected[:, 2 * width :] + qv_bias[width:]).astype(jnp.bfloat16)
    query_heads = queries.reshape(row_count, HEADS, head_dim)

    def scored(key_block, start):
        count = key_block.shape[0]
        key_heads = key_block.reshape(count, HEADS, head_dim)
        raw_scores = (
            jnp.einsum("qhd,khd->hqk", query_heads, key_heads, preferred_element_type=jnp.float32)
            * factor
        )
        k_labels = lax.dynamic_slice_in_dim(labels, start, count, 0)
        k_spots = start + jnp.arange(count, dtype=jnp.int32)
        visible = (k_labels[None, :] == q_labels[:, None]) & (k_spots[None, :] <= q_spots[:, None])
        return (raw_scores, visible[None], key_heads)

    def by_blocks(step_fn, carry, pieces):
        count = pieces[0].shape[0]
        unit = max(1, 1024 // row_count) * row_count
        step = count if count <= unit else math.gcd(count, unit)

        def inner(block_index, state):
            offset = block_index * step
            sub_pieces = tuple((lax.dynamic_slice_in_dim(item, offset, step, 0) for item in pieces))
            return step_fn(state, sub_pieces, offset)

        return lax.fori_loop(0, count // step, inner, carry)

    def max_step(carry, pieces, start):
        top_score, totals = carry
        raw_scores, visible, key_heads = scored(pieces[0], start)
        raw_scores = jnp.where(visible, raw_scores, -1e30)
        new_top = jnp.maximum(top_score, jnp.max(raw_scores, axis=-1))
        totals = totals * jnp.exp(top_score - new_top) + jnp.sum(
            jnp.where(visible, jnp.exp(raw_scores - new_top[..., None]), 0.0), axis=-1
        )
        return (new_top, totals)

    start_top = jnp.full((HEADS, row_count), -1e30, jnp.float32)
    start_total = jnp.zeros((HEADS, row_count), jnp.float32)
    top_score, totals = by_blocks(
        max_step, (start_top, start_total), (lax.all_gather(key_rows, "blk", axis=0, tiled=True),)
    )
    log_total = top_score + jnp.log(totals)

    def value_step(carry, pieces, start):
        weighted, leftover = carry
        raw_scores, visible, key_heads = scored(pieces[0], start)
        value_heads = pieces[1].reshape(pieces[1].shape[0], HEADS, head_dim)
        probs = jnp.where(visible, jnp.exp(raw_scores - log_total[..., None]), 0.0)
        low_probs = probs.astype(jnp.bfloat16)
        rest_probs = (probs - low_probs.astype(jnp.float32)).astype(jnp.bfloat16)
        weighted = weighted + jnp.einsum(
            "hqk,khd->qhd", low_probs, value_heads, preferred_element_type=jnp.float32
        )
        leftover = leftover + jnp.einsum(
            "hqk,khd->qhd", rest_probs, value_heads, preferred_element_type=jnp.float32
        )
        return (weighted, leftover)

    empty_heads = jnp.zeros((row_count, HEADS, head_dim), jnp.float32)
    weighted, leftover = by_blocks(
        value_step,
        (empty_heads, empty_heads),
        (
            lax.all_gather(key_rows, "blk", axis=0, tiled=True),
            lax.all_gather(value_rows, "blk", axis=0, tiled=True),
        ),
    )
    attended = weighted.reshape(row_count, width)
    head_gain = jnp.repeat(head_scale, head_dim)
    scaled = (attended * head_gain).astype(jnp.bfloat16)
    attn_out = jnp.dot(scaled, w_out, preferred_element_type=jnp.float32) + out_bias
    branch, pa_back = jax.vjp(norm_rows, attn_out, lnpa_gain, lnpa_bias)
    first_sum = inputs + branch
    normed_mid, ln2_back = jax.vjp(norm_rows, first_sum, ln2_gain, ln2_bias)
    low_mid = normed_mid.astype(jnp.bfloat16)
    pre_act = jnp.dot(low_mid, w_fc1, preferred_element_type=jnp.float32) + fc1_bias
    activated, gelu_back = jax.vjp(gelu_exact, pre_act)
    ffn_normed, lnf_back = jax.vjp(norm_rows, activated, lnf_gain, lnf_bias)
    low_ffn = ffn_normed.astype(jnp.bfloat16)
    layer_out = (
        first_sum + jnp.dot(low_ffn, w_fc2, preferred_element_type=jnp.float32) + fc2_bias
    ).astype(jnp.bfloat16)
    d_output = cotangent.astype(jnp.float32)
    grad_w2 = over_rows(low_ffn, cotangent)
    grad_c2 = jnp.sum(d_output, axis=0)
    d_ffn = over_cols(cotangent, w_fc2)
    d_active, grad_lnf_gain, grad_lnf_bias = lnf_back(d_ffn)
    (d_pre,) = gelu_back(d_active)
    low_pre = d_pre.astype(jnp.bfloat16)
    grad_w1 = over_rows(low_mid, low_pre)
    grad_c1 = jnp.sum(low_pre.astype(jnp.float32), axis=0)
    d_mid = over_cols(low_pre, w_fc1)
    d_first_norm, grad_ln2_gain, grad_ln2_bias = ln2_back(d_mid)
    d_first = d_output + d_first_norm
    d_attn, grad_pa_gain, grad_pa_bias = pa_back(d_first)
    low_attn = d_attn.astype(jnp.bfloat16)
    grad_bo = jnp.sum(low_attn.astype(jnp.float32), axis=0)
    grad_wo = over_rows(scaled, low_attn)
    d_scaled = over_cols(low_attn, w_out)
    grad_hs = jnp.sum((d_scaled * attended).reshape(row_count, HEADS, head_dim), axis=(0, 2))
    d_attended = (d_scaled * head_gain).astype(jnp.bfloat16)
    d_heads = d_attended.reshape(row_count, HEADS, head_dim)
    delta_rows = jnp.sum(d_heads.astype(jnp.float32) * (weighted + leftover), axis=-1)
    delta = delta_rows.T

    def back_step(carry, pieces, start):
        count = pieces[0].shape[0]
        raw_scores, visible, key_heads = scored(pieces[0], start)
        value_heads = pieces[1].reshape(count, HEADS, head_dim)
        probs = jnp.where(visible, jnp.exp(raw_scores - log_total[..., None]), 0.0)
        d_probs = jnp.einsum(
            "qhd,khd->hqk", d_heads, value_heads, preferred_element_type=jnp.float32
        )
        d_scores = (probs * (d_probs - delta[..., None])).astype(jnp.bfloat16)
        d_query = (
            carry[0]
            + jnp.einsum("hqk,khd->qhd", d_scores, key_heads, preferred_element_type=jnp.float32)
            * factor
        )
        key_grad, value_grad = (carry[1], carry[2])
        low_probs = probs.astype(jnp.bfloat16)
        d_value = jnp.einsum(
            "hqk,qhd->khd", low_probs, d_heads, preferred_element_type=jnp.float32
        ).reshape(count, width)
        d_key = (
            jnp.einsum("hqk,qhd->khd", d_scores, query_heads, preferred_element_type=jnp.float32)
            * factor
        ).reshape(count, width)
        key_grad = lax.dynamic_update_slice_in_dim(
            key_grad, lax.dynamic_slice_in_dim(key_grad, start, count, 0) + d_key, start, 0
        )
        value_grad = lax.dynamic_update_slice_in_dim(
            value_grad, lax.dynamic_slice_in_dim(value_grad, start, count, 0) + d_value, start, 0
        )
        return (d_query, key_grad, value_grad)

    empty_group = jnp.zeros((group, width), jnp.float32)
    start_carry = (empty_heads, empty_group, empty_group)
    results = by_blocks(
        back_step,
        start_carry,
        (
            lax.all_gather(key_rows, "blk", axis=0, tiled=True),
            lax.all_gather(value_rows, "blk", axis=0, tiled=True),
        ),
    )
    d_query = results[0]
    own_keys, own_values = (
        lax.psum_scatter(
            results[1].astype(jnp.bfloat16), "blk", scatter_dimension=0, tiled=True
        ).astype(jnp.float32),
        lax.psum_scatter(
            results[2].astype(jnp.bfloat16), "blk", scatter_dimension=0, tiled=True
        ).astype(jnp.float32),
    )
    low_q = d_query.reshape(row_count, width).astype(jnp.bfloat16)
    low_k = own_keys.astype(jnp.bfloat16)
    low_v = own_values.astype(jnp.bfloat16)
    d_projected = jnp.concatenate([low_q, low_k, low_v], axis=1)
    grad_wqkv = over_rows(low_in, d_projected)
    grad_qv = jnp.concatenate(
        [jnp.sum(low_q.astype(jnp.float32), axis=0), jnp.sum(low_v.astype(jnp.float32), axis=0)]
    )
    d_in = over_cols(d_projected, w_qkv)
    d_in_norm, grad_ln1_gain, grad_ln1_bias = ln1_back(d_in)
    grad_tokens = d_first + d_in_norm
    share_wqkv, share_wo, share_w1, share_w2 = (
        lax.psum_scatter(grad_wqkv, ("dp", "blk"), scatter_dimension=0, tiled=True),
        lax.psum_scatter(grad_wo, ("dp", "blk"), scatter_dimension=0, tiled=True),
        lax.psum_scatter(grad_w1, ("dp", "blk"), scatter_dimension=0, tiled=True),
        lax.psum_scatter(grad_w2, ("dp", "blk"), scatter_dimension=0, tiled=True),
    )
    summed = lax.psum(
        (
            grad_ln1_gain,
            grad_ln1_bias,
            grad_qv,
            grad_hs,
            grad_bo,
            grad_pa_gain,
            grad_pa_bias,
            grad_ln2_gain,
            grad_ln2_bias,
            grad_c1,
            grad_lnf_gain,
            grad_lnf_bias,
            grad_c2,
        ),
        ("dp", "blk"),
    )
    return (
        layer_out,
        grad_tokens,
        summed[0],
        summed[1],
        share_wqkv,
        summed[2],
        summed[3],
        share_wo,
        summed[4],
        summed[5],
        summed[6],
        summed[7],
        summed[8],
        share_w1,
        summed[9],
        summed[10],
        summed[11],
        share_w2,
        summed[12],
    )


def solution(mesh):
    in_specs = (
        P(("dp", "blk"), None),
        P("dp", None),
        P(),
        P(),
        P(),
        P(),
        P(),
        P(),
        P(),
        P(),
        P(),
        P(),
        P(),
        P(),
        P(),
        P(),
        P(),
        P(),
        P(),
        P(("dp", "blk"), None),
    )
    out_specs = (
        P(("dp", "blk"), None),
        P(("dp", "blk"), None),
        P(),
        P(),
        P(("dp", "blk"), None),
        P(),
        P(),
        P(("dp", "blk"), None),
        P(),
        P(),
        P(),
        P(),
        P(),
        P(("dp", "blk"), None),
        P(),
        P(),
        P(),
        P(("dp", "blk"), None),
        P(),
    )
    body = fast_shards if dict(mesh.shape) == {"dp": 8, "blk": 4} else shards
    return jax.shard_map(body, mesh=mesh, in_specs=in_specs, out_specs=out_specs, check_vma=False)
```

```python
import functools
import math

import jax
import jax.numpy as jnp
from jax import lax
from jax.experimental import pallas as pl
from jax.experimental.pallas import tpu as pltpu
from jax.sharding import PartitionSpec as P

HEADS = 16
MESH = pl.DeviceIdType.MESH
F32, BF16 = jnp.float32, jnp.bfloat16
WX = 384
WZ = 256
WR = 2 * WX + WZ
ROWS = 16


def norm_rows(values_in, gain_vec, bias_vec):
    row_mean = jnp.mean(values_in, axis=-1, keepdims=True)
    centered = values_in - row_mean
    variance = jnp.mean(centered * centered, axis=-1, keepdims=True)
    return centered * lax.rsqrt(variance + 1e-05) * gain_vec + bias_vec


def gelu_exact(pre_values):
    return 0.5 * pre_values * (1.0 + lax.erf(pre_values * 0.7071067811865476))


def over_rows(left, right):
    return lax.dot_general(
        left, right, (((0,), (0,)), ((), ())), preferred_element_type=jnp.float32
    )


def over_cols(left, right):
    return lax.dot_general(
        left, right, (((1,), (1,)), ((), ())), preferred_element_type=jnp.float32
    )


def dot32(left, right):
    return jnp.dot(left, right, preferred_element_type=F32)


def dot_nt(left, right):
    return lax.dot_general(left, right, (((1,), (1,)), ((), ())), preferred_element_type=F32)


def dot_tn(left, right):
    return lax.dot_general(left, right, (((0,), (0,)), ((), ())), preferred_element_type=F32)


def norm_in(rows, gain, bias):
    mean = jnp.mean(rows, axis=-1, keepdims=True)
    centered = rows - mean
    variance = jnp.mean(centered * centered, axis=-1, keepdims=True)
    return centered * lax.rsqrt(variance + 1e-05) * gain + bias


def sequence_starts(lens, spots):
    start = jnp.zeros_like(spots)
    end = jnp.int32(0)
    for j in range(lens.shape[1]):
        end = end + lens[0, j]
        start = jnp.where(spots >= end, jnp.maximum(start, end), start)
    return start


def lane_sums(values):
    total = values[:, 0:128]
    for k in range(1, values.shape[1] // 128):
        total = total + values[:, k * 128:(k + 1) * 128]
    return total


FC = 512


def forward_kernel(lens, tok, gain, bias, w_hbm, qv_bias, head_gain, wo_hbm, out_bias, pa_gain, pa_bias, mid_gain, mid_bias,
                   w1_hbm, fc1_bias, ffn_gain, ffn_bias,
                   low_in_t, qw_out, kw_out, vw_out, att_out, lse, scaled_t, attn_out, first_out, low_mid_t, normed_out, slope_out,
                   scale_out, low_ffn_out, low_ffn_t,
                   w, wo, w1, tok_y, low_in, low_y, qw, kw, vw, mask, acc, att, attn, first, low_mid, act, part, turned, normed,
                   slope, low_ffn, ffn_turned, w_sem, sends, recvs, out_sem):
    dp, blk = lax.axis_index("dp"), lax.axis_index("blk")
    y, c = blk // 2, blk % 2
    core_dev, y_dev = (dp, blk + 1 - 2 * c), (dp, blk + 2 - 4 * y)
    rows, width = tok.shape
    dim = width // HEADS
    half = rows // 2
    ff = w1.shape[1]
    n_ff = ff // FC

    def remote(src, dst, i, dev):
        return pltpu.make_async_remote_copy(src, dst, sends.at[i], recvs.at[i], device_id=dev, device_id_type=MESH)

    n_w = 6
    wc = 3 * width // n_w
    loads = [pltpu.make_async_copy(w_hbm.at[:, pl.ds(i * wc, wc)], w.at[:, pl.ds(i * wc, wc)], w_sem.at[i]) for i in range(n_w)]
    loads.append(pltpu.make_async_copy(wo_hbm, wo, w_sem.at[6]))
    loads.append(pltpu.make_async_copy(w1_hbm, w1, w_sem.at[7]))
    for i in (2, 3, 4, 5, 0, 1, 6, 7):
        loads[i].start()
    bar = pltpu.get_barrier_semaphore()
    for dev in (core_dev, y_dev):
        pl.semaphore_signal(bar, inc=1, device_id=dev, device_id_type=MESH)
    pl.semaphore_wait(bar, 2)
    cross = [remote(tok.at[pl.ds(i * half, half)], tok_y.at[pl.ds(i * half, half)], i, y_dev) for i in range(2)]
    for cp in cross:
        cp.start()

    outs = []

    def emit(src, dst):
        cp = pltpu.make_async_copy(src, dst, out_sem.at[len(outs)])
        cp.start()
        outs.append(cp)

    q_spots = blk * rows + lax.broadcasted_iota(jnp.int32, (1, rows), 1)
    starts = sequence_starts(lens, q_spots)
    k_spots = (blk - 2) * rows + lax.broadcasted_iota(jnp.int32, (3 * rows, 1), 0)
    mask[...] = jnp.where((k_spots >= starts) & (k_spots <= q_spots), 0.0, -1e30)

    low_in[...] = norm_in(tok[...].astype(F32), gain[...], bias[...]).astype(BF16)

    def project(src, r0, n, which):
        res = dot32(src[r0:r0 + n], w[:, which * width:(which + 1) * width])
        if which == 0:
            res = (res + qv_bias[:, 0:width]).astype(BF16).astype(F32) * (dim ** -0.5)
        if which == 2:
            res = res + qv_bias[:, width:]
        return res.astype(BF16)

    own_q = remote(qw.at[0], qw.at[1], 2, core_dev)
    own_k = remote(kw.at[2], kw.at[1], 3, core_dev)
    own_v = remote(vw.at[2], vw.at[1], 4, core_dev)
    relay_q = remote(qw.at[2], qw.at[1], 5, core_dev)
    relay_k = remote(kw.at[0], kw.at[1], 6, core_dev)
    relay_v = remote(vw.at[0], vw.at[1], 7, core_dev)

    for cp in loads[2:4]:
        cp.wait()
    kw[2] = project(low_in, 0, rows, 1)

    @pl.when(c == 0)
    def _():
        own_k.start()

    for cp in loads[4:6]:
        cp.wait()
    vw[2] = project(low_in, 0, rows, 2)

    @pl.when(c == 0)
    def _():
        own_v.start()

    for cp in loads[0:2]:
        cp.wait()
    qw[0] = project(low_in, 0, rows, 0)

    @pl.when(c == 1)
    def _():
        own_q.start()

    turned[0] = low_in[...].T
    emit(turned.at[0], low_in_t)

    for i in range(2):
        cross[i].wait_recv()
        low_y[i * half:(i + 1) * half] = norm_in(tok_y[i * half:(i + 1) * half].astype(F32), gain[...], bias[...]).astype(BF16)

        @pl.when(y == 1)
        def _():
            kw[0, i * half:(i + 1) * half] = project(low_y, i * half, half, 1)
            vw[0, i * half:(i + 1) * half] = project(low_y, i * half, half, 2)

        @pl.when(y == 0)
        def _():
            qw[2, i * half:(i + 1) * half] = project(low_y, i * half, half, 0)

    @pl.when((y == 1) & (c == 1))
    def _():
        relay_k.start()
        relay_v.start()

    @pl.when((y == 0) & (c == 0))
    def _():
        relay_q.start()

    @pl.when(c == 1)
    def _():
        own_k.wait_recv()
        own_v.wait_recv()

    @pl.when((y == 1) & (c == 0))
    def _():
        relay_k.wait_recv()
        relay_v.wait_recv()

    emit(kw, kw_out)
    emit(vw, vw_out)

    def heads(lowest):
        def pair(i, carry):
            cols = pl.ds(pl.multiple_of(i * 2 * dim, 2 * dim), 2 * dim)
            q2 = qw[0, :, cols]
            k2 = [kw[j, :, cols] for j in range(lowest, 3)]
            v2 = [vw[j, :, cols] for j in range(lowest, 3)]
            for sub in range(2):
                one_head = slice(sub * dim, (sub + 1) * dim)
                scores = [dot_nt(k[:, one_head], q2[:, one_head]) + mask[(lowest + n) * rows:(lowest + n + 1) * rows]
                          for n, k in enumerate(k2)]
                top = jnp.max(scores[0], axis=0, keepdims=True)
                for s in scores[1:]:
                    top = jnp.maximum(top, jnp.max(s, axis=0, keepdims=True))
                total, out = None, None
                for s, v in zip(scores, v2):
                    p = jnp.exp(s - top)
                    one = jnp.sum(p, axis=0, keepdims=True)
                    term = dot_tn(v[:, one_head], p.astype(BF16))
                    total = one if total is None else total + one
                    out = term if out is None else out + term
                acc[one_head] = out / total
                lse[pl.ds(2 * i + sub, 1)] = top + jnp.log(total)
            att[:, cols] = acc[...].T
            return carry

        lax.fori_loop(0, HEADS // 2, pair, 0)

    @pl.when(blk == 0)
    def _():
        heads(2)

    @pl.when(blk == 1)
    def _():
        heads(1)

    @pl.when(blk >= 2)
    def _():
        heads(0)

    @pl.when(c == 0)
    def _():
        own_q.wait_recv()

    @pl.when((y == 0) & (c == 1))
    def _():
        relay_q.wait_recv()

    emit(qw, qw_out)
    emit(att, att_out)

    scaled = (att[...] * head_gain[...]).astype(BF16)
    loads[6].wait()
    attn[...] = dot32(scaled, wo[...]) + out_bias[...]
    emit(attn, attn_out)
    first[...] = tok[...].astype(F32) + norm_in(attn[...], pa_gain[...], pa_bias[...])
    emit(first, first_out)
    low_mid[...] = norm_in(first[...], mid_gain[...], mid_bias[...]).astype(BF16)
    loads[7].wait()
    part[...] = jnp.zeros_like(part)

    def ffn_cols(j):
        return pl.ds(pl.multiple_of(j * FC, FC), FC)

    def gelu_part(j, carry):
        cols = ffn_cols(j)
        pre = dot32(low_mid[...], w1[:, cols]) + fc1_bias[:, cols]
        gate = 0.5 * (1.0 + lax.erf(pre * 0.7071067811865476))
        out = pre * gate
        act[:, cols] = out
        slope[:, cols] = (gate + pre * (jnp.exp(-0.5 * (pre * pre)) * 0.3989422804014327)).astype(BF16)
        part[0] = part[0] + lane_sums(out)
        return carry

    lax.fori_loop(0, n_ff, gelu_part, 0)
    emit(slope, slope_out)
    mean = jnp.sum(part[0], axis=-1, keepdims=True) * (1.0 / ff)

    def spread_part(j, carry):
        centered = act[:, ffn_cols(j)] - mean
        part[1] = part[1] + lane_sums(centered * centered)
        return carry

    lax.fori_loop(0, n_ff, spread_part, 0)
    scale = lax.rsqrt(jnp.sum(part[1], axis=-1, keepdims=True) * (1.0 / ff) + 1e-05)
    scale_out[...] = jnp.broadcast_to(scale, scale_out.shape)

    def norm_part(j, carry):
        cols = ffn_cols(j)
        unit = (act[:, cols] - mean) * scale
        normed[:, cols] = unit.astype(BF16)
        low = (unit * ffn_gain[:, cols] + ffn_bias[:, cols]).astype(BF16)
        low_ffn[:, cols] = low
        ffn_turned[cols] = low.T
        return carry

    lax.fori_loop(0, n_ff, norm_part, 0)
    emit(normed, normed_out)
    emit(low_ffn, low_ffn_out)
    emit(ffn_turned, low_ffn_t)
    turned[1] = scaled.T
    emit(turned.at[1], scaled_t)
    turned[2] = low_mid[...].T
    emit(turned.at[2], low_mid_t)

    for cp in cross:
        cp.wait_send()

    @pl.when(c == 0)
    def _():
        own_k.wait_send()
        own_v.wait_send()

    @pl.when(c == 1)
    def _():
        own_q.wait_send()

    @pl.when((y == 1) & (c == 1))
    def _():
        relay_k.wait_send()
        relay_v.wait_send()

    @pl.when((y == 0) & (c == 0))
    def _():
        relay_q.wait_send()

    for cp in outs:
        cp.wait()


def forward(lengths, tokens, ln1_gain, ln1_bias, w_qkv, qv_bias, head_gain, w_out, out_bias, pa_gain, pa_bias, mid_gain, mid_bias,
            w_fc1, fc1_bias, ffn_gain, ffn_bias):
    rows, width = tokens.shape
    ff = w_fc1.shape[1]
    vmem, hbm = pl.BlockSpec(memory_space=pltpu.VMEM), pl.BlockSpec(memory_space=pl.ANY)
    shape = jax.ShapeDtypeStruct
    window, wide, tall = (3, rows, width), (rows, ff), (ff, rows)
    dma = pltpu.SemaphoreType.DMA
    return pl.pallas_call(
        forward_kernel,
        out_shape=[shape((width, rows), BF16), shape(window, BF16), shape(window, BF16), shape(window, BF16),
                   shape((rows, width), F32), shape((HEADS, rows), F32), shape((width, rows), BF16), shape((rows, width), F32),
                   shape((rows, width), F32), shape((width, rows), BF16), shape(wide, BF16), shape(wide, BF16),
                   shape((rows, 128), F32), shape(wide, BF16), shape(tall, BF16)],
        in_specs=[pl.BlockSpec(memory_space=pltpu.SMEM), vmem, vmem, vmem, hbm, vmem, vmem, hbm] + [vmem] * 5 + [hbm] + [vmem] * 3,
        out_specs=[hbm] * 5 + [vmem] + [hbm] * 6 + [vmem] + [hbm] * 2,
        scratch_shapes=[pltpu.VMEM((width, 3 * width), BF16), pltpu.VMEM((width, width), BF16), pltpu.VMEM((width, ff), BF16),
                        pltpu.VMEM((rows, width), BF16), pltpu.VMEM((rows, width), BF16), pltpu.VMEM((rows, width), BF16),
                        pltpu.VMEM(window, BF16), pltpu.VMEM(window, BF16), pltpu.VMEM(window, BF16),
                        pltpu.VMEM((3 * rows, rows), F32), pltpu.VMEM((2 * width // HEADS, rows), F32),
                        pltpu.VMEM((rows, width), F32), pltpu.VMEM((rows, width), F32), pltpu.VMEM((rows, width), F32),
                        pltpu.VMEM((rows, width), BF16), pltpu.VMEM(wide, F32), pltpu.VMEM((2, rows, 128), F32),
                        pltpu.VMEM((3, width, rows), BF16), pltpu.VMEM(wide, BF16), pltpu.VMEM(wide, BF16), pltpu.VMEM(wide, BF16),
                        pltpu.VMEM(tall, BF16), dma((8,)), dma((8,)), dma((8,)), dma((13,))],
        compiler_params=pltpu.CompilerParams(collective_id=1, has_side_effects=True, vmem_limit_bytes=60 << 20),
        cost_estimate=pl.CostEstimate(flops=12 << 30, bytes_accessed=40 << 20, transcendentals=5 << 20),
    )(lengths, tokens, ln1_gain[None], ln1_bias[None], w_qkv, qv_bias[None], head_gain[None], w_out, out_bias[None],
      pa_gain[None], pa_bias[None], mid_gain[None], mid_bias[None], w_fc1, fc1_bias[None], ffn_gain[None], ffn_bias[None])


SEND = 4
RECV = 8
KEEP = 8
LAG_XY = (0, 2, 4, 6, 8, 10)
LAG_Z = (0, 2, 4, 6, 8, 10)
PAIR0 = 9
PIECES = 3


def back_kernel(tok, a2, a1, ao, aq, cot, lens, qw_in, kw_in, vw_in, lse, att, attn, first, scale_ffn, tokens,
                gain, pa_gain, mid_gain, ffn_gain, head_gain, fc2_bias, normed_in, slope_in, low_ffn_in, w2_in, w1_in, wo_in, wq_in,
                out2, out1, outo, outq, vout, grad_tok, layer_out,
                am, ap, bm, bp, s1x, s1y, s2x, s2y, sr, sl, szr, szl, szx, szy, swx, swy,
                r1x, r1y, r2x, r2y, rr, rl, rzr, rzl, rzx, rzy, rwx, rwy,
                k2x, k2y, t3, kzx, kzy, kwx, kwy, out, vec, vown, vrecv,
                qw, kw, vw, dow, stw, mask, mask_q, dqa, dka, dva, total, d_first, d_ffn, parts,
                normed, w2b, colb, lowb, slopeb,
                load_sem, peer_send, peer_recv, send, recv, vsend, vrecv_sem, asend, arecv, in_sem, w2_sem, col_sem, low_sem, slope_sem,
                out_sem):
    dp, blk = lax.axis_index("dp"), lax.axis_index("blk")
    z, x = dp // 2, dp % 2
    y, c = blk // 2, blk % 2
    core_dev, x_dev, y_dev = (dp, blk + 1 - 2 * c), (dp + 1 - 2 * x, blk), (dp, blk + 2 - 4 * y)
    up_dev, down_dev = (dp + 2, blk), (dp - 2, blk)
    rounds = 24
    rows, width = tokens.shape
    dim = width // HEADS

    ff = normed.shape[1]
    n_ff = ff // FC
    n_o, n_q = width // FC, 3 * width // FC

    def piece2(j):
        return [pltpu.make_async_copy(w2_in.at[pl.ds(j * FC, FC)], w2b.at[j % PIECES], w2_sem.at[j % PIECES]),
                pltpu.make_async_copy(low_ffn_in.at[:, pl.ds(j * FC, FC)], lowb.at[j % PIECES], low_sem.at[j % PIECES])]

    def piece_slope(j):
        return pltpu.make_async_copy(slope_in.at[:, pl.ds(j * FC, FC)], slopeb.at[j % PIECES], slope_sem.at[j % PIECES])

    def piece_col(q, ref, j):
        return pltpu.make_async_copy(ref.at[:, pl.ds(j * FC, FC)], colb.at[q % PIECES], col_sem.at[q % PIECES])

    def start_col(q):
        def go(ref, low, high):
            def start():
                piece_col(q, ref, q - low).start()
            if isinstance(q, int):
                if low <= q < high:
                    start()
            else:
                pl.when((q >= low) & (q < high))(start)
        go(w1_in, 0, n_ff)
        go(wo_in, n_ff, n_ff + n_o)
        go(wq_in, n_ff + n_o, n_ff + n_o + n_q)

    early = [pltpu.make_async_copy(qw_in, qw, in_sem.at[0]), pltpu.make_async_copy(kw_in, kw, in_sem.at[1]),
             pltpu.make_async_copy(vw_in, vw, in_sem.at[2])]
    normed_load = pltpu.make_async_copy(normed_in, normed, in_sem.at[3])

    bar = pltpu.get_barrier_semaphore()
    z_devs = [((dp + 2 * k) % 8, blk) for k in range(1, 4)]
    for dev in [core_dev, x_dev, y_dev] + z_devs:
        pl.semaphore_signal(bar, inc=1, device_id=dev, device_id_type=MESH)
    pl.semaphore_wait(bar, 6)

    def remote(src, dst, ssem, rsem, dev):
        return pltpu.make_async_remote_copy(src, dst, ssem, rsem, device_id=dev, device_id_type=MESH)

    def window(kind):
        src, dst, dev = {"cross": (0, 2, y_dev), "own": (0, 1, core_dev), "relay": (2, 1, core_dev)}[kind]
        k = {"cross": 0, "own": 2, "relay": 4}[kind]
        return [remote(dow.at[src], dow.at[dst], asend.at[k], arecv.at[k], dev),
                remote(stw.at[src], stw.at[dst], asend.at[k + 1], arecv.at[k + 1], dev)]

    a_src = [(a2, g) for g in range(8)] + [(a1, 0), (a1, 1), (ao, 0), (ao, 1), (aq, 0), (aq, 1)]
    b_src = [(cot, 0)]
    n_a = len(a_src)

    def loads(kind, i, own):
        k = i if kind == "a" else n_a + i
        if kind == "a":
            ref, g = a_src[i]
            if own:
                return pltpu.make_async_copy(ref.at[:, :, :, c, g], am.at[i], load_sem.at[k])
            return remote(ref.at[:, :, :, 1 - c, g], ap.at[i], peer_send.at[k], peer_recv.at[k], core_dev)
        ref, g = b_src[i]
        part = ref.at[:, pl.ds(g * WR, WR)]
        if own:
            return pltpu.make_async_copy(part, bm.at[i], load_sem.at[k])
        return remote(part, bp.at[i], peer_send.at[k], peer_recv.at[k], core_dev)

    phases = [([("b", 0)] + [("a", g) for g in range(8)]), [("a", 8), ("a", 9)], [("a", 10), ("a", 11), ("a", 12), ("a", 13)]]
    for item in phases[0]:
        loads(*item, True).start()
        loads(*item, False).start()
    normed_load.start()
    for j in range(PIECES):
        for cp in piece2(j):
            cp.start()
    for phase in phases[1:]:
        for item in phase:
            loads(*item, True).start()
            loads(*item, False).start()
    for j in range(PIECES):
        start_col(j)
        piece_slope(j).start()
    for cp in early:
        cp.start()

    def peer_b(i):
        k = n_a + i
        return remote(bm.at[i], bp.at[i], peer_send.at[k], peer_recv.at[k], core_dev)

    def arrive(phase):
        for item in phase:
            loads(*item, True).wait()
            loads(*item, False).wait_recv()

    vec[...] = jnp.zeros_like(vec)
    total[...] = jnp.zeros_like(total)
    parts[...] = jnp.zeros_like(parts)
    q_spots = blk * rows + lax.broadcasted_iota(jnp.int32, (1, rows), 1)
    k_spots = (blk - 2) * rows + lax.broadcasted_iota(jnp.int32, (3 * rows, 1), 0)
    mask[...] = jnp.where((k_spots >= sequence_starts(lens, q_spots)) & (k_spots <= q_spots), 0.0, -1e30)
    q_spots = (blk + 1) * rows + lax.broadcasted_iota(jnp.int32, (1, 2 * rows), 1)
    k_spots = blk * rows + lax.broadcasted_iota(jnp.int32, (rows, 1), 0)
    mask_q[...] = jnp.where(k_spots >= sequence_starts(lens, q_spots), 0.0, -1e30)

    def place(r):
        g = jnp.where(r < 8, r, jnp.where(r < 16, 8 + r % 2, jnp.where(r < 18, 10 + r % 2, 12 + r % 2)))
        b = jnp.where(r < 8, 0, (r - 8) // 2 + 1)
        return g, b

    def product(r, zs, xs, ys, col, width):
        g, b = place(r)
        cols = pl.ds(col, width)
        la, lp = am[g, zs, xs, ys], ap[g, zs, xs, ys]
        lead = la.shape[:-1]
        m = 1
        for d in lead:
            m *= d
        res = dot32(la.reshape(m, tok), bm[b, :, cols]) + dot32(lp.reshape(m, tok), bp[b, :, cols])
        return res.reshape(lead + (width,))

    ALL = slice(None)
    col_y, col_z = WX, 2 * WX
    S1X, S1Y, S2X, S2Y, SR, SL, SZR, SZL, SZX, SZY, SWX, SWY = range(12)

    def message(src, dst, kind, dev):
        def make(r):
            return remote(src.at[r % SEND], dst.at[r % RECV], send.at[kind, r % SEND], recv.at[kind, r % RECV], dev)
        return make

    step1x, step1y = message(s1x, r1x, S1X, x_dev), message(s1y, r1y, S1Y, y_dev)
    step2x, step2y = message(s2x, r2x, S2X, y_dev), message(s2y, r2y, S2Y, x_dev)
    stepzx, stepzy = message(szx, rzx, SZX, x_dev), message(szy, rzy, SZY, y_dev)
    stepwx, stepwy = message(swx, rwx, SWX, y_dev), message(swy, rwy, SWY, x_dev)
    steps = (step1x, step1y, step2x, step2y, stepzx, stepzy, stepwx, stepwy)

    def put(step, ref, r, value):
        @pl.when(r >= SEND)
        def _():
            step(r - SEND).wait_send()

        ref[r % SEND] = value.astype(BF16)
        step(r).start()

    def chain(src, dst, kind, r, lo, hi, dev):
        return remote(src.at[r % SEND, lo:hi], dst.at[r % RECV, lo:hi], send.at[kind, r % SEND], recv.at[kind, r % RECV], dev)

    def chain_hop(hop, r, src, dst, kind_r, kind_l, term):
        slot, rslot = r % SEND, r % RECV

        @pl.when(z == hop)
        def _():
            if hop > 0:
                chain(src[0], dst[0], kind_r, r, hop - 1, 3, up_dev).wait_recv()

            @pl.when(r >= SEND)
            def _():
                chain(src[0], dst[0], kind_r, r - SEND, hop, 3, up_dev).wait_send()

            for d in range(hop + 1, 4):
                value = term(r, d)
                if hop > 0:
                    value = value + dst[0][rslot, d - 1].astype(F32)
                src[0][slot, d - 1] = value.astype(BF16)
            chain(src[0], dst[0], kind_r, r, hop, 3, up_dev).start()

        @pl.when(z == 3 - hop)
        def _():
            if hop > 0:
                chain(src[1], dst[1], kind_l, r, 0, 4 - hop, down_dev).wait_recv()

            @pl.when(r >= SEND)
            def _():
                chain(src[1], dst[1], kind_l, r - SEND, 0, 3 - hop, down_dev).wait_send()

            for d in range(0, 3 - hop):
                value = term(r, d)
                if hop > 0:
                    value = value + dst[1][rslot, d].astype(F32)
                src[1][slot, d] = value.astype(BF16)
            chain(src[1], dst[1], kind_l, r, 0, 3 - hop, down_dev).start()

    def chain_last(r, src, dst, kind_r, kind_l, total_ref):
        rslot = r % RECV
        for at in range(4):
            @pl.when(z == at)
            def _():
                if at == 3:
                    chain(src[0], dst[0], kind_r, r, 2, 3, up_dev).wait_recv()
                if at == 0:
                    chain(src[1], dst[1], kind_l, r, 0, 1, down_dev).wait_recv()
                value = None
                if at > 0:
                    value = dst[0][rslot, at - 1].astype(F32)
                if at < 3:
                    down = dst[1][rslot, at].astype(F32)
                    value = down if value is None else value + down
                total_ref[...] = value

    def chain_drain(r, src, dst, kind_r, kind_l):
        for hop in range(3):
            @pl.when(z == hop)
            def _():
                chain(src[0], dst[0], kind_r, r, hop, 3, up_dev).wait_send()

            @pl.when(z == 3 - hop)
            def _():
                chain(src[1], dst[1], kind_l, r, 0, 3 - hop, down_dev).wait_send()

    def z_term(r, d):
        return product(r, d, ALL, ALL, col_z, WZ)

    def t_term(r, d):
        return t3[r % KEEP, d]

    zsrc, zdst = (szr, szl), (rzr, rzl)
    csrc, cdst = (sr, sl), (rr, rl)

    def xy0(r):
        put(step1x, s1x, r, product(r, ALL, 1 - x, ALL, 0, WX))
        put(step1y, s1y, r, product(r, ALL, ALL, 1 - y, col_y, WX))

    def xy1(r):
        slot = r % KEEP
        step1x(r).wait_recv()
        k2x[...] = product(r, ALL, x, ALL, 0, WX) + r1x[r % RECV].astype(F32)
        put(step2x, s2x, r, k2x[:, 1 - y])
        kwx[slot] = k2x[:, y]
        step1y(r).wait_recv()
        k2y[...] = product(r, ALL, ALL, y, col_y, WX) + r1y[r % RECV].astype(F32)
        put(step2y, s2y, r, k2y[:, 1 - x])
        kwy[slot] = k2y[:, x]

    def xy2(r):
        slot = r % KEEP
        step2x(r).wait_recv()
        t3[slot, :, :, 0:WX] = kwx[slot] + r2x[r % RECV].astype(F32)
        step2y(r).wait_recv()
        t3[slot, :, :, WX:2 * WX] = kwy[slot] + r2y[r % RECV].astype(F32)
        chain_hop(0, r, csrc, cdst, SR, SL, t_term)

    def xy3(r):
        chain_hop(1, r, csrc, cdst, SR, SL, t_term)

    def xy4(r):
        chain_hop(2, r, csrc, cdst, SR, SL, t_term)

    def xy5(r):
        chain_last(r, csrc, cdst, SR, SL, out.at[r, :, 0:2 * WX])
        out[r, :, 0:2 * WX] = out[r, :, 0:2 * WX] + t3[r % KEEP, z]

    def z0(r):
        chain_hop(0, r, zsrc, zdst, SZR, SZL, z_term)

    def z1(r):
        chain_hop(1, r, zsrc, zdst, SZR, SZL, z_term)

    def z2(r):
        chain_hop(2, r, zsrc, zdst, SZR, SZL, z_term)

    def z3(r):
        slot = r % KEEP
        chain_last(r, zsrc, zdst, SZR, SZL, kzx)
        kzx[...] = kzx[...] + product(r, z, ALL, ALL, col_z, WZ)
        put(stepzx, szx, r, kzx[1 - x, :, :, 0:WZ // 2])
        put(stepzy, szy, r, kzx[:, 1 - y, :, WZ // 2:WZ])
        kzy[slot, 0] = kzx[x, :, :, 0:WZ // 2]
        kzy[slot, 1] = kzx[:, y, :, WZ // 2:WZ]

    def z4(r):
        slot = r % KEEP
        stepzx(r).wait_recv()
        kzy[slot, 0] = kzy[slot, 0] + rzx[r % RECV].astype(F32)
        put(stepwx, swx, r, kzy[slot, 0, 1 - y])
        stepzy(r).wait_recv()
        kzy[slot, 1] = kzy[slot, 1] + rzy[r % RECV].astype(F32)
        put(stepwy, swy, r, kzy[slot, 1, 1 - x])

    def z5(r):
        slot = r % KEEP
        stepwx(r).wait_recv()
        out[r, :, 2 * WX:2 * WX + WZ // 2] = kzy[slot, 0, y] + rwx[r % RECV].astype(F32)
        stepwy(r).wait_recv()
        out[r, :, 2 * WX + WZ // 2:] = kzy[slot, 1, x] + rwy[r % RECV].astype(F32)

    def drain(r):
        for step in steps:
            step(r).wait_send()
        chain_drain(r, csrc, cdst, SR, SL)
        chain_drain(r, zsrc, zdst, SZR, SZL)

    v = vec.shape[0]
    h1, h2, h3 = v // 2, v // 4, v // 8
    o1 = c * h1
    o2 = o1 + x * h2
    o3 = o2 + y * h3
    base = h1 + h2 + h3

    def vstep(i):
        if i == 0:
            return [remote(vec.at[pl.ds((1 - c) * h1, h1)], vrecv.at[pl.ds(0, h1)], vsend.at[0], vrecv_sem.at[0], core_dev)]
        if i == 1:
            return [remote(vown.at[pl.ds(o1 + (1 - x) * h2, h2)], vrecv.at[pl.ds(h1, h2)], vsend.at[1], vrecv_sem.at[1], x_dev)]
        if i == 2:
            return [remote(vown.at[pl.ds(o2 + (1 - y) * h3, h3)], vrecv.at[pl.ds(h1 + h2, h3)], vsend.at[2], vrecv_sem.at[2], y_dev)]
        if i == 3:
            return [remote(vown.at[pl.ds(o3, h3)], vrecv.at[pl.ds(base + z * h3, h3)], vsend.at[3 + k], vrecv_sem.at[3 + k],
                           z_devs[k - 1]) for k in range(1, 4)]
        if i == 4:
            return [remote(vout.at[pl.ds(o3, h3)], vout.at[pl.ds(o3, h3)], vsend.at[7], vrecv_sem.at[7], y_dev)]
        if i == 5:
            return [remote(vout.at[pl.ds(o2, h2)], vout.at[pl.ds(o2, h2)], vsend.at[8], vrecv_sem.at[8], x_dev)]
        return [remote(vout.at[pl.ds(o1, h1)], vout.at[pl.ds(o1, h1)], vsend.at[9], vrecv_sem.at[9], core_dev)]

    def vector_step(i):
        if i > 0:
            for cp in vstep(i - 1):
                cp.wait_recv()
        if i == 1:
            vown[pl.ds(o1, h1)] = vec[pl.ds(o1, h1)] + vrecv[0:h1]
        if i == 2:
            vown[pl.ds(o2, h2)] = vown[pl.ds(o2, h2)] + vrecv[h1:h1 + h2]
        if i == 3:
            vown[pl.ds(o3, h3)] = vown[pl.ds(o3, h3)] + vrecv[h1 + h2:base]
            vrecv[pl.ds(base + z * h3, h3)] = vown[pl.ds(o3, h3)]
        if i == 4:
            total = vrecv[base:base + h3]
            for k in range(1, 4):
                total = total + vrecv[base + k * h3:base + (k + 1) * h3]
            vout[pl.ds(o3, h3)] = total
        if i < 7:
            for cp in vstep(i):
                cp.start()

    def windows_arrive():
        for cp in early:
            cp.wait()

        @pl.when(y == 0)
        def _():
            for cp in window("cross"):
                cp.wait_recv()

        @pl.when((y == 0) & (c == 0))
        def _():
            for cp in window("relay"):
                cp.start()

        @pl.when(c == 0)
        def _():
            for cp in window("own"):
                cp.wait_recv()

        @pl.when((y == 0) & (c == 1))
        def _():
            for cp in window("relay"):
                cp.wait_recv()

    def windows_drain():
        @pl.when(y == 1)
        def _():
            for cp in window("cross"):
                cp.wait_send()

        @pl.when(c == 1)
        def _():
            for cp in window("own"):
                cp.wait_send()

        @pl.when((y == 0) & (c == 0))
        def _():
            for cp in window("relay"):
                cp.wait_send()

    def attend_back(i):
        cols = pl.ds(pl.multiple_of(i * 2 * dim, 2 * dim), 2 * dim)

        def pairs(kj, qj, bias, to_q, to_k, first):
            k2, v2, q2, d2 = kw[kj, :, cols], vw[kj, :, cols], qw[qj, :, cols], dow[qj, :, cols]
            for sub in range(2):
                part = slice(sub * dim, (sub + 1) * dim)
                k1, v1, q1, d1 = k2[:, part], v2[:, part], q2[:, part], d2[:, part]
                log_total = stw[qj, pl.ds(2 * i + sub, 1)]
                delta = stw[qj, pl.ds(HEADS + 2 * i + sub, 1)]
                probs = jnp.exp(dot_nt(k1, q1) + bias[...] - log_total)
                low_s = (probs * (dot_nt(v1, d1) - delta)).astype(BF16)
                if to_q:
                    term = dot_tn(k1, low_s)
                    dqa[part] = term if first else dqa[part] + term
                if to_k:
                    term = dot32(low_s, q1)
                    dka[sub] = term if first else dka[sub] + term
                    term = dot32(probs.astype(BF16), d1)
                    dva[sub] = term if first else dva[sub] + term

        pairs(2, 0, mask.at[2 * rows:3 * rows], True, True, True)

        @pl.when(blk >= 1)
        def _():
            pairs(1, 0, mask.at[rows:2 * rows], True, False, False)

        @pl.when(blk >= 2)
        def _():
            pairs(0, 0, mask.at[0:rows], True, False, False)

        @pl.when(blk <= 2)
        def _():
            pairs(2, 1, mask_q.at[:, 0:rows], False, True, False)

        @pl.when(blk <= 1)
        def _():
            pairs(2, 2, mask_q.at[:, rows:2 * rows], False, True, False)

        bm[6, :, cols] = (dqa[...].T * (dim ** -0.5)).astype(BF16)
        bm[7, :, cols] = jnp.concatenate([dka[0], dka[1]], axis=1).astype(BF16)
        bm[8, :, cols] = jnp.concatenate([dva[0], dva[1]], axis=1).astype(BF16)

    V_IN_GAIN, V_IN_BIAS, V_QV, V_OUT, V_PA_GAIN, V_PA_BIAS, V_MID_GAIN, V_MID_BIAS, V_FC2, V_HEADS = (
        k * (width // 128) for k in (0, 1, 2, 4, 5, 6, 7, 8, 9, 10))
    V_FC1 = 11 * (width // 128)
    V_FFN_GAIN = V_FC1 + ff // 128
    V_FFN_BIAS = V_FFN_GAIN + ff // 128

    def put_row(first_row, row):
        for k in range(row.shape[1] // 128):
            vec[first_row + k:first_row + k + 1, :] = row[:, k * 128:(k + 1) * 128]

    def put_row_at(first_row, j, row):
        for k in range(FC // 128):
            vec[pl.ds(first_row + j * (FC // 128) + k, 1), :] = row[:, k * 128:(k + 1) * 128]

    def chunk_cols(j):
        return pl.ds(pl.multiple_of(j * FC, FC), FC)

    def ffn_first(j):
        cols = chunk_cols(j)
        for cp in piece2(j):
            cp.wait()
        weights = w2b[j % PIECES]
        total[...] = total[...] + dot32(lowb[j % PIECES], weights)
        grad = dot_nt(bm[0], weights)
        unit = normed[:, cols].astype(F32)
        d_ffn[:, cols] = grad
        put_row_at(V_FFN_GAIN, j, jnp.sum(grad * unit, axis=0, keepdims=True))
        put_row_at(V_FFN_BIAS, j, jnp.sum(grad, axis=0, keepdims=True))
        grad = grad * ffn_gain[:, cols]
        parts[0] = parts[0] + lane_sums(grad)
        parts[1] = parts[1] + lane_sums(grad * unit)

        @pl.when(j + PIECES < n_ff)
        def _():
            for cp in piece2(j + PIECES):
                cp.start()

    def ffn_between():
        layer_out[...] = (first[...] + total[...] + fc2_bias[...]).astype(BF16)
        total[...] = jnp.zeros_like(total)
        parts[2] = jnp.broadcast_to(jnp.sum(parts[0], axis=-1, keepdims=True) * (1.0 / ff), parts.shape[1:])
        parts[3] = jnp.broadcast_to(jnp.sum(parts[1], axis=-1, keepdims=True) * (1.0 / ff), parts.shape[1:])

    def ffn_second(j):
        cols = chunk_cols(j)
        piece_col(j, w1_in, j).wait()
        piece_slope(j).wait()
        grad = d_ffn[:, cols] * ffn_gain[:, cols]
        grad = scale_ffn[:, 0:1] * (grad - parts[2][:, 0:1] - normed[:, cols].astype(F32) * parts[3][:, 0:1])
        low = (grad * slopeb[j % PIECES].astype(F32)).astype(BF16)
        bm[1 + j // 2, :, pl.ds(pl.multiple_of((j % 2) * FC, FC), FC)] = low
        put_row_at(V_FC1, j, jnp.sum(low.astype(F32), axis=0, keepdims=True))
        total[...] = total[...] + dot_nt(low, colb[j % PIECES])

        @pl.when(j % 2 == 1)
        def _():
            peer_b(1 + j // 2).start()

        @pl.when(j + PIECES < n_ff)
        def _():
            piece_slope(j + PIECES).start()

        start_col(j + PIECES)

    def unit_rows(values):
        centered = values - jnp.mean(values, axis=-1, keepdims=True)
        scale = lax.rsqrt(jnp.mean(centered * centered, axis=-1, keepdims=True) + 1e-05)
        return centered * scale, scale

    def norm_back(grad, values, gain_row, gain_at, bias_at):
        unit, scale = unit_rows(values)
        put_row(gain_at, jnp.sum(grad * unit, axis=0, keepdims=True))
        put_row(bias_at, jnp.sum(grad, axis=0, keepdims=True))
        grad = grad * gain_row
        return scale * (grad - jnp.mean(grad, axis=-1, keepdims=True) - unit * jnp.mean(grad * unit, axis=-1, keepdims=True))

    def middle_first():
        d_out = bm[0].astype(F32)
        put_row(V_FC2, jnp.sum(d_out, axis=0, keepdims=True))
        d_first[...] = d_out + norm_back(total[...], first[...], mid_gain[...], V_MID_GAIN, V_MID_BIAS)
        low = norm_back(d_first[...], attn[...], pa_gain[...], V_PA_GAIN, V_PA_BIAS).astype(BF16)
        bm[5] = low
        peer_b(5).start()
        put_row(V_OUT, jnp.sum(low.astype(F32), axis=0, keepdims=True))

    def middle_second():
        for k in range(n_o):
            piece_col(n_ff + k, wo_in, k).wait()
        total[...] = dot_nt(bm[5, :, 0:FC], colb[n_ff % PIECES])
        for k in range(1, n_o):
            total[...] = total[...] + dot_nt(bm[5, :, k * FC:(k + 1) * FC], colb[(n_ff + k) % PIECES])
        for k in range(n_o):
            start_col(n_ff + k + PIECES)
        attended = att[...]
        put_row(V_HEADS, jnp.sum(total[...] * attended, axis=0, keepdims=True))
        low = (total[...] * head_gain[...]).astype(BF16)
        dow[0] = low
        both = low.astype(F32) * attended
        high = both.astype(BF16)
        rest = (both - high.astype(F32)).astype(BF16)
        head_of = lax.broadcasted_iota(jnp.int32, (HEADS, width), 1) // dim
        pick = jnp.where(head_of == lax.broadcasted_iota(jnp.int32, (HEADS, width), 0), 1.0, 0.0).astype(BF16)
        stw[0, 0:HEADS] = lse[...]
        stw[0, HEADS:2 * HEADS] = dot_nt(pick, high) + dot_nt(pick, rest)

        @pl.when(y == 1)
        def _():
            for cp in window("cross"):
                cp.start()

        @pl.when(c == 1)
        def _():
            for cp in window("own"):
                cp.start()

    def input_first():
        for i in range(6, 9):
            peer_b(i).start()
        base_q = n_ff + n_o
        for k in range(n_q):
            piece_col(base_q + k, wq_in, k).wait()
            at = k * FC
            term = dot_nt(bm[6 + at // width, :, at % width:at % width + FC], colb[(base_q + k) % PIECES])
            total[...] = term if k == 0 else total[...] + term
            start_col(base_q + k + PIECES)

    def input_second():
        grad = norm_back(total[...], tokens[...].astype(F32), gain[...], V_IN_GAIN, V_IN_BIAS)
        grad_tok[...] = d_first[...] + grad
        put_row(V_QV, jnp.sum(bm[6].astype(F32), axis=0, keepdims=True))
        put_row(V_QV + width // 128, jnp.sum(bm[8].astype(F32), axis=0, keepdims=True))

    def share(r):
        half = pl.ds((r % 2) * ROWS, ROWS)
        return [((r >= 0) & (r < 8), pltpu.make_async_copy(out.at[r], out2.at[pl.ds(r * ROWS, ROWS)], out_sem.at[0])),
                ((r >= 8) & (r < 16), pltpu.make_async_copy(out.at[r], out1.at[half, pl.ds((r - 8) // 2 * WR, WR)], out_sem.at[0])),
                ((r >= 16) & (r < 18), pltpu.make_async_copy(out.at[r], outo.at[half], out_sem.at[0])),
                ((r >= 18) & (r < rounds), pltpu.make_async_copy(out.at[r], outq.at[half, pl.ds((r - 18) // 2 * WR, WR)], out_sem.at[0]))]

    n_pairs = HEADS // 2
    after = PAIR0 + n_pairs
    plan = sorted(list(zip(LAG_XY, (xy0, xy1, xy2, xy3, xy4, xy5))) + list(zip(LAG_Z, (z0, z1, z2, z3, z4, z5))),
                  key=lambda item: -item[0])
    last = max(LAG_XY + LAG_Z)

    def at_slot(s, number, work):
        @pl.when(s == number)
        def _():
            work()

    def slot_step(s, carry):
        at_slot(s, 0, lambda: arrive(phases[0]))
        at_slot(s, 7, lambda: arrive(phases[1]))
        at_slot(s, 15, lambda: arrive(phases[2]))

        @pl.when((s >= 8) & (s < 16) & (s % 2 == 0))
        def _():
            peer_b(1 + (s - 8) // 2).wait_recv()

        at_slot(s, 16, lambda: peer_b(5).wait_recv())
        at_slot(s, 18, lambda: [peer_b(i).wait_recv() for i in range(6, 9)])

        for lag, work in plan:
            r = s - lag

            @pl.when((r >= 0) & (r < rounds))
            def _():
                work(r)

        r = s - last

        @pl.when(r >= 0)
        def _():
            for here, cp in share(r):
                pl.when(here)(cp.start)

        at_slot(s, 0, normed_load.wait)
        for u in range(2):
            @pl.when(s < 4)
            def _():
                ffn_first(2 * s + u)

            @pl.when((s >= 4) & (s < 8))
            def _():
                ffn_second(2 * (s - 4) + u)

        at_slot(s, 3, ffn_between)
        at_slot(s, 8, middle_first)
        at_slot(s, 8, middle_second)
        at_slot(s, PAIR0, windows_arrive)

        @pl.when((s >= PAIR0) & (s < after))
        def _():
            attend_back(s - PAIR0)

        at_slot(s, after - 1, input_first)
        at_slot(s, after, input_second)
        for i in range(8):
            @pl.when(s == after + i)
            def _():
                vector_step(i)

        return carry

    lax.fori_loop(0, rounds + last, slot_step, 0)
    lax.fori_loop(rounds - SEND, rounds, lambda r, carry: (drain(r), carry)[1], 0)
    windows_drain()
    for phase in phases:
        for item in phase:
            loads(*item, False).wait_send()
    for i in range(1, 9):
        peer_b(i).wait_send()
    for i in range(7):
        for cp in vstep(i):
            cp.wait_send()

    def share_wait(r, carry):
        share(jnp.int32(0))[0][1].wait()
        return carry

    lax.fori_loop(0, rounds, share_wait, 0)


def blocks_first(turned):
    return turned.reshape(4, 2, 2, 2, turned.shape[0] // 32 // ROWS, ROWS, turned.shape[1])


def fast_shards(
    tokens, lengths, ln1_gain, ln1_bias, w_qkv, qv_bias, head_scale, w_out, out_bias, lnpa_gain, lnpa_bias,
    ln2_gain, ln2_bias, w_fc1, fc1_bias, lnf_gain, lnf_bias, w_fc2, fc2_bias, cotangent,
):
    tok, width = tokens.shape
    ff = w_fc1.shape[1]
    head_gain = jnp.repeat(head_scale, width // HEADS)
    (low_in_t, q_win, k_win, v_win, att, lse, scaled_t, attn, first, low_mid_t, normed, slope, scale_ffn, low_ffn, low_ffn_t) = forward(
        lengths, tokens, ln1_gain, ln1_bias, w_qkv, qv_bias, head_gain, w_out, out_bias, lnpa_gain, lnpa_bias, ln2_gain, ln2_bias,
        w_fc1, fc1_bias, lnf_gain, lnf_bias)
    rounds = 24
    hbm, vmem = pl.BlockSpec(memory_space=pl.ANY), pl.BlockSpec(memory_space=pltpu.VMEM)
    a_shape = (14, 4, 2, 2, ROWS, tok)
    b_shape = (9, tok, WR)
    msgs = [(4, 2, ROWS, WX), (4, 2, ROWS, WX), (4, ROWS, WX), (4, ROWS, WX), (3, ROWS, 2 * WX), (3, ROWS, 2 * WX),
            (3, 2, 2, ROWS, WZ), (3, 2, 2, ROWS, WZ), (2, ROWS, WZ // 2), (2, ROWS, WZ // 2), (ROWS, WZ // 2), (ROWS, WZ // 2)]
    sizes = (width, width, 2 * width) + (width,) * 7 + (ff, ff, ff)
    v = -(-sum(sizes) // 8192) * 64
    dma, shape = pltpu.SemaphoreType.DMA, jax.ShapeDtypeStruct
    f32s = [(4, 2, ROWS, WX), (4, 2, ROWS, WX), (KEEP, 4, ROWS, 2 * WX), (2, 2, ROWS, WZ), (KEEP, 2, 2, ROWS, WZ // 2),
            (KEEP, 4, ROWS, WX), (KEEP, 4, ROWS, WX), (rounds, ROWS, WR), (v, 128), (v, 128), (v // 2 + v // 4 + v // 8 * 5, 128)]
    windows = [pltpu.VMEM((3, tok, width), BF16)] * 4 + [pltpu.VMEM((3, 2 * HEADS, tok), F32)]
    more = [(3 * tok, tok), (tok, 2 * tok), (2 * width // HEADS, tok), (2, tok, width // HEADS), (2, tok, width // HEADS),
            (tok, width), (tok, width), (tok, ff), (4, tok, 128)]
    out2, out1, outo, outq, flat, grad_tokens, layer_out = pl.pallas_call(
        functools.partial(back_kernel, tok),
        out_shape=[shape((ff // 32, width), F32), shape((width // 32, ff), F32), shape((width // 32, width), F32),
                   shape((width // 32, 3 * width), F32), shape((v, 128), F32), shape((tok, width), F32), shape((tok, width), BF16)],
        in_specs=[hbm] * 5 + [pl.BlockSpec(memory_space=pltpu.SMEM)] + [hbm] * 3 + [vmem] * 12 + [hbm] * 7,
        out_specs=[hbm] * 4 + [vmem] * 3,
        scratch_shapes=[pltpu.VMEM(a_shape, BF16), pltpu.VMEM(a_shape, BF16), pltpu.VMEM(b_shape, BF16), pltpu.VMEM(b_shape, BF16)]
        + [pltpu.VMEM((SEND,) + m, BF16) for m in msgs]
        + [pltpu.VMEM((RECV,) + m, BF16) for m in msgs]
        + [pltpu.VMEM(m, F32) for m in f32s] + windows + [pltpu.VMEM(m, F32) for m in more]
        + [pltpu.VMEM((tok, ff), BF16), pltpu.VMEM((PIECES, FC, width), BF16), pltpu.VMEM((PIECES, width, FC), BF16),
           pltpu.VMEM((PIECES, tok, FC), BF16), pltpu.VMEM((PIECES, tok, FC), BF16),
           dma((15,)), dma((23,)), dma((23,)), dma((12, SEND)), dma((12, RECV)), dma((10,)), dma((10,)), dma((6,)), dma((6,)),
           dma((4,)), dma((PIECES,)), dma((PIECES,)), dma((PIECES,)), dma((PIECES,)), dma((1,))],
        compiler_params=pltpu.CompilerParams(collective_id=0, has_side_effects=True, vmem_limit_bytes=63 << 20),
        cost_estimate=pl.CostEstimate(flops=30 << 30, bytes_accessed=50 << 20, transcendentals=4 << 20),
    )(blocks_first(low_ffn_t), blocks_first(low_mid_t), blocks_first(scaled_t), blocks_first(low_in_t),
      cotangent, lengths, q_win, k_win, v_win, lse, att, attn, first, scale_ffn, tokens,
      ln1_gain[None], lnpa_gain[None], ln2_gain[None], lnf_gain[None], head_gain[None], fc2_bias[None],
      normed, slope, low_ffn, w_fc2, w_fc1, w_out, w_qkv)
    flat = flat.reshape(-1)
    starts = [sum(sizes[:i]) for i in range(len(sizes))]
    ln1g, ln1b, qv, bo, pag, pab, ln2g, ln2b, c2, hs, c1, lnfg, lnfb = (
        lax.slice(flat, (start,), (start + size,)) for start, size in zip(starts, sizes))
    hs = jnp.sum(hs.reshape(HEADS, width // HEADS), axis=1)
    return (layer_out, grad_tokens, ln1g, ln1b, outq, qv, hs, outo, bo, pag, pab, ln2g, ln2b, out1, c1, lnfg, lnfb, out2, c2)


def shards(
    tokens,
    lengths,
    ln1_gain,
    ln1_bias,
    w_qkv,
    qv_bias,
    head_scale,
    w_out,
    out_bias,
    lnpa_gain,
    lnpa_bias,
    ln2_gain,
    ln2_bias,
    w_fc1,
    fc1_bias,
    lnf_gain,
    lnf_bias,
    w_fc2,
    fc2_bias,
    cotangent,
):
    row_count, width = tokens.shape
    head_dim = width // HEADS
    factor = head_dim ** (-0.5)
    group = row_count * lax.axis_size("blk")
    own_start = lax.axis_index("blk") * row_count
    seq_ends = jnp.cumsum(lengths[0])
    positions = jnp.arange(group, dtype=jnp.int32)
    labels = jnp.sum((positions[:, None] >= seq_ends[None, :]).astype(jnp.int32), axis=1)
    q_labels = lax.dynamic_slice_in_dim(labels, own_start, row_count, 0)
    q_spots = own_start + jnp.arange(row_count, dtype=jnp.int32)
    inputs = tokens.astype(jnp.float32)
    normed_in, ln1_back = jax.vjp(norm_rows, inputs, ln1_gain, ln1_bias)
    low_in = normed_in.astype(jnp.bfloat16)
    projected = jnp.dot(low_in, w_qkv, preferred_element_type=jnp.float32)
    queries = (projected[:, :width] + qv_bias[:width]).astype(jnp.bfloat16)
    key_rows = projected[:, width : 2 * width].astype(jnp.bfloat16)
    value_rows = (projected[:, 2 * width :] + qv_bias[width:]).astype(jnp.bfloat16)
    query_heads = queries.reshape(row_count, HEADS, head_dim)

    def scored(key_block, start):
        count = key_block.shape[0]
        key_heads = key_block.reshape(count, HEADS, head_dim)
        raw_scores = (
            jnp.einsum("qhd,khd->hqk", query_heads, key_heads, preferred_element_type=jnp.float32)
            * factor
        )
        k_labels = lax.dynamic_slice_in_dim(labels, start, count, 0)
        k_spots = start + jnp.arange(count, dtype=jnp.int32)
        visible = (k_labels[None, :] == q_labels[:, None]) & (k_spots[None, :] <= q_spots[:, None])
        return (raw_scores, visible[None], key_heads)

    def by_blocks(step_fn, carry, pieces):
        count = pieces[0].shape[0]
        unit = max(1, 1024 // row_count) * row_count
        step = count if count <= unit else math.gcd(count, unit)

        def inner(block_index, state):
            offset = block_index * step
            sub_pieces = tuple((lax.dynamic_slice_in_dim(item, offset, step, 0) for item in pieces))
            return step_fn(state, sub_pieces, offset)

        return lax.fori_loop(0, count // step, inner, carry)

    def max_step(carry, pieces, start):
        top_score, totals = carry
        raw_scores, visible, key_heads = scored(pieces[0], start)
        raw_scores = jnp.where(visible, raw_scores, -1e30)
        new_top = jnp.maximum(top_score, jnp.max(raw_scores, axis=-1))
        totals = totals * jnp.exp(top_score - new_top) + jnp.sum(
            jnp.where(visible, jnp.exp(raw_scores - new_top[..., None]), 0.0), axis=-1
        )
        return (new_top, totals)

    start_top = jnp.full((HEADS, row_count), -1e30, jnp.float32)
    start_total = jnp.zeros((HEADS, row_count), jnp.float32)
    top_score, totals = by_blocks(
        max_step, (start_top, start_total), (lax.all_gather(key_rows, "blk", axis=0, tiled=True),)
    )
    log_total = top_score + jnp.log(totals)

    def value_step(carry, pieces, start):
        weighted, leftover = carry
        raw_scores, visible, key_heads = scored(pieces[0], start)
        value_heads = pieces[1].reshape(pieces[1].shape[0], HEADS, head_dim)
        probs = jnp.where(visible, jnp.exp(raw_scores - log_total[..., None]), 0.0)
        low_probs = probs.astype(jnp.bfloat16)
        rest_probs = (probs - low_probs.astype(jnp.float32)).astype(jnp.bfloat16)
        weighted = weighted + jnp.einsum(
            "hqk,khd->qhd", low_probs, value_heads, preferred_element_type=jnp.float32
        )
        leftover = leftover + jnp.einsum(
            "hqk,khd->qhd", rest_probs, value_heads, preferred_element_type=jnp.float32
        )
        return (weighted, leftover)

    empty_heads = jnp.zeros((row_count, HEADS, head_dim), jnp.float32)
    weighted, leftover = by_blocks(
        value_step,
        (empty_heads, empty_heads),
        (
            lax.all_gather(key_rows, "blk", axis=0, tiled=True),
            lax.all_gather(value_rows, "blk", axis=0, tiled=True),
        ),
    )
    attended = weighted.reshape(row_count, width)
    head_gain = jnp.repeat(head_scale, head_dim)
    scaled = (attended * head_gain).astype(jnp.bfloat16)
    attn_out = jnp.dot(scaled, w_out, preferred_element_type=jnp.float32) + out_bias
    branch, pa_back = jax.vjp(norm_rows, attn_out, lnpa_gain, lnpa_bias)
    first_sum = inputs + branch
    normed_mid, ln2_back = jax.vjp(norm_rows, first_sum, ln2_gain, ln2_bias)
    low_mid = normed_mid.astype(jnp.bfloat16)
    pre_act = jnp.dot(low_mid, w_fc1, preferred_element_type=jnp.float32) + fc1_bias
    activated, gelu_back = jax.vjp(gelu_exact, pre_act)
    ffn_normed, lnf_back = jax.vjp(norm_rows, activated, lnf_gain, lnf_bias)
    low_ffn = ffn_normed.astype(jnp.bfloat16)
    layer_out = (
        first_sum + jnp.dot(low_ffn, w_fc2, preferred_element_type=jnp.float32) + fc2_bias
    ).astype(jnp.bfloat16)
    d_output = cotangent.astype(jnp.float32)
    grad_w2 = over_rows(low_ffn, cotangent)
    grad_c2 = jnp.sum(d_output, axis=0)
    d_ffn = over_cols(cotangent, w_fc2)
    d_active, grad_lnf_gain, grad_lnf_bias = lnf_back(d_ffn)
    (d_pre,) = gelu_back(d_active)
    low_pre = d_pre.astype(jnp.bfloat16)
    grad_w1 = over_rows(low_mid, low_pre)
    grad_c1 = jnp.sum(low_pre.astype(jnp.float32), axis=0)
    d_mid = over_cols(low_pre, w_fc1)
    d_first_norm, grad_ln2_gain, grad_ln2_bias = ln2_back(d_mid)
    d_first = d_output + d_first_norm
    d_attn, grad_pa_gain, grad_pa_bias = pa_back(d_first)
    low_attn = d_attn.astype(jnp.bfloat16)
    grad_bo = jnp.sum(low_attn.astype(jnp.float32), axis=0)
    grad_wo = over_rows(scaled, low_attn)
    d_scaled = over_cols(low_attn, w_out)
    grad_hs = jnp.sum((d_scaled * attended).reshape(row_count, HEADS, head_dim), axis=(0, 2))
    d_attended = (d_scaled * head_gain).astype(jnp.bfloat16)
    d_heads = d_attended.reshape(row_count, HEADS, head_dim)
    delta_rows = jnp.sum(d_heads.astype(jnp.float32) * (weighted + leftover), axis=-1)
    delta = delta_rows.T

    def back_step(carry, pieces, start):
        count = pieces[0].shape[0]
        raw_scores, visible, key_heads = scored(pieces[0], start)
        value_heads = pieces[1].reshape(count, HEADS, head_dim)
        probs = jnp.where(visible, jnp.exp(raw_scores - log_total[..., None]), 0.0)
        d_probs = jnp.einsum(
            "qhd,khd->hqk", d_heads, value_heads, preferred_element_type=jnp.float32
        )
        d_scores = (probs * (d_probs - delta[..., None])).astype(jnp.bfloat16)
        d_query = (
            carry[0]
            + jnp.einsum("hqk,khd->qhd", d_scores, key_heads, preferred_element_type=jnp.float32)
            * factor
        )
        key_grad, value_grad = (carry[1], carry[2])
        low_probs = probs.astype(jnp.bfloat16)
        d_value = jnp.einsum(
            "hqk,qhd->khd", low_probs, d_heads, preferred_element_type=jnp.float32
        ).reshape(count, width)
        d_key = (
            jnp.einsum("hqk,qhd->khd", d_scores, query_heads, preferred_element_type=jnp.float32)
            * factor
        ).reshape(count, width)
        key_grad = lax.dynamic_update_slice_in_dim(
            key_grad, lax.dynamic_slice_in_dim(key_grad, start, count, 0) + d_key, start, 0
        )
        value_grad = lax.dynamic_update_slice_in_dim(
            value_grad, lax.dynamic_slice_in_dim(value_grad, start, count, 0) + d_value, start, 0
        )
        return (d_query, key_grad, value_grad)

    empty_group = jnp.zeros((group, width), jnp.float32)
    start_carry = (empty_heads, empty_group, empty_group)
    results = by_blocks(
        back_step,
        start_carry,
        (
            lax.all_gather(key_rows, "blk", axis=0, tiled=True),
            lax.all_gather(value_rows, "blk", axis=0, tiled=True),
        ),
    )
    d_query = results[0]
    own_keys, own_values = (
        lax.psum_scatter(
            results[1].astype(jnp.bfloat16), "blk", scatter_dimension=0, tiled=True
        ).astype(jnp.float32),
        lax.psum_scatter(
            results[2].astype(jnp.bfloat16), "blk", scatter_dimension=0, tiled=True
        ).astype(jnp.float32),
    )
    low_q = d_query.reshape(row_count, width).astype(jnp.bfloat16)
    low_k = own_keys.astype(jnp.bfloat16)
    low_v = own_values.astype(jnp.bfloat16)
    d_projected = jnp.concatenate([low_q, low_k, low_v], axis=1)
    grad_wqkv = over_rows(low_in, d_projected)
    grad_qv = jnp.concatenate(
        [jnp.sum(low_q.astype(jnp.float32), axis=0), jnp.sum(low_v.astype(jnp.float32), axis=0)]
    )
    d_in = over_cols(d_projected, w_qkv)
    d_in_norm, grad_ln1_gain, grad_ln1_bias = ln1_back(d_in)
    grad_tokens = d_first + d_in_norm
    share_wqkv, share_wo, share_w1, share_w2 = (
        lax.psum_scatter(grad_wqkv, ("dp", "blk"), scatter_dimension=0, tiled=True),
        lax.psum_scatter(grad_wo, ("dp", "blk"), scatter_dimension=0, tiled=True),
        lax.psum_scatter(grad_w1, ("dp", "blk"), scatter_dimension=0, tiled=True),
        lax.psum_scatter(grad_w2, ("dp", "blk"), scatter_dimension=0, tiled=True),
    )
    summed = lax.psum(
        (
            grad_ln1_gain,
            grad_ln1_bias,
            grad_qv,
            grad_hs,
            grad_bo,
            grad_pa_gain,
            grad_pa_bias,
            grad_ln2_gain,
            grad_ln2_bias,
            grad_c1,
            grad_lnf_gain,
            grad_lnf_bias,
            grad_c2,
        ),
        ("dp", "blk"),
    )
    return (
        layer_out,
        grad_tokens,
        summed[0],
        summed[1],
        share_wqkv,
        summed[2],
        summed[3],
        share_wo,
        summed[4],
        summed[5],
        summed[6],
        summed[7],
        summed[8],
        share_w1,
        summed[9],
        summed[10],
        summed[11],
        share_w2,
        summed[12],
    )


def solution(mesh):
    in_specs = (
        P(("dp", "blk"), None),
        P("dp", None),
        P(),
        P(),
        P(),
        P(),
        P(),
        P(),
        P(),
        P(),
        P(),
        P(),
        P(),
        P(),
        P(),
        P(),
        P(),
        P(),
        P(),
        P(("dp", "blk"), None),
    )
    out_specs = (
        P(("dp", "blk"), None),
        P(("dp", "blk"), None),
        P(),
        P(),
        P(("dp", "blk"), None),
        P(),
        P(),
        P(("dp", "blk"), None),
        P(),
        P(),
        P(),
        P(),
        P(),
        P(("dp", "blk"), None),
        P(),
        P(),
        P(),
        P(("dp", "blk"), None),
        P(),
    )
    body = fast_shards if dict(mesh.shape) == {"dp": 8, "blk": 4} else shards
    return jax.shard_map(body, mesh=mesh, in_specs=in_specs, out_specs=out_specs, check_vma=False)
```

```python
import functools
import math

import jax
import jax.numpy as jnp
from jax import lax
from jax.experimental import pallas as pl
from jax.experimental.pallas import tpu as pltpu
from jax.sharding import PartitionSpec as P

HEADS = 16
MESH = pl.DeviceIdType.MESH
F32, BF16 = jnp.float32, jnp.bfloat16
WX = 384
WZ = 256
WR = 2 * WX + WZ
ROWS = 16


def norm_rows(values_in, gain_vec, bias_vec):
    row_mean = jnp.mean(values_in, axis=-1, keepdims=True)
    centered = values_in - row_mean
    variance = jnp.mean(centered * centered, axis=-1, keepdims=True)
    return centered * lax.rsqrt(variance + 1e-05) * gain_vec + bias_vec


def gelu_exact(pre_values):
    return 0.5 * pre_values * (1.0 + lax.erf(pre_values * 0.7071067811865476))


def over_rows(left, right):
    return lax.dot_general(
        left, right, (((0,), (0,)), ((), ())), preferred_element_type=jnp.float32
    )


def over_cols(left, right):
    return lax.dot_general(
        left, right, (((1,), (1,)), ((), ())), preferred_element_type=jnp.float32
    )


def dot32(left, right):
    return jnp.dot(left, right, preferred_element_type=F32)


def dot_nt(left, right):
    return lax.dot_general(left, right, (((1,), (1,)), ((), ())), preferred_element_type=F32)


def dot_tn(left, right):
    return lax.dot_general(left, right, (((0,), (0,)), ((), ())), preferred_element_type=F32)


def norm_in(rows, gain, bias):
    mean = jnp.mean(rows, axis=-1, keepdims=True)
    centered = rows - mean
    variance = jnp.mean(centered * centered, axis=-1, keepdims=True)
    return centered * lax.rsqrt(variance + 1e-05) * gain + bias


def sequence_starts(lens, spots):
    start = jnp.zeros_like(spots)
    end = jnp.int32(0)
    for j in range(lens.shape[1]):
        end = end + lens[0, j]
        start = jnp.where(spots >= end, jnp.maximum(start, end), start)
    return start


def lane_sums(values):
    total = values[:, 0:128]
    for k in range(1, values.shape[1] // 128):
        total = total + values[:, k * 128:(k + 1) * 128]
    return total


def head_row(scales, width):
    head_of = lax.broadcasted_iota(jnp.int32, (1, width), 1) // (width // HEADS)
    row = jnp.full((1, width), scales[0, 0], F32)
    for h in range(1, HEADS):
        row = jnp.where(head_of == h, scales[0, h], row)
    return row


FC = 512


def forward_kernel(lens, tok, gain, bias, w_hbm, qv_bias, head_scale, wo_hbm, out_bias, pa_gain, pa_bias, mid_gain, mid_bias,
                   w1_hbm, fc1_bias, ffn_gain, ffn_bias,
                   low_in_t, qw_out, kw_out, vw_out, att_out, lse, scaled_t, attn_out, first_out, low_mid_t, normed_out, slope_out,
                   scale_out, low_ffn_out, low_ffn_t,
                   w, wo, w1, tok_y, low_in, low_y, qw, kw, vw, mask, acc, att, attn, first, low_mid, act, part, turned, normed,
                   slope, low_ffn, ffn_turned, w_sem, sends, recvs, out_sem):
    dp, blk = lax.axis_index("dp"), lax.axis_index("blk")
    y, c = blk // 2, blk % 2
    core_dev, y_dev = (dp, blk + 1 - 2 * c), (dp, blk + 2 - 4 * y)
    rows, width = tok.shape
    dim = width // HEADS
    half = rows // 2
    ff = w1.shape[1]
    n_ff = ff // FC

    def remote(src, dst, i, dev):
        return pltpu.make_async_remote_copy(src, dst, sends.at[i], recvs.at[i], device_id=dev, device_id_type=MESH)

    n_w = 6
    wc = 3 * width // n_w
    loads = [pltpu.make_async_copy(w_hbm.at[:, pl.ds(i * wc, wc)], w.at[:, pl.ds(i * wc, wc)], w_sem.at[i]) for i in range(n_w)]
    loads.append(pltpu.make_async_copy(wo_hbm, wo, w_sem.at[6]))
    loads.append(pltpu.make_async_copy(w1_hbm, w1, w_sem.at[7]))
    for i in (2, 3, 4, 5, 0, 1, 6, 7):
        loads[i].start()
    bar = pltpu.get_barrier_semaphore()
    for dev in (core_dev, y_dev):
        pl.semaphore_signal(bar, inc=1, device_id=dev, device_id_type=MESH)
    pl.semaphore_wait(bar, 2)
    cross = [remote(tok.at[pl.ds(i * half, half)], tok_y.at[pl.ds(i * half, half)], i, y_dev) for i in range(2)]
    for cp in cross:
        cp.start()

    outs = []

    def emit(src, dst):
        cp = pltpu.make_async_copy(src, dst, out_sem.at[len(outs)])
        cp.start()
        outs.append(cp)

    q_spots = blk * rows + lax.broadcasted_iota(jnp.int32, (1, rows), 1)
    starts = sequence_starts(lens, q_spots)
    k_spots = (blk - 2) * rows + lax.broadcasted_iota(jnp.int32, (3 * rows, 1), 0)
    mask[...] = jnp.where((k_spots >= starts) & (k_spots <= q_spots), 0.0, -1e30)

    low_in[...] = norm_in(tok[...].astype(F32), gain[...], bias[...]).astype(BF16)

    def project(src, r0, n, which):
        res = dot32(src[r0:r0 + n], w[:, which * width:(which + 1) * width])
        if which == 0:
            res = (res + qv_bias[:, 0:width]).astype(BF16).astype(F32) * (dim ** -0.5)
        if which == 2:
            res = res + qv_bias[:, width:]
        return res.astype(BF16)

    own_q = remote(qw.at[0], qw.at[1], 2, core_dev)
    own_k = remote(kw.at[2], kw.at[1], 3, core_dev)
    own_v = remote(vw.at[2], vw.at[1], 4, core_dev)
    relay_q = remote(qw.at[2], qw.at[1], 5, core_dev)
    relay_k = remote(kw.at[0], kw.at[1], 6, core_dev)
    relay_v = remote(vw.at[0], vw.at[1], 7, core_dev)

    for cp in loads[2:4]:
        cp.wait()
    kw[2] = project(low_in, 0, rows, 1)

    @pl.when(c == 0)
    def _():
        own_k.start()

    for cp in loads[4:6]:
        cp.wait()
    vw[2] = project(low_in, 0, rows, 2)

    @pl.when(c == 0)
    def _():
        own_v.start()

    for cp in loads[0:2]:
        cp.wait()
    qw[0] = project(low_in, 0, rows, 0)

    @pl.when(c == 1)
    def _():
        own_q.start()

    turned[0] = low_in[...].T
    emit(turned.at[0], low_in_t)

    for i in range(2):
        cross[i].wait_recv()
        low_y[i * half:(i + 1) * half] = norm_in(tok_y[i * half:(i + 1) * half].astype(F32), gain[...], bias[...]).astype(BF16)

        @pl.when(y == 1)
        def _():
            kw[0, i * half:(i + 1) * half] = project(low_y, i * half, half, 1)
            vw[0, i * half:(i + 1) * half] = project(low_y, i * half, half, 2)

        @pl.when(y == 0)
        def _():
            qw[2, i * half:(i + 1) * half] = project(low_y, i * half, half, 0)

    @pl.when((y == 1) & (c == 1))
    def _():
        relay_k.start()
        relay_v.start()

    @pl.when((y == 0) & (c == 0))
    def _():
        relay_q.start()

    @pl.when(c == 1)
    def _():
        own_k.wait_recv()
        own_v.wait_recv()

    @pl.when((y == 1) & (c == 0))
    def _():
        relay_k.wait_recv()
        relay_v.wait_recv()

    emit(kw, kw_out)
    emit(vw, vw_out)

    def heads(lowest):
        def pair(i, carry):
            cols = pl.ds(pl.multiple_of(i * 2 * dim, 2 * dim), 2 * dim)
            q2 = qw[0, :, cols]
            k2 = [kw[j, :, cols] for j in range(lowest, 3)]
            v2 = [vw[j, :, cols] for j in range(lowest, 3)]
            for sub in range(2):
                one_head = slice(sub * dim, (sub + 1) * dim)
                scores = [dot_nt(k[:, one_head], q2[:, one_head]) + mask[(lowest + n) * rows:(lowest + n + 1) * rows]
                          for n, k in enumerate(k2)]
                top = jnp.max(scores[0], axis=0, keepdims=True)
                for s in scores[1:]:
                    top = jnp.maximum(top, jnp.max(s, axis=0, keepdims=True))
                total, out = None, None
                for s, v in zip(scores, v2):
                    p = jnp.exp(s - top)
                    one = jnp.sum(p, axis=0, keepdims=True)
                    term = dot_tn(v[:, one_head], p.astype(BF16))
                    total = one if total is None else total + one
                    out = term if out is None else out + term
                acc[one_head] = out / total
                lse[pl.ds(2 * i + sub, 1)] = top + jnp.log(total)
            att[:, cols] = acc[...].T
            return carry

        lax.fori_loop(0, HEADS // 2, pair, 0)

    @pl.when(blk == 0)
    def _():
        heads(2)

    @pl.when(blk == 1)
    def _():
        heads(1)

    @pl.when(blk >= 2)
    def _():
        heads(0)

    @pl.when(c == 0)
    def _():
        own_q.wait_recv()

    @pl.when((y == 0) & (c == 1))
    def _():
        relay_q.wait_recv()

    emit(qw, qw_out)
    emit(att, att_out)

    scaled = (att[...] * head_row(head_scale, width)).astype(BF16)
    loads[6].wait()
    attn[...] = dot32(scaled, wo[...]) + out_bias[...]
    emit(attn, attn_out)
    first[...] = tok[...].astype(F32) + norm_in(attn[...], pa_gain[...], pa_bias[...])
    emit(first, first_out)
    low_mid[...] = norm_in(first[...], mid_gain[...], mid_bias[...]).astype(BF16)
    loads[7].wait()
    part[...] = jnp.zeros_like(part)

    def ffn_cols(j):
        return pl.ds(pl.multiple_of(j * FC, FC), FC)

    def gelu_part(j, carry):
        cols = ffn_cols(j)
        pre = dot32(low_mid[...], w1[:, cols]) + fc1_bias[:, cols]
        gate = 0.5 * (1.0 + lax.erf(pre * 0.7071067811865476))
        out = pre * gate
        act[:, cols] = out
        slope[:, cols] = (gate + pre * (jnp.exp(-0.5 * (pre * pre)) * 0.3989422804014327)).astype(BF16)
        part[0] = part[0] + lane_sums(out)
        return carry

    lax.fori_loop(0, n_ff, gelu_part, 0)
    emit(slope, slope_out)
    mean = jnp.sum(part[0], axis=-1, keepdims=True) * (1.0 / ff)

    def spread_part(j, carry):
        centered = act[:, ffn_cols(j)] - mean
        part[1] = part[1] + lane_sums(centered * centered)
        return carry

    lax.fori_loop(0, n_ff, spread_part, 0)
    scale = lax.rsqrt(jnp.sum(part[1], axis=-1, keepdims=True) * (1.0 / ff) + 1e-05)
    scale_out[...] = jnp.broadcast_to(scale, scale_out.shape)

    def norm_part(j, carry):
        cols = ffn_cols(j)
        unit = (act[:, cols] - mean) * scale
        normed[:, cols] = unit.astype(BF16)
        low = (unit * ffn_gain[:, cols] + ffn_bias[:, cols]).astype(BF16)
        low_ffn[:, cols] = low
        ffn_turned[cols] = low.T
        return carry

    lax.fori_loop(0, n_ff, norm_part, 0)
    emit(normed, normed_out)
    emit(low_ffn, low_ffn_out)
    emit(ffn_turned, low_ffn_t)
    turned[1] = scaled.T
    emit(turned.at[1], scaled_t)
    turned[2] = low_mid[...].T
    emit(turned.at[2], low_mid_t)

    for cp in cross:
        cp.wait_send()

    @pl.when(c == 0)
    def _():
        own_k.wait_send()
        own_v.wait_send()

    @pl.when(c == 1)
    def _():
        own_q.wait_send()

    @pl.when((y == 1) & (c == 1))
    def _():
        relay_k.wait_send()
        relay_v.wait_send()

    @pl.when((y == 0) & (c == 0))
    def _():
        relay_q.wait_send()

    for cp in outs:
        cp.wait()


def forward(lengths, tokens, ln1_gain, ln1_bias, w_qkv, qv_bias, head_scale, w_out, out_bias, pa_gain, pa_bias, mid_gain, mid_bias,
            w_fc1, fc1_bias, ffn_gain, ffn_bias):
    rows, width = tokens.shape
    ff = w_fc1.shape[1]
    hbm, vmem, smem = (pl.BlockSpec(memory_space=space) for space in (pl.ANY, pltpu.VMEM, pltpu.SMEM))
    shape = jax.ShapeDtypeStruct
    window, wide, tall = (3, rows, width), (rows, ff), (ff, rows)
    dma = pltpu.SemaphoreType.DMA
    return pl.pallas_call(
        forward_kernel,
        out_shape=[shape((width, rows), BF16), shape(window, BF16), shape(window, BF16), shape(window, BF16),
                   shape((rows, width), F32), shape((HEADS, rows), F32), shape((width, rows), BF16), shape((rows, width), F32),
                   shape((rows, width), F32), shape((width, rows), BF16), shape(wide, BF16), shape(wide, BF16),
                   shape((rows, 128), F32), shape(wide, BF16), shape(tall, BF16)],
        in_specs=[smem, vmem, vmem, vmem, hbm, vmem, smem, hbm] + [vmem] * 5 + [hbm] + [vmem] * 3,
        out_specs=[hbm] * 5 + [vmem] + [hbm] * 6 + [vmem] + [hbm] * 2,
        scratch_shapes=[pltpu.VMEM((width, 3 * width), BF16), pltpu.VMEM((width, width), BF16), pltpu.VMEM((width, ff), BF16),
                        pltpu.VMEM((rows, width), BF16), pltpu.VMEM((rows, width), BF16), pltpu.VMEM((rows, width), BF16),
                        pltpu.VMEM(window, BF16), pltpu.VMEM(window, BF16), pltpu.VMEM(window, BF16),
                        pltpu.VMEM((3 * rows, rows), F32), pltpu.VMEM((2 * width // HEADS, rows), F32),
                        pltpu.VMEM((rows, width), F32), pltpu.VMEM((rows, width), F32), pltpu.VMEM((rows, width), F32),
                        pltpu.VMEM((rows, width), BF16), pltpu.VMEM(wide, F32), pltpu.VMEM((2, rows, 128), F32),
                        pltpu.VMEM((3, width, rows), BF16), pltpu.VMEM(wide, BF16), pltpu.VMEM(wide, BF16), pltpu.VMEM(wide, BF16),
                        pltpu.VMEM(tall, BF16), dma((8,)), dma((8,)), dma((8,)), dma((13,))],
        compiler_params=pltpu.CompilerParams(collective_id=1, has_side_effects=True, vmem_limit_bytes=60 << 20),
        cost_estimate=pl.CostEstimate(flops=12 << 30, bytes_accessed=40 << 20, transcendentals=5 << 20),
    )(lengths, tokens, ln1_gain[None], ln1_bias[None], w_qkv, qv_bias[None], head_scale[None], w_out, out_bias[None],
      pa_gain[None], pa_bias[None], mid_gain[None], mid_bias[None], w_fc1, fc1_bias[None], ffn_gain[None], ffn_bias[None])


SEND = 4
RECV = 8
KEEP = 8
LAG_XY = (0, 2, 4, 6, 8, 10)
LAG_Z = (0, 2, 4, 6, 8, 10)
MIDDLE = 6
PIECES = 3


def back_kernel(tok, a2, a1, ao, aq, cot, lens, qw_in, kw_in, vw_in, lse, att, attn, first, scale_ffn, tokens,
                gain, pa_gain, mid_gain, ffn_gain, head_scale, fc2_bias, normed_in, slope_in, low_ffn_in, w2_in, w1_in, wo_in, wq_in,
                out2, out1, outo, outq, vout, grad_tok, layer_out,
                am, ap, bm, bp, s1x, s1y, s2x, s2y, sr, sl, szr, szl, szx, szy, swx, swy,
                r1x, r1y, r2x, r2y, rr, rl, rzr, rzl, rzx, rzy, rwx, rwy,
                k2x, k2y, t3, kzx, kzy, kwx, kwy, out, vec, vown, vrecv,
                qw, kw, vw, dow, stw, mask, mask_q, dqa, dka, dva, total, d_first, d_ffn, parts,
                normed, w2b, colb, lowb, slopeb,
                load_sem, peer_send, peer_recv, send, recv, vsend, vrecv_sem, asend, arecv, in_sem, w2_sem, col_sem, low_sem, slope_sem,
                out_sem):
    dp, blk = lax.axis_index("dp"), lax.axis_index("blk")
    z, x = dp // 2, dp % 2
    y, c = blk // 2, blk % 2
    core_dev, x_dev, y_dev = (dp, blk + 1 - 2 * c), (dp + 1 - 2 * x, blk), (dp, blk + 2 - 4 * y)
    up_dev, down_dev = (dp + 2, blk), (dp - 2, blk)
    rounds = 24
    rows, width = tokens.shape
    dim = width // HEADS

    ff = normed.shape[1]
    n_ff = ff // FC
    n_o, n_q = width // FC, 3 * width // FC

    def piece2(j):
        return [pltpu.make_async_copy(w2_in.at[pl.ds(j * FC, FC)], w2b.at[j % PIECES], w2_sem.at[j % PIECES]),
                pltpu.make_async_copy(low_ffn_in.at[:, pl.ds(j * FC, FC)], lowb.at[j % PIECES], low_sem.at[j % PIECES])]

    def piece_slope(j):
        return pltpu.make_async_copy(slope_in.at[:, pl.ds(j * FC, FC)], slopeb.at[j % PIECES], slope_sem.at[j % PIECES])

    def piece_col(q, ref, j):
        return pltpu.make_async_copy(ref.at[:, pl.ds(j * FC, FC)], colb.at[q % PIECES], col_sem.at[q % PIECES])

    def start_col(q):
        def go(ref, low, high):
            def start():
                piece_col(q, ref, q - low).start()
            if isinstance(q, int):
                if low <= q < high:
                    start()
            else:
                pl.when((q >= low) & (q < high))(start)
        go(w1_in, 0, n_ff)
        go(wo_in, n_ff, n_ff + n_o)
        go(wq_in, n_ff + n_o, n_ff + n_o + n_q)

    early = [pltpu.make_async_copy(qw_in, qw, in_sem.at[0]), pltpu.make_async_copy(kw_in, kw, in_sem.at[1]),
             pltpu.make_async_copy(vw_in, vw, in_sem.at[2])]
    normed_load = pltpu.make_async_copy(normed_in, normed, in_sem.at[3])

    bar = pltpu.get_barrier_semaphore()
    z_devs = [((dp + 2 * k) % 8, blk) for k in range(1, 4)]
    for dev in [core_dev, x_dev, y_dev] + z_devs:
        pl.semaphore_signal(bar, inc=1, device_id=dev, device_id_type=MESH)
    def remote(src, dst, ssem, rsem, dev):
        return pltpu.make_async_remote_copy(src, dst, ssem, rsem, device_id=dev, device_id_type=MESH)

    def window_rows(kind):
        src, dst, dev, k = {"cross": (0, 2, y_dev, 0), "own": (0, 1, core_dev, 1), "relay": (2, 1, core_dev, 2)}[kind]
        copies = [remote(stw.at[src], stw.at[dst], asend.at[k], arecv.at[k], dev)]
        if kind == "own":
            copies.append(remote(dow.at[src], dow.at[dst], asend.at[3], arecv.at[3], dev))
        return copies

    def window_piece(kind, i):
        src, dst, dev, k = {"cross": (0, 2, y_dev, 4), "relay": (2, 1, core_dev, 4 + HEADS // 2)}[kind]
        cols = pl.ds(pl.multiple_of(i * 2 * dim, 2 * dim), 2 * dim)
        return remote(dow.at[src, :, cols], dow.at[dst, :, cols], asend.at[k + i], arecv.at[k + i], dev)

    a_src = [(a2, g) for g in range(8)] + [(a1, 0), (a1, 1), (ao, 0), (ao, 1), (aq, 0), (aq, 1)]
    b_src = [(cot, 0)]
    n_a = len(a_src)

    def loads(kind, i, own):
        k = i if kind == "a" else n_a + i
        if kind == "a":
            ref, g = a_src[i]
            if own:
                return pltpu.make_async_copy(ref.at[:, :, :, c, g], am.at[i], load_sem.at[k])
            return remote(ref.at[:, :, :, 1 - c, g], ap.at[i], peer_send.at[k], peer_recv.at[k], core_dev)
        ref, g = b_src[i]
        part = ref.at[:, pl.ds(g * WR, WR)]
        if own:
            return pltpu.make_async_copy(part, bm.at[i], load_sem.at[k])
        return remote(part, bp.at[i], peer_send.at[k], peer_recv.at[k], core_dev)

    phases = [([("b", 0)] + [("a", g) for g in range(8)]), [("a", 8), ("a", 9)], [("a", 10), ("a", 11), ("a", 12), ("a", 13)]]
    for item in phases[0]:
        loads(*item, True).start()
    normed_load.start()
    for j in range(PIECES):
        for cp in piece2(j):
            cp.start()
    for phase in phases[1:]:
        for item in phase:
            loads(*item, True).start()
    for j in range(PIECES):
        start_col(j)
        piece_slope(j).start()
    for cp in early:
        cp.start()

    def peer_b(i):
        k = n_a + i
        return remote(bm.at[i], bp.at[i], peer_send.at[k], peer_recv.at[k], core_dev)

    def arrive(phase):
        for item in phase:
            loads(*item, True).wait()
            loads(*item, False).wait_recv()

    vec[...] = jnp.zeros_like(vec)
    total[...] = jnp.zeros_like(total)
    parts[...] = jnp.zeros_like(parts)
    q_spots = blk * rows + lax.broadcasted_iota(jnp.int32, (1, rows), 1)
    k_spots = (blk - 2) * rows + lax.broadcasted_iota(jnp.int32, (3 * rows, 1), 0)
    mask[...] = jnp.where((k_spots >= sequence_starts(lens, q_spots)) & (k_spots <= q_spots), 0.0, -1e30)
    q_spots = (blk + 1) * rows + lax.broadcasted_iota(jnp.int32, (1, 2 * rows), 1)
    k_spots = blk * rows + lax.broadcasted_iota(jnp.int32, (rows, 1), 0)
    mask_q[...] = jnp.where(k_spots >= sequence_starts(lens, q_spots), 0.0, -1e30)

    pl.semaphore_wait(bar, 6)
    for phase in phases:
        for item in phase:
            loads(*item, False).start()

    def place(r):
        g = jnp.where(r < 8, r, jnp.where(r < 16, 8 + r % 2, jnp.where(r < 18, 10 + r % 2, 12 + r % 2)))
        b = jnp.where(r < 8, 0, (r - 8) // 2 + 1)
        return g, b

    def product(r, zs, xs, ys, col, width):
        g, b = place(r)
        cols = pl.ds(col, width)
        la, lp = am[g, zs, xs, ys], ap[g, zs, xs, ys]
        lead = la.shape[:-1]
        m = 1
        for d in lead:
            m *= d
        res = dot32(la.reshape(m, tok), bm[b, :, cols]) + dot32(lp.reshape(m, tok), bp[b, :, cols])
        return res.reshape(lead + (width,))

    ALL = slice(None)
    col_y, col_z = WX, 2 * WX
    S1X, S1Y, S2X, S2Y, SR, SL, SZR, SZL, SZX, SZY, SWX, SWY = range(12)

    def message(src, dst, kind, dev):
        def make(r):
            return remote(src.at[r % SEND], dst.at[r % RECV], send.at[kind, r % SEND], recv.at[kind, r % RECV], dev)
        return make

    step1x, step1y = message(s1x, r1x, S1X, x_dev), message(s1y, r1y, S1Y, y_dev)
    step2x, step2y = message(s2x, r2x, S2X, y_dev), message(s2y, r2y, S2Y, x_dev)
    stepzx, stepzy = message(szx, rzx, SZX, x_dev), message(szy, rzy, SZY, y_dev)
    stepwx, stepwy = message(swx, rwx, SWX, y_dev), message(swy, rwy, SWY, x_dev)
    steps = (step1x, step1y, step2x, step2y, stepzx, stepzy, stepwx, stepwy)

    def put(step, ref, r, value):
        @pl.when(r >= SEND)
        def _():
            step(r - SEND).wait_send()

        ref[r % SEND] = value.astype(BF16)
        step(r).start()

    def chain(src, dst, kind, r, lo, hi, dev):
        return remote(src.at[r % SEND, lo:hi], dst.at[r % RECV, lo:hi], send.at[kind, r % SEND], recv.at[kind, r % RECV], dev)

    def chain_hop(hop, r, src, dst, kind_r, kind_l, term):
        slot, rslot = r % SEND, r % RECV

        @pl.when(z == hop)
        def _():
            if hop > 0:
                chain(src[0], dst[0], kind_r, r, hop - 1, 3, up_dev).wait_recv()

            @pl.when(r >= SEND)
            def _():
                chain(src[0], dst[0], kind_r, r - SEND, hop, 3, up_dev).wait_send()

            for d in range(hop + 1, 4):
                value = term(r, d)
                if hop > 0:
                    value = value + dst[0][rslot, d - 1].astype(F32)
                src[0][slot, d - 1] = value.astype(BF16)
            chain(src[0], dst[0], kind_r, r, hop, 3, up_dev).start()

        @pl.when(z == 3 - hop)
        def _():
            if hop > 0:
                chain(src[1], dst[1], kind_l, r, 0, 4 - hop, down_dev).wait_recv()

            @pl.when(r >= SEND)
            def _():
                chain(src[1], dst[1], kind_l, r - SEND, 0, 3 - hop, down_dev).wait_send()

            for d in range(0, 3 - hop):
                value = term(r, d)
                if hop > 0:
                    value = value + dst[1][rslot, d].astype(F32)
                src[1][slot, d] = value.astype(BF16)
            chain(src[1], dst[1], kind_l, r, 0, 3 - hop, down_dev).start()

    def chain_last(r, src, dst, kind_r, kind_l, total_ref):
        rslot = r % RECV
        for at in range(4):
            @pl.when(z == at)
            def _():
                if at == 3:
                    chain(src[0], dst[0], kind_r, r, 2, 3, up_dev).wait_recv()
                if at == 0:
                    chain(src[1], dst[1], kind_l, r, 0, 1, down_dev).wait_recv()
                value = None
                if at > 0:
                    value = dst[0][rslot, at - 1].astype(F32)
                if at < 3:
                    down = dst[1][rslot, at].astype(F32)
                    value = down if value is None else value + down
                total_ref[...] = value

    def chain_drain(r, src, dst, kind_r, kind_l):
        for hop in range(3):
            @pl.when(z == hop)
            def _():
                chain(src[0], dst[0], kind_r, r, hop, 3, up_dev).wait_send()

            @pl.when(z == 3 - hop)
            def _():
                chain(src[1], dst[1], kind_l, r, 0, 3 - hop, down_dev).wait_send()

    def z_term(r, d):
        return product(r, d, ALL, ALL, col_z, WZ)

    def t_term(r, d):
        return t3[r % KEEP, d]

    zsrc, zdst = (szr, szl), (rzr, rzl)
    csrc, cdst = (sr, sl), (rr, rl)

    def xy0(r):
        put(step1x, s1x, r, product(r, ALL, 1 - x, ALL, 0, WX))
        put(step1y, s1y, r, product(r, ALL, ALL, 1 - y, col_y, WX))

    def xy1(r):
        slot = r % KEEP
        step1x(r).wait_recv()
        k2x[...] = product(r, ALL, x, ALL, 0, WX) + r1x[r % RECV].astype(F32)
        put(step2x, s2x, r, k2x[:, 1 - y])
        kwx[slot] = k2x[:, y]
        step1y(r).wait_recv()
        k2y[...] = product(r, ALL, ALL, y, col_y, WX) + r1y[r % RECV].astype(F32)
        put(step2y, s2y, r, k2y[:, 1 - x])
        kwy[slot] = k2y[:, x]

    def xy2(r):
        slot = r % KEEP
        step2x(r).wait_recv()
        t3[slot, :, :, 0:WX] = kwx[slot] + r2x[r % RECV].astype(F32)
        step2y(r).wait_recv()
        t3[slot, :, :, WX:2 * WX] = kwy[slot] + r2y[r % RECV].astype(F32)
        chain_hop(0, r, csrc, cdst, SR, SL, t_term)

    def xy3(r):
        chain_hop(1, r, csrc, cdst, SR, SL, t_term)

    def xy4(r):
        chain_hop(2, r, csrc, cdst, SR, SL, t_term)

    def xy5(r):
        chain_last(r, csrc, cdst, SR, SL, out.at[r, :, 0:2 * WX])
        out[r, :, 0:2 * WX] = out[r, :, 0:2 * WX] + t3[r % KEEP, z]

    def z0(r):
        chain_hop(0, r, zsrc, zdst, SZR, SZL, z_term)

    def z1(r):
        chain_hop(1, r, zsrc, zdst, SZR, SZL, z_term)

    def z2(r):
        chain_hop(2, r, zsrc, zdst, SZR, SZL, z_term)

    def z3(r):
        slot = r % KEEP
        chain_last(r, zsrc, zdst, SZR, SZL, kzx)
        kzx[...] = kzx[...] + product(r, z, ALL, ALL, col_z, WZ)
        put(stepzx, szx, r, kzx[1 - x, :, :, 0:WZ // 2])
        put(stepzy, szy, r, kzx[:, 1 - y, :, WZ // 2:WZ])
        kzy[slot, 0] = kzx[x, :, :, 0:WZ // 2]
        kzy[slot, 1] = kzx[:, y, :, WZ // 2:WZ]

    def z4(r):
        slot = r % KEEP
        stepzx(r).wait_recv()
        kzy[slot, 0] = kzy[slot, 0] + rzx[r % RECV].astype(F32)
        put(stepwx, swx, r, kzy[slot, 0, 1 - y])
        stepzy(r).wait_recv()
        kzy[slot, 1] = kzy[slot, 1] + rzy[r % RECV].astype(F32)
        put(stepwy, swy, r, kzy[slot, 1, 1 - x])

    def z5(r):
        slot = r % KEEP
        stepwx(r).wait_recv()
        out[r, :, 2 * WX:2 * WX + WZ // 2] = kzy[slot, 0, y] + rwx[r % RECV].astype(F32)
        stepwy(r).wait_recv()
        out[r, :, 2 * WX + WZ // 2:] = kzy[slot, 1, x] + rwy[r % RECV].astype(F32)

    def drain(r):
        for step in steps:
            step(r).wait_send()
        chain_drain(r, csrc, cdst, SR, SL)
        chain_drain(r, zsrc, zdst, SZR, SZL)

    v = vec.shape[0]
    h1, h2, h3 = v // 2, v // 4, v // 8
    o1 = c * h1
    o2 = o1 + x * h2
    o3 = o2 + y * h3
    base = h1 + h2 + h3

    def vstep(i):
        if i == 0:
            return [remote(vec.at[pl.ds((1 - c) * h1, h1)], vrecv.at[pl.ds(0, h1)], vsend.at[0], vrecv_sem.at[0], core_dev)]
        if i == 1:
            return [remote(vown.at[pl.ds(o1 + (1 - x) * h2, h2)], vrecv.at[pl.ds(h1, h2)], vsend.at[1], vrecv_sem.at[1], x_dev)]
        if i == 2:
            return [remote(vown.at[pl.ds(o2 + (1 - y) * h3, h3)], vrecv.at[pl.ds(h1 + h2, h3)], vsend.at[2], vrecv_sem.at[2], y_dev)]
        if i == 3:
            return [remote(vown.at[pl.ds(o3, h3)], vrecv.at[pl.ds(base + z * h3, h3)], vsend.at[3 + k], vrecv_sem.at[3 + k],
                           z_devs[k - 1]) for k in range(1, 4)]
        if i == 4:
            return [remote(vout.at[pl.ds(o3, h3)], vout.at[pl.ds(o3, h3)], vsend.at[7], vrecv_sem.at[7], y_dev)]
        if i == 5:
            return [remote(vout.at[pl.ds(o2, h2)], vout.at[pl.ds(o2, h2)], vsend.at[8], vrecv_sem.at[8], x_dev)]
        return [remote(vout.at[pl.ds(o1, h1)], vout.at[pl.ds(o1, h1)], vsend.at[9], vrecv_sem.at[9], core_dev)]

    def vector_step(i):
        if i > 0:
            for cp in vstep(i - 1):
                cp.wait_recv()
        if i == 1:
            vown[pl.ds(o1, h1)] = vec[pl.ds(o1, h1)] + vrecv[0:h1]
        if i == 2:
            vown[pl.ds(o2, h2)] = vown[pl.ds(o2, h2)] + vrecv[h1:h1 + h2]
        if i == 3:
            vown[pl.ds(o3, h3)] = vown[pl.ds(o3, h3)] + vrecv[h1 + h2:base]
            vrecv[pl.ds(base + z * h3, h3)] = vown[pl.ds(o3, h3)]
        if i == 4:
            total = vrecv[base:base + h3]
            for k in range(1, 4):
                total = total + vrecv[base + k * h3:base + (k + 1) * h3]
            vout[pl.ds(o3, h3)] = total
        if i < 7:
            for cp in vstep(i):
                cp.start()

    def rows_arrive():
        for cp in early:
            cp.wait()

    def cross_arrive():
        @pl.when(y == 0)
        def _():
            for cp in window_rows("cross"):
                cp.wait_recv()

        @pl.when((y == 0) & (c == 0))
        def _():
            for cp in window_rows("relay"):
                cp.start()

        @pl.when(c == 0)
        def _():
            for cp in window_rows("own"):
                cp.wait_recv()

        @pl.when((y == 0) & (c == 1))
        def _():
            for cp in window_rows("relay"):
                cp.wait_recv()

    def cross_send(i):
        @pl.when(y == 1)
        def _():
            window_piece("cross", i).start()

    def cross_relay(i):
        @pl.when(y == 0)
        def _():
            window_piece("cross", i).wait_recv()

        @pl.when((y == 0) & (c == 0))
        def _():
            window_piece("relay", i).start()

    def windows_drain():
        @pl.when(y == 1)
        def _():
            for cp in window_rows("cross"):
                cp.wait_send()
            for i in range(HEADS // 2):
                window_piece("cross", i).wait_send()

        @pl.when(c == 1)
        def _():
            for cp in window_rows("own"):
                cp.wait_send()

        @pl.when((y == 0) & (c == 0))
        def _():
            for cp in window_rows("relay"):
                cp.wait_send()
            for i in range(HEADS // 2):
                window_piece("relay", i).wait_send()

    def attend_pairs(i, kj, qj, bias, to_q, to_k, first):
        cols = pl.ds(pl.multiple_of(i * 2 * dim, 2 * dim), 2 * dim)
        k2, v2, q2, d2 = kw[kj, :, cols], vw[kj, :, cols], qw[qj, :, cols], dow[qj, :, cols]
        for sub in range(2):
            part = slice(sub * dim, (sub + 1) * dim)
            k1, v1, q1, d1 = k2[:, part], v2[:, part], q2[:, part], d2[:, part]
            log_total = stw[qj, pl.ds(2 * i + sub, 1)]
            delta = stw[qj, pl.ds(HEADS + 2 * i + sub, 1)]
            probs = jnp.exp(dot_nt(k1, q1) + bias[...] - log_total)
            low_s = (probs * (dot_nt(v1, d1) - delta)).astype(BF16)
            if to_q:
                term = dot_tn(k1, low_s)
                dqa[part] = term if first else dqa[part] + term
            if to_k:
                term = dot32(low_s, q1)
                dka[sub] = term if first else dka[sub] + term
                term = dot32(probs.astype(BF16), d1)
                dva[sub] = term if first else dva[sub] + term

    def attend_near(i):
        cols = pl.ds(pl.multiple_of(i * 2 * dim, 2 * dim), 2 * dim)
        attend_pairs(i, 2, 0, mask.at[2 * rows:3 * rows], True, True, True)

        @pl.when(blk >= 1)
        def _():
            attend_pairs(i, 1, 0, mask.at[rows:2 * rows], True, False, False)

        @pl.when(blk >= 2)
        def _():
            attend_pairs(i, 0, 0, mask.at[0:rows], True, False, False)

        bm[6, :, cols] = (dqa[...].T * (dim ** -0.5)).astype(BF16)
        d_ffn[:, cols] = jnp.concatenate([dka[0], dka[1]], axis=1)
        d_ffn[:, pl.ds(pl.multiple_of(width + i * 2 * dim, 2 * dim), 2 * dim)] = jnp.concatenate([dva[0], dva[1]], axis=1)

    def attend_far(i):
        cols = pl.ds(pl.multiple_of(i * 2 * dim, 2 * dim), 2 * dim)
        dk_sum, dv_sum = d_ffn[:, cols], d_ffn[:, pl.ds(pl.multiple_of(width + i * 2 * dim, 2 * dim), 2 * dim)]

        @pl.when(blk == 3)
        def _():
            bm[7, :, cols] = dk_sum.astype(BF16)
            bm[8, :, cols] = dv_sum.astype(BF16)

        @pl.when((y == 0) & (c == 1))
        def _():
            window_piece("relay", i).wait_recv()

        @pl.when(blk <= 2)
        def _():
            attend_pairs(i, 2, 1, mask_q.at[:, 0:rows], False, True, True)

        @pl.when(blk <= 1)
        def _():
            attend_pairs(i, 2, 2, mask_q.at[:, rows:2 * rows], False, True, False)

        @pl.when(blk <= 2)
        def _():
            bm[7, :, cols] = (dk_sum + jnp.concatenate([dka[0], dka[1]], axis=1)).astype(BF16)
            bm[8, :, cols] = (dv_sum + jnp.concatenate([dva[0], dva[1]], axis=1)).astype(BF16)

    V_IN_GAIN, V_IN_BIAS, V_QV, V_OUT, V_PA_GAIN, V_PA_BIAS, V_MID_GAIN, V_MID_BIAS, V_FC2 = (
        k * (width // 128) for k in (0, 1, 2, 4, 5, 6, 7, 8, 9))
    V_FC1 = 10 * (width // 128)
    V_FFN_GAIN = V_FC1 + ff // 128
    V_FFN_BIAS = V_FFN_GAIN + ff // 128
    V_HEADS = V_FFN_BIAS + ff // 128

    def put_row(first_row, row):
        for k in range(row.shape[1] // 128):
            vec[first_row + k:first_row + k + 1, :] = row[:, k * 128:(k + 1) * 128]

    def put_row_at(first_row, j, row):
        for k in range(FC // 128):
            vec[pl.ds(first_row + j * (FC // 128) + k, 1), :] = row[:, k * 128:(k + 1) * 128]

    def chunk_cols(j):
        return pl.ds(pl.multiple_of(j * FC, FC), FC)

    def ffn_first(j):
        cols = chunk_cols(j)
        for cp in piece2(j):
            cp.wait()
        weights = w2b[j % PIECES]
        total[...] = total[...] + dot32(lowb[j % PIECES], weights)
        grad = dot_nt(bm[0], weights)
        unit = normed[:, cols].astype(F32)
        d_ffn[:, cols] = grad
        put_row_at(V_FFN_GAIN, j, jnp.sum(grad * unit, axis=0, keepdims=True))
        put_row_at(V_FFN_BIAS, j, jnp.sum(grad, axis=0, keepdims=True))
        grad = grad * ffn_gain[:, cols]
        parts[0] = parts[0] + lane_sums(grad)
        parts[1] = parts[1] + lane_sums(grad * unit)

        @pl.when(j + PIECES < n_ff)
        def _():
            for cp in piece2(j + PIECES):
                cp.start()

    def ffn_between():
        layer_out[...] = (first[...] + total[...] + fc2_bias[...]).astype(BF16)
        total[...] = jnp.zeros_like(total)
        parts[2] = jnp.broadcast_to(jnp.sum(parts[0], axis=-1, keepdims=True) * (1.0 / ff), parts.shape[1:])
        parts[3] = jnp.broadcast_to(jnp.sum(parts[1], axis=-1, keepdims=True) * (1.0 / ff), parts.shape[1:])

    def ffn_second(j):
        cols = chunk_cols(j)
        piece_col(j, w1_in, j).wait()
        piece_slope(j).wait()
        grad = d_ffn[:, cols] * ffn_gain[:, cols]
        grad = scale_ffn[:, 0:1] * (grad - parts[2][:, 0:1] - normed[:, cols].astype(F32) * parts[3][:, 0:1])
        low = (grad * slopeb[j % PIECES].astype(F32)).astype(BF16)
        bm[1 + j // 2, :, pl.ds(pl.multiple_of((j % 2) * FC, FC), FC)] = low
        put_row_at(V_FC1, j, jnp.sum(low.astype(F32), axis=0, keepdims=True))
        total[...] = total[...] + dot_nt(low, colb[j % PIECES])

        @pl.when(j % 2 == 1)
        def _():
            peer_b(1 + j // 2).start()

        @pl.when(j + PIECES < n_ff)
        def _():
            piece_slope(j + PIECES).start()

        start_col(j + PIECES)

    def unit_rows(values):
        centered = values - jnp.mean(values, axis=-1, keepdims=True)
        scale = lax.rsqrt(jnp.mean(centered * centered, axis=-1, keepdims=True) + 1e-05)
        return centered * scale, scale

    def norm_back(grad, values, gain_row, gain_at, bias_at):
        unit, scale = unit_rows(values)
        put_row(gain_at, jnp.sum(grad * unit, axis=0, keepdims=True))
        put_row(bias_at, jnp.sum(grad, axis=0, keepdims=True))
        grad = grad * gain_row
        return scale * (grad - jnp.mean(grad, axis=-1, keepdims=True) - unit * jnp.mean(grad * unit, axis=-1, keepdims=True))

    def middle_first():
        d_out = bm[0].astype(F32)
        put_row(V_FC2, jnp.sum(d_out, axis=0, keepdims=True))
        d_first[...] = d_out + norm_back(total[...], first[...], mid_gain[...], V_MID_GAIN, V_MID_BIAS)
        low = norm_back(d_first[...], attn[...], pa_gain[...], V_PA_GAIN, V_PA_BIAS).astype(BF16)
        bm[5] = low
        peer_b(5).start()
        put_row(V_OUT, jnp.sum(low.astype(F32), axis=0, keepdims=True))

    def middle_second():
        for k in range(n_o):
            piece_col(n_ff + k, wo_in, k).wait()
        total[...] = dot_nt(bm[5, :, 0:FC], colb[n_ff % PIECES])
        for k in range(1, n_o):
            total[...] = total[...] + dot_nt(bm[5, :, k * FC:(k + 1) * FC], colb[(n_ff + k) % PIECES])
        for k in range(n_o):
            start_col(n_ff + k + PIECES)
        attended = att[...]
        low = (total[...] * head_row(head_scale, width)).astype(BF16)
        dow[0] = low
        both = low.astype(F32) * attended
        high = both.astype(BF16)
        rest = (both - high.astype(F32)).astype(BF16)
        head_of = lax.broadcasted_iota(jnp.int32, (HEADS, width), 1) // dim
        pick = jnp.where(head_of == lax.broadcasted_iota(jnp.int32, (HEADS, width), 0), 1.0, 0.0).astype(BF16)
        by_column = jnp.broadcast_to(jnp.sum(total[...] * attended, axis=0, keepdims=True), (8, width))
        high_sum = by_column.astype(BF16)
        rest_sum = (by_column - high_sum.astype(F32)).astype(BF16)
        by_head = dot_nt(high_sum, pick) + dot_nt(rest_sum, pick)
        vec[V_HEADS:V_HEADS + 1, 0:HEADS] = by_head[0:1]
        stw[0, 0:HEADS] = lse[...]
        stw[0, HEADS:2 * HEADS] = dot_nt(pick, high) + dot_nt(pick, rest)

        @pl.when(y == 1)
        def _():
            for cp in window_rows("cross"):
                cp.start()

        @pl.when(c == 1)
        def _():
            for cp in window_rows("own"):
                cp.start()

    def input_first():
        for i in range(6, 9):
            peer_b(i).start()
        base_q = n_ff + n_o
        for k in range(n_q):
            piece_col(base_q + k, wq_in, k).wait()
            at = k * FC
            term = dot_nt(bm[6 + at // width, :, at % width:at % width + FC], colb[(base_q + k) % PIECES])
            total[...] = term if k == 0 else total[...] + term
            start_col(base_q + k + PIECES)

    def input_second():
        grad = norm_back(total[...], tokens[...].astype(F32), gain[...], V_IN_GAIN, V_IN_BIAS)
        grad_tok[...] = d_first[...] + grad
        put_row(V_QV, jnp.sum(bm[6].astype(F32), axis=0, keepdims=True))
        put_row(V_QV + width // 128, jnp.sum(bm[8].astype(F32), axis=0, keepdims=True))

    def share(r):
        half = pl.ds((r % 2) * ROWS, ROWS)
        return [((r >= 0) & (r < 8), pltpu.make_async_copy(out.at[r], out2.at[pl.ds(r * ROWS, ROWS)], out_sem.at[0])),
                ((r >= 8) & (r < 16), pltpu.make_async_copy(out.at[r], out1.at[half, pl.ds((r - 8) // 2 * WR, WR)], out_sem.at[0])),
                ((r >= 16) & (r < 18), pltpu.make_async_copy(out.at[r], outo.at[half], out_sem.at[0])),
                ((r >= 18) & (r < rounds), pltpu.make_async_copy(out.at[r], outq.at[half, pl.ds((r - 18) // 2 * WR, WR)], out_sem.at[0]))]

    n_pairs = HEADS // 2
    after = MIDDLE + n_pairs + 3
    plan = sorted(list(zip(LAG_XY, (xy0, xy1, xy2, xy3, xy4, xy5))) + list(zip(LAG_Z, (z0, z1, z2, z3, z4, z5))),
                  key=lambda item: -item[0])
    last = max(LAG_XY + LAG_Z)

    def at_slot(s, number, work):
        @pl.when(s == number)
        def _():
            work()

    def slot_step(s, carry):
        at_slot(s, 0, lambda: arrive(phases[0]))
        at_slot(s, 7, lambda: arrive(phases[1]))
        at_slot(s, 15, lambda: arrive(phases[2]))

        @pl.when((s >= 8) & (s < 16) & (s % 2 == 0))
        def _():
            peer_b(1 + (s - 8) // 2).wait_recv()

        at_slot(s, 16, lambda: peer_b(5).wait_recv())
        at_slot(s, 18, lambda: [peer_b(i).wait_recv() for i in range(6, 9)])

        for lag, work in plan:
            r = s - lag

            @pl.when((r >= 0) & (r < rounds))
            def _():
                work(r)

        r = s - last

        @pl.when(r >= 0)
        def _():
            for here, cp in share(r):
                pl.when(here)(cp.start)

        at_slot(s, 0, normed_load.wait)
        for u in range(3):
            j = 3 * s + u

            @pl.when(j < n_ff)
            def _():
                ffn_first(j)

        at_slot(s, 2, ffn_between)
        for u in range(3):
            j = 3 * (s - 3) + u

            @pl.when((j >= 0) & (j < n_ff))
            def _():
                ffn_second(j)

        at_slot(s, MIDDLE, middle_first)
        at_slot(s, MIDDLE, middle_second)
        at_slot(s, MIDDLE, rows_arrive)
        at_slot(s, MIDDLE + 2, cross_arrive)
        i = s - MIDDLE

        @pl.when((i >= 0) & (i < n_pairs))
        def _():
            cross_send(i)

        @pl.when((i >= 1) & (i < n_pairs + 1))
        def _():
            attend_near(i - 1)

        @pl.when((i >= 2) & (i < n_pairs + 2))
        def _():
            cross_relay(i - 2)

        @pl.when((i >= 3) & (i < n_pairs + 3))
        def _():
            attend_far(i - 3)

        at_slot(s, after - 1, input_first)
        at_slot(s, after, input_second)
        for i in range(8):
            @pl.when(s == after + i)
            def _():
                vector_step(i)

        return carry

    lax.fori_loop(0, rounds + last, slot_step, 0)
    lax.fori_loop(rounds - SEND, rounds, lambda r, carry: (drain(r), carry)[1], 0)
    windows_drain()
    for phase in phases:
        for item in phase:
            loads(*item, False).wait_send()
    for i in range(1, 9):
        peer_b(i).wait_send()
    for i in range(7):
        for cp in vstep(i):
            cp.wait_send()

    def share_wait(r, carry):
        share(jnp.int32(0))[0][1].wait()
        return carry

    lax.fori_loop(0, rounds, share_wait, 0)


def blocks_first(turned):
    return turned.reshape(4, 2, 2, 2, turned.shape[0] // 32 // ROWS, ROWS, turned.shape[1])


def finish_kernel(n_big, rows_of, *refs):
    n_vec = len(rows_of)
    n_in = n_big + 1
    big = refs[:n_in]
    out_big, out_vec = refs[n_in:n_in + n_big], refs[n_in + n_big:n_in + n_big + n_vec]
    out_heads = refs[n_in + n_big + n_vec]
    held, in_sem, out_sem = refs[n_in + n_big + n_vec + 1:-2], refs[-2], refs[-1]
    loads = [pltpu.make_async_copy(src, dst, in_sem.at[k]) for k, (src, dst) in enumerate(zip(big, held))]
    for cp in loads:
        cp.start()
    stores = [[pltpu.make_async_copy(src, dst, out_sem.at[k])] for k, (src, dst) in enumerate(zip(held, out_big))]
    stores.append([pltpu.make_async_copy(held[-1].at[pl.ds(first, count)], dst, out_sem.at[n_big + k])
                   for k, ((first, count), dst) in enumerate(zip(rows_of, out_vec))])
    for load, group in zip(loads, stores):
        load.wait()
        for cp in group:
            cp.start()
    at = sum(rows_of[-1])
    out_heads[...] = held[-1][at:at + 1, 0:HEADS]
    for group in stores:
        for cp in group:
            cp.wait()


def finish(layer_out, grad_tokens, out2, out1, outo, outq, flat, sizes):
    big = (layer_out, grad_tokens, out2, out1, outo, outq)
    rows_of, at = [], 0
    for size in sizes:
        rows_of.append((at, size // 128))
        at += size // 128
    hbm, vmem = pl.BlockSpec(memory_space=pl.ANY), pl.BlockSpec(memory_space=pltpu.VMEM)
    res = pl.pallas_call(
        functools.partial(finish_kernel, len(big), tuple(rows_of)),
        out_shape=[jax.ShapeDtypeStruct(item.shape, item.dtype) for item in big]
        + [jax.ShapeDtypeStruct((count, 128), F32) for _, count in rows_of] + [jax.ShapeDtypeStruct((1, HEADS), F32)],
        in_specs=[hbm] * (len(big) + 1),
        out_specs=[hbm] * (len(big) + len(rows_of)) + [vmem],
        scratch_shapes=[pltpu.VMEM(item.shape, item.dtype) for item in big + (flat,)]
        + [pltpu.SemaphoreType.DMA((len(big) + 1,)), pltpu.SemaphoreType.DMA((len(big) + len(rows_of),))],
    )(*big, flat)
    layer_out, grad_tokens, out2, out1, outo, outq = res[:6]
    ln1g, ln1b, qv, bo, pag, pab, ln2g, ln2b, c2, c1, lnfg, lnfb = (item.reshape(-1) for item in res[6:-1])
    return (layer_out, grad_tokens, ln1g, ln1b, outq, qv, res[-1].reshape(-1), outo, bo, pag, pab, ln2g, ln2b, out1, c1, lnfg, lnfb,
            out2, c2)


def fast_shards(
    tokens, lengths, ln1_gain, ln1_bias, w_qkv, qv_bias, head_scale, w_out, out_bias, lnpa_gain, lnpa_bias,
    ln2_gain, ln2_bias, w_fc1, fc1_bias, lnf_gain, lnf_bias, w_fc2, fc2_bias, cotangent,
):
    tok, width = tokens.shape
    ff = w_fc1.shape[1]
    (low_in_t, q_win, k_win, v_win, att, lse, scaled_t, attn, first, low_mid_t, normed, slope, scale_ffn, low_ffn, low_ffn_t) = forward(
        lengths, tokens, ln1_gain, ln1_bias, w_qkv, qv_bias, head_scale, w_out, out_bias, lnpa_gain, lnpa_bias, ln2_gain, ln2_bias,
        w_fc1, fc1_bias, lnf_gain, lnf_bias)
    rounds = 24
    hbm, vmem, smem = (pl.BlockSpec(memory_space=space) for space in (pl.ANY, pltpu.VMEM, pltpu.SMEM))
    a_shape = (14, 4, 2, 2, ROWS, tok)
    b_shape = (9, tok, WR)
    msgs = [(4, 2, ROWS, WX), (4, 2, ROWS, WX), (4, ROWS, WX), (4, ROWS, WX), (3, ROWS, 2 * WX), (3, ROWS, 2 * WX),
            (3, 2, 2, ROWS, WZ), (3, 2, 2, ROWS, WZ), (2, ROWS, WZ // 2), (2, ROWS, WZ // 2), (ROWS, WZ // 2), (ROWS, WZ // 2)]
    sizes = (width, width, 2 * width) + (width,) * 6 + (ff, ff, ff)
    v = -(-(sum(sizes) + 128) // 8192) * 64
    dma, shape = pltpu.SemaphoreType.DMA, jax.ShapeDtypeStruct
    f32s = [(4, 2, ROWS, WX), (4, 2, ROWS, WX), (KEEP, 4, ROWS, 2 * WX), (2, 2, ROWS, WZ), (KEEP, 2, 2, ROWS, WZ // 2),
            (KEEP, 4, ROWS, WX), (KEEP, 4, ROWS, WX), (rounds, ROWS, WR), (v, 128), (v, 128), (v // 2 + v // 4 + v // 8 * 5, 128)]
    windows = [pltpu.VMEM((3, tok, width), BF16)] * 4 + [pltpu.VMEM((3, 2 * HEADS, tok), F32)]
    more = [(3 * tok, tok), (tok, 2 * tok), (2 * width // HEADS, tok), (2, tok, width // HEADS), (2, tok, width // HEADS),
            (tok, width), (tok, width), (tok, ff), (4, tok, 128)]
    out2, out1, outo, outq, flat, grad_tokens, layer_out = pl.pallas_call(
        functools.partial(back_kernel, tok),
        out_shape=[shape((ff // 32, width), F32), shape((width // 32, ff), F32), shape((width // 32, width), F32),
                   shape((width // 32, 3 * width), F32), shape((v, 128), F32), shape((tok, width), F32), shape((tok, width), BF16)],
        in_specs=[hbm] * 5 + [smem] + [hbm] * 3 + [vmem] * 10 + [smem, vmem] + [hbm] * 7,
        out_specs=[hbm] * 4 + [vmem] * 3,
        scratch_shapes=[pltpu.VMEM(a_shape, BF16), pltpu.VMEM(a_shape, BF16), pltpu.VMEM(b_shape, BF16), pltpu.VMEM(b_shape, BF16)]
        + [pltpu.VMEM((SEND,) + m, BF16) for m in msgs]
        + [pltpu.VMEM((RECV,) + m, BF16) for m in msgs]
        + [pltpu.VMEM(m, F32) for m in f32s] + windows + [pltpu.VMEM(m, F32) for m in more]
        + [pltpu.VMEM((tok, ff), BF16), pltpu.VMEM((PIECES, FC, width), BF16), pltpu.VMEM((PIECES, width, FC), BF16),
           pltpu.VMEM((PIECES, tok, FC), BF16), pltpu.VMEM((PIECES, tok, FC), BF16),
           dma((15,)), dma((23,)), dma((23,)), dma((12, SEND)), dma((12, RECV)), dma((10,)), dma((10,)), dma((4 + HEADS,)), dma((4 + HEADS,)),
           dma((4,)), dma((PIECES,)), dma((PIECES,)), dma((PIECES,)), dma((PIECES,)), dma((1,))],
        compiler_params=pltpu.CompilerParams(collective_id=0, has_side_effects=True, vmem_limit_bytes=63 << 20),
        cost_estimate=pl.CostEstimate(flops=30 << 30, bytes_accessed=50 << 20, transcendentals=4 << 20),
    )(blocks_first(low_ffn_t), blocks_first(low_mid_t), blocks_first(scaled_t), blocks_first(low_in_t),
      cotangent, lengths, q_win, k_win, v_win, lse, att, attn, first, scale_ffn, tokens,
      ln1_gain[None], lnpa_gain[None], ln2_gain[None], lnf_gain[None], head_scale[None], fc2_bias[None],
      normed, slope, low_ffn, w_fc2, w_fc1, w_out, w_qkv)
    return finish(layer_out, grad_tokens, out2, out1, outo, outq, flat, sizes)


def shards(
    tokens,
    lengths,
    ln1_gain,
    ln1_bias,
    w_qkv,
    qv_bias,
    head_scale,
    w_out,
    out_bias,
    lnpa_gain,
    lnpa_bias,
    ln2_gain,
    ln2_bias,
    w_fc1,
    fc1_bias,
    lnf_gain,
    lnf_bias,
    w_fc2,
    fc2_bias,
    cotangent,
):
    row_count, width = tokens.shape
    head_dim = width // HEADS
    factor = head_dim ** (-0.5)
    group = row_count * lax.axis_size("blk")
    own_start = lax.axis_index("blk") * row_count
    seq_ends = jnp.cumsum(lengths[0])
    positions = jnp.arange(group, dtype=jnp.int32)
    labels = jnp.sum((positions[:, None] >= seq_ends[None, :]).astype(jnp.int32), axis=1)
    q_labels = lax.dynamic_slice_in_dim(labels, own_start, row_count, 0)
    q_spots = own_start + jnp.arange(row_count, dtype=jnp.int32)
    inputs = tokens.astype(jnp.float32)
    normed_in, ln1_back = jax.vjp(norm_rows, inputs, ln1_gain, ln1_bias)
    low_in = normed_in.astype(jnp.bfloat16)
    projected = jnp.dot(low_in, w_qkv, preferred_element_type=jnp.float32)
    queries = (projected[:, :width] + qv_bias[:width]).astype(jnp.bfloat16)
    key_rows = projected[:, width : 2 * width].astype(jnp.bfloat16)
    value_rows = (projected[:, 2 * width :] + qv_bias[width:]).astype(jnp.bfloat16)
    query_heads = queries.reshape(row_count, HEADS, head_dim)

    def scored(key_block, start):
        count = key_block.shape[0]
        key_heads = key_block.reshape(count, HEADS, head_dim)
        raw_scores = (
            jnp.einsum("qhd,khd->hqk", query_heads, key_heads, preferred_element_type=jnp.float32)
            * factor
        )
        k_labels = lax.dynamic_slice_in_dim(labels, start, count, 0)
        k_spots = start + jnp.arange(count, dtype=jnp.int32)
        visible = (k_labels[None, :] == q_labels[:, None]) & (k_spots[None, :] <= q_spots[:, None])
        return (raw_scores, visible[None], key_heads)

    def by_blocks(step_fn, carry, pieces):
        count = pieces[0].shape[0]
        unit = max(1, 1024 // row_count) * row_count
        step = count if count <= unit else math.gcd(count, unit)

        def inner(block_index, state):
            offset = block_index * step
            sub_pieces = tuple((lax.dynamic_slice_in_dim(item, offset, step, 0) for item in pieces))
            return step_fn(state, sub_pieces, offset)

        return lax.fori_loop(0, count // step, inner, carry)

    def max_step(carry, pieces, start):
        top_score, totals = carry
        raw_scores, visible, key_heads = scored(pieces[0], start)
        raw_scores = jnp.where(visible, raw_scores, -1e30)
        new_top = jnp.maximum(top_score, jnp.max(raw_scores, axis=-1))
        totals = totals * jnp.exp(top_score - new_top) + jnp.sum(
            jnp.where(visible, jnp.exp(raw_scores - new_top[..., None]), 0.0), axis=-1
        )
        return (new_top, totals)

    start_top = jnp.full((HEADS, row_count), -1e30, jnp.float32)
    start_total = jnp.zeros((HEADS, row_count), jnp.float32)
    top_score, totals = by_blocks(
        max_step, (start_top, start_total), (lax.all_gather(key_rows, "blk", axis=0, tiled=True),)
    )
    log_total = top_score + jnp.log(totals)

    def value_step(carry, pieces, start):
        weighted, leftover = carry
        raw_scores, visible, key_heads = scored(pieces[0], start)
        value_heads = pieces[1].reshape(pieces[1].shape[0], HEADS, head_dim)
        probs = jnp.where(visible, jnp.exp(raw_scores - log_total[..., None]), 0.0)
        low_probs = probs.astype(jnp.bfloat16)
        rest_probs = (probs - low_probs.astype(jnp.float32)).astype(jnp.bfloat16)
        weighted = weighted + jnp.einsum(
            "hqk,khd->qhd", low_probs, value_heads, preferred_element_type=jnp.float32
        )
        leftover = leftover + jnp.einsum(
            "hqk,khd->qhd", rest_probs, value_heads, preferred_element_type=jnp.float32
        )
        return (weighted, leftover)

    empty_heads = jnp.zeros((row_count, HEADS, head_dim), jnp.float32)
    weighted, leftover = by_blocks(
        value_step,
        (empty_heads, empty_heads),
        (
            lax.all_gather(key_rows, "blk", axis=0, tiled=True),
            lax.all_gather(value_rows, "blk", axis=0, tiled=True),
        ),
    )
    attended = weighted.reshape(row_count, width)
    head_gain = jnp.repeat(head_scale, head_dim)
    scaled = (attended * head_gain).astype(jnp.bfloat16)
    attn_out = jnp.dot(scaled, w_out, preferred_element_type=jnp.float32) + out_bias
    branch, pa_back = jax.vjp(norm_rows, attn_out, lnpa_gain, lnpa_bias)
    first_sum = inputs + branch
    normed_mid, ln2_back = jax.vjp(norm_rows, first_sum, ln2_gain, ln2_bias)
    low_mid = normed_mid.astype(jnp.bfloat16)
    pre_act = jnp.dot(low_mid, w_fc1, preferred_element_type=jnp.float32) + fc1_bias
    activated, gelu_back = jax.vjp(gelu_exact, pre_act)
    ffn_normed, lnf_back = jax.vjp(norm_rows, activated, lnf_gain, lnf_bias)
    low_ffn = ffn_normed.astype(jnp.bfloat16)
    layer_out = (
        first_sum + jnp.dot(low_ffn, w_fc2, preferred_element_type=jnp.float32) + fc2_bias
    ).astype(jnp.bfloat16)
    d_output = cotangent.astype(jnp.float32)
    grad_w2 = over_rows(low_ffn, cotangent)
    grad_c2 = jnp.sum(d_output, axis=0)
    d_ffn = over_cols(cotangent, w_fc2)
    d_active, grad_lnf_gain, grad_lnf_bias = lnf_back(d_ffn)
    (d_pre,) = gelu_back(d_active)
    low_pre = d_pre.astype(jnp.bfloat16)
    grad_w1 = over_rows(low_mid, low_pre)
    grad_c1 = jnp.sum(low_pre.astype(jnp.float32), axis=0)
    d_mid = over_cols(low_pre, w_fc1)
    d_first_norm, grad_ln2_gain, grad_ln2_bias = ln2_back(d_mid)
    d_first = d_output + d_first_norm
    d_attn, grad_pa_gain, grad_pa_bias = pa_back(d_first)
    low_attn = d_attn.astype(jnp.bfloat16)
    grad_bo = jnp.sum(low_attn.astype(jnp.float32), axis=0)
    grad_wo = over_rows(scaled, low_attn)
    d_scaled = over_cols(low_attn, w_out)
    grad_hs = jnp.sum((d_scaled * attended).reshape(row_count, HEADS, head_dim), axis=(0, 2))
    d_attended = (d_scaled * head_gain).astype(jnp.bfloat16)
    d_heads = d_attended.reshape(row_count, HEADS, head_dim)
    delta_rows = jnp.sum(d_heads.astype(jnp.float32) * (weighted + leftover), axis=-1)
    delta = delta_rows.T

    def back_step(carry, pieces, start):
        count = pieces[0].shape[0]
        raw_scores, visible, key_heads = scored(pieces[0], start)
        value_heads = pieces[1].reshape(count, HEADS, head_dim)
        probs = jnp.where(visible, jnp.exp(raw_scores - log_total[..., None]), 0.0)
        d_probs = jnp.einsum(
            "qhd,khd->hqk", d_heads, value_heads, preferred_element_type=jnp.float32
        )
        d_scores = (probs * (d_probs - delta[..., None])).astype(jnp.bfloat16)
        d_query = (
            carry[0]
            + jnp.einsum("hqk,khd->qhd", d_scores, key_heads, preferred_element_type=jnp.float32)
            * factor
        )
        key_grad, value_grad = (carry[1], carry[2])
        low_probs = probs.astype(jnp.bfloat16)
        d_value = jnp.einsum(
            "hqk,qhd->khd", low_probs, d_heads, preferred_element_type=jnp.float32
        ).reshape(count, width)
        d_key = (
            jnp.einsum("hqk,qhd->khd", d_scores, query_heads, preferred_element_type=jnp.float32)
            * factor
        ).reshape(count, width)
        key_grad = lax.dynamic_update_slice_in_dim(
            key_grad, lax.dynamic_slice_in_dim(key_grad, start, count, 0) + d_key, start, 0
        )
        value_grad = lax.dynamic_update_slice_in_dim(
            value_grad, lax.dynamic_slice_in_dim(value_grad, start, count, 0) + d_value, start, 0
        )
        return (d_query, key_grad, value_grad)

    empty_group = jnp.zeros((group, width), jnp.float32)
    start_carry = (empty_heads, empty_group, empty_group)
    results = by_blocks(
        back_step,
        start_carry,
        (
            lax.all_gather(key_rows, "blk", axis=0, tiled=True),
            lax.all_gather(value_rows, "blk", axis=0, tiled=True),
        ),
    )
    d_query = results[0]
    own_keys, own_values = (
        lax.psum_scatter(
            results[1].astype(jnp.bfloat16), "blk", scatter_dimension=0, tiled=True
        ).astype(jnp.float32),
        lax.psum_scatter(
            results[2].astype(jnp.bfloat16), "blk", scatter_dimension=0, tiled=True
        ).astype(jnp.float32),
    )
    low_q = d_query.reshape(row_count, width).astype(jnp.bfloat16)
    low_k = own_keys.astype(jnp.bfloat16)
    low_v = own_values.astype(jnp.bfloat16)
    d_projected = jnp.concatenate([low_q, low_k, low_v], axis=1)
    grad_wqkv = over_rows(low_in, d_projected)
    grad_qv = jnp.concatenate(
        [jnp.sum(low_q.astype(jnp.float32), axis=0), jnp.sum(low_v.astype(jnp.float32), axis=0)]
    )
    d_in = over_cols(d_projected, w_qkv)
    d_in_norm, grad_ln1_gain, grad_ln1_bias = ln1_back(d_in)
    grad_tokens = d_first + d_in_norm
    share_wqkv, share_wo, share_w1, share_w2 = (
        lax.psum_scatter(grad_wqkv, ("dp", "blk"), scatter_dimension=0, tiled=True),
        lax.psum_scatter(grad_wo, ("dp", "blk"), scatter_dimension=0, tiled=True),
        lax.psum_scatter(grad_w1, ("dp", "blk"), scatter_dimension=0, tiled=True),
        lax.psum_scatter(grad_w2, ("dp", "blk"), scatter_dimension=0, tiled=True),
    )
    summed = lax.psum(
        (
            grad_ln1_gain,
            grad_ln1_bias,
            grad_qv,
            grad_hs,
            grad_bo,
            grad_pa_gain,
            grad_pa_bias,
            grad_ln2_gain,
            grad_ln2_bias,
            grad_c1,
            grad_lnf_gain,
            grad_lnf_bias,
            grad_c2,
        ),
        ("dp", "blk"),
    )
    return (
        layer_out,
        grad_tokens,
        summed[0],
        summed[1],
        share_wqkv,
        summed[2],
        summed[3],
        share_wo,
        summed[4],
        summed[5],
        summed[6],
        summed[7],
        summed[8],
        share_w1,
        summed[9],
        summed[10],
        summed[11],
        share_w2,
        summed[12],
    )


def solution(mesh):
    in_specs = (
        P(("dp", "blk"), None),
        P("dp", None),
        P(),
        P(),
        P(),
        P(),
        P(),
        P(),
        P(),
        P(),
        P(),
        P(),
        P(),
        P(),
        P(),
        P(),
        P(),
        P(),
        P(),
        P(("dp", "blk"), None),
    )
    out_specs = (
        P(("dp", "blk"), None),
        P(("dp", "blk"), None),
        P(),
        P(),
        P(("dp", "blk"), None),
        P(),
        P(),
        P(("dp", "blk"), None),
        P(),
        P(),
        P(),
        P(),
        P(),
        P(("dp", "blk"), None),
        P(),
        P(),
        P(),
        P(("dp", "blk"), None),
        P(),
    )
    body = fast_shards if dict(mesh.shape) == {"dp": 8, "blk": 4} else shards
    return jax.shard_map(body, mesh=mesh, in_specs=in_specs, out_specs=out_specs, check_vma=False)
```

```python
import functools
import math

import jax
import jax.numpy as jnp
from jax import lax
from jax.experimental import pallas as pl
from jax.experimental.pallas import tpu as pltpu
from jax.sharding import PartitionSpec as P

HEADS = 16
MESH = pl.DeviceIdType.MESH
F32, BF16 = jnp.float32, jnp.bfloat16


def norm_rows(values_in, gain_vec, bias_vec):
    row_mean = jnp.mean(values_in, axis=-1, keepdims=True)
    centered = values_in - row_mean
    variance = jnp.mean(centered * centered, axis=-1, keepdims=True)
    return centered * lax.rsqrt(variance + 1e-05) * gain_vec + bias_vec


def gelu_exact(pre_values):
    return 0.5 * pre_values * (1.0 + lax.erf(pre_values * 0.7071067811865476))


def over_rows(left, right):
    return lax.dot_general(
        left, right, (((0,), (0,)), ((), ())), preferred_element_type=jnp.float32
    )


def over_cols(left, right):
    return lax.dot_general(
        left, right, (((1,), (1,)), ((), ())), preferred_element_type=jnp.float32
    )


def dot32(left, right):
    return jnp.dot(left, right, preferred_element_type=F32)


def dot_nt(left, right):
    return lax.dot_general(left, right, (((1,), (1,)), ((), ())), preferred_element_type=F32)


def dot_tn(left, right):
    return lax.dot_general(left, right, (((0,), (0,)), ((), ())), preferred_element_type=F32)


def norm_in(rows, gain, bias):
    mean = jnp.mean(rows, axis=-1, keepdims=True)
    centered = rows - mean
    variance = jnp.mean(centered * centered, axis=-1, keepdims=True)
    return centered * lax.rsqrt(variance + 1e-05) * gain + bias


def sequence_starts(lens, spots):
    start = jnp.zeros_like(spots)
    end = jnp.int32(0)
    for j in range(lens.shape[1]):
        end = end + lens[0, j]
        start = jnp.where(spots >= end, jnp.maximum(start, end), start)
    return start


def lane_sums(values):
    total = values[:, 0:128]
    for k in range(1, values.shape[1] // 128):
        total = total + values[:, k * 128:(k + 1) * 128]
    return total


def head_row(scales, width):
    head_of = lax.broadcasted_iota(jnp.int32, (1, width), 1) // (width // HEADS)
    row = jnp.full((1, width), scales[0, 0], F32)
    for h in range(1, HEADS):
        row = jnp.where(head_of == h, scales[0, h], row)
    return row


FC = 512


def forward_kernel(lens, tok, gain, bias, w_hbm, qv_bias, head_scale, wo_hbm, out_bias, pa_gain, pa_bias, mid_gain, mid_bias,
                   w1_hbm, fc1_bias, ffn_gain, ffn_bias, cot,
                   low_in_t, qw_out, kw_out, vw_out, att_out, lse, scaled_t, attn_out, first_out, low_mid_t, normed_out, slope_out,
                   scale_out, low_ffn_out, low_ffn_t, cot_x, low_in_x, low_mid_x, scaled_y,
                   w, wo, w1, tok_y, low_in, low_y, qw, kw, vw, mask, acc, att, attn, first, low_mid, act, part, turned, normed,
                   slope, low_ffn, ffn_turned, w_sem, sends, recvs, out_sem):
    dp, blk = lax.axis_index("dp"), lax.axis_index("blk")
    x, y, c = dp % 2, blk // 2, blk % 2
    core_dev, x_dev, y_dev = (dp, blk + 1 - 2 * c), (dp + 1 - 2 * x, blk), (dp, blk + 2 - 4 * y)
    rows, width = tok.shape
    dim = width // HEADS
    half = rows // 2
    ff = w1.shape[1]
    n_ff = ff // FC

    def remote(src, dst, i, dev):
        return pltpu.make_async_remote_copy(src, dst, sends.at[i], recvs.at[i], device_id=dev, device_id_type=MESH)

    n_w = 6
    wc = 3 * width // n_w
    loads = [pltpu.make_async_copy(w_hbm.at[:, pl.ds(i * wc, wc)], w.at[:, pl.ds(i * wc, wc)], w_sem.at[i]) for i in range(n_w)]
    loads.append(pltpu.make_async_copy(wo_hbm, wo, w_sem.at[6]))
    loads.append(pltpu.make_async_copy(w1_hbm, w1, w_sem.at[7]))
    for i in (2, 3, 4, 5, 0, 1, 6, 7):
        loads[i].start()
    bar = pltpu.get_barrier_semaphore()
    for dev in (core_dev, x_dev, y_dev):
        pl.semaphore_signal(bar, inc=1, device_id=dev, device_id_type=MESH)
    pl.semaphore_wait(bar, 3)
    cross = [remote(tok.at[pl.ds(i * half, half)], tok_y.at[pl.ds(i * half, half)], i, y_dev) for i in range(2)]
    for cp in cross:
        cp.start()

    ahead = [remote(cot, cot_x, 8, x_dev), remote(turned.at[0], low_in_x, 9, x_dev), remote(turned.at[2], low_mid_x, 10, x_dev),
             remote(turned.at[1], scaled_y, 11, y_dev)]
    ahead[0].start()
    outs = []

    def emit(src, dst):
        cp = pltpu.make_async_copy(src, dst, out_sem.at[len(outs)])
        cp.start()
        outs.append(cp)

    q_spots = blk * rows + lax.broadcasted_iota(jnp.int32, (1, rows), 1)
    starts = sequence_starts(lens, q_spots)
    k_spots = (blk - 2) * rows + lax.broadcasted_iota(jnp.int32, (3 * rows, 1), 0)
    mask[...] = jnp.where((k_spots >= starts) & (k_spots <= q_spots), 0.0, -1e30)

    low_in[...] = norm_in(tok[...].astype(F32), gain[...], bias[...]).astype(BF16)

    def project(src, r0, n, which):
        res = dot32(src[r0:r0 + n], w[:, which * width:(which + 1) * width])
        if which == 0:
            res = (res + qv_bias[:, 0:width]).astype(BF16).astype(F32) * (dim ** -0.5)
        if which == 2:
            res = res + qv_bias[:, width:]
        return res.astype(BF16)

    own_q = remote(qw.at[0], qw.at[1], 2, core_dev)
    own_k = remote(kw.at[2], kw.at[1], 3, core_dev)
    own_v = remote(vw.at[2], vw.at[1], 4, core_dev)
    relay_q = remote(qw.at[2], qw.at[1], 5, core_dev)
    relay_k = remote(kw.at[0], kw.at[1], 6, core_dev)
    relay_v = remote(vw.at[0], vw.at[1], 7, core_dev)

    for cp in loads[2:4]:
        cp.wait()
    kw[2] = project(low_in, 0, rows, 1)

    @pl.when(c == 0)
    def _():
        own_k.start()

    for cp in loads[4:6]:
        cp.wait()
    vw[2] = project(low_in, 0, rows, 2)

    @pl.when(c == 0)
    def _():
        own_v.start()

    for cp in loads[0:2]:
        cp.wait()
    qw[0] = project(low_in, 0, rows, 0)

    @pl.when(c == 1)
    def _():
        own_q.start()

    turned[0] = low_in[...].T
    ahead[1].start()
    emit(turned.at[0], low_in_t)

    for i in range(2):
        cross[i].wait_recv()
        low_y[i * half:(i + 1) * half] = norm_in(tok_y[i * half:(i + 1) * half].astype(F32), gain[...], bias[...]).astype(BF16)

        @pl.when(y == 1)
        def _():
            kw[0, i * half:(i + 1) * half] = project(low_y, i * half, half, 1)
            vw[0, i * half:(i + 1) * half] = project(low_y, i * half, half, 2)

        @pl.when(y == 0)
        def _():
            qw[2, i * half:(i + 1) * half] = project(low_y, i * half, half, 0)

    @pl.when((y == 1) & (c == 1))
    def _():
        relay_k.start()
        relay_v.start()

    @pl.when((y == 0) & (c == 0))
    def _():
        relay_q.start()

    @pl.when(c == 1)
    def _():
        own_k.wait_recv()
        own_v.wait_recv()

    @pl.when((y == 1) & (c == 0))
    def _():
        relay_k.wait_recv()
        relay_v.wait_recv()

    emit(kw, kw_out)
    emit(vw, vw_out)

    def heads(lowest):
        def pair(i, carry):
            cols = pl.ds(pl.multiple_of(i * 2 * dim, 2 * dim), 2 * dim)
            q2 = qw[0, :, cols]
            k2 = [kw[j, :, cols] for j in range(lowest, 3)]
            v2 = [vw[j, :, cols] for j in range(lowest, 3)]
            for sub in range(2):
                one_head = slice(sub * dim, (sub + 1) * dim)
                scores = [dot_nt(k[:, one_head], q2[:, one_head]) + mask[(lowest + n) * rows:(lowest + n + 1) * rows]
                          for n, k in enumerate(k2)]
                top = jnp.max(scores[0], axis=0, keepdims=True)
                for s in scores[1:]:
                    top = jnp.maximum(top, jnp.max(s, axis=0, keepdims=True))
                total, out = None, None
                for s, v in zip(scores, v2):
                    p = jnp.exp(s - top)
                    one = jnp.sum(p, axis=0, keepdims=True)
                    term = dot_tn(v[:, one_head], p.astype(BF16))
                    total = one if total is None else total + one
                    out = term if out is None else out + term
                acc[one_head] = out / total
                lse[pl.ds(2 * i + sub, 1)] = top + jnp.log(total)
            att[:, cols] = acc[...].T
            return carry

        lax.fori_loop(0, HEADS // 2, pair, 0)

    @pl.when(blk == 0)
    def _():
        heads(2)

    @pl.when(blk == 1)
    def _():
        heads(1)

    @pl.when(blk >= 2)
    def _():
        heads(0)

    @pl.when(c == 0)
    def _():
        own_q.wait_recv()

    @pl.when((y == 0) & (c == 1))
    def _():
        relay_q.wait_recv()

    emit(qw, qw_out)
    emit(att, att_out)

    scaled = (att[...] * head_row(head_scale, width)).astype(BF16)
    turned[1] = scaled.T
    ahead[3].start()
    emit(turned.at[1], scaled_t)
    loads[6].wait()
    attn[...] = dot32(scaled, wo[...]) + out_bias[...]
    emit(attn, attn_out)
    first[...] = tok[...].astype(F32) + norm_in(attn[...], pa_gain[...], pa_bias[...])
    emit(first, first_out)
    low_mid[...] = norm_in(first[...], mid_gain[...], mid_bias[...]).astype(BF16)
    turned[2] = low_mid[...].T
    ahead[2].start()
    emit(turned.at[2], low_mid_t)
    loads[7].wait()
    part[...] = jnp.zeros_like(part)

    def ffn_cols(j):
        return pl.ds(pl.multiple_of(j * FC, FC), FC)

    def gelu_part(j, carry):
        cols = ffn_cols(j)
        pre = dot32(low_mid[...], w1[:, cols]) + fc1_bias[:, cols]
        gate = 0.5 * (1.0 + lax.erf(pre * 0.7071067811865476))
        out = pre * gate
        act[:, cols] = out
        slope[:, cols] = (gate + pre * (jnp.exp(-0.5 * (pre * pre)) * 0.3989422804014327)).astype(BF16)
        part[0] = part[0] + lane_sums(out)
        return carry

    lax.fori_loop(0, n_ff, gelu_part, 0)
    emit(slope, slope_out)
    mean = jnp.sum(part[0], axis=-1, keepdims=True) * (1.0 / ff)

    def spread_part(j, carry):
        centered = act[:, ffn_cols(j)] - mean
        part[1] = part[1] + lane_sums(centered * centered)
        return carry

    lax.fori_loop(0, n_ff, spread_part, 0)
    scale = lax.rsqrt(jnp.sum(part[1], axis=-1, keepdims=True) * (1.0 / ff) + 1e-05)
    scale_out[...] = jnp.broadcast_to(scale, scale_out.shape)

    def norm_part(j, carry):
        cols = ffn_cols(j)
        unit = (act[:, cols] - mean) * scale
        normed[:, cols] = unit.astype(BF16)
        low = (unit * ffn_gain[:, cols] + ffn_bias[:, cols]).astype(BF16)
        low_ffn[:, cols] = low
        ffn_turned[cols] = low.T
        return carry

    lax.fori_loop(0, n_ff, norm_part, 0)
    emit(normed, normed_out)
    emit(low_ffn, low_ffn_out)
    emit(ffn_turned, low_ffn_t)
    for cp in cross:
        cp.wait_send()
    for cp in ahead:
        cp.wait()

    @pl.when(c == 0)
    def _():
        own_k.wait_send()
        own_v.wait_send()

    @pl.when(c == 1)
    def _():
        own_q.wait_send()

    @pl.when((y == 1) & (c == 1))
    def _():
        relay_k.wait_send()
        relay_v.wait_send()

    @pl.when((y == 0) & (c == 0))
    def _():
        relay_q.wait_send()

    for cp in outs:
        cp.wait()


def forward(lengths, tokens, ln1_gain, ln1_bias, w_qkv, qv_bias, head_scale, w_out, out_bias, pa_gain, pa_bias, mid_gain, mid_bias,
            w_fc1, fc1_bias, ffn_gain, ffn_bias, cotangent):
    rows, width = tokens.shape
    ff = w_fc1.shape[1]
    hbm, vmem, smem = (pl.BlockSpec(memory_space=space) for space in (pl.ANY, pltpu.VMEM, pltpu.SMEM))
    shape = jax.ShapeDtypeStruct
    window, wide, tall = (3, rows, width), (rows, ff), (ff, rows)
    dma = pltpu.SemaphoreType.DMA
    return pl.pallas_call(
        forward_kernel,
        out_shape=[shape((width, rows), BF16), shape(window, BF16), shape(window, BF16), shape(window, BF16),
                   shape((rows, width), F32), shape((HEADS, rows), F32), shape((width, rows), BF16), shape((rows, width), F32),
                   shape((rows, width), F32), shape((width, rows), BF16), shape(wide, BF16), shape(wide, BF16),
                   shape((rows, 128), F32), shape(wide, BF16), shape(tall, BF16), shape((rows, width), BF16), shape((width, rows), BF16),
                   shape((width, rows), BF16), shape((width, rows), BF16)],
        in_specs=[smem, vmem, vmem, vmem, hbm, vmem, smem, hbm] + [vmem] * 5 + [hbm] + [vmem] * 3 + [hbm],
        out_specs=[hbm] * 5 + [vmem] + [hbm] * 6 + [vmem] + [hbm] * 6,
        scratch_shapes=[pltpu.VMEM((width, 3 * width), BF16), pltpu.VMEM((width, width), BF16), pltpu.VMEM((width, ff), BF16),
                        pltpu.VMEM((rows, width), BF16), pltpu.VMEM((rows, width), BF16), pltpu.VMEM((rows, width), BF16),
                        pltpu.VMEM(window, BF16), pltpu.VMEM(window, BF16), pltpu.VMEM(window, BF16),
                        pltpu.VMEM((3 * rows, rows), F32), pltpu.VMEM((2 * width // HEADS, rows), F32),
                        pltpu.VMEM((rows, width), F32), pltpu.VMEM((rows, width), F32), pltpu.VMEM((rows, width), F32),
                        pltpu.VMEM((rows, width), BF16), pltpu.VMEM(wide, F32), pltpu.VMEM((2, rows, 128), F32),
                        pltpu.VMEM((3, width, rows), BF16), pltpu.VMEM(wide, BF16), pltpu.VMEM(wide, BF16), pltpu.VMEM(wide, BF16),
                        pltpu.VMEM(tall, BF16), dma((8,)), dma((12,)), dma((12,)), dma((13,))],
        compiler_params=pltpu.CompilerParams(collective_id=1, has_side_effects=True, vmem_limit_bytes=60 << 20),
        cost_estimate=pl.CostEstimate(flops=12 << 30, bytes_accessed=40 << 20, transcendentals=5 << 20),
    )(lengths, tokens, ln1_gain[None], ln1_bias[None], w_qkv, qv_bias[None], head_scale[None], w_out, out_bias[None],
      pa_gain[None], pa_bias[None], mid_gain[None], mid_bias[None], w_fc1, fc1_bias[None], ffn_gain[None], ffn_bias[None], cotangent)


SEND = 4
RECV = 8
KEEP = 8
WY = 384
WZ = 128
WR = WY + WZ
ROWS = 32
FIRST = 2
LAG_Y = (0, 2, 4, 6, 8)
LAG_Z = (0, 2, 4, 6, 8)
LAG_SWAP = (9, 11)
MIDDLE = 6
FAR = 3
PIECES = 3


def back_kernel(tok, a2, a1, a1x, ao, aoy, aq, aqx, cot, cot_x, lens, qw_in, kw_in, vw_in, lse, att_in, attn_in, first_in, scale_ffn, tokens,
                gain, pa_gain, mid_gain, ffn_gain, head_scale, fc2_bias, normed_in, slope_in, low_ffn_in, w2_in, w1_in, wo_in, wq_in,
                out2, out1, outo, outq, vout, grad_tok, layer_out,
                am, bm, pre_other, attn_other, dpj, s1, sr, sl, szr, szl, szy, sswap, r1, rr, rl, rzr, rzl, rzy, rswap,
                prod, kz, kzy, out, swapped, vec, vown, vrecv,
                qw, kw, vw, dow, stw, mask, mask_q, total, d_first, d_ffn, parts, att, attn, first, layer_held,
                normed, w2b, colb, lowb, slopeb,
                a_send, a_recv, b_send, b_recv, send, recv, vsend, vrecv_sem, asend, arecv, in_sem, w2_sem, col_sem, low_sem, slope_sem,
                swap_sems, attn_sems, out_sem):
    dp, blk = lax.axis_index("dp"), lax.axis_index("blk")
    z, x = dp // 2, dp % 2
    y, c = blk // 2, blk % 2
    core_dev, x_dev, y_dev = (dp, blk + 1 - 2 * c), (dp + 1 - 2 * x, blk), (dp, blk + 2 - 4 * y)
    cross_dev = (dp + 1 - 2 * x, blk + 1 - 2 * c)
    up_dev, down_dev = (dp + 2, blk), (dp - 2, blk)
    rounds = 24
    rows, width = tokens.shape
    dim = width // HEADS
    n_attn = WR // (2 * dim)

    ff = normed.shape[1]
    n_ff = ff // FC
    n_o, n_q = width // FC, 3 * width // FC

    def piece2(j):
        return [pltpu.make_async_copy(w2_in.at[pl.ds(j * FC, FC)], w2b.at[j % PIECES], w2_sem.at[j % PIECES]),
                pltpu.make_async_copy(low_ffn_in.at[:, pl.ds(j * FC, FC)], lowb.at[j % PIECES], low_sem.at[j % PIECES])]

    def pre_place(q):
        half = n_ff // 2
        return ((q + 1) % 2 + x * (2 * (q % 2) - 1)) * half + q // 2

    def piece_slope(q):
        return pltpu.make_async_copy(slope_in.at[:, pl.ds(pre_place(q) * FC, FC)], slopeb.at[q % PIECES], slope_sem.at[q % PIECES])

    def piece_col(q, ref, j):
        return pltpu.make_async_copy(ref.at[:, pl.ds(j * FC, FC)], colb.at[q % PIECES], col_sem.at[q % PIECES])

    def start_col(q):
        def go(ref, low, high, where=None):
            def start():
                piece_col(q, ref, q - low if where is None else where(q)).start()
            if isinstance(q, int):
                if low <= q < high:
                    start()
            else:
                pl.when((q >= low) & (q < high))(start)
        go(w1_in, 0, n_ff, pre_place)
        go(wo_in, n_ff, n_ff + n_o)
        go(wq_in, n_ff + n_o, n_ff + n_o + n_q)

    early = [pltpu.make_async_copy(qw_in, qw, in_sem.at[0]), pltpu.make_async_copy(kw_in, kw, in_sem.at[1]),
             pltpu.make_async_copy(vw_in, vw, in_sem.at[2])]
    normed_load = pltpu.make_async_copy(normed_in, normed, in_sem.at[3])
    layer_copy = pltpu.make_async_copy(layer_held, layer_out, in_sem.at[4])
    grad_copy = pltpu.make_async_copy(d_first, grad_tok, in_sem.at[5])
    first_load = pltpu.make_async_copy(first_in, first, in_sem.at[6])
    attn_load = pltpu.make_async_copy(attn_in, attn, in_sem.at[7])
    att_load = pltpu.make_async_copy(att_in, att, in_sem.at[8])

    bar = pltpu.get_barrier_semaphore()
    z_devs = [((dp + 2 * k) % 8, blk) for k in range(1, 4)]
    for dev in [core_dev, x_dev, y_dev, cross_dev] + z_devs:
        pl.semaphore_signal(bar, inc=1, device_id=dev, device_id_type=MESH)
    def remote(src, dst, ssem, rsem, dev):
        return pltpu.make_async_remote_copy(src, dst, ssem, rsem, device_id=dev, device_id_type=MESH)

    def window_rows(kind):
        src, dst, dev, k = {"cross": (0, 2, y_dev, 0), "own": (0, 1, core_dev, 1), "relay": (2, 1, core_dev, 2)}[kind]
        copies = [remote(stw.at[src], stw.at[dst], asend.at[k], arecv.at[k], dev)]
        if kind == "own":
            copies.append(remote(dow.at[src], dow.at[dst], asend.at[3], arecv.at[3], dev))
        return copies

    def window_piece(kind, i):
        src, dst, dev, k = {"cross": (0, 2, y_dev, 4), "relay": (2, 1, core_dev, 4 + HEADS // 2)}[kind]
        cols = pl.ds(pl.multiple_of(i * 2 * dim, 2 * dim), 2 * dim)
        return remote(dow.at[src, :, cols], dow.at[dst, :, cols], asend.at[k + i], arecv.at[k + i], dev)

    def rows_of(ref, g, who, core):
        if g < 4:
            return ref.at[:, who, :, core, g]
        if g in (6, 7):
            return ref.at[:, :, g % 2, core, 0]
        return ref.at[:, g % 2, :, core, 0]

    a_own = [a2] * 4 + [a1] * 2 + [ao] * 2 + [aq] * 2
    a_far = [None] * 4 + [a1x] * 2 + [aoy] * 2 + [aqx] * 2

    def a_load(g, t):
        sems = (a_send.at[g, t], a_recv.at[g, t])
        if t == 0:
            return pltpu.make_async_copy(rows_of(a_own[g], g, x, c), am.at[g, 0], a_recv.at[g, 0])
        if t == 1:
            return remote(rows_of(a_own[g], g, x, 1 - c), am.at[g, 1], *sems, core_dev)
        if g < 4:
            return remote(rows_of(a2, g, 1 - x, c if t == 2 else 1 - c), am.at[g, t], *sems, x_dev if t == 2 else cross_dev)
        if t == 2:
            return pltpu.make_async_copy(rows_of(a_far[g], g, x, c), am.at[g, 2], a_recv.at[g, 2])
        return remote(rows_of(a_far[g], g, x, 1 - c), am.at[g, 3], *sems, core_dev)

    def cot_load(b, t):
        part = (cot if t < 2 else cot_x).at[:, pl.ds(b * WR, WR)]
        if t % 2 == 0:
            return pltpu.make_async_copy(part, bm.at[b, t], b_recv.at[b, t])
        return remote(part, bm.at[b, t], b_send.at[b, t], b_recv.at[b, t], core_dev)

    def local(g, t):
        return t == 0 or (t == 2 and g >= 4)

    def a_arrive(g):
        for t in range(4):
            if local(g, t):
                a_load(g, t).wait()
            else:
                a_load(g, t).wait_recv()

    def b_to_core(b, t):
        return remote(bm.at[b, t], bm.at[b, t + 1], b_send.at[b, t + 1], b_recv.at[b, t + 1], core_dev)

    def b_far(b, src, dev):
        return remote(src, bm.at[b, 2], b_send.at[b, 2], b_recv.at[b, 2], dev)

    def pre_far(k):
        return b_far(2 + k, pre_other.at[k], x_dev)

    def attn_far(k):
        cols = pl.ds(k * 2 * dim, 2 * dim)
        return remote(attn_other.at[:, cols], bm.at[6, 2, :, cols], attn_sems.at[0, k], attn_sems.at[1, k], y_dev)

    def proj_block(who, k):
        return jnp.where(who == 0, k, jnp.where(k == 0, 4, jnp.where(k == 1, 3, 5)))

    def proj_far(k):
        return b_far(7 + k, dpj.at[proj_block(1 - x, k)], x_dev)

    for b in range(2):
        cot_load(b, 0).start()
    for g in range(4):
        a_load(g, 0).start()
    normed_load.start()
    for j in range(PIECES):
        for cp in piece2(j):
            cp.start()
    for b in range(2):
        cot_load(b, 2).start()
    for j in range(PIECES):
        start_col(j)
        piece_slope(j).start()
    for g in range(4, 10):
        a_load(g, 0).start()
        a_load(g, 2).start()
    for cp in early + [first_load, attn_load, att_load]:
        cp.start()

    vec[...] = jnp.zeros_like(vec)
    total[...] = jnp.zeros_like(total)
    parts[...] = jnp.zeros_like(parts)
    q_spots = blk * rows + lax.broadcasted_iota(jnp.int32, (1, rows), 1)
    k_spots = (blk - 2) * rows + lax.broadcasted_iota(jnp.int32, (3 * rows, 1), 0)
    mask[...] = jnp.where((k_spots >= sequence_starts(lens, q_spots)) & (k_spots <= q_spots), 0.0, -1e30)
    q_spots = (blk + 1) * rows + lax.broadcasted_iota(jnp.int32, (1, 2 * rows), 1)
    k_spots = blk * rows + lax.broadcasted_iota(jnp.int32, (rows, 1), 0)
    mask_q[...] = jnp.where(k_spots >= sequence_starts(lens, q_spots), 0.0, -1e30)

    pl.semaphore_wait(bar, 7)
    for g in range(4):
        for t in (2, 3, 1):
            a_load(g, t).start()
        if g < 2:
            cot_load(g, 1).start()
            cot_load(g, 3).start()
    for g in range(4, 10):
        a_load(g, 1).start()
        a_load(g, 3).start()

    def is_out(r):
        return (r >= 18) & (r < 20)

    def proj_turn(r):
        return jnp.where(r < 18, 0, (r - 18) // 2)

    def place(r):
        q = r % 2
        g = jnp.where(r < 8, r // 2, jnp.where(r < 16, 4 + q, jnp.where(is_out(r), 6 + q, 8 + q)))
        b = jnp.where(r < 8, q, jnp.where(r < 16, 2 + (r - 8) // 2, jnp.where(is_out(r), 6, 7 + proj_turn(r))))
        return g, b

    def turned_axes(r):
        is_o = is_out(r)
        here = jnp.where(is_o, x, y)
        sum_dev = (jnp.where(is_o, x_dev[0], y_dev[0]), jnp.where(is_o, x_dev[1], y_dev[1]))
        swap_dev = (jnp.where(is_o, y_dev[0], x_dev[0]), jnp.where(is_o, y_dev[1], x_dev[1]))
        return here, sum_dev, swap_dev

    def multiply(r):
        g, b = place(r)
        res = None
        for t in range(4):
            term = dot32(am[g, t].reshape(8 * ROWS, tok), bm[b, t])
            res = term if res is None else res + term
        prod[r % KEEP] = res.reshape(4, 2, ROWS, WR)

    S1, SR, SL, SZR, SZL, SZY = range(6)

    def from_slot(r):
        return jnp.where(is_out(r), RECV + r % 2, r % RECV)

    def message(src, dst, kind, which):
        def make(r):
            slot = from_slot(r)
            return remote(src.at[r % SEND], dst.at[slot], send.at[kind, r % SEND], recv.at[kind, slot], turned_axes(r)[which])
        return make

    step1, stepz = message(s1, r1, S1, 1), message(szy, rzy, SZY, 1)

    def put(step, ref, r, value):
        @pl.when(r >= SEND)
        def _():
            step(r - SEND).wait_send()

        ref[r % SEND] = value.astype(BF16)
        step(r).start()

    def chain(src, dst, kind, r, lo, hi, dev):
        return remote(src.at[r % SEND, lo:hi], dst.at[r % RECV, lo:hi], send.at[kind, r % SEND], recv.at[kind, r % RECV], dev)

    def chain_hop(hop, r, src, dst, kind_r, kind_l, term):
        slot, rslot = r % SEND, r % RECV

        @pl.when(z == hop)
        def _():
            if hop > 0:
                chain(src[0], dst[0], kind_r, r, hop - 1, 3, up_dev).wait_recv()

            @pl.when(r >= SEND)
            def _():
                chain(src[0], dst[0], kind_r, r - SEND, hop, 3, up_dev).wait_send()

            for d in range(hop + 1, 4):
                value = term(r, d)
                if hop > 0:
                    value = value + dst[0][rslot, d - 1].astype(F32)
                src[0][slot, d - 1] = value.astype(BF16)
            chain(src[0], dst[0], kind_r, r, hop, 3, up_dev).start()

        @pl.when(z == 3 - hop)
        def _():
            if hop > 0:
                chain(src[1], dst[1], kind_l, r, 0, 4 - hop, down_dev).wait_recv()

            @pl.when(r >= SEND)
            def _():
                chain(src[1], dst[1], kind_l, r - SEND, 0, 3 - hop, down_dev).wait_send()

            for d in range(0, 3 - hop):
                value = term(r, d)
                if hop > 0:
                    value = value + dst[1][rslot, d].astype(F32)
                src[1][slot, d] = value.astype(BF16)
            chain(src[1], dst[1], kind_l, r, 0, 3 - hop, down_dev).start()

    def chain_last(r, src, dst, kind_r, kind_l, total_ref):
        rslot = r % RECV
        for at in range(4):
            @pl.when(z == at)
            def _():
                if at == 3:
                    chain(src[0], dst[0], kind_r, r, 2, 3, up_dev).wait_recv()
                if at == 0:
                    chain(src[1], dst[1], kind_l, r, 0, 1, down_dev).wait_recv()
                value = None
                if at > 0:
                    value = dst[0][rslot, at - 1].astype(F32)
                if at < 3:
                    down = dst[1][rslot, at].astype(F32)
                    value = down if value is None else value + down
                total_ref[...] = value

    def chain_drain(r, src, dst, kind_r, kind_l):
        for hop in range(3):
            @pl.when(z == hop)
            def _():
                chain(src[0], dst[0], kind_r, r, hop, 3, up_dev).wait_send()

            @pl.when(z == 3 - hop)
            def _():
                chain(src[1], dst[1], kind_l, r, 0, 3 - hop, down_dev).wait_send()

    def z_term(r, d):
        return prod[r % KEEP, d, :, :, WY:WR]

    def t_term(r, d):
        return prod[r % KEEP, d, turned_axes(r)[0], :, 0:WY]

    zsrc, zdst = (szr, szl), (rzr, rzl)
    csrc, cdst = (sr, sl), (rr, rl)

    def y0(r):
        multiply(r)
        put(step1, s1, r, prod[r % KEEP, :, 1 - turned_axes(r)[0], :, 0:WY])

    def y1(r):
        step1(r).wait_recv()
        here = turned_axes(r)[0]
        prod[r % KEEP, :, here, :, 0:WY] = prod[r % KEEP, :, here, :, 0:WY] + r1[from_slot(r)].astype(F32)
        chain_hop(0, r, csrc, cdst, SR, SL, t_term)

    def y2(r):
        chain_hop(1, r, csrc, cdst, SR, SL, t_term)

    def y3(r):
        chain_hop(2, r, csrc, cdst, SR, SL, t_term)

    def y4(r):
        chain_last(r, csrc, cdst, SR, SL, out.at[r, :, 0:WY])
        out[r, :, 0:WY] = out[r, :, 0:WY] + prod[r % KEEP, z, turned_axes(r)[0], :, 0:WY]

    def z0(r):
        chain_hop(0, r, zsrc, zdst, SZR, SZL, z_term)

    def z1(r):
        chain_hop(1, r, zsrc, zdst, SZR, SZL, z_term)

    def z2(r):
        chain_hop(2, r, zsrc, zdst, SZR, SZL, z_term)

    def z3(r):
        here = turned_axes(r)[0]
        chain_last(r, zsrc, zdst, SZR, SZL, kz)
        kz[...] = kz[...] + prod[r % KEEP, z, :, :, WY:WR]
        put(stepz, szy, r, kz[1 - here])
        kzy[r % KEEP] = kz[here]

    def z4(r):
        stepz(r).wait_recv()
        out[r, :, WY:WR] = kzy[r % KEEP] + rzy[from_slot(r)].astype(F32)

    def swapping(r):
        return r >= 8

    def mine(r):
        return (r % 2) == jnp.where(is_out(r), y, x)

    def swap_slot(r):
        return (r - 8) // 2

    def swap0(r):
        @pl.when(swapping(r) & ~mine(r))
        def _():
            k = swap_slot(r)
            sswap[k] = out[r].astype(BF16)
            step_swap(r).start()

        @pl.when(~swapping(r) | mine(r))
        def _():
            share(r)

    def swap1(r):
        @pl.when(swapping(r) & mine(r))
        def _():
            k = swap_slot(r)
            step_swap(r).wait_recv()
            swapped[k] = rswap[k].astype(F32)
            share_far(r)

    def step_swap(r):
        k = swap_slot(r)
        return remote(sswap.at[k], rswap.at[k], send_swap(k), recv_swap(k), turned_axes(r)[2])

    def send_swap(k):
        return swap_sems.at[0, k]

    def recv_swap(k):
        return swap_sems.at[1, k]

    def cols_at(start):
        return pl.ds(pl.multiple_of(start, WR), WR)

    def share_copies(r, src, who):
        k = (r - 8) // 2
        return [((r < 8), pltpu.make_async_copy(src, out2.at[pl.ds(pl.multiple_of(r // 2 * ROWS, ROWS), ROWS), cols_at(r % 2 * WR)], out_sem.at[0])),
                ((r >= 8) & (r < 16), pltpu.make_async_copy(src, out1.at[:, cols_at(who * (ff // 2) + k * WR)], out_sem.at[0])),
                (is_out(r), pltpu.make_async_copy(src, outo.at[:, cols_at(who * WR)], out_sem.at[0])),
                ((r >= 16) & ~is_out(r), pltpu.make_async_copy(src, outq.at[:, cols_at(proj_block(who, proj_turn(r)) * WR)], out_sem.at[0]))]

    def share(r):
        for here, cp in share_copies(r, out.at[r], jnp.where(is_out(r), y, x)):
            pl.when(here)(cp.start)

    def share_far(r):
        for here, cp in share_copies(r, swapped.at[swap_slot(r)], 1 - jnp.where(is_out(r), y, x)):
            pl.when(here)(cp.start)

    def drain(r):
        step1(r).wait_send()
        stepz(r).wait_send()
        chain_drain(r, csrc, cdst, SR, SL)
        chain_drain(r, zsrc, zdst, SZR, SZL)

    v = vec.shape[0]
    h1, h2, h3 = v // 2, v // 4, v // 8
    o1 = c * h1
    o2 = o1 + x * h2
    o3 = o2 + y * h3
    base = h1 + h2 + h3

    def vstep(i):
        if i == 0:
            return [remote(vec.at[pl.ds((1 - c) * h1, h1)], vrecv.at[pl.ds(0, h1)], vsend.at[0], vrecv_sem.at[0], core_dev)]
        if i == 1:
            return [remote(vown.at[pl.ds(o1 + (1 - x) * h2, h2)], vrecv.at[pl.ds(h1, h2)], vsend.at[1], vrecv_sem.at[1], x_dev)]
        if i == 2:
            return [remote(vown.at[pl.ds(o2 + (1 - y) * h3, h3)], vrecv.at[pl.ds(h1 + h2, h3)], vsend.at[2], vrecv_sem.at[2], y_dev)]
        if i == 3:
            return [remote(vown.at[pl.ds(o3, h3)], vrecv.at[pl.ds(base + z * h3, h3)], vsend.at[3 + k], vrecv_sem.at[3 + k],
                           z_devs[k - 1]) for k in range(1, 4)]
        if i == 4:
            return [remote(vout.at[pl.ds(o3, h3)], vout.at[pl.ds(o3, h3)], vsend.at[7], vrecv_sem.at[7], y_dev)]
        if i == 5:
            return [remote(vout.at[pl.ds(o2, h2)], vout.at[pl.ds(o2, h2)], vsend.at[8], vrecv_sem.at[8], x_dev)]
        return [remote(vout.at[pl.ds(o1, h1)], vout.at[pl.ds(o1, h1)], vsend.at[9], vrecv_sem.at[9], core_dev)]

    def vector_step(i):
        if i > 0:
            for cp in vstep(i - 1):
                cp.wait_recv()
        if i == 1:
            vown[pl.ds(o1, h1)] = vec[pl.ds(o1, h1)] + vrecv[0:h1]
        if i == 2:
            vown[pl.ds(o2, h2)] = vown[pl.ds(o2, h2)] + vrecv[h1:h1 + h2]
        if i == 3:
            vown[pl.ds(o3, h3)] = vown[pl.ds(o3, h3)] + vrecv[h1 + h2:base]
            vrecv[pl.ds(base + z * h3, h3)] = vown[pl.ds(o3, h3)]
        if i == 4:
            total = vrecv[base:base + h3]
            for k in range(1, 4):
                total = total + vrecv[base + k * h3:base + (k + 1) * h3]
            vout[pl.ds(o3, h3)] = total
        if i < 7:
            for cp in vstep(i):
                cp.start()

    def rows_arrive():
        for cp in early:
            cp.wait()

    def cross_arrive():
        @pl.when(y == 0)
        def _():
            for cp in window_rows("cross"):
                cp.wait_recv()

        @pl.when((y == 0) & (c == 0))
        def _():
            for cp in window_rows("relay"):
                cp.start()

    def others_arrive():
        @pl.when(c == 0)
        def _():
            for cp in window_rows("own"):
                cp.wait_recv()

        @pl.when((y == 0) & (c == 1))
        def _():
            for cp in window_rows("relay"):
                cp.wait_recv()

    def cross_send(i):
        @pl.when(y == 1)
        def _():
            window_piece("cross", i).start()

    def cross_relay(i):
        @pl.when(y == 0)
        def _():
            window_piece("cross", i).wait_recv()

        @pl.when((y == 0) & (c == 0))
        def _():
            window_piece("relay", i).start()

    def windows_drain():
        @pl.when(y == 1)
        def _():
            for cp in window_rows("cross"):
                cp.wait_send()
            for i in range(HEADS // 2):
                window_piece("cross", i).wait_send()

        @pl.when(c == 1)
        def _():
            for cp in window_rows("own"):
                cp.wait_send()

        @pl.when((y == 0) & (c == 0))
        def _():
            for cp in window_rows("relay"):
                cp.wait_send()
            for i in range(HEADS // 2):
                window_piece("relay", i).wait_send()

    lower = lax.broadcasted_iota(jnp.int32, (1, 2 * dim), 1) < dim

    def one_head(values, sub):
        return jnp.where(lower if sub == 0 else ~lower, values, jnp.zeros_like(values))

    def both_heads(terms):
        return jnp.where(lower, terms[0], terms[1])

    def weights_of(i, sub, k1, v1, qj, q2, d2, bias):
        log_total = stw[qj, pl.ds(2 * i + sub, 1)]
        delta = stw[qj, pl.ds(HEADS + 2 * i + sub, 1)]
        probs = jnp.exp(dot_nt(k1, q2) + bias - log_total)
        return probs.astype(BF16), (probs * (dot_nt(v1, d2) - delta)).astype(BF16)

    def add(total_sum, term):
        return term if total_sum is None else total_sum + term

    def attend_near(i):
        cols = pl.ds(pl.multiple_of(i * 2 * dim, 2 * dim), 2 * dim)
        part_cols = pl.ds(pl.multiple_of(i % 4 * 2 * dim, 2 * dim), 2 * dim)

        def blocks(lowest):
            q2, d2 = qw[0, :, cols], dow[0, :, cols]
            dq, dk, dv = None, [None, None], [None, None]
            for kj in range(lowest, 3):
                k2, v2 = kw[kj, :, cols], vw[kj, :, cols]
                for sub in range(2):
                    k1 = one_head(k2, sub)
                    low_p, low_s = weights_of(i, sub, k1, one_head(v2, sub), 0, q2, d2, mask[kj * rows:(kj + 1) * rows])
                    dq = add(dq, dot_tn(k1, low_s))
                    if kj == 2:
                        dk[sub], dv[sub] = dot32(low_s, q2), dot32(low_p, d2)
            dpj[i // 4, :, part_cols] = (dq.T * (dim ** -0.5)).astype(BF16)
            d_ffn[:, cols] = both_heads(dk)
            d_ffn[:, pl.ds(pl.multiple_of(width + i * 2 * dim, 2 * dim), 2 * dim)] = both_heads(dv)

        for number in range(3):
            pl.when(blk == number if number < 2 else blk >= 2)(functools.partial(blocks, 2 - number))

    def attend_far(i):
        cols = pl.ds(pl.multiple_of(i * 2 * dim, 2 * dim), 2 * dim)
        part_cols = pl.ds(pl.multiple_of(i % 4 * 2 * dim, 2 * dim), 2 * dim)

        @pl.when((y == 0) & (c == 1))
        def _():
            window_piece("relay", i).wait_recv()

        def blocks(count):
            k2, v2 = kw[2, :, cols], vw[2, :, cols]
            dk, dv = [None, None], [None, None]
            for sub in range(2):
                k1, v1 = one_head(k2, sub), one_head(v2, sub)
                for qj in range(1, count + 1):
                    q2, d2 = qw[qj, :, cols], dow[qj, :, cols]
                    low_p, low_s = weights_of(i, sub, k1, v1, qj, q2, d2, mask_q[:, (qj - 1) * rows:qj * rows])
                    dk[sub], dv[sub] = add(dk[sub], dot32(low_s, q2)), add(dv[sub], dot32(low_p, d2))
            dk_sum, dv_sum = d_ffn[:, cols], d_ffn[:, pl.ds(pl.multiple_of(width + i * 2 * dim, 2 * dim), 2 * dim)]
            if count > 0:
                dk_sum, dv_sum = dk_sum + both_heads(dk), dv_sum + both_heads(dv)
            dpj[2 + i // 4, :, part_cols] = dk_sum.astype(BF16)
            dpj[4 + i // 4, :, part_cols] = dv_sum.astype(BF16)

        for number in range(3):
            pl.when(blk == 3 - number if number < 2 else blk <= 1)(functools.partial(blocks, number))

    V_IN_GAIN, V_IN_BIAS, V_QV, V_OUT, V_PA_GAIN, V_PA_BIAS, V_MID_GAIN, V_MID_BIAS, V_FC2 = (
        k * (width // 128) for k in (0, 1, 2, 4, 5, 6, 7, 8, 9))
    V_FC1 = 10 * (width // 128)
    V_FFN_GAIN = V_FC1 + ff // 128
    V_FFN_BIAS = V_FFN_GAIN + ff // 128
    V_HEADS = V_FFN_BIAS + ff // 128

    def put_row(first_row, row):
        for k in range(row.shape[1] // 128):
            vec[first_row + k:first_row + k + 1, :] = row[:, k * 128:(k + 1) * 128]

    def put_row_at(first_row, j, row):
        for k in range(FC // 128):
            vec[pl.ds(first_row + j * (FC // 128) + k, 1), :] = row[:, k * 128:(k + 1) * 128]

    def chunk_cols(j):
        return pl.ds(pl.multiple_of(j * FC, FC), FC)

    def ffn_first(j):
        cols = chunk_cols(j)
        for cp in piece2(j):
            cp.wait()
        weights = w2b[j % PIECES]
        total[...] = total[...] + dot32(lowb[j % PIECES], weights)
        grad = dot_nt(bm[0, 0], weights[:, 0:WR]) + dot_nt(bm[1, 0], weights[:, WR:])
        unit = normed[:, cols].astype(F32)
        d_ffn[:, cols] = grad
        put_row_at(V_FFN_GAIN, j, jnp.sum(grad * unit, axis=0, keepdims=True))
        put_row_at(V_FFN_BIAS, j, jnp.sum(grad, axis=0, keepdims=True))
        grad = grad * ffn_gain[:, cols]
        parts[0] = parts[0] + lane_sums(grad)
        parts[1] = parts[1] + lane_sums(grad * unit)

        @pl.when(j + PIECES < n_ff)
        def _():
            for cp in piece2(j + PIECES):
                cp.start()

    def ffn_between():
        layer_held[...] = (first[...] + total[...] + fc2_bias[...]).astype(BF16)
        layer_copy.start()
        total[...] = jnp.zeros_like(total)
        parts[2] = jnp.broadcast_to(jnp.sum(parts[0], axis=-1, keepdims=True) * (1.0 / ff), parts.shape[1:])
        parts[3] = jnp.broadcast_to(jnp.sum(parts[1], axis=-1, keepdims=True) * (1.0 / ff), parts.shape[1:])

    def ffn_second(q):
        j = pre_place(q)
        k = q // 2
        cols = chunk_cols(j)
        piece_col(q, w1_in, j).wait()
        piece_slope(q).wait()
        grad = d_ffn[:, cols] * ffn_gain[:, cols]
        grad = scale_ffn[:, 0:1] * (grad - parts[2][:, 0:1] - normed[:, cols].astype(F32) * parts[3][:, 0:1])
        low = (grad * slopeb[q % PIECES].astype(F32)).astype(BF16)
        put_row_at(V_FC1, j, jnp.sum(low.astype(F32), axis=0, keepdims=True))
        total[...] = total[...] + dot_nt(low, colb[q % PIECES])

        @pl.when(q % 2 == 0)
        def _():
            pre_other[k] = low
            pre_far(k).start()

        @pl.when(q % 2 == 1)
        def _():
            bm[2 + k, 0] = low
            b_to_core(2 + k, 0).start()

        @pl.when(q + PIECES < n_ff)
        def _():
            piece_slope(q + PIECES).start()

        start_col(q + PIECES)

    def unit_rows(values):
        centered = values - jnp.mean(values, axis=-1, keepdims=True)
        scale = lax.rsqrt(jnp.mean(centered * centered, axis=-1, keepdims=True) + 1e-05)
        return centered * scale, scale

    def norm_back(grad, values, gain_row, gain_at, bias_at):
        unit, scale = unit_rows(values)
        put_row(gain_at, jnp.sum(grad * unit, axis=0, keepdims=True))
        put_row(bias_at, jnp.sum(grad, axis=0, keepdims=True))
        grad = grad * gain_row
        return scale * (grad - jnp.mean(grad, axis=-1, keepdims=True) - unit * jnp.mean(grad * unit, axis=-1, keepdims=True))

    def middle_first():
        d_out = jnp.concatenate([bm[0, 0], bm[1, 0]], axis=1).astype(F32)
        put_row(V_FC2, jnp.sum(d_out, axis=0, keepdims=True))
        d_first[...] = d_out + norm_back(total[...], first[...], mid_gain[...], V_MID_GAIN, V_MID_BIAS)
        low = norm_back(d_first[...], attn[...], pa_gain[...], V_PA_GAIN, V_PA_BIAS).astype(BF16)
        for who in range(2):
            @pl.when(y == who)
            def _():
                bm[6, 0] = low[:, who * WR:(who + 1) * WR]
                attn_other[...] = low[:, (1 - who) * WR:(2 - who) * WR]

        b_to_core(6, 0).start()
        put_row(V_OUT, jnp.sum(low.astype(F32), axis=0, keepdims=True))

    def middle_second():
        for k in range(n_o):
            piece_col(n_ff + k, wo_in, k).wait()
        for who in range(2):
            @pl.when(y == who)
            def _():
                total[...] = (dot_nt(bm[6, 0], colb[(n_ff + who) % PIECES]) + dot_nt(attn_other[...], colb[(n_ff + 1 - who) % PIECES]))

        for k in range(n_o):
            start_col(n_ff + k + PIECES)
        attended = att[...]
        low = (total[...] * head_row(head_scale, width)).astype(BF16)
        dow[0] = low
        both = low.astype(F32) * attended
        high = both.astype(BF16)
        rest = (both - high.astype(F32)).astype(BF16)
        head_of = lax.broadcasted_iota(jnp.int32, (HEADS, width), 1) // dim
        pick = jnp.where(head_of == lax.broadcasted_iota(jnp.int32, (HEADS, width), 0), 1.0, 0.0).astype(BF16)
        by_column = jnp.broadcast_to(jnp.sum(total[...] * attended, axis=0, keepdims=True), (8, width))
        high_sum = by_column.astype(BF16)
        rest_sum = (by_column - high_sum.astype(F32)).astype(BF16)
        by_head = dot_nt(high_sum, pick) + dot_nt(rest_sum, pick)
        vec[V_HEADS:V_HEADS + 1, 0:HEADS] = by_head[0:1]
        stw[0, 0:HEADS] = lse[...]
        stw[0, HEADS:2 * HEADS] = dot_nt(pick, high) + dot_nt(pick, rest)

        @pl.when(y == 1)
        def _():
            for cp in window_rows("cross"):
                cp.start()

        @pl.when(c == 1)
        def _():
            for cp in window_rows("own"):
                cp.start()

    def proj_out(blocks):
        for who, k in blocks:
            @pl.when(x == who)
            def _():
                bm[7 + k, 0] = dpj[(0, 1, 2)[k] if who == 0 else (4, 3, 5)[k]]
                b_to_core(7 + k, 0).start()

            @pl.when(x != who)
            def _():
                proj_far(k).start()

    def input_first():
        base_q = n_ff + n_o
        for k in range(n_q):
            piece_col(base_q + k, wq_in, k).wait()
            term = dot_nt(dpj[k], colb[(base_q + k) % PIECES])
            total[...] = term if k == 0 else total[...] + term
            start_col(base_q + k + PIECES)

    def input_second():
        grad = norm_back(total[...], tokens[...].astype(F32), gain[...], V_IN_GAIN, V_IN_BIAS)
        d_first[...] = d_first[...] + grad
        grad_copy.start()
        for k, block in enumerate((0, 1, 4, 5)):
            put_row(V_QV + k * (WR // 128), jnp.sum(dpj[block].astype(F32), axis=0, keepdims=True))

    n_pairs = HEADS // 2
    after = MIDDLE + n_pairs + FAR
    plan = sorted(list(zip(LAG_Y, (y0, y1, y2, y3, y4))) + list(zip(LAG_Z, (z0, z1, z2, z3, z4)))
                  + list(zip(LAG_SWAP, (swap0, swap1))), key=lambda item: -item[0])
    last = max(LAG_Y + LAG_Z + LAG_SWAP)

    def relay(b):
        b_far(b, pre_other.at[0], x_dev).wait_recv()
        b_to_core(b, 2).start()

    def attn_relay():
        for k in range(n_attn):
            attn_far(k).wait_recv()
        b_to_core(6, 2).start()

    def b_arrive(b):
        b_to_core(b, 0).wait_recv()
        b_to_core(b, 2).wait_recv()

    def at_slot(s, number, work):
        @pl.when(s == number)
        def _():
            work()

    def sent_drain():
        windows_drain()
        for g in range(10):
            for t in range(1, 4):
                if not local(g, t):
                    a_load(g, t).wait_send()
        for b in range(2):
            cot_load(b, 1).wait_send()
            cot_load(b, 3).wait_send()
        for b in range(2, 10):
            b_to_core(b, 0).wait_send()
            b_to_core(b, 2).wait_send()
            if b != 6:
                b_far(b, pre_other.at[0], x_dev).wait_send()
        for k in range(n_attn):
            attn_far(k).wait_send()

    def slot_step(s, carry):
        at_slot(s, 0, lambda: [cot_load(b, 0).wait() for b in range(2)])
        at_slot(s, 0, normed_load.wait)
        for u in range(3):
            j = 3 * s + u

            @pl.when(j < n_ff)
            def _():
                ffn_first(j)

        at_slot(s, 2, first_load.wait)
        at_slot(s, 2, ffn_between)
        for u in range(3):
            j = 3 * (s - 3) + u

            @pl.when((j >= 0) & (j < n_ff))
            def _():
                ffn_second(j)

        at_slot(s, MIDDLE, attn_load.wait)
        at_slot(s, MIDDLE, att_load.wait)
        at_slot(s, MIDDLE, middle_first)
        at_slot(s, MIDDLE, middle_second)
        at_slot(s, MIDDLE, rows_arrive)

        def relay_blocks(low, high, first_round, ahead):
            k = s + ahead - FIRST - first_round

            @pl.when((k >= 0) & (k < 2 * (high - low)) & (k % 2 == 0))
            def _():
                relay(low + k // 2)

        def arrive_blocks(low, high, first_round):
            k = s - FIRST - first_round

            @pl.when((k >= 0) & (k < 2 * (high - low)) & (k % 2 == 0))
            def _():
                b_arrive(low + k // 2)

        at_slot(s, FIRST, lambda: [[cot_load(b, 1).wait_recv(), cot_load(b, 2).wait(), cot_load(b, 3).wait_recv()] for b in range(2)])
        for g in range(4):
            at_slot(s, FIRST + 2 * g, functools.partial(a_arrive, g))
        for g in range(4, 10):
            at_slot(s, FIRST + (7, 17, 15)[(g - 4) // 2], functools.partial(a_arrive, g))
        relay_blocks(2, 6, 8, 1)
        at_slot(s, FIRST + 17, attn_relay)
        relay_blocks(7, 8, 16, 1)
        relay_blocks(8, 10, 20, 1)
        arrive_blocks(2, 6, 8)
        arrive_blocks(6, 7, 18)
        arrive_blocks(7, 8, 16)
        arrive_blocks(8, 10, 20)

        at_slot(s, FIRST + rounds + 2, sent_drain)
        for lag, work in plan:
            r = s - lag - FIRST

            @pl.when((r >= 0) & (r < rounds))
            def _():
                work(r)

        i = s - MIDDLE

        @pl.when((i >= 0) & (i < n_pairs))
        def _():
            cross_send(i)

        @pl.when((i >= 1) & (i < n_pairs + 1))
        def _():
            attend_near(i - 1)

        at_slot(s, MIDDLE + FAR - 1, cross_arrive)
        at_slot(s, MIDDLE + FAR, others_arrive)

        @pl.when((i >= FAR - 1) & (i < n_pairs + FAR - 1))
        def _():
            cross_relay(i - (FAR - 1))

        @pl.when((i >= FAR) & (i < n_pairs + FAR))
        def _():
            attend_far(i - FAR)

        for k in range(n_attn):
            at_slot(s, FIRST + 12 + k, attn_far(k).start)
        at_slot(s, MIDDLE + 4, lambda: proj_out([(0, 0)]))
        at_slot(s, MIDDLE + FAR + 3, lambda: proj_out([(1, 0), (0, 2)]))
        at_slot(s, MIDDLE + 8, lambda: proj_out([(0, 1)]))
        at_slot(s, after - 1, lambda: proj_out([(1, 1), (1, 2)]))
        at_slot(s, after - 1, input_first)
        at_slot(s, after, input_second)
        for i in range(8):
            @pl.when(s == after + 2 * i)
            def _():
                vector_step(i)

        return carry

    lax.fori_loop(0, FIRST + rounds + last, slot_step, 0)
    lax.fori_loop(rounds - SEND, rounds, lambda r, carry: (drain(r), carry)[1], 0)

    def swap_drain(r, carry):
        @pl.when(~mine(r))
        def _():
            step_swap(r).wait_send()

        return carry

    lax.fori_loop(8, rounds, swap_drain, 0)
    for i in range(7):
        for cp in vstep(i):
            cp.wait_send()

    layer_copy.wait()
    grad_copy.wait()

    def share_wait(r, carry):
        share_copies(jnp.int32(0), out.at[0], x)[0][1].wait()
        return carry

    lax.fori_loop(0, rounds, share_wait, 0)


def blocks_first(turned):
    return turned.reshape(4, 2, 2, 2, turned.shape[0] // 32 // ROWS, ROWS, turned.shape[1])


def finish_kernel(n_big, rows_of, *refs):
    n_vec = len(rows_of)
    n_in = n_big + 1
    big = refs[:n_in]
    out_big, out_vec = refs[n_in:n_in + n_big], refs[n_in + n_big:n_in + n_big + n_vec]
    out_heads = refs[n_in + n_big + n_vec]
    held, in_sem, out_sem = refs[n_in + n_big + n_vec + 1:-2], refs[-2], refs[-1]
    loads = [pltpu.make_async_copy(src, dst, in_sem.at[k]) for k, (src, dst) in enumerate(zip(big, held))]
    for cp in loads:
        cp.start()
    stores = [[pltpu.make_async_copy(src, dst, out_sem.at[k])] for k, (src, dst) in enumerate(zip(held, out_big))]
    stores.append([pltpu.make_async_copy(held[-1].at[pl.ds(first, count)], dst, out_sem.at[n_big + k])
                   for k, ((first, count), dst) in enumerate(zip(rows_of, out_vec))])
    for load, group in zip(loads, stores):
        load.wait()
        for cp in group:
            cp.start()
    at = sum(rows_of[-1])
    out_heads[...] = held[-1][at:at + 1, 0:HEADS]
    for group in stores:
        for cp in group:
            cp.wait()


def finish(layer_out, grad_tokens, out2, out1, outo, outq, flat, sizes):
    big = (layer_out, grad_tokens, out2, out1, outo, outq)
    rows_of, at = [], 0
    for size in sizes:
        rows_of.append((at, size // 128))
        at += size // 128
    hbm, vmem = pl.BlockSpec(memory_space=pl.ANY), pl.BlockSpec(memory_space=pltpu.VMEM)
    res = pl.pallas_call(
        functools.partial(finish_kernel, len(big), tuple(rows_of)),
        out_shape=[jax.ShapeDtypeStruct(item.shape, item.dtype) for item in big]
        + [jax.ShapeDtypeStruct((count, 128), F32) for _, count in rows_of] + [jax.ShapeDtypeStruct((1, HEADS), F32)],
        in_specs=[hbm] * (len(big) + 1),
        out_specs=[hbm] * (len(big) + len(rows_of)) + [vmem],
        scratch_shapes=[pltpu.VMEM(item.shape, item.dtype) for item in big + (flat,)]
        + [pltpu.SemaphoreType.DMA((len(big) + 1,)), pltpu.SemaphoreType.DMA((len(big) + len(rows_of),))],
    )(*big, flat)
    layer_out, grad_tokens, out2, out1, outo, outq = res[:6]
    ln1g, ln1b, qv, bo, pag, pab, ln2g, ln2b, c2, c1, lnfg, lnfb = (item.reshape(-1) for item in res[6:-1])
    return (layer_out, grad_tokens, ln1g, ln1b, outq, qv, res[-1].reshape(-1), outo, bo, pag, pab, ln2g, ln2b, out1, c1, lnfg, lnfb,
            out2, c2)


def fast_shards(
    tokens, lengths, ln1_gain, ln1_bias, w_qkv, qv_bias, head_scale, w_out, out_bias, lnpa_gain, lnpa_bias,
    ln2_gain, ln2_bias, w_fc1, fc1_bias, lnf_gain, lnf_bias, w_fc2, fc2_bias, cotangent,
):
    tok, width = tokens.shape
    ff = w_fc1.shape[1]
    (low_in_t, q_win, k_win, v_win, att, lse, scaled_t, attn, first, low_mid_t, normed, slope, scale_ffn, low_ffn, low_ffn_t,
     cot_x, low_in_x, low_mid_x, scaled_y) = forward(
        lengths, tokens, ln1_gain, ln1_bias, w_qkv, qv_bias, head_scale, w_out, out_bias, lnpa_gain, lnpa_bias, ln2_gain, ln2_bias,
        w_fc1, fc1_bias, lnf_gain, lnf_bias, cotangent)
    rounds = 24
    hbm, vmem, smem = (pl.BlockSpec(memory_space=space) for space in (pl.ANY, pltpu.VMEM, pltpu.SMEM))
    msgs = [(4, ROWS, WY), (3, ROWS, WY), (3, ROWS, WY), (3, 2, ROWS, WZ), (3, 2, ROWS, WZ), (ROWS, WZ)]
    n_swap = 8
    sizes = (width, width, 2 * width) + (width,) * 6 + (ff, ff, ff)
    v = -(-(sum(sizes) + 128) // 8192) * 64
    dma, shape = pltpu.SemaphoreType.DMA, jax.ShapeDtypeStruct
    f32s = [(KEEP, 4, 2, ROWS, WR), (2, ROWS, WZ), (KEEP, ROWS, WZ), (rounds, ROWS, WR), (n_swap, ROWS, WR),
            (v, 128), (v, 128), (v // 2 + v // 4 + v // 8 * 5, 128)]
    windows = [pltpu.VMEM((3, tok, width), BF16)] * 4 + [pltpu.VMEM((3, 2 * HEADS, tok), F32)]
    more = [(3 * tok, tok), (tok, 2 * tok), (tok, width), (tok, width), (tok, ff), (4, tok, 128), (tok, width), (tok, width), (tok, width)]
    out2, out1, outo, outq, flat, grad_tokens, layer_out = pl.pallas_call(
        functools.partial(back_kernel, tok),
        out_shape=[shape((ff // 32, width), F32), shape((width // 32, ff), F32), shape((width // 32, width), F32),
                   shape((width // 32, 3 * width), F32), shape((v, 128), F32), shape((tok, width), F32), shape((tok, width), BF16)],
        in_specs=[hbm] * 9 + [smem] + [hbm] * 3 + [vmem] + [hbm] * 3 + [vmem] * 6 + [smem, vmem] + [hbm] * 7,
        out_specs=[hbm] * 4 + [vmem] + [hbm] * 2,
        scratch_shapes=[pltpu.VMEM((10, 4, 4, 2, ROWS, tok), BF16), pltpu.VMEM((10, 4, tok, WR), BF16), pltpu.VMEM((4, tok, WR), BF16),
                        pltpu.VMEM((tok, WR), BF16), pltpu.VMEM((6, tok, WR), BF16)]
        + [pltpu.VMEM((SEND,) + m, BF16) for m in msgs] + [pltpu.VMEM((n_swap, ROWS, WR), BF16)]
        + [pltpu.VMEM((RECV + (2 if m[0] in (4, ROWS) else 0),) + m, BF16) for m in msgs] + [pltpu.VMEM((n_swap, ROWS, WR), BF16)]
        + [pltpu.VMEM(m, F32) for m in f32s] + windows + [pltpu.VMEM(m, F32) for m in more]
        + [pltpu.VMEM((tok, width), BF16), pltpu.VMEM((tok, ff), BF16), pltpu.VMEM((PIECES, FC, width), BF16), pltpu.VMEM((PIECES, width, FC), BF16),
           pltpu.VMEM((PIECES, tok, FC), BF16), pltpu.VMEM((PIECES, tok, FC), BF16),
           dma((10, 4)), dma((10, 4)), dma((10, 4)), dma((10, 4)), dma((6, SEND)), dma((6, RECV + 2)), dma((10,)), dma((10,)), dma((4 + HEADS,)), dma((4 + HEADS,)),
           dma((9,)), dma((PIECES,)), dma((PIECES,)), dma((PIECES,)), dma((PIECES,)), dma((2, n_swap)), dma((2, WR * HEADS // (2 * width))), dma((1,))],
        compiler_params=pltpu.CompilerParams(collective_id=0, has_side_effects=True, vmem_limit_bytes=63 << 20),
        cost_estimate=pl.CostEstimate(flops=30 << 30, bytes_accessed=50 << 20, transcendentals=4 << 20),
    )(blocks_first(low_ffn_t), blocks_first(low_mid_t), blocks_first(low_mid_x), blocks_first(scaled_t), blocks_first(scaled_y),
      blocks_first(low_in_t), blocks_first(low_in_x), cotangent, cot_x, lengths, q_win, k_win, v_win, lse, att, attn, first, scale_ffn, tokens,
      ln1_gain[None], lnpa_gain[None], ln2_gain[None], lnf_gain[None], head_scale[None], fc2_bias[None],
      normed, slope, low_ffn, w_fc2, w_fc1, w_out, w_qkv)
    return finish(layer_out, grad_tokens, out2, out1, outo, outq, flat, sizes)


def shards(
    tokens,
    lengths,
    ln1_gain,
    ln1_bias,
    w_qkv,
    qv_bias,
    head_scale,
    w_out,
    out_bias,
    lnpa_gain,
    lnpa_bias,
    ln2_gain,
    ln2_bias,
    w_fc1,
    fc1_bias,
    lnf_gain,
    lnf_bias,
    w_fc2,
    fc2_bias,
    cotangent,
):
    row_count, width = tokens.shape
    head_dim = width // HEADS
    factor = head_dim ** (-0.5)
    group = row_count * lax.axis_size("blk")
    own_start = lax.axis_index("blk") * row_count
    seq_ends = jnp.cumsum(lengths[0])
    positions = jnp.arange(group, dtype=jnp.int32)
    labels = jnp.sum((positions[:, None] >= seq_ends[None, :]).astype(jnp.int32), axis=1)
    q_labels = lax.dynamic_slice_in_dim(labels, own_start, row_count, 0)
    q_spots = own_start + jnp.arange(row_count, dtype=jnp.int32)
    inputs = tokens.astype(jnp.float32)
    normed_in, ln1_back = jax.vjp(norm_rows, inputs, ln1_gain, ln1_bias)
    low_in = normed_in.astype(jnp.bfloat16)
    projected = jnp.dot(low_in, w_qkv, preferred_element_type=jnp.float32)
    queries = (projected[:, :width] + qv_bias[:width]).astype(jnp.bfloat16)
    key_rows = projected[:, width : 2 * width].astype(jnp.bfloat16)
    value_rows = (projected[:, 2 * width :] + qv_bias[width:]).astype(jnp.bfloat16)
    query_heads = queries.reshape(row_count, HEADS, head_dim)

    def scored(key_block, start):
        count = key_block.shape[0]
        key_heads = key_block.reshape(count, HEADS, head_dim)
        raw_scores = (
            jnp.einsum("qhd,khd->hqk", query_heads, key_heads, preferred_element_type=jnp.float32)
            * factor
        )
        k_labels = lax.dynamic_slice_in_dim(labels, start, count, 0)
        k_spots = start + jnp.arange(count, dtype=jnp.int32)
        visible = (k_labels[None, :] == q_labels[:, None]) & (k_spots[None, :] <= q_spots[:, None])
        return (raw_scores, visible[None], key_heads)

    def by_blocks(step_fn, carry, pieces):
        count = pieces[0].shape[0]
        unit = max(1, 1024 // row_count) * row_count
        step = count if count <= unit else math.gcd(count, unit)

        def inner(block_index, state):
            offset = block_index * step
            sub_pieces = tuple((lax.dynamic_slice_in_dim(item, offset, step, 0) for item in pieces))
            return step_fn(state, sub_pieces, offset)

        return lax.fori_loop(0, count // step, inner, carry)

    def max_step(carry, pieces, start):
        top_score, totals = carry
        raw_scores, visible, key_heads = scored(pieces[0], start)
        raw_scores = jnp.where(visible, raw_scores, -1e30)
        new_top = jnp.maximum(top_score, jnp.max(raw_scores, axis=-1))
        totals = totals * jnp.exp(top_score - new_top) + jnp.sum(
            jnp.where(visible, jnp.exp(raw_scores - new_top[..., None]), 0.0), axis=-1
        )
        return (new_top, totals)

    start_top = jnp.full((HEADS, row_count), -1e30, jnp.float32)
    start_total = jnp.zeros((HEADS, row_count), jnp.float32)
    top_score, totals = by_blocks(
        max_step, (start_top, start_total), (lax.all_gather(key_rows, "blk", axis=0, tiled=True),)
    )
    log_total = top_score + jnp.log(totals)

    def value_step(carry, pieces, start):
        weighted, leftover = carry
        raw_scores, visible, key_heads = scored(pieces[0], start)
        value_heads = pieces[1].reshape(pieces[1].shape[0], HEADS, head_dim)
        probs = jnp.where(visible, jnp.exp(raw_scores - log_total[..., None]), 0.0)
        low_probs = probs.astype(jnp.bfloat16)
        rest_probs = (probs - low_probs.astype(jnp.float32)).astype(jnp.bfloat16)
        weighted = weighted + jnp.einsum(
            "hqk,khd->qhd", low_probs, value_heads, preferred_element_type=jnp.float32
        )
        leftover = leftover + jnp.einsum(
            "hqk,khd->qhd", rest_probs, value_heads, preferred_element_type=jnp.float32
        )
        return (weighted, leftover)

    empty_heads = jnp.zeros((row_count, HEADS, head_dim), jnp.float32)
    weighted, leftover = by_blocks(
        value_step,
        (empty_heads, empty_heads),
        (
            lax.all_gather(key_rows, "blk", axis=0, tiled=True),
            lax.all_gather(value_rows, "blk", axis=0, tiled=True),
        ),
    )
    attended = weighted.reshape(row_count, width)
    head_gain = jnp.repeat(head_scale, head_dim)
    scaled = (attended * head_gain).astype(jnp.bfloat16)
    attn_out = jnp.dot(scaled, w_out, preferred_element_type=jnp.float32) + out_bias
    branch, pa_back = jax.vjp(norm_rows, attn_out, lnpa_gain, lnpa_bias)
    first_sum = inputs + branch
    normed_mid, ln2_back = jax.vjp(norm_rows, first_sum, ln2_gain, ln2_bias)
    low_mid = normed_mid.astype(jnp.bfloat16)
    pre_act = jnp.dot(low_mid, w_fc1, preferred_element_type=jnp.float32) + fc1_bias
    activated, gelu_back = jax.vjp(gelu_exact, pre_act)
    ffn_normed, lnf_back = jax.vjp(norm_rows, activated, lnf_gain, lnf_bias)
    low_ffn = ffn_normed.astype(jnp.bfloat16)
    layer_out = (
        first_sum + jnp.dot(low_ffn, w_fc2, preferred_element_type=jnp.float32) + fc2_bias
    ).astype(jnp.bfloat16)
    d_output = cotangent.astype(jnp.float32)
    grad_w2 = over_rows(low_ffn, cotangent)
    grad_c2 = jnp.sum(d_output, axis=0)
    d_ffn = over_cols(cotangent, w_fc2)
    d_active, grad_lnf_gain, grad_lnf_bias = lnf_back(d_ffn)
    (d_pre,) = gelu_back(d_active)
    low_pre = d_pre.astype(jnp.bfloat16)
    grad_w1 = over_rows(low_mid, low_pre)
    grad_c1 = jnp.sum(low_pre.astype(jnp.float32), axis=0)
    d_mid = over_cols(low_pre, w_fc1)
    d_first_norm, grad_ln2_gain, grad_ln2_bias = ln2_back(d_mid)
    d_first = d_output + d_first_norm
    d_attn, grad_pa_gain, grad_pa_bias = pa_back(d_first)
    low_attn = d_attn.astype(jnp.bfloat16)
    grad_bo = jnp.sum(low_attn.astype(jnp.float32), axis=0)
    grad_wo = over_rows(scaled, low_attn)
    d_scaled = over_cols(low_attn, w_out)
    grad_hs = jnp.sum((d_scaled * attended).reshape(row_count, HEADS, head_dim), axis=(0, 2))
    d_attended = (d_scaled * head_gain).astype(jnp.bfloat16)
    d_heads = d_attended.reshape(row_count, HEADS, head_dim)
    delta_rows = jnp.sum(d_heads.astype(jnp.float32) * (weighted + leftover), axis=-1)
    delta = delta_rows.T

    def back_step(carry, pieces, start):
        count = pieces[0].shape[0]
        raw_scores, visible, key_heads = scored(pieces[0], start)
        value_heads = pieces[1].reshape(count, HEADS, head_dim)
        probs = jnp.where(visible, jnp.exp(raw_scores - log_total[..., None]), 0.0)
        d_probs = jnp.einsum(
            "qhd,khd->hqk", d_heads, value_heads, preferred_element_type=jnp.float32
        )
        d_scores = (probs * (d_probs - delta[..., None])).astype(jnp.bfloat16)
        d_query = (
            carry[0]
            + jnp.einsum("hqk,khd->qhd", d_scores, key_heads, preferred_element_type=jnp.float32)
            * factor
        )
        key_grad, value_grad = (carry[1], carry[2])
        low_probs = probs.astype(jnp.bfloat16)
        d_value = jnp.einsum(
            "hqk,qhd->khd", low_probs, d_heads, preferred_element_type=jnp.float32
        ).reshape(count, width)
        d_key = (
            jnp.einsum("hqk,qhd->khd", d_scores, query_heads, preferred_element_type=jnp.float32)
            * factor
        ).reshape(count, width)
        key_grad = lax.dynamic_update_slice_in_dim(
            key_grad, lax.dynamic_slice_in_dim(key_grad, start, count, 0) + d_key, start, 0
        )
        value_grad = lax.dynamic_update_slice_in_dim(
            value_grad, lax.dynamic_slice_in_dim(value_grad, start, count, 0) + d_value, start, 0
        )
        return (d_query, key_grad, value_grad)

    empty_group = jnp.zeros((group, width), jnp.float32)
    start_carry = (empty_heads, empty_group, empty_group)
    results = by_blocks(
        back_step,
        start_carry,
        (
            lax.all_gather(key_rows, "blk", axis=0, tiled=True),
            lax.all_gather(value_rows, "blk", axis=0, tiled=True),
        ),
    )
    d_query = results[0]
    own_keys, own_values = (
        lax.psum_scatter(
            results[1].astype(jnp.bfloat16), "blk", scatter_dimension=0, tiled=True
        ).astype(jnp.float32),
        lax.psum_scatter(
            results[2].astype(jnp.bfloat16), "blk", scatter_dimension=0, tiled=True
        ).astype(jnp.float32),
    )
    low_q = d_query.reshape(row_count, width).astype(jnp.bfloat16)
    low_k = own_keys.astype(jnp.bfloat16)
    low_v = own_values.astype(jnp.bfloat16)
    d_projected = jnp.concatenate([low_q, low_k, low_v], axis=1)
    grad_wqkv = over_rows(low_in, d_projected)
    grad_qv = jnp.concatenate(
        [jnp.sum(low_q.astype(jnp.float32), axis=0), jnp.sum(low_v.astype(jnp.float32), axis=0)]
    )
    d_in = over_cols(d_projected, w_qkv)
    d_in_norm, grad_ln1_gain, grad_ln1_bias = ln1_back(d_in)
    grad_tokens = d_first + d_in_norm
    share_wqkv, share_wo, share_w1, share_w2 = (
        lax.psum_scatter(grad_wqkv, ("dp", "blk"), scatter_dimension=0, tiled=True),
        lax.psum_scatter(grad_wo, ("dp", "blk"), scatter_dimension=0, tiled=True),
        lax.psum_scatter(grad_w1, ("dp", "blk"), scatter_dimension=0, tiled=True),
        lax.psum_scatter(grad_w2, ("dp", "blk"), scatter_dimension=0, tiled=True),
    )
    summed = lax.psum(
        (
            grad_ln1_gain,
            grad_ln1_bias,
            grad_qv,
            grad_hs,
            grad_bo,
            grad_pa_gain,
            grad_pa_bias,
            grad_ln2_gain,
            grad_ln2_bias,
            grad_c1,
            grad_lnf_gain,
            grad_lnf_bias,
            grad_c2,
        ),
        ("dp", "blk"),
    )
    return (
        layer_out,
        grad_tokens,
        summed[0],
        summed[1],
        share_wqkv,
        summed[2],
        summed[3],
        share_wo,
        summed[4],
        summed[5],
        summed[6],
        summed[7],
        summed[8],
        share_w1,
        summed[9],
        summed[10],
        summed[11],
        share_w2,
        summed[12],
    )


def solution(mesh):
    in_specs = (
        P(("dp", "blk"), None),
        P("dp", None),
        P(),
        P(),
        P(),
        P(),
        P(),
        P(),
        P(),
        P(),
        P(),
        P(),
        P(),
        P(),
        P(),
        P(),
        P(),
        P(),
        P(),
        P(("dp", "blk"), None),
    )
    out_specs = (
        P(("dp", "blk"), None),
        P(("dp", "blk"), None),
        P(),
        P(),
        P(("dp", "blk"), None),
        P(),
        P(),
        P(("dp", "blk"), None),
        P(),
        P(),
        P(),
        P(),
        P(),
        P(("dp", "blk"), None),
        P(),
        P(),
        P(),
        P(("dp", "blk"), None),
        P(),
    )
    body = fast_shards if dict(mesh.shape) == {"dp": 8, "blk": 4} else shards
    return jax.shard_map(body, mesh=mesh, in_specs=in_specs, out_specs=out_specs, check_vma=False)
```

```python
import functools
import math

import jax
import jax.numpy as jnp
from jax import lax
from jax.experimental import pallas as pl
from jax.experimental.pallas import tpu as pltpu
from jax.sharding import PartitionSpec as P

HEADS = 16
MESH = pl.DeviceIdType.MESH
F32, BF16 = jnp.float32, jnp.bfloat16


def norm_rows(values_in, gain_vec, bias_vec):
    row_mean = jnp.mean(values_in, axis=-1, keepdims=True)
    centered = values_in - row_mean
    variance = jnp.mean(centered * centered, axis=-1, keepdims=True)
    return centered * lax.rsqrt(variance + 1e-05) * gain_vec + bias_vec


def gelu_exact(pre_values):
    return 0.5 * pre_values * (1.0 + lax.erf(pre_values * 0.7071067811865476))


def over_rows(left, right):
    return lax.dot_general(
        left, right, (((0,), (0,)), ((), ())), preferred_element_type=jnp.float32
    )


def over_cols(left, right):
    return lax.dot_general(
        left, right, (((1,), (1,)), ((), ())), preferred_element_type=jnp.float32
    )


def dot32(left, right):
    return jnp.dot(left, right, preferred_element_type=F32)


def dot_nt(left, right):
    return lax.dot_general(left, right, (((1,), (1,)), ((), ())), preferred_element_type=F32)


def dot_tn(left, right):
    return lax.dot_general(left, right, (((0,), (0,)), ((), ())), preferred_element_type=F32)


def norm_in(rows, gain, bias):
    mean = jnp.mean(rows, axis=-1, keepdims=True)
    centered = rows - mean
    variance = jnp.mean(centered * centered, axis=-1, keepdims=True)
    return centered * lax.rsqrt(variance + 1e-05) * gain + bias


def sequence_starts(lens, spots):
    start = jnp.zeros_like(spots)
    end = jnp.int32(0)
    for j in range(lens.shape[1]):
        end = end + lens[0, j]
        start = jnp.where(spots >= end, jnp.maximum(start, end), start)
    return start


def lane_sums(values):
    total = values[:, 0:128]
    for k in range(1, values.shape[1] // 128):
        total = total + values[:, k * 128:(k + 1) * 128]
    return total


def head_row(scales, width):
    head_of = lax.broadcasted_iota(jnp.int32, (1, width), 1) // (width // HEADS)
    row = jnp.full((1, width), scales[0, 0], F32)
    for h in range(1, HEADS):
        row = jnp.where(head_of == h, scales[0, h], row)
    return row


FC = 512


def forward_kernel(lens, tok, gain, bias, w_hbm, qv_bias, head_scale, wo_hbm, out_bias, pa_gain, pa_bias, mid_gain, mid_bias,
                   w1_hbm, fc1_bias, ffn_gain, ffn_bias, cot,
                   low_in_t, qw_out, kw_out, vw_out, att_out, lse, scaled_t, attn_out, first_out, low_mid_t, normed_out, slope_out,
                   scale_out, low_ffn_out, low_ffn_t, cot_x, low_in_x, low_mid_x, scaled_y,
                   w, wo, w1, tok_y, low_in, low_y, qw, kw, vw, mask, acc, att, attn, first, low_mid, act, part, turned_in, turned, normed,
                   slope, low_ffn, ffn_turned, w_sem, sends, recvs, out_sem):
    dp, blk = lax.axis_index("dp"), lax.axis_index("blk")
    x, y, c = dp % 2, blk // 2, blk % 2
    core_dev, x_dev, y_dev = (dp, blk + 1 - 2 * c), (dp + 1 - 2 * x, blk), (dp, blk + 2 - 4 * y)
    rows, width = tok.shape
    dim = width // HEADS
    parts_y = 4
    half = rows // parts_y
    ff = w1.shape[1]
    n_ff = ff // FC

    def remote(src, dst, i, dev):
        return pltpu.make_async_remote_copy(src, dst, sends.at[i], recvs.at[i], device_id=dev, device_id_type=MESH)

    n_w = 6
    wc = 3 * width // n_w
    loads = [pltpu.make_async_copy(w_hbm.at[:, pl.ds(i * wc, wc)], w.at[:, pl.ds(i * wc, wc)], w_sem.at[i]) for i in range(n_w)]
    loads.append(pltpu.make_async_copy(wo_hbm, wo, w_sem.at[6]))
    loads.append(pltpu.make_async_copy(w1_hbm, w1, w_sem.at[7]))
    for i in (2, 3, 4, 5, 0, 1, 6, 7):
        loads[i].start()
    bar = pltpu.get_barrier_semaphore()
    for dev in (core_dev, x_dev, y_dev):
        pl.semaphore_signal(bar, inc=1, device_id=dev, device_id_type=MESH)
    pl.semaphore_wait(bar, 3)
    cross = [remote(tok.at[pl.ds(i * half, half)], tok_y.at[pl.ds(i * half, half)], (0, 1, 12, 13)[i], y_dev) for i in range(parts_y)]
    for cp in cross:
        cp.start()

    ahead = [remote(cot, cot_x, 8, x_dev), remote(turned_in.at[:, c], low_in_x, 9, x_dev), remote(turned.at[0], low_mid_x, 10, x_dev),
             remote(turned.at[1], scaled_y, 11, y_dev)]
    ahead[0].start()
    outs = []

    def emit(src, dst):
        cp = pltpu.make_async_copy(src, dst, out_sem.at[len(outs)])
        cp.start()
        outs.append(cp)

    q_spots = blk * rows + lax.broadcasted_iota(jnp.int32, (1, rows), 1)
    starts = sequence_starts(lens, q_spots)
    k_spots = (blk - 2) * rows + lax.broadcasted_iota(jnp.int32, (3 * rows, 1), 0)
    mask[...] = jnp.where((k_spots >= starts) & (k_spots <= q_spots), 0.0, -1e30)

    low_in[...] = norm_in(tok[...].astype(F32), gain[...], bias[...]).astype(BF16)

    def project(src, r0, n, which):
        res = dot32(src[r0:r0 + n], w[:, which * width:(which + 1) * width])
        if which == 0:
            res = (res + qv_bias[:, 0:width]).astype(BF16).astype(F32) * (dim ** -0.5)
        if which == 2:
            res = res + qv_bias[:, width:]
        return res.astype(BF16)

    own_q = remote(qw.at[0], qw.at[1], 2, core_dev)
    own_k = remote(kw.at[2], kw.at[1], 3, core_dev)
    own_v = remote(vw.at[2], vw.at[1], 4, core_dev)
    relay_q = remote(qw.at[2], qw.at[1], 5, core_dev)
    relay_k = remote(kw.at[0], kw.at[1], 6, core_dev)
    relay_v = remote(vw.at[0], vw.at[1], 7, core_dev)

    for cp in loads[2:4]:
        cp.wait()
    kw[2] = project(low_in, 0, rows, 1)

    @pl.when(c == 0)
    def _():
        own_k.start()

    for cp in loads[4:6]:
        cp.wait()
    vw[2] = project(low_in, 0, rows, 2)

    @pl.when(c == 0)
    def _():
        own_v.start()

    for cp in loads[0:2]:
        cp.wait()
    qw[0] = project(low_in, 0, rows, 0)

    @pl.when(c == 1)
    def _():
        own_q.start()

    turned_in[...] = low_in[...].T.reshape(turned_in.shape)
    ahead[1].start()
    emit(turned_in, low_in_t)

    for i in range(parts_y):
        cross[i].wait_recv()
        low_y[i * half:(i + 1) * half] = norm_in(tok_y[i * half:(i + 1) * half].astype(F32), gain[...], bias[...]).astype(BF16)

        @pl.when(y == 1)
        def _():
            kw[0, i * half:(i + 1) * half] = project(low_y, i * half, half, 1)
            vw[0, i * half:(i + 1) * half] = project(low_y, i * half, half, 2)

        @pl.when(y == 0)
        def _():
            qw[2, i * half:(i + 1) * half] = project(low_y, i * half, half, 0)

    @pl.when((y == 1) & (c == 1))
    def _():
        relay_k.start()
        relay_v.start()

    @pl.when((y == 0) & (c == 0))
    def _():
        relay_q.start()

    @pl.when(c == 1)
    def _():
        own_k.wait_recv()
        own_v.wait_recv()

    @pl.when((y == 1) & (c == 0))
    def _():
        relay_k.wait_recv()
        relay_v.wait_recv()

    emit(kw, kw_out)
    emit(vw, vw_out)

    group = 8

    def heads(lowest):
        def some(i, carry):
            scores, tops, values = [], [], []
            for h in range(group):
                cols = pl.ds(pl.multiple_of((i * group + h // 2 * 2) * dim, 2 * dim), 2 * dim)
                q2 = qw[0, :, cols]
                one = slice(h % 2 * dim, (h % 2 + 1) * dim)
                scores.append([])
                for j in range(lowest, 3):
                    k = kw[j, :, cols]
                    scores[h].append(dot_nt(k[:, one], q2[:, one]) + mask[j * rows:(j + 1) * rows])
            for h in range(group):
                top = jnp.max(scores[h][0], axis=0, keepdims=True)
                for s in scores[h][1:]:
                    top = jnp.maximum(top, jnp.max(s, axis=0, keepdims=True))
                tops.append(top)
            for h in range(group):
                cols = pl.ds(pl.multiple_of((i * group + h // 2 * 2) * dim, 2 * dim), 2 * dim)
                total, out = None, None
                for j, s in zip(range(lowest, 3), scores[h]):
                    p = jnp.exp(s - tops[h])
                    one = jnp.sum(p, axis=0, keepdims=True)
                    term = dot_tn(vw[j, :, cols], p.astype(BF16))[h % 2 * dim:(h % 2 + 1) * dim]
                    total = one if total is None else total + one
                    out = term if out is None else out + term
                acc[h * dim:(h + 1) * dim] = out / total
                lse[pl.ds(i * group + h, 1)] = tops[h] + jnp.log(total)
            att[:, pl.ds(pl.multiple_of(i * group * dim, group * dim), group * dim)] = acc[...].T
            return carry

        lax.fori_loop(0, HEADS // group, some, 0)

    @pl.when(blk == 0)
    def _():
        heads(2)

    @pl.when(blk == 1)
    def _():
        heads(1)

    @pl.when(blk >= 2)
    def _():
        heads(0)

    @pl.when(c == 0)
    def _():
        own_q.wait_recv()

    @pl.when((y == 0) & (c == 1))
    def _():
        relay_q.wait_recv()

    emit(qw, qw_out)
    emit(att, att_out)

    scaled = (att[...] * head_row(head_scale, width)).astype(BF16)
    turned[1] = scaled.T
    ahead[3].start()
    emit(turned.at[1], scaled_t)
    loads[6].wait()
    attn[...] = dot32(scaled, wo[...]) + out_bias[...]
    emit(attn, attn_out)
    first[...] = tok[...].astype(F32) + norm_in(attn[...], pa_gain[...], pa_bias[...])
    emit(first, first_out)
    low_mid[...] = norm_in(first[...], mid_gain[...], mid_bias[...]).astype(BF16)
    turned[0] = low_mid[...].T
    ahead[2].start()
    emit(turned.at[0], low_mid_t)
    loads[7].wait()
    part[...] = jnp.zeros_like(part)

    def ffn_cols(j):
        return pl.ds(pl.multiple_of(j * FC, FC), FC)

    def gelu_part(j, carry):
        cols = ffn_cols(j)
        pre = dot32(low_mid[...], w1[:, cols]) + fc1_bias[:, cols]
        gate = 0.5 * (1.0 + lax.erf(pre * 0.7071067811865476))
        out = pre * gate
        act[:, cols] = out
        slope[:, cols] = (gate + pre * (jnp.exp(-0.5 * (pre * pre)) * 0.3989422804014327)).astype(BF16)
        part[0] = part[0] + lane_sums(out)
        return carry

    lax.fori_loop(0, n_ff, gelu_part, 0)
    emit(slope, slope_out)
    mean = jnp.sum(part[0], axis=-1, keepdims=True) * (1.0 / ff)

    def spread_part(j, carry):
        centered = act[:, ffn_cols(j)] - mean
        part[1] = part[1] + lane_sums(centered * centered)
        return carry

    lax.fori_loop(0, n_ff, spread_part, 0)
    scale = lax.rsqrt(jnp.sum(part[1], axis=-1, keepdims=True) * (1.0 / ff) + 1e-05)
    scale_out[...] = jnp.broadcast_to(scale, scale_out.shape)

    def norm_part(j, carry):
        cols = ffn_cols(j)
        unit = (act[:, cols] - mean) * scale
        normed[:, cols] = unit.astype(BF16)
        low = (unit * ffn_gain[:, cols] + ffn_bias[:, cols]).astype(BF16)
        low_ffn[:, cols] = low
        ffn_turned[cols] = low.T
        return carry

    lax.fori_loop(0, n_ff, norm_part, 0)
    emit(normed, normed_out)
    emit(low_ffn, low_ffn_out)
    emit(ffn_turned, low_ffn_t)
    for cp in cross:
        cp.wait_send()
    for cp in ahead:
        cp.wait()

    @pl.when(c == 0)
    def _():
        own_k.wait_send()
        own_v.wait_send()

    @pl.when(c == 1)
    def _():
        own_q.wait_send()

    @pl.when((y == 1) & (c == 1))
    def _():
        relay_k.wait_send()
        relay_v.wait_send()

    @pl.when((y == 0) & (c == 0))
    def _():
        relay_q.wait_send()

    for cp in outs:
        cp.wait()


def forward(lengths, tokens, ln1_gain, ln1_bias, w_qkv, qv_bias, head_scale, w_out, out_bias, pa_gain, pa_bias, mid_gain, mid_bias,
            w_fc1, fc1_bias, ffn_gain, ffn_bias, cotangent):
    rows, width = tokens.shape
    ff = w_fc1.shape[1]
    hbm, vmem, smem = (pl.BlockSpec(memory_space=space) for space in (pl.ANY, pltpu.VMEM, pltpu.SMEM))
    shape = jax.ShapeDtypeStruct
    window, wide, tall = (3, rows, width), (rows, ff), (ff, rows)
    dma = pltpu.SemaphoreType.DMA
    return pl.pallas_call(
        forward_kernel,
        out_shape=[shape((16, 2, width // 32, rows), BF16), shape(window, BF16), shape(window, BF16), shape(window, BF16),
                   shape((rows, width), F32), shape((HEADS, rows), F32), shape((width, rows), BF16), shape((rows, width), F32),
                   shape((rows, width), F32), shape((width, rows), BF16), shape(wide, BF16), shape(wide, BF16),
                   shape((rows, 128), F32), shape(wide, BF16), shape(tall, BF16), shape((rows, width), BF16), shape((16, width // 32, rows), BF16),
                   shape((width, rows), BF16), shape((width, rows), BF16)],
        in_specs=[smem, vmem, vmem, vmem, hbm, vmem, smem, hbm] + [vmem] * 5 + [hbm] + [vmem] * 3 + [hbm],
        out_specs=[hbm] * 5 + [vmem] + [hbm] * 6 + [vmem] + [hbm] * 6,
        scratch_shapes=[pltpu.VMEM((width, 3 * width), BF16), pltpu.VMEM((width, width), BF16), pltpu.VMEM((width, ff), BF16),
                        pltpu.VMEM((rows, width), BF16), pltpu.VMEM((rows, width), BF16), pltpu.VMEM((rows, width), BF16),
                        pltpu.VMEM(window, BF16), pltpu.VMEM(window, BF16), pltpu.VMEM(window, BF16),
                        pltpu.VMEM((3 * rows, rows), F32), pltpu.VMEM((8 * width // HEADS, rows), F32),
                        pltpu.VMEM((rows, width), F32), pltpu.VMEM((rows, width), F32), pltpu.VMEM((rows, width), F32),
                        pltpu.VMEM((rows, width), BF16), pltpu.VMEM(wide, F32), pltpu.VMEM((2, rows, 128), F32),
                        pltpu.VMEM((16, 2, width // 32, rows), BF16), pltpu.VMEM((2, width, rows), BF16), pltpu.VMEM(wide, BF16), pltpu.VMEM(wide, BF16), pltpu.VMEM(wide, BF16),
                        pltpu.VMEM(tall, BF16), dma((8,)), dma((14,)), dma((14,)), dma((13,))],
        compiler_params=pltpu.CompilerParams(collective_id=1, has_side_effects=True, vmem_limit_bytes=60 << 20),
        cost_estimate=pl.CostEstimate(flops=12 << 30, bytes_accessed=40 << 20, transcendentals=5 << 20),
    )(lengths, tokens, ln1_gain[None], ln1_bias[None], w_qkv, qv_bias[None], head_scale[None], w_out, out_bias[None],
      pa_gain[None], pa_bias[None], mid_gain[None], mid_bias[None], w_fc1, fc1_bias[None], ffn_gain[None], ffn_bias[None], cotangent)


SEND = 4
RECV = 8
KEEP = 8
WY = 384
WZ = 128
WR = WY + WZ
ROWS = 32
FIRST = 2
LAG_Y = (0, 2, 4, 6, 8)
LAG_Z = (0, 2, 4, 6, 8)
LAG_SWAP = (8, 10)
MIDDLE = 6
FAR = 3
PIECES = 3


def back_kernel(tok, a2, a1, a1x, ao, aoy, aq, aqx, cot, cot_x, lens, qw_in, kw_in, vw_in, lse, att_in, attn_in, first_in, scale_ffn, tokens,
                gain, pa_gain, mid_gain, ffn_gain, head_scale, fc2_bias, normed_in, slope_in, low_ffn_in, w2_in, w1_in, wo_in, wq_in,
                out2, out1, outo, outq, vout, grad_tok, layer_out,
                am, bm, pre_other, attn_other, dpj, s1, sr, sl, szr, szl, szy, sswap, r1, rr, rl, rzr, rzl, rzy, rswap,
                prod, kz, kzy, out, swapped, vec, vown, vrecv,
                qw, kw, vw, dow, stw, mask, mask_q, total, d_first, d_ffn, parts, att, attn, first, layer_held,
                normed, w2b, colb, lowb, slopeb,
                a_send, a_recv, b_send, b_recv, send, recv, vsend, vrecv_sem, asend, arecv, in_sem, w2_sem, col_sem, low_sem, slope_sem,
                swap_sems, attn_sems, out_sem):
    dp, blk = lax.axis_index("dp"), lax.axis_index("blk")
    z, x = dp // 2, dp % 2
    y, c = blk // 2, blk % 2
    core_dev, x_dev, y_dev = (dp, blk + 1 - 2 * c), (dp + 1 - 2 * x, blk), (dp, blk + 2 - 4 * y)
    cross_dev = (dp + 1 - 2 * x, blk + 1 - 2 * c)
    up_dev, down_dev = (dp + 2, blk), (dp - 2, blk)
    rounds = 24
    rows, width = tokens.shape
    dim = width // HEADS
    n_attn = WR // (2 * dim)

    ff = normed.shape[1]
    n_ff = ff // FC
    n_o, n_q = width // FC, 3 * width // FC

    def piece2(j):
        return [pltpu.make_async_copy(w2_in.at[pl.ds(j * FC, FC)], w2b.at[j % PIECES], w2_sem.at[j % PIECES]),
                pltpu.make_async_copy(low_ffn_in.at[:, pl.ds(j * FC, FC)], lowb.at[j % PIECES], low_sem.at[j % PIECES])]

    def pre_place(q):
        half = n_ff // 2
        return ((q + 1) % 2 + x * (2 * (q % 2) - 1)) * half + q // 2

    def piece_slope(q):
        return pltpu.make_async_copy(slope_in.at[:, pl.ds(pre_place(q) * FC, FC)], slopeb.at[q % PIECES], slope_sem.at[q % PIECES])

    def piece_col(q, ref, j):
        return pltpu.make_async_copy(ref.at[:, pl.ds(j * FC, FC)], colb.at[q % PIECES], col_sem.at[q % PIECES])

    def start_col(q):
        def go(ref, low, high, where=None):
            def start():
                piece_col(q, ref, q - low if where is None else where(q)).start()
            if isinstance(q, int):
                if low <= q < high:
                    start()
            else:
                pl.when((q >= low) & (q < high))(start)
        go(w1_in, 0, n_ff, pre_place)
        go(wo_in, n_ff, n_ff + n_o)
        go(wq_in, n_ff + n_o, n_ff + n_o + n_q)

    early = [pltpu.make_async_copy(qw_in, qw, in_sem.at[0]), pltpu.make_async_copy(kw_in, kw, in_sem.at[1]),
             pltpu.make_async_copy(vw_in, vw, in_sem.at[2])]
    normed_load = pltpu.make_async_copy(normed_in, normed, in_sem.at[3])
    layer_copy = pltpu.make_async_copy(layer_held, layer_out, in_sem.at[4])
    grad_copy = pltpu.make_async_copy(d_first, grad_tok, in_sem.at[5])
    first_load = pltpu.make_async_copy(first_in, first, in_sem.at[6])
    attn_load = pltpu.make_async_copy(attn_in, attn, in_sem.at[7])
    att_load = pltpu.make_async_copy(att_in, att, in_sem.at[8])

    bar = pltpu.get_barrier_semaphore()
    z_devs = [((dp + 2 * k) % 8, blk) for k in range(1, 4)]
    for dev in [core_dev, x_dev, y_dev, cross_dev] + z_devs:
        pl.semaphore_signal(bar, inc=1, device_id=dev, device_id_type=MESH)
    def remote(src, dst, ssem, rsem, dev):
        return pltpu.make_async_remote_copy(src, dst, ssem, rsem, device_id=dev, device_id_type=MESH)

    def window_rows(kind):
        src, dst, dev, k = {"cross": (0, 2, y_dev, 0), "own": (0, 1, core_dev, 1), "relay": (2, 1, core_dev, 2)}[kind]
        copies = [remote(stw.at[src], stw.at[dst], asend.at[k], arecv.at[k], dev)]
        if kind == "own":
            copies.append(remote(dow.at[src], dow.at[dst], asend.at[3], arecv.at[3], dev))
        return copies

    def window_piece(kind, i):
        src, dst, dev, k = {"cross": (0, 2, y_dev, 4), "relay": (2, 1, core_dev, 4 + HEADS // 2)}[kind]
        cols = pl.ds(pl.multiple_of(i * 2 * dim, 2 * dim), 2 * dim)
        return remote(dow.at[src, :, cols], dow.at[dst, :, cols], asend.at[k + i], arecv.at[k + i], dev)

    def rows_of(ref, g, who, core):
        if g < 4:
            return ref.at[:, who, :, core, g]
        if g in (6, 7):
            return ref.at[:, :, g % 2, core, 0]
        return ref.at[:, g % 2, :, core, 0]

    a_own = [a2] * 4 + [a1] * 2 + [ao] * 2 + [aq] * 2
    a_far = [None] * 4 + [a1x] * 2 + [aoy] * 2 + [aqx] * 2

    def a_load(g, t):
        sems = (a_send.at[g, t], a_recv.at[g, t])
        if t == 0:
            return pltpu.make_async_copy(rows_of(a_own[g], g, x, c), am.at[g, 0], a_recv.at[g, 0])
        if t == 1:
            return remote(rows_of(a_own[g], g, x, 1 - c), am.at[g, 1], *sems, core_dev)
        if g < 4 or (g >= 8 and t == 3):
            return remote(rows_of(a_own[g], g, 1 - x, c if t == 2 else 1 - c), am.at[g, t], *sems, x_dev if t == 2 else cross_dev)
        if t == 2:
            part = rows_of(a_far[g], g, x, c) if g < 8 else aqx.at[:, g % 2]
            return pltpu.make_async_copy(part, am.at[g, 2], a_recv.at[g, 2])
        return remote(rows_of(a_far[g], g, x, 1 - c), am.at[g, 3], *sems, core_dev)

    def cot_load(b, t):
        part = (cot if t < 2 else cot_x).at[:, pl.ds(b * WR, WR)]
        if t % 2 == 0:
            return pltpu.make_async_copy(part, bm.at[b, t], b_recv.at[b, t])
        return remote(part, bm.at[b, t], b_send.at[b, t], b_recv.at[b, t], core_dev)

    def local(g, t):
        return t == 0 or (t == 2 and g >= 4)

    def a_arrive(g):
        for t in range(4):
            if local(g, t):
                a_load(g, t).wait()
            else:
                a_load(g, t).wait_recv()

    def b_to_core(b, t):
        return remote(bm.at[b, t], bm.at[b, t + 1], b_send.at[b, t + 1], b_recv.at[b, t + 1], core_dev)

    def b_far(b, src, dev):
        return remote(src, bm.at[b, 2], b_send.at[b, 2], b_recv.at[b, 2], dev)

    def pre_far(k):
        return b_far(2 + k, pre_other.at[k], x_dev)

    def attn_far(k):
        cols = pl.ds(k * 2 * dim, 2 * dim)
        return remote(attn_other.at[:, cols], bm.at[6, 2, :, cols], attn_sems.at[0, k], attn_sems.at[1, k], y_dev)

    def proj_block(who, k):
        return jnp.where(who == 0, k + k // 2, jnp.where(k == 0, 4, 3 * k - 1))

    def proj_far(k):
        return b_far(7 + k, dpj.at[proj_block(1 - x, k)], x_dev)

    for b in range(2):
        cot_load(b, 0).start()
    for g in range(4):
        a_load(g, 0).start()
    normed_load.start()
    for j in range(PIECES):
        for cp in piece2(j):
            cp.start()
    for b in range(2):
        cot_load(b, 2).start()
    for j in range(PIECES):
        start_col(j)
        piece_slope(j).start()
    for g in range(4, 10):
        a_load(g, 0).start()
        a_load(g, 2).start()
    for cp in early + [first_load, attn_load, att_load]:
        cp.start()

    vec[...] = jnp.zeros_like(vec)
    total[...] = jnp.zeros_like(total)
    parts[...] = jnp.zeros_like(parts)
    q_spots = blk * rows + lax.broadcasted_iota(jnp.int32, (1, rows), 1)
    k_spots = (blk - 2) * rows + lax.broadcasted_iota(jnp.int32, (3 * rows, 1), 0)
    mask[...] = jnp.where((k_spots >= sequence_starts(lens, q_spots)) & (k_spots <= q_spots), 0.0, -1e30)
    q_spots = (blk + 1) * rows + lax.broadcasted_iota(jnp.int32, (1, 2 * rows), 1)
    k_spots = blk * rows + lax.broadcasted_iota(jnp.int32, (rows, 1), 0)
    mask_q[...] = jnp.where(k_spots >= sequence_starts(lens, q_spots), 0.0, -1e30)

    pl.semaphore_wait(bar, 7)
    for g in range(4):
        for t in (2, 3, 1):
            a_load(g, t).start()
        if g < 2:
            cot_load(g, 1).start()
            cot_load(g, 3).start()
    for g in range(4, 10):
        a_load(g, 1).start()
        if g < 8:
            a_load(g, 3).start()

    def is_out(r):
        return (r >= 20) & (r < 22)

    def proj_turn(r):
        return jnp.where(r < 20, (r - 16) // 2, 2)

    def place(r):
        q = r % 2
        g = jnp.where(r < 8, r // 2, jnp.where(r < 16, 4 + q, jnp.where(is_out(r), 6 + q, 8 + q)))
        b = jnp.where(r < 8, q, jnp.where(r < 16, 2 + (r - 8) // 2, jnp.where(is_out(r), 6, 7 + proj_turn(r))))
        return g, b

    def turned_axes(r):
        is_o = is_out(r)
        here = jnp.where(is_o, x, y)
        sum_dev = (jnp.where(is_o, x_dev[0], y_dev[0]), jnp.where(is_o, x_dev[1], y_dev[1]))
        swap_dev = (jnp.where(is_o, y_dev[0], x_dev[0]), jnp.where(is_o, y_dev[1], x_dev[1]))
        return here, sum_dev, swap_dev

    def multiply(r):
        g, b = place(r)
        res = None
        for t in range(4):
            term = dot32(am[g, t].reshape(8 * ROWS, tok), bm[b, t])
            res = term if res is None else res + term
        prod[r % KEEP] = res.reshape(4, 2, ROWS, WR)

    S1, SR, SL, SZR, SZL, SZY = range(6)

    def from_slot(r):
        return jnp.where(is_out(r), RECV + r % 2, r % RECV)

    def message(src, dst, kind, which):
        def make(r):
            slot = from_slot(r)
            return remote(src.at[r % SEND], dst.at[slot], send.at[kind, r % SEND], recv.at[kind, slot], turned_axes(r)[which])
        return make

    step1, stepz = message(s1, r1, S1, 1), message(szy, rzy, SZY, 1)

    def put(step, ref, r, value):
        @pl.when(r >= SEND)
        def _():
            step(r - SEND).wait_send()

        ref[r % SEND] = value.astype(BF16)
        step(r).start()

    def chain(src, dst, kind, r, lo, hi, dev):
        return remote(src.at[r % SEND, lo:hi], dst.at[r % RECV, lo:hi], send.at[kind, r % SEND], recv.at[kind, r % RECV], dev)

    def chain_hop(hop, r, src, dst, kind_r, kind_l, term):
        slot, rslot = r % SEND, r % RECV

        @pl.when(z == hop)
        def _():
            if hop > 0:
                chain(src[0], dst[0], kind_r, r, hop - 1, 3, up_dev).wait_recv()

            @pl.when(r >= SEND)
            def _():
                chain(src[0], dst[0], kind_r, r - SEND, hop, 3, up_dev).wait_send()

            for d in range(hop + 1, 4):
                value = term(r, d)
                if hop > 0:
                    value = value + dst[0][rslot, d - 1].astype(F32)
                src[0][slot, d - 1] = value.astype(BF16)
            chain(src[0], dst[0], kind_r, r, hop, 3, up_dev).start()

        @pl.when(z == 3 - hop)
        def _():
            if hop > 0:
                chain(src[1], dst[1], kind_l, r, 0, 4 - hop, down_dev).wait_recv()

            @pl.when(r >= SEND)
            def _():
                chain(src[1], dst[1], kind_l, r - SEND, 0, 3 - hop, down_dev).wait_send()

            for d in range(0, 3 - hop):
                value = term(r, d)
                if hop > 0:
                    value = value + dst[1][rslot, d].astype(F32)
                src[1][slot, d] = value.astype(BF16)
            chain(src[1], dst[1], kind_l, r, 0, 3 - hop, down_dev).start()

    def chain_last(r, src, dst, kind_r, kind_l, total_ref):
        rslot = r % RECV
        for at in range(4):
            @pl.when(z == at)
            def _():
                if at == 3:
                    chain(src[0], dst[0], kind_r, r, 2, 3, up_dev).wait_recv()
                if at == 0:
                    chain(src[1], dst[1], kind_l, r, 0, 1, down_dev).wait_recv()
                value = None
                if at > 0:
                    value = dst[0][rslot, at - 1].astype(F32)
                if at < 3:
                    down = dst[1][rslot, at].astype(F32)
                    value = down if value is None else value + down
                total_ref[...] = value

    def chain_drain(r, src, dst, kind_r, kind_l):
        for hop in range(3):
            @pl.when(z == hop)
            def _():
                chain(src[0], dst[0], kind_r, r, hop, 3, up_dev).wait_send()

            @pl.when(z == 3 - hop)
            def _():
                chain(src[1], dst[1], kind_l, r, 0, 3 - hop, down_dev).wait_send()

    def z_term(r, d):
        return prod[r % KEEP, d, :, :, WY:WR]

    def t_term(r, d):
        return prod[r % KEEP, d, turned_axes(r)[0], :, 0:WY]

    zsrc, zdst = (szr, szl), (rzr, rzl)
    csrc, cdst = (sr, sl), (rr, rl)

    def y0(r):
        multiply(r)
        put(step1, s1, r, prod[r % KEEP, :, 1 - turned_axes(r)[0], :, 0:WY])

    def y1(r):
        step1(r).wait_recv()
        here = turned_axes(r)[0]
        prod[r % KEEP, :, here, :, 0:WY] = prod[r % KEEP, :, here, :, 0:WY] + r1[from_slot(r)].astype(F32)
        chain_hop(0, r, csrc, cdst, SR, SL, t_term)

    def y2(r):
        chain_hop(1, r, csrc, cdst, SR, SL, t_term)

    def y3(r):
        chain_hop(2, r, csrc, cdst, SR, SL, t_term)

    def y4(r):
        chain_last(r, csrc, cdst, SR, SL, out.at[r, :, 0:WY])
        out[r, :, 0:WY] = out[r, :, 0:WY] + prod[r % KEEP, z, turned_axes(r)[0], :, 0:WY]

    def z0(r):
        chain_hop(0, r, zsrc, zdst, SZR, SZL, z_term)

    def z1(r):
        chain_hop(1, r, zsrc, zdst, SZR, SZL, z_term)

    def z2(r):
        chain_hop(2, r, zsrc, zdst, SZR, SZL, z_term)

    def z3(r):
        here = turned_axes(r)[0]
        chain_last(r, zsrc, zdst, SZR, SZL, kz)
        kz[...] = kz[...] + prod[r % KEEP, z, :, :, WY:WR]
        put(stepz, szy, r, kz[1 - here])
        kzy[r % KEEP] = kz[here]

    def z4(r):
        stepz(r).wait_recv()
        out[r, :, WY:WR] = kzy[r % KEEP] + rzy[from_slot(r)].astype(F32)

    def swapping(r):
        return r >= 8

    def mine(r):
        return (r % 2) == jnp.where(is_out(r), y, x)

    def swap_slot(r):
        return (r - 8) // 2

    def swap0(r):
        @pl.when(swapping(r) & ~mine(r))
        def _():
            k = swap_slot(r)
            sswap[k] = out[r].astype(BF16)
            step_swap(r).start()

        @pl.when(~swapping(r) | mine(r))
        def _():
            share(r)

    def swap1(r):
        @pl.when(swapping(r) & mine(r))
        def _():
            k = swap_slot(r)
            step_swap(r).wait_recv()
            swapped[k] = rswap[k].astype(F32)
            share_far(r)

    def step_swap(r):
        k = swap_slot(r)
        return remote(sswap.at[k], rswap.at[k], send_swap(k), recv_swap(k), turned_axes(r)[2])

    def send_swap(k):
        return swap_sems.at[0, k]

    def recv_swap(k):
        return swap_sems.at[1, k]

    def cols_at(start):
        return pl.ds(pl.multiple_of(start, WR), WR)

    def share_copies(r, src, who):
        k = (r - 8) // 2
        return [((r < 8), pltpu.make_async_copy(src, out2.at[pl.ds(pl.multiple_of(r // 2 * ROWS, ROWS), ROWS), cols_at(r % 2 * WR)], out_sem.at[0])),
                ((r >= 8) & (r < 16), pltpu.make_async_copy(src, out1.at[:, cols_at(who * (ff // 2) + k * WR)], out_sem.at[0])),
                (is_out(r), pltpu.make_async_copy(src, outo.at[:, cols_at(who * WR)], out_sem.at[0])),
                ((r >= 16) & ~is_out(r), pltpu.make_async_copy(src, outq.at[:, cols_at(proj_block(who, proj_turn(r)) * WR)], out_sem.at[0]))]

    def share(r):
        for here, cp in share_copies(r, out.at[r], jnp.where(is_out(r), y, x)):
            pl.when(here)(cp.start)

    def share_far(r):
        for here, cp in share_copies(r, swapped.at[swap_slot(r)], 1 - jnp.where(is_out(r), y, x)):
            pl.when(here)(cp.start)

    def drain(r):
        step1(r).wait_send()
        stepz(r).wait_send()
        chain_drain(r, csrc, cdst, SR, SL)
        chain_drain(r, zsrc, zdst, SZR, SZL)

    v = vec.shape[0]
    h1, h2, h3 = v // 2, v // 4, v // 8
    o1 = c * h1
    o2 = o1 + x * h2
    o3 = o2 + y * h3
    base = h1 + h2 + h3

    def vstep(i):
        if i == 0:
            return [remote(vec.at[pl.ds((1 - c) * h1, h1)], vrecv.at[pl.ds(0, h1)], vsend.at[0], vrecv_sem.at[0], core_dev)]
        if i == 1:
            return [remote(vown.at[pl.ds(o1 + (1 - x) * h2, h2)], vrecv.at[pl.ds(h1, h2)], vsend.at[1], vrecv_sem.at[1], x_dev)]
        if i == 2:
            return [remote(vown.at[pl.ds(o2 + (1 - y) * h3, h3)], vrecv.at[pl.ds(h1 + h2, h3)], vsend.at[2], vrecv_sem.at[2], y_dev)]
        if i == 3:
            return [remote(vown.at[pl.ds(o3, h3)], vrecv.at[pl.ds(base + z * h3, h3)], vsend.at[3 + k], vrecv_sem.at[3 + k],
                           z_devs[k - 1]) for k in range(1, 4)]
        if i == 4:
            return [remote(vout.at[pl.ds(o3, h3)], vout.at[pl.ds(o3, h3)], vsend.at[7], vrecv_sem.at[7], y_dev)]
        if i == 5:
            return [remote(vout.at[pl.ds(o2, h2)], vout.at[pl.ds(o2, h2)], vsend.at[8], vrecv_sem.at[8], x_dev)]
        return [remote(vout.at[pl.ds(o1, h1)], vout.at[pl.ds(o1, h1)], vsend.at[9], vrecv_sem.at[9], core_dev)]

    def vector_step(i):
        if i > 0:
            for cp in vstep(i - 1):
                cp.wait_recv()
        if i == 1:
            vown[pl.ds(o1, h1)] = vec[pl.ds(o1, h1)] + vrecv[0:h1]
        if i == 2:
            vown[pl.ds(o2, h2)] = vown[pl.ds(o2, h2)] + vrecv[h1:h1 + h2]
        if i == 3:
            vown[pl.ds(o3, h3)] = vown[pl.ds(o3, h3)] + vrecv[h1 + h2:base]
            vrecv[pl.ds(base + z * h3, h3)] = vown[pl.ds(o3, h3)]
        if i == 4:
            total = vrecv[base:base + h3]
            for k in range(1, 4):
                total = total + vrecv[base + k * h3:base + (k + 1) * h3]
            vout[pl.ds(o3, h3)] = total
        if i < 7:
            for cp in vstep(i):
                cp.start()

    def rows_arrive():
        for cp in early:
            cp.wait()

    def cross_arrive():
        @pl.when(y == 0)
        def _():
            for cp in window_rows("cross"):
                cp.wait_recv()

        @pl.when((y == 0) & (c == 0))
        def _():
            for cp in window_rows("relay"):
                cp.start()

    def others_arrive():
        @pl.when(c == 0)
        def _():
            for cp in window_rows("own"):
                cp.wait_recv()

        @pl.when((y == 0) & (c == 1))
        def _():
            for cp in window_rows("relay"):
                cp.wait_recv()

    def cross_send(i):
        @pl.when(y == 1)
        def _():
            window_piece("cross", i).start()

    def cross_relay(i):
        @pl.when(y == 0)
        def _():
            window_piece("cross", i).wait_recv()

        @pl.when((y == 0) & (c == 0))
        def _():
            window_piece("relay", i).start()

    def windows_drain():
        @pl.when(y == 1)
        def _():
            for cp in window_rows("cross"):
                cp.wait_send()
            for i in range(HEADS // 2):
                window_piece("cross", i).wait_send()

        @pl.when(c == 1)
        def _():
            for cp in window_rows("own"):
                cp.wait_send()

        @pl.when((y == 0) & (c == 0))
        def _():
            for cp in window_rows("relay"):
                cp.wait_send()
            for i in range(HEADS // 2):
                window_piece("relay", i).wait_send()

    lower = lax.broadcasted_iota(jnp.int32, (1, 2 * dim), 1) < dim

    def one_head(values, sub):
        return jnp.where(lower if sub == 0 else ~lower, values, jnp.zeros_like(values))

    def both_heads(terms):
        return jnp.where(lower, terms[0], terms[1])

    def weights_of(i, sub, k1, v1, qj, q2, d2, bias):
        log_total = stw[qj, pl.ds(2 * i + sub, 1)]
        delta = stw[qj, pl.ds(HEADS + 2 * i + sub, 1)]
        probs = jnp.exp(dot_nt(k1, q2) + bias - log_total)
        return probs.astype(BF16), (probs * (dot_nt(v1, d2) - delta)).astype(BF16)

    def add(total_sum, term):
        return term if total_sum is None else total_sum + term

    def attend_near(i):
        cols = pl.ds(pl.multiple_of(i * 2 * dim, 2 * dim), 2 * dim)
        part_cols = pl.ds(pl.multiple_of(i % 4 * 2 * dim, 2 * dim), 2 * dim)

        def blocks(lowest):
            q2, d2 = qw[0, :, cols], dow[0, :, cols]
            dq, dk, dv = None, [None, None], [None, None]
            for kj in range(lowest, 3):
                k2, v2 = kw[kj, :, cols], vw[kj, :, cols]
                for sub in range(2):
                    k1 = one_head(k2, sub)
                    low_p, low_s = weights_of(i, sub, k1, one_head(v2, sub), 0, q2, d2, mask[kj * rows:(kj + 1) * rows])
                    dq = add(dq, dot_tn(k1, low_s))
                    if kj == 2:
                        dk[sub], dv[sub] = dot32(low_s, q2), dot32(low_p, d2)
            dpj[i // 4, :, part_cols] = (dq.T * (dim ** -0.5)).astype(BF16)
            d_ffn[:, cols] = both_heads(dk)
            d_ffn[:, pl.ds(pl.multiple_of(width + i * 2 * dim, 2 * dim), 2 * dim)] = both_heads(dv)

        for number in range(3):
            pl.when(blk == number if number < 2 else blk >= 2)(functools.partial(blocks, 2 - number))

    def attend_far(i):
        cols = pl.ds(pl.multiple_of(i * 2 * dim, 2 * dim), 2 * dim)
        part_cols = pl.ds(pl.multiple_of(i % 4 * 2 * dim, 2 * dim), 2 * dim)

        @pl.when((y == 0) & (c == 1))
        def _():
            window_piece("relay", i).wait_recv()

        def blocks(count):
            k2, v2 = kw[2, :, cols], vw[2, :, cols]
            dk, dv = [None, None], [None, None]
            for sub in range(2):
                k1, v1 = one_head(k2, sub), one_head(v2, sub)
                for qj in range(1, count + 1):
                    q2, d2 = qw[qj, :, cols], dow[qj, :, cols]
                    low_p, low_s = weights_of(i, sub, k1, v1, qj, q2, d2, mask_q[:, (qj - 1) * rows:qj * rows])
                    dk[sub], dv[sub] = add(dk[sub], dot32(low_s, q2)), add(dv[sub], dot32(low_p, d2))
            dk_sum, dv_sum = d_ffn[:, cols], d_ffn[:, pl.ds(pl.multiple_of(width + i * 2 * dim, 2 * dim), 2 * dim)]
            if count > 0:
                dk_sum, dv_sum = dk_sum + both_heads(dk), dv_sum + both_heads(dv)
            dpj[2 + i // 4, :, part_cols] = dk_sum.astype(BF16)
            dpj[4 + i // 4, :, part_cols] = dv_sum.astype(BF16)

        for number in range(3):
            pl.when(blk == 3 - number if number < 2 else blk <= 1)(functools.partial(blocks, number))

    V_IN_GAIN, V_IN_BIAS, V_QV, V_OUT, V_PA_GAIN, V_PA_BIAS, V_MID_GAIN, V_MID_BIAS, V_FC2 = (
        k * (width // 128) for k in (0, 1, 2, 4, 5, 6, 7, 8, 9))
    V_FC1 = 10 * (width // 128)
    V_FFN_GAIN = V_FC1 + ff // 128
    V_FFN_BIAS = V_FFN_GAIN + ff // 128
    V_HEADS = V_FFN_BIAS + ff // 128

    def put_row(first_row, row):
        for k in range(row.shape[1] // 128):
            vec[first_row + k:first_row + k + 1, :] = row[:, k * 128:(k + 1) * 128]

    def put_row_at(first_row, j, row):
        for k in range(FC // 128):
            vec[pl.ds(first_row + j * (FC // 128) + k, 1), :] = row[:, k * 128:(k + 1) * 128]

    def chunk_cols(j):
        return pl.ds(pl.multiple_of(j * FC, FC), FC)

    def ffn_first(j):
        cols = chunk_cols(j)
        for cp in piece2(j):
            cp.wait()
        weights = w2b[j % PIECES]
        total[...] = total[...] + dot32(lowb[j % PIECES], weights)
        grad = dot_nt(bm[0, 0], weights[:, 0:WR]) + dot_nt(bm[1, 0], weights[:, WR:])
        unit = normed[:, cols].astype(F32)
        d_ffn[:, cols] = grad
        put_row_at(V_FFN_GAIN, j, jnp.sum(grad * unit, axis=0, keepdims=True))
        put_row_at(V_FFN_BIAS, j, jnp.sum(grad, axis=0, keepdims=True))
        grad = grad * ffn_gain[:, cols]
        parts[0] = parts[0] + lane_sums(grad)
        parts[1] = parts[1] + lane_sums(grad * unit)

        @pl.when(j + PIECES < n_ff)
        def _():
            for cp in piece2(j + PIECES):
                cp.start()

    def ffn_between():
        layer_held[...] = (first[...] + total[...] + fc2_bias[...]).astype(BF16)
        layer_copy.start()
        total[...] = jnp.zeros_like(total)
        parts[2] = jnp.broadcast_to(jnp.sum(parts[0], axis=-1, keepdims=True) * (1.0 / ff), parts.shape[1:])
        parts[3] = jnp.broadcast_to(jnp.sum(parts[1], axis=-1, keepdims=True) * (1.0 / ff), parts.shape[1:])

    def ffn_second(q):
        j = pre_place(q)
        k = q // 2
        cols = chunk_cols(j)
        piece_col(q, w1_in, j).wait()
        piece_slope(q).wait()
        grad = d_ffn[:, cols] * ffn_gain[:, cols]
        grad = scale_ffn[:, 0:1] * (grad - parts[2][:, 0:1] - normed[:, cols].astype(F32) * parts[3][:, 0:1])
        low = (grad * slopeb[q % PIECES].astype(F32)).astype(BF16)
        put_row_at(V_FC1, j, jnp.sum(low.astype(F32), axis=0, keepdims=True))
        total[...] = total[...] + dot_nt(low, colb[q % PIECES])

        @pl.when(q % 2 == 0)
        def _():
            pre_other[k] = low
            pre_far(k).start()

        @pl.when(q % 2 == 1)
        def _():
            bm[2 + k, 0] = low
            b_to_core(2 + k, 0).start()

        @pl.when(q + PIECES < n_ff)
        def _():
            piece_slope(q + PIECES).start()

        start_col(q + PIECES)

    def unit_rows(values):
        centered = values - jnp.mean(values, axis=-1, keepdims=True)
        scale = lax.rsqrt(jnp.mean(centered * centered, axis=-1, keepdims=True) + 1e-05)
        return centered * scale, scale

    def norm_back(grad, values, gain_row, gain_at, bias_at):
        unit, scale = unit_rows(values)
        put_row(gain_at, jnp.sum(grad * unit, axis=0, keepdims=True))
        put_row(bias_at, jnp.sum(grad, axis=0, keepdims=True))
        grad = grad * gain_row
        return scale * (grad - jnp.mean(grad, axis=-1, keepdims=True) - unit * jnp.mean(grad * unit, axis=-1, keepdims=True))

    def middle_first():
        d_out = jnp.concatenate([bm[0, 0], bm[1, 0]], axis=1).astype(F32)
        put_row(V_FC2, jnp.sum(d_out, axis=0, keepdims=True))
        d_first[...] = d_out + norm_back(total[...], first[...], mid_gain[...], V_MID_GAIN, V_MID_BIAS)
        low = norm_back(d_first[...], attn[...], pa_gain[...], V_PA_GAIN, V_PA_BIAS).astype(BF16)
        for who in range(2):
            @pl.when(y == who)
            def _():
                bm[6, 0] = low[:, who * WR:(who + 1) * WR]
                attn_other[...] = low[:, (1 - who) * WR:(2 - who) * WR]

        b_to_core(6, 0).start()
        put_row(V_OUT, jnp.sum(low.astype(F32), axis=0, keepdims=True))

    def middle_second():
        for k in range(n_o):
            piece_col(n_ff + k, wo_in, k).wait()
        for who in range(2):
            @pl.when(y == who)
            def _():
                total[...] = (dot_nt(bm[6, 0], colb[(n_ff + who) % PIECES]) + dot_nt(attn_other[...], colb[(n_ff + 1 - who) % PIECES]))

        for k in range(n_o):
            start_col(n_ff + k + PIECES)
        attended = att[...]
        low = (total[...] * head_row(head_scale, width)).astype(BF16)
        dow[0] = low
        both = low.astype(F32) * attended
        high = both.astype(BF16)
        rest = (both - high.astype(F32)).astype(BF16)
        head_of = lax.broadcasted_iota(jnp.int32, (HEADS, width), 1) // dim
        pick = jnp.where(head_of == lax.broadcasted_iota(jnp.int32, (HEADS, width), 0), 1.0, 0.0).astype(BF16)
        by_column = jnp.broadcast_to(jnp.sum(total[...] * attended, axis=0, keepdims=True), (8, width))
        high_sum = by_column.astype(BF16)
        rest_sum = (by_column - high_sum.astype(F32)).astype(BF16)
        by_head = dot_nt(high_sum, pick) + dot_nt(rest_sum, pick)
        vec[V_HEADS:V_HEADS + 1, 0:HEADS] = by_head[0:1]
        stw[0, 0:HEADS] = lse[...]
        stw[0, HEADS:2 * HEADS] = dot_nt(pick, high) + dot_nt(pick, rest)

        @pl.when(y == 1)
        def _():
            for cp in window_rows("cross"):
                cp.start()

        @pl.when(c == 1)
        def _():
            for cp in window_rows("own"):
                cp.start()

    def proj_out(blocks):
        for who, k in blocks:
            @pl.when(x == who)
            def _():
                bm[7 + k, 0] = dpj[((0, 1, 3), (4, 2, 5))[who][k]]
                b_to_core(7 + k, 0).start()

            @pl.when(x != who)
            def _():
                proj_far(k).start()

    def input_first():
        base_q = n_ff + n_o
        for k in range(n_q):
            piece_col(base_q + k, wq_in, k).wait()
            term = dot_nt(dpj[k], colb[(base_q + k) % PIECES])
            total[...] = term if k == 0 else total[...] + term
            start_col(base_q + k + PIECES)

    def input_second():
        grad = norm_back(total[...], tokens[...].astype(F32), gain[...], V_IN_GAIN, V_IN_BIAS)
        d_first[...] = d_first[...] + grad
        grad_copy.start()
        for k, block in enumerate((0, 1, 4, 5)):
            put_row(V_QV + k * (WR // 128), jnp.sum(dpj[block].astype(F32), axis=0, keepdims=True))

    n_pairs = HEADS // 2
    after = MIDDLE + n_pairs + FAR
    plan = sorted(list(zip(LAG_Y, (y0, y1, y2, y3, y4))) + list(zip(LAG_Z, (z0, z1, z2, z3, z4)))
                  + list(zip(LAG_SWAP, (swap0, swap1))), key=lambda item: -item[0])
    last = max(LAG_Y + LAG_Z + LAG_SWAP)

    def relay(b):
        b_far(b, pre_other.at[0], x_dev).wait_recv()
        b_to_core(b, 2).start()

    def attn_relay():
        for k in range(n_attn):
            attn_far(k).wait_recv()
        b_to_core(6, 2).start()

    def b_arrive(b):
        b_to_core(b, 0).wait_recv()
        b_to_core(b, 2).wait_recv()

    def at_slot(s, number, work):
        @pl.when(s == number)
        def _():
            work()

    def sent_drain():
        windows_drain()
        for g in range(10):
            for t in range(1, 4):
                if not local(g, t):
                    a_load(g, t).wait_send()
        for b in range(2):
            cot_load(b, 1).wait_send()
            cot_load(b, 3).wait_send()
        for b in range(2, 10):
            b_to_core(b, 0).wait_send()
            b_to_core(b, 2).wait_send()
            if b != 6:
                b_far(b, pre_other.at[0], x_dev).wait_send()
        for k in range(n_attn):
            attn_far(k).wait_send()

    def slot_step(s, carry):
        at_slot(s, 0, lambda: [cot_load(b, 0).wait() for b in range(2)])
        at_slot(s, 0, normed_load.wait)
        for u in range(3):
            j = 3 * s + u

            @pl.when(j < n_ff)
            def _():
                ffn_first(j)

        at_slot(s, 2, first_load.wait)
        at_slot(s, 2, ffn_between)
        for u in range(3):
            j = 3 * (s - 3) + u

            @pl.when((j >= 0) & (j < n_ff))
            def _():
                ffn_second(j)

        at_slot(s, MIDDLE + 6, lambda: [a_load(g, 3).start() for g in (8, 9)])
        at_slot(s, MIDDLE, attn_load.wait)
        at_slot(s, MIDDLE, att_load.wait)
        at_slot(s, MIDDLE, middle_first)
        at_slot(s, MIDDLE, middle_second)
        at_slot(s, MIDDLE, rows_arrive)

        def relay_blocks(low, high, first_round, ahead):
            k = s + ahead - FIRST - first_round

            @pl.when((k >= 0) & (k < 2 * (high - low)) & (k % 2 == 0))
            def _():
                relay(low + k // 2)

        def arrive_blocks(low, high, first_round):
            k = s - FIRST - first_round

            @pl.when((k >= 0) & (k < 2 * (high - low)) & (k % 2 == 0))
            def _():
                b_arrive(low + k // 2)

        at_slot(s, FIRST, lambda: [[cot_load(b, 1).wait_recv(), cot_load(b, 2).wait(), cot_load(b, 3).wait_recv()] for b in range(2)])
        for g in range(4):
            at_slot(s, FIRST + 2 * g, functools.partial(a_arrive, g))
        for g in range(4, 10):
            at_slot(s, FIRST + (7, 19, 15)[(g - 4) // 2], functools.partial(a_arrive, g))
        relay_blocks(2, 6, 8, 1)
        at_slot(s, FIRST + 19, attn_relay)
        relay_blocks(7, 9, 16, 1)
        relay_blocks(9, 10, 22, 1)
        arrive_blocks(2, 6, 8)
        arrive_blocks(6, 7, 20)
        arrive_blocks(7, 9, 16)
        arrive_blocks(9, 10, 22)

        at_slot(s, FIRST + rounds + 3, sent_drain)
        for lag, work in plan:
            r = s - lag - FIRST

            @pl.when((r >= 0) & (r < rounds))
            def _():
                work(r)

        i = s - MIDDLE

        @pl.when((i >= 0) & (i < n_pairs))
        def _():
            cross_send(i)

        @pl.when((i >= 1) & (i < n_pairs + 1))
        def _():
            attend_near(i - 1)

        at_slot(s, MIDDLE + FAR - 1, cross_arrive)
        at_slot(s, MIDDLE + FAR, others_arrive)

        @pl.when((i >= FAR - 1) & (i < n_pairs + FAR - 1))
        def _():
            cross_relay(i - (FAR - 1))

        @pl.when((i >= FAR) & (i < n_pairs + FAR))
        def _():
            attend_far(i - FAR)

        for k in range(n_attn):
            at_slot(s, FIRST + 12 + k, attn_far(k).start)
        at_slot(s, MIDDLE + 4, lambda: proj_out([(0, 0)]))
        at_slot(s, MIDDLE + FAR + 3, lambda: proj_out([(1, 0), (1, 1)]))
        at_slot(s, MIDDLE + 8, lambda: proj_out([(0, 1)]))
        at_slot(s, after - 1, lambda: proj_out([(0, 2), (1, 2)]))
        at_slot(s, after - 1, input_first)
        at_slot(s, after, input_second)
        for i in range(8):
            @pl.when(s == after + 2 * i + (2 if i > 3 else 0))
            def _():
                vector_step(i)

        return carry

    lax.fori_loop(0, FIRST + rounds + last, slot_step, 0)
    lax.fori_loop(rounds - SEND, rounds, lambda r, carry: (drain(r), carry)[1], 0)

    def swap_drain(r, carry):
        @pl.when(~mine(r))
        def _():
            step_swap(r).wait_send()

        return carry

    lax.fori_loop(8, rounds, swap_drain, 0)
    for i in range(7):
        for cp in vstep(i):
            cp.wait_send()

    layer_copy.wait()
    grad_copy.wait()

    def share_wait(r, carry):
        share_copies(jnp.int32(0), out.at[0], x)[0][1].wait()
        return carry

    lax.fori_loop(0, rounds, share_wait, 0)


def blocks_first(turned):
    return turned.reshape(4, 2, 2, 2, turned.shape[0] // 32 // ROWS, ROWS, turned.shape[1])


def finish_kernel(n_big, rows_of, *refs):
    n_vec = len(rows_of)
    n_in = n_big + 1
    big = refs[:n_in]
    out_big, out_vec = refs[n_in:n_in + n_big], refs[n_in + n_big:n_in + n_big + n_vec]
    out_heads = refs[n_in + n_big + n_vec]
    held, in_sem, out_sem = refs[n_in + n_big + n_vec + 1:-2], refs[-2], refs[-1]
    loads = [pltpu.make_async_copy(src, dst, in_sem.at[k]) for k, (src, dst) in enumerate(zip(big, held))]
    for cp in loads:
        cp.start()
    stores = [[pltpu.make_async_copy(src, dst, out_sem.at[k])] for k, (src, dst) in enumerate(zip(held, out_big))]
    stores.append([pltpu.make_async_copy(held[-1].at[pl.ds(first, count)], dst, out_sem.at[n_big + k])
                   for k, ((first, count), dst) in enumerate(zip(rows_of, out_vec))])
    for load, group in zip(loads, stores):
        load.wait()
        for cp in group:
            cp.start()
    at = sum(rows_of[-1])
    out_heads[...] = held[-1][at:at + 1, 0:HEADS]
    for group in stores:
        for cp in group:
            cp.wait()


def finish(layer_out, grad_tokens, out2, out1, outo, outq, flat, sizes):
    big = (layer_out, grad_tokens, out2, out1, outo, outq)
    rows_of, at = [], 0
    for size in sizes:
        rows_of.append((at, size // 128))
        at += size // 128
    hbm, vmem = pl.BlockSpec(memory_space=pl.ANY), pl.BlockSpec(memory_space=pltpu.VMEM)
    res = pl.pallas_call(
        functools.partial(finish_kernel, len(big), tuple(rows_of)),
        out_shape=[jax.ShapeDtypeStruct(item.shape, item.dtype) for item in big]
        + [jax.ShapeDtypeStruct((count, 128), F32) for _, count in rows_of] + [jax.ShapeDtypeStruct((1, HEADS), F32)],
        in_specs=[hbm] * (len(big) + 1),
        out_specs=[hbm] * (len(big) + len(rows_of)) + [vmem],
        scratch_shapes=[pltpu.VMEM(item.shape, item.dtype) for item in big + (flat,)]
        + [pltpu.SemaphoreType.DMA((len(big) + 1,)), pltpu.SemaphoreType.DMA((len(big) + len(rows_of),))],
    )(*big, flat)
    layer_out, grad_tokens, out2, out1, outo, outq = res[:6]
    ln1g, ln1b, qv, bo, pag, pab, ln2g, ln2b, c2, c1, lnfg, lnfb = (item.reshape(-1) for item in res[6:-1])
    return (layer_out, grad_tokens, ln1g, ln1b, outq, qv, res[-1].reshape(-1), outo, bo, pag, pab, ln2g, ln2b, out1, c1, lnfg, lnfb,
            out2, c2)


def fast_shards(
    tokens, lengths, ln1_gain, ln1_bias, w_qkv, qv_bias, head_scale, w_out, out_bias, lnpa_gain, lnpa_bias,
    ln2_gain, ln2_bias, w_fc1, fc1_bias, lnf_gain, lnf_bias, w_fc2, fc2_bias, cotangent,
):
    tok, width = tokens.shape
    ff = w_fc1.shape[1]
    (low_in_t, q_win, k_win, v_win, att, lse, scaled_t, attn, first, low_mid_t, normed, slope, scale_ffn, low_ffn, low_ffn_t,
     cot_x, low_in_x, low_mid_x, scaled_y) = forward(
        lengths, tokens, ln1_gain, ln1_bias, w_qkv, qv_bias, head_scale, w_out, out_bias, lnpa_gain, lnpa_bias, ln2_gain, ln2_bias,
        w_fc1, fc1_bias, lnf_gain, lnf_bias, cotangent)
    rounds = 24
    hbm, vmem, smem = (pl.BlockSpec(memory_space=space) for space in (pl.ANY, pltpu.VMEM, pltpu.SMEM))
    msgs = [(4, ROWS, WY), (3, ROWS, WY), (3, ROWS, WY), (3, 2, ROWS, WZ), (3, 2, ROWS, WZ), (ROWS, WZ)]
    n_swap = 8
    sizes = (width, width, 2 * width) + (width,) * 6 + (ff, ff, ff)
    v = -(-(sum(sizes) + 128) // 8192) * 64
    dma, shape = pltpu.SemaphoreType.DMA, jax.ShapeDtypeStruct
    f32s = [(KEEP, 4, 2, ROWS, WR), (2, ROWS, WZ), (KEEP, ROWS, WZ), (rounds, ROWS, WR), (n_swap, ROWS, WR),
            (v, 128), (v, 128), (v // 2 + v // 4 + v // 8 * 5, 128)]
    windows = [pltpu.VMEM((3, tok, width), BF16)] * 4 + [pltpu.VMEM((3, 2 * HEADS, tok), F32)]
    more = [(3 * tok, tok), (tok, 2 * tok), (tok, width), (tok, width), (tok, ff), (4, tok, 128), (tok, width), (tok, width), (tok, width)]
    out2, out1, outo, outq, flat, grad_tokens, layer_out = pl.pallas_call(
        functools.partial(back_kernel, tok),
        out_shape=[shape((ff // 32, width), F32), shape((width // 32, ff), F32), shape((width // 32, width), F32),
                   shape((width // 32, 3 * width), F32), shape((v, 128), F32), shape((tok, width), F32), shape((tok, width), BF16)],
        in_specs=[hbm] * 9 + [smem] + [hbm] * 3 + [vmem] + [hbm] * 3 + [vmem] * 6 + [smem, vmem] + [hbm] * 7,
        out_specs=[hbm] * 4 + [vmem] + [hbm] * 2,
        scratch_shapes=[pltpu.VMEM((10, 4, 4, 2, ROWS, tok), BF16), pltpu.VMEM((10, 4, tok, WR), BF16), pltpu.VMEM((4, tok, WR), BF16),
                        pltpu.VMEM((tok, WR), BF16), pltpu.VMEM((6, tok, WR), BF16)]
        + [pltpu.VMEM((SEND,) + m, BF16) for m in msgs] + [pltpu.VMEM((n_swap, ROWS, WR), BF16)]
        + [pltpu.VMEM((RECV + (2 if m[0] in (4, ROWS) else 0),) + m, BF16) for m in msgs] + [pltpu.VMEM((n_swap, ROWS, WR), BF16)]
        + [pltpu.VMEM(m, F32) for m in f32s] + windows + [pltpu.VMEM(m, F32) for m in more]
        + [pltpu.VMEM((tok, width), BF16), pltpu.VMEM((tok, ff), BF16), pltpu.VMEM((PIECES, FC, width), BF16), pltpu.VMEM((PIECES, width, FC), BF16),
           pltpu.VMEM((PIECES, tok, FC), BF16), pltpu.VMEM((PIECES, tok, FC), BF16),
           dma((10, 4)), dma((10, 4)), dma((10, 4)), dma((10, 4)), dma((6, SEND)), dma((6, RECV + 2)), dma((10,)), dma((10,)), dma((4 + HEADS,)), dma((4 + HEADS,)),
           dma((9,)), dma((PIECES,)), dma((PIECES,)), dma((PIECES,)), dma((PIECES,)), dma((2, n_swap)), dma((2, WR * HEADS // (2 * width))), dma((1,))],
        compiler_params=pltpu.CompilerParams(collective_id=0, has_side_effects=True, vmem_limit_bytes=63 << 20),
        cost_estimate=pl.CostEstimate(flops=30 << 30, bytes_accessed=50 << 20, transcendentals=4 << 20),
    )(blocks_first(low_ffn_t), blocks_first(low_mid_t), blocks_first(low_mid_x), blocks_first(scaled_t), blocks_first(scaled_y),
      blocks_first(low_in_t.reshape(width, tok)), low_in_x.reshape(4, 2, 2, ROWS, tok), cotangent, cot_x, lengths, q_win, k_win, v_win, lse, att, attn, first, scale_ffn, tokens,
      ln1_gain[None], lnpa_gain[None], ln2_gain[None], lnf_gain[None], head_scale[None], fc2_bias[None],
      normed, slope, low_ffn, w_fc2, w_fc1, w_out, w_qkv)
    return finish(layer_out, grad_tokens, out2, out1, outo, outq, flat, sizes)


def shards(
    tokens,
    lengths,
    ln1_gain,
    ln1_bias,
    w_qkv,
    qv_bias,
    head_scale,
    w_out,
    out_bias,
    lnpa_gain,
    lnpa_bias,
    ln2_gain,
    ln2_bias,
    w_fc1,
    fc1_bias,
    lnf_gain,
    lnf_bias,
    w_fc2,
    fc2_bias,
    cotangent,
):
    row_count, width = tokens.shape
    head_dim = width // HEADS
    factor = head_dim ** (-0.5)
    group = row_count * lax.axis_size("blk")
    own_start = lax.axis_index("blk") * row_count
    seq_ends = jnp.cumsum(lengths[0])
    positions = jnp.arange(group, dtype=jnp.int32)
    labels = jnp.sum((positions[:, None] >= seq_ends[None, :]).astype(jnp.int32), axis=1)
    q_labels = lax.dynamic_slice_in_dim(labels, own_start, row_count, 0)
    q_spots = own_start + jnp.arange(row_count, dtype=jnp.int32)
    inputs = tokens.astype(jnp.float32)
    normed_in, ln1_back = jax.vjp(norm_rows, inputs, ln1_gain, ln1_bias)
    low_in = normed_in.astype(jnp.bfloat16)
    projected = jnp.dot(low_in, w_qkv, preferred_element_type=jnp.float32)
    queries = (projected[:, :width] + qv_bias[:width]).astype(jnp.bfloat16)
    key_rows = projected[:, width : 2 * width].astype(jnp.bfloat16)
    value_rows = (projected[:, 2 * width :] + qv_bias[width:]).astype(jnp.bfloat16)
    query_heads = queries.reshape(row_count, HEADS, head_dim)

    def scored(key_block, start):
        count = key_block.shape[0]
        key_heads = key_block.reshape(count, HEADS, head_dim)
        raw_scores = (
            jnp.einsum("qhd,khd->hqk", query_heads, key_heads, preferred_element_type=jnp.float32)
            * factor
        )
        k_labels = lax.dynamic_slice_in_dim(labels, start, count, 0)
        k_spots = start + jnp.arange(count, dtype=jnp.int32)
        visible = (k_labels[None, :] == q_labels[:, None]) & (k_spots[None, :] <= q_spots[:, None])
        return (raw_scores, visible[None], key_heads)

    def by_blocks(step_fn, carry, pieces):
        count = pieces[0].shape[0]
        unit = max(1, 1024 // row_count) * row_count
        step = count if count <= unit else math.gcd(count, unit)

        def inner(block_index, state):
            offset = block_index * step
            sub_pieces = tuple((lax.dynamic_slice_in_dim(item, offset, step, 0) for item in pieces))
            return step_fn(state, sub_pieces, offset)

        return lax.fori_loop(0, count // step, inner, carry)

    def max_step(carry, pieces, start):
        top_score, totals = carry
        raw_scores, visible, key_heads = scored(pieces[0], start)
        raw_scores = jnp.where(visible, raw_scores, -1e30)
        new_top = jnp.maximum(top_score, jnp.max(raw_scores, axis=-1))
        totals = totals * jnp.exp(top_score - new_top) + jnp.sum(
            jnp.where(visible, jnp.exp(raw_scores - new_top[..., None]), 0.0), axis=-1
        )
        return (new_top, totals)

    start_top = jnp.full((HEADS, row_count), -1e30, jnp.float32)
    start_total = jnp.zeros((HEADS, row_count), jnp.float32)
    top_score, totals = by_blocks(
        max_step, (start_top, start_total), (lax.all_gather(key_rows, "blk", axis=0, tiled=True),)
    )
    log_total = top_score + jnp.log(totals)

    def value_step(carry, pieces, start):
        weighted, leftover = carry
        raw_scores, visible, key_heads = scored(pieces[0], start)
        value_heads = pieces[1].reshape(pieces[1].shape[0], HEADS, head_dim)
        probs = jnp.where(visible, jnp.exp(raw_scores - log_total[..., None]), 0.0)
        low_probs = probs.astype(jnp.bfloat16)
        rest_probs = (probs - low_probs.astype(jnp.float32)).astype(jnp.bfloat16)
        weighted = weighted + jnp.einsum(
            "hqk,khd->qhd", low_probs, value_heads, preferred_element_type=jnp.float32
        )
        leftover = leftover + jnp.einsum(
            "hqk,khd->qhd", rest_probs, value_heads, preferred_element_type=jnp.float32
        )
        return (weighted, leftover)

    empty_heads = jnp.zeros((row_count, HEADS, head_dim), jnp.float32)
    weighted, leftover = by_blocks(
        value_step,
        (empty_heads, empty_heads),
        (
            lax.all_gather(key_rows, "blk", axis=0, tiled=True),
            lax.all_gather(value_rows, "blk", axis=0, tiled=True),
        ),
    )
    attended = weighted.reshape(row_count, width)
    head_gain = jnp.repeat(head_scale, head_dim)
    scaled = (attended * head_gain).astype(jnp.bfloat16)
    attn_out = jnp.dot(scaled, w_out, preferred_element_type=jnp.float32) + out_bias
    branch, pa_back = jax.vjp(norm_rows, attn_out, lnpa_gain, lnpa_bias)
    first_sum = inputs + branch
    normed_mid, ln2_back = jax.vjp(norm_rows, first_sum, ln2_gain, ln2_bias)
    low_mid = normed_mid.astype(jnp.bfloat16)
    pre_act = jnp.dot(low_mid, w_fc1, preferred_element_type=jnp.float32) + fc1_bias
    activated, gelu_back = jax.vjp(gelu_exact, pre_act)
    ffn_normed, lnf_back = jax.vjp(norm_rows, activated, lnf_gain, lnf_bias)
    low_ffn = ffn_normed.astype(jnp.bfloat16)
    layer_out = (
        first_sum + jnp.dot(low_ffn, w_fc2, preferred_element_type=jnp.float32) + fc2_bias
    ).astype(jnp.bfloat16)
    d_output = cotangent.astype(jnp.float32)
    grad_w2 = over_rows(low_ffn, cotangent)
    grad_c2 = jnp.sum(d_output, axis=0)
    d_ffn = over_cols(cotangent, w_fc2)
    d_active, grad_lnf_gain, grad_lnf_bias = lnf_back(d_ffn)
    (d_pre,) = gelu_back(d_active)
    low_pre = d_pre.astype(jnp.bfloat16)
    grad_w1 = over_rows(low_mid, low_pre)
    grad_c1 = jnp.sum(low_pre.astype(jnp.float32), axis=0)
    d_mid = over_cols(low_pre, w_fc1)
    d_first_norm, grad_ln2_gain, grad_ln2_bias = ln2_back(d_mid)
    d_first = d_output + d_first_norm
    d_attn, grad_pa_gain, grad_pa_bias = pa_back(d_first)
    low_attn = d_attn.astype(jnp.bfloat16)
    grad_bo = jnp.sum(low_attn.astype(jnp.float32), axis=0)
    grad_wo = over_rows(scaled, low_attn)
    d_scaled = over_cols(low_attn, w_out)
    grad_hs = jnp.sum((d_scaled * attended).reshape(row_count, HEADS, head_dim), axis=(0, 2))
    d_attended = (d_scaled * head_gain).astype(jnp.bfloat16)
    d_heads = d_attended.reshape(row_count, HEADS, head_dim)
    delta_rows = jnp.sum(d_heads.astype(jnp.float32) * (weighted + leftover), axis=-1)
    delta = delta_rows.T

    def back_step(carry, pieces, start):
        count = pieces[0].shape[0]
        raw_scores, visible, key_heads = scored(pieces[0], start)
        value_heads = pieces[1].reshape(count, HEADS, head_dim)
        probs = jnp.where(visible, jnp.exp(raw_scores - log_total[..., None]), 0.0)
        d_probs = jnp.einsum(
            "qhd,khd->hqk", d_heads, value_heads, preferred_element_type=jnp.float32
        )
        d_scores = (probs * (d_probs - delta[..., None])).astype(jnp.bfloat16)
        d_query = (
            carry[0]
            + jnp.einsum("hqk,khd->qhd", d_scores, key_heads, preferred_element_type=jnp.float32)
            * factor
        )
        key_grad, value_grad = (carry[1], carry[2])
        low_probs = probs.astype(jnp.bfloat16)
        d_value = jnp.einsum(
            "hqk,qhd->khd", low_probs, d_heads, preferred_element_type=jnp.float32
        ).reshape(count, width)
        d_key = (
            jnp.einsum("hqk,qhd->khd", d_scores, query_heads, preferred_element_type=jnp.float32)
            * factor
        ).reshape(count, width)
        key_grad = lax.dynamic_update_slice_in_dim(
            key_grad, lax.dynamic_slice_in_dim(key_grad, start, count, 0) + d_key, start, 0
        )
        value_grad = lax.dynamic_update_slice_in_dim(
            value_grad, lax.dynamic_slice_in_dim(value_grad, start, count, 0) + d_value, start, 0
        )
        return (d_query, key_grad, value_grad)

    empty_group = jnp.zeros((group, width), jnp.float32)
    start_carry = (empty_heads, empty_group, empty_group)
    results = by_blocks(
        back_step,
        start_carry,
        (
            lax.all_gather(key_rows, "blk", axis=0, tiled=True),
            lax.all_gather(value_rows, "blk", axis=0, tiled=True),
        ),
    )
    d_query = results[0]
    own_keys, own_values = (
        lax.psum_scatter(
            results[1].astype(jnp.bfloat16), "blk", scatter_dimension=0, tiled=True
        ).astype(jnp.float32),
        lax.psum_scatter(
            results[2].astype(jnp.bfloat16), "blk", scatter_dimension=0, tiled=True
        ).astype(jnp.float32),
    )
    low_q = d_query.reshape(row_count, width).astype(jnp.bfloat16)
    low_k = own_keys.astype(jnp.bfloat16)
    low_v = own_values.astype(jnp.bfloat16)
    d_projected = jnp.concatenate([low_q, low_k, low_v], axis=1)
    grad_wqkv = over_rows(low_in, d_projected)
    grad_qv = jnp.concatenate(
        [jnp.sum(low_q.astype(jnp.float32), axis=0), jnp.sum(low_v.astype(jnp.float32), axis=0)]
    )
    d_in = over_cols(d_projected, w_qkv)
    d_in_norm, grad_ln1_gain, grad_ln1_bias = ln1_back(d_in)
    grad_tokens = d_first + d_in_norm
    share_wqkv, share_wo, share_w1, share_w2 = (
        lax.psum_scatter(grad_wqkv, ("dp", "blk"), scatter_dimension=0, tiled=True),
        lax.psum_scatter(grad_wo, ("dp", "blk"), scatter_dimension=0, tiled=True),
        lax.psum_scatter(grad_w1, ("dp", "blk"), scatter_dimension=0, tiled=True),
        lax.psum_scatter(grad_w2, ("dp", "blk"), scatter_dimension=0, tiled=True),
    )
    summed = lax.psum(
        (
            grad_ln1_gain,
            grad_ln1_bias,
            grad_qv,
            grad_hs,
            grad_bo,
            grad_pa_gain,
            grad_pa_bias,
            grad_ln2_gain,
            grad_ln2_bias,
            grad_c1,
            grad_lnf_gain,
            grad_lnf_bias,
            grad_c2,
        ),
        ("dp", "blk"),
    )
    return (
        layer_out,
        grad_tokens,
        summed[0],
        summed[1],
        share_wqkv,
        summed[2],
        summed[3],
        share_wo,
        summed[4],
        summed[5],
        summed[6],
        summed[7],
        summed[8],
        share_w1,
        summed[9],
        summed[10],
        summed[11],
        share_w2,
        summed[12],
    )


def solution(mesh):
    in_specs = (
        P(("dp", "blk"), None),
        P("dp", None),
        P(),
        P(),
        P(),
        P(),
        P(),
        P(),
        P(),
        P(),
        P(),
        P(),
        P(),
        P(),
        P(),
        P(),
        P(),
        P(),
        P(),
        P(("dp", "blk"), None),
    )
    out_specs = (
        P(("dp", "blk"), None),
        P(("dp", "blk"), None),
        P(),
        P(),
        P(("dp", "blk"), None),
        P(),
        P(),
        P(("dp", "blk"), None),
        P(),
        P(),
        P(),
        P(),
        P(),
        P(("dp", "blk"), None),
        P(),
        P(),
        P(),
        P(("dp", "blk"), None),
        P(),
    )
    body = fast_shards if dict(mesh.shape) == {"dp": 8, "blk": 4} else shards
    return jax.shard_map(body, mesh=mesh, in_specs=in_specs, out_specs=out_specs, check_vma=False)
```

```python
import functools
import math

import jax
import jax.numpy as jnp
from jax import lax
from jax.experimental import pallas as pl
from jax.experimental.pallas import tpu as pltpu
from jax.sharding import PartitionSpec as P

HEADS = 16
MESH = pl.DeviceIdType.MESH
F32, BF16 = jnp.float32, jnp.bfloat16


def norm_rows(values_in, gain_vec, bias_vec):
    row_mean = jnp.mean(values_in, axis=-1, keepdims=True)
    centered = values_in - row_mean
    variance = jnp.mean(centered * centered, axis=-1, keepdims=True)
    return centered * lax.rsqrt(variance + 1e-05) * gain_vec + bias_vec


def gelu_exact(pre_values):
    return 0.5 * pre_values * (1.0 + lax.erf(pre_values * 0.7071067811865476))


def over_rows(left, right):
    return lax.dot_general(
        left, right, (((0,), (0,)), ((), ())), preferred_element_type=jnp.float32
    )


def over_cols(left, right):
    return lax.dot_general(
        left, right, (((1,), (1,)), ((), ())), preferred_element_type=jnp.float32
    )


def dot32(left, right):
    return jnp.dot(left, right, preferred_element_type=F32)


def dot_nt(left, right):
    return lax.dot_general(left, right, (((1,), (1,)), ((), ())), preferred_element_type=F32)


def dot_tn(left, right):
    return lax.dot_general(left, right, (((0,), (0,)), ((), ())), preferred_element_type=F32)


def norm_in(rows, gain, bias):
    mean = jnp.mean(rows, axis=-1, keepdims=True)
    centered = rows - mean
    variance = jnp.mean(centered * centered, axis=-1, keepdims=True)
    return centered * lax.rsqrt(variance + 1e-05) * gain + bias


def sequence_starts(lens, spots):
    start = jnp.zeros_like(spots)
    end = jnp.int32(0)
    for j in range(lens.shape[1]):
        end = end + lens[0, j]
        start = jnp.where(spots >= end, jnp.maximum(start, end), start)
    return start


def lane_sums(values):
    total = values[:, 0:128]
    for k in range(1, values.shape[1] // 128):
        total = total + values[:, k * 128:(k + 1) * 128]
    return total


def head_row(scales, width):
    head_of = lax.broadcasted_iota(jnp.int32, (1, width), 1) // (width // HEADS)
    row = jnp.full((1, width), scales[0, 0], F32)
    for h in range(1, HEADS):
        row = jnp.where(head_of == h, scales[0, h], row)
    return row


FC = 512


def forward_kernel(lens, tok, gain, bias, w_hbm, qv_bias, head_scale, wo_hbm, out_bias, pa_gain, pa_bias, mid_gain, mid_bias,
                   w1_hbm, fc1_bias, ffn_gain, ffn_bias, cot,
                   low_in_t, qw_out, kw_out, vw_out, att_out, lse, scaled_t, attn_out, first_out, low_mid_t, normed_out, slope_out,
                   scale_out, low_ffn_out, low_ffn_t, cot_x, low_in_x, low_mid_x, scaled_y,
                   w, wo, w1, tok_y, low_in, low_y, qw, kw, vw, mask, acc, att, attn, first, low_mid, act, part, turned_in, turned, normed,
                   slope, low_ffn, ffn_turned, w_sem, sends, recvs, out_sem):
    dp, blk = lax.axis_index("dp"), lax.axis_index("blk")
    x, y, c = dp % 2, blk // 2, blk % 2
    core_dev, x_dev, y_dev = (dp, blk + 1 - 2 * c), (dp + 1 - 2 * x, blk), (dp, blk + 2 - 4 * y)
    rows, width = tok.shape
    dim = width // HEADS
    parts_y = 4
    half = rows // parts_y
    ff = w1.shape[1]
    n_ff = ff // FC

    def remote(src, dst, i, dev):
        return pltpu.make_async_remote_copy(src, dst, sends.at[i], recvs.at[i], device_id=dev, device_id_type=MESH)

    n_w = 6
    wc = 3 * width // n_w
    loads = [pltpu.make_async_copy(w_hbm.at[:, pl.ds(i * wc, wc)], w.at[:, pl.ds(i * wc, wc)], w_sem.at[i]) for i in range(n_w)]
    loads.append(pltpu.make_async_copy(wo_hbm, wo, w_sem.at[6]))
    loads.append(pltpu.make_async_copy(w1_hbm, w1, w_sem.at[7]))
    for i in (2, 3, 4, 5, 0, 1, 6, 7):
        loads[i].start()
    bar = pltpu.get_barrier_semaphore()
    for dev in (core_dev, x_dev, y_dev):
        pl.semaphore_signal(bar, inc=1, device_id=dev, device_id_type=MESH)
    pl.semaphore_wait(bar, 3)
    cross = [remote(tok.at[pl.ds(i * half, half)], tok_y.at[pl.ds(i * half, half)], (0, 1, 12, 13)[i], y_dev) for i in range(parts_y)]
    for cp in cross:
        cp.start()

    ahead = [remote(cot, cot_x, 8, x_dev), remote(turned_in.at[:, c], low_in_x, 9, x_dev), remote(turned.at[0], low_mid_x, 10, x_dev),
             remote(turned.at[1], scaled_y, 11, y_dev)]
    ahead[0].start()
    outs = []

    def emit(src, dst):
        cp = pltpu.make_async_copy(src, dst, out_sem.at[len(outs)])
        cp.start()
        outs.append(cp)

    q_spots = blk * rows + lax.broadcasted_iota(jnp.int32, (1, rows), 1)
    starts = sequence_starts(lens, q_spots)
    k_spots = (blk - 2) * rows + lax.broadcasted_iota(jnp.int32, (3 * rows, 1), 0)
    mask[...] = jnp.where((k_spots >= starts) & (k_spots <= q_spots), 0.0, -1e30)

    low_in[...] = norm_in(tok[...].astype(F32), gain[...], bias[...]).astype(BF16)

    def project(src, r0, n, which):
        res = dot32(src[r0:r0 + n], w[:, which * width:(which + 1) * width])
        if which == 0:
            res = (res + qv_bias[:, 0:width]).astype(BF16).astype(F32) * (dim ** -0.5)
        if which == 2:
            res = res + qv_bias[:, width:]
        return res.astype(BF16)

    own_q = remote(qw.at[0], qw.at[1], 2, core_dev)
    own_k = remote(kw.at[2], kw.at[1], 3, core_dev)
    own_v = remote(vw.at[2], vw.at[1], 4, core_dev)
    relay_q = remote(qw.at[2], qw.at[1], 5, core_dev)
    relay_k = remote(kw.at[0], kw.at[1], 6, core_dev)
    relay_v = remote(vw.at[0], vw.at[1], 7, core_dev)

    for cp in loads[2:4]:
        cp.wait()
    kw[2] = project(low_in, 0, rows, 1)

    @pl.when(c == 0)
    def _():
        own_k.start()

    for cp in loads[4:6]:
        cp.wait()
    vw[2] = project(low_in, 0, rows, 2)

    @pl.when(c == 0)
    def _():
        own_v.start()

    for cp in loads[0:2]:
        cp.wait()
    qw[0] = project(low_in, 0, rows, 0)

    @pl.when(c == 1)
    def _():
        own_q.start()

    turned_in[...] = low_in[...].T.reshape(turned_in.shape)
    ahead[1].start()
    emit(turned_in, low_in_t)

    for i in range(parts_y):
        cross[i].wait_recv()
        low_y[i * half:(i + 1) * half] = norm_in(tok_y[i * half:(i + 1) * half].astype(F32), gain[...], bias[...]).astype(BF16)

        @pl.when(y == 1)
        def _():
            kw[0, i * half:(i + 1) * half] = project(low_y, i * half, half, 1)
            vw[0, i * half:(i + 1) * half] = project(low_y, i * half, half, 2)

        @pl.when(y == 0)
        def _():
            qw[2, i * half:(i + 1) * half] = project(low_y, i * half, half, 0)

    @pl.when((y == 1) & (c == 1))
    def _():
        relay_k.start()
        relay_v.start()

    @pl.when((y == 0) & (c == 0))
    def _():
        relay_q.start()

    @pl.when(c == 1)
    def _():
        own_k.wait_recv()
        own_v.wait_recv()

    @pl.when((y == 1) & (c == 0))
    def _():
        relay_k.wait_recv()
        relay_v.wait_recv()

    emit(kw, kw_out)
    emit(vw, vw_out)

    group = 8

    def heads(lowest):
        def some(i, carry):
            scores, tops, values = [], [], []
            for h in range(group):
                cols = pl.ds(pl.multiple_of((i * group + h // 2 * 2) * dim, 2 * dim), 2 * dim)
                q2 = qw[0, :, cols]
                one = slice(h % 2 * dim, (h % 2 + 1) * dim)
                scores.append([])
                for j in range(lowest, 3):
                    k = kw[j, :, cols]
                    scores[h].append(dot_nt(k[:, one], q2[:, one]) + mask[j * rows:(j + 1) * rows])
            for h in range(group):
                top = jnp.max(scores[h][0], axis=0, keepdims=True)
                for s in scores[h][1:]:
                    top = jnp.maximum(top, jnp.max(s, axis=0, keepdims=True))
                tops.append(top)
            for h in range(group):
                cols = pl.ds(pl.multiple_of((i * group + h // 2 * 2) * dim, 2 * dim), 2 * dim)
                total, out = None, None
                for j, s in zip(range(lowest, 3), scores[h]):
                    p = jnp.exp(s - tops[h])
                    one = jnp.sum(p, axis=0, keepdims=True)
                    term = dot_tn(vw[j, :, cols], p.astype(BF16))[h % 2 * dim:(h % 2 + 1) * dim]
                    total = one if total is None else total + one
                    out = term if out is None else out + term
                acc[h * dim:(h + 1) * dim] = out / total
                lse[pl.ds(i * group + h, 1)] = tops[h] + jnp.log(total)
            att[:, pl.ds(pl.multiple_of(i * group * dim, group * dim), group * dim)] = acc[...].T
            return carry

        lax.fori_loop(0, HEADS // group, some, 0)

    @pl.when(blk == 0)
    def _():
        heads(2)

    @pl.when(blk == 1)
    def _():
        heads(1)

    @pl.when(blk >= 2)
    def _():
        heads(0)

    @pl.when(c == 0)
    def _():
        own_q.wait_recv()

    @pl.when((y == 0) & (c == 1))
    def _():
        relay_q.wait_recv()

    emit(qw, qw_out)
    emit(att, att_out)

    scaled = (att[...] * head_row(head_scale, width)).astype(BF16)
    turned[1] = scaled.T
    ahead[3].start()
    emit(turned.at[1], scaled_t)
    loads[6].wait()
    attn[...] = dot32(scaled, wo[...]) + out_bias[...]
    emit(attn, attn_out)
    first[...] = tok[...].astype(F32) + norm_in(attn[...], pa_gain[...], pa_bias[...])
    emit(first, first_out)
    low_mid[...] = norm_in(first[...], mid_gain[...], mid_bias[...]).astype(BF16)
    turned[0] = low_mid[...].T
    ahead[2].start()
    emit(turned.at[0], low_mid_t)
    loads[7].wait()
    part[...] = jnp.zeros_like(part)

    def ffn_cols(j):
        return pl.ds(pl.multiple_of(j * FC, FC), FC)

    def gelu_part(j, carry):
        cols = ffn_cols(j)
        pre = dot32(low_mid[...], w1[:, cols]) + fc1_bias[:, cols]
        gate = 0.5 * (1.0 + lax.erf(pre * 0.7071067811865476))
        out = pre * gate
        act[:, cols] = out
        slope[:, cols] = (gate + pre * (jnp.exp(-0.5 * (pre * pre)) * 0.3989422804014327)).astype(BF16)
        part[0] = part[0] + lane_sums(out)
        return carry

    lax.fori_loop(0, n_ff, gelu_part, 0)
    emit(slope, slope_out)
    mean = jnp.sum(part[0], axis=-1, keepdims=True) * (1.0 / ff)

    def spread_part(j, carry):
        centered = act[:, ffn_cols(j)] - mean
        part[1] = part[1] + lane_sums(centered * centered)
        return carry

    lax.fori_loop(0, n_ff, spread_part, 0)
    scale = lax.rsqrt(jnp.sum(part[1], axis=-1, keepdims=True) * (1.0 / ff) + 1e-05)
    scale_out[...] = jnp.broadcast_to(scale, scale_out.shape)

    def norm_part(j, carry):
        cols = ffn_cols(j)
        unit = (act[:, cols] - mean) * scale
        normed[:, cols] = unit.astype(BF16)
        low = (unit * ffn_gain[:, cols] + ffn_bias[:, cols]).astype(BF16)
        low_ffn[:, cols] = low
        ffn_turned[cols] = low.T
        return carry

    lax.fori_loop(0, n_ff, norm_part, 0)
    emit(normed, normed_out)
    emit(low_ffn, low_ffn_out)
    emit(ffn_turned, low_ffn_t)
    for cp in cross:
        cp.wait_send()
    for cp in ahead:
        cp.wait()

    @pl.when(c == 0)
    def _():
        own_k.wait_send()
        own_v.wait_send()

    @pl.when(c == 1)
    def _():
        own_q.wait_send()

    @pl.when((y == 1) & (c == 1))
    def _():
        relay_k.wait_send()
        relay_v.wait_send()

    @pl.when((y == 0) & (c == 0))
    def _():
        relay_q.wait_send()

    for cp in outs:
        cp.wait()


def forward(lengths, tokens, ln1_gain, ln1_bias, w_qkv, qv_bias, head_scale, w_out, out_bias, pa_gain, pa_bias, mid_gain, mid_bias,
            w_fc1, fc1_bias, ffn_gain, ffn_bias, cotangent):
    rows, width = tokens.shape
    ff = w_fc1.shape[1]
    hbm, vmem, smem = (pl.BlockSpec(memory_space=space) for space in (pl.ANY, pltpu.VMEM, pltpu.SMEM))
    shape = jax.ShapeDtypeStruct
    window, wide, tall = (3, rows, width), (rows, ff), (ff, rows)
    dma = pltpu.SemaphoreType.DMA
    return pl.pallas_call(
        forward_kernel,
        out_shape=[shape((16, 2, width // 32, rows), BF16), shape(window, BF16), shape(window, BF16), shape(window, BF16),
                   shape((rows, width), F32), shape((HEADS, rows), F32), shape((width, rows), BF16), shape((rows, width), F32),
                   shape((rows, width), F32), shape((width, rows), BF16), shape(wide, BF16), shape(wide, BF16),
                   shape((rows, 128), F32), shape(wide, BF16), shape(tall, BF16), shape((rows, width), BF16), shape((16, width // 32, rows), BF16),
                   shape((width, rows), BF16), shape((width, rows), BF16)],
        in_specs=[smem, vmem, vmem, vmem, hbm, vmem, smem, hbm] + [vmem] * 5 + [hbm] + [vmem] * 3 + [hbm],
        out_specs=[hbm] * 5 + [vmem] + [hbm] * 6 + [vmem] + [hbm] * 6,
        scratch_shapes=[pltpu.VMEM((width, 3 * width), BF16), pltpu.VMEM((width, width), BF16), pltpu.VMEM((width, ff), BF16),
                        pltpu.VMEM((rows, width), BF16), pltpu.VMEM((rows, width), BF16), pltpu.VMEM((rows, width), BF16),
                        pltpu.VMEM(window, BF16), pltpu.VMEM(window, BF16), pltpu.VMEM(window, BF16),
                        pltpu.VMEM((3 * rows, rows), F32), pltpu.VMEM((8 * width // HEADS, rows), F32),
                        pltpu.VMEM((rows, width), F32), pltpu.VMEM((rows, width), F32), pltpu.VMEM((rows, width), F32),
                        pltpu.VMEM((rows, width), BF16), pltpu.VMEM(wide, F32), pltpu.VMEM((2, rows, 128), F32),
                        pltpu.VMEM((16, 2, width // 32, rows), BF16), pltpu.VMEM((2, width, rows), BF16), pltpu.VMEM(wide, BF16), pltpu.VMEM(wide, BF16), pltpu.VMEM(wide, BF16),
                        pltpu.VMEM(tall, BF16), dma((8,)), dma((14,)), dma((14,)), dma((13,))],
        compiler_params=pltpu.CompilerParams(collective_id=1, has_side_effects=True, vmem_limit_bytes=60 << 20),
        cost_estimate=pl.CostEstimate(flops=12 << 30, bytes_accessed=40 << 20, transcendentals=5 << 20),
    )(lengths, tokens, ln1_gain[None], ln1_bias[None], w_qkv, qv_bias[None], head_scale[None], w_out, out_bias[None],
      pa_gain[None], pa_bias[None], mid_gain[None], mid_bias[None], w_fc1, fc1_bias[None], ffn_gain[None], ffn_bias[None], cotangent)


SEND = 4
RECV = 8
KEEP = 8
WY = 384
WZ = 128
WR = WY + WZ
ROWS = 32
FIRST = 2
LAG_Y = (0, 2, 4, 6, 8)
LAG_Z = (0, 2, 4, 6, 8)
LAG_SWAP = (8, 10)
MIDDLE = 6
FAR = 3
PIECES = 3


def back_kernel(tok, a2, a1, a1x, ao, aoy, aq, aqx, cot, cot_x, lens, qw_in, kw_in, vw_in, lse, att_in, attn_in, first_in, scale_ffn, tokens,
                gain, pa_gain, mid_gain, ffn_gain, head_scale, fc2_bias, normed_in, slope_in, low_ffn_in, w2_in, w1_in, wo_in, wq_in,
                out2, out1, outo, outq, vout, grad_tok, layer_out,
                am, bm, pre_other, attn_other, dpj, s1, sr, sl, szr, szl, szy, sswap, r1, rr, rl, rzr, rzl, rzy, rswap,
                prod, kz, kzy, out, swapped, vec, vown, vrecv,
                qw, kw, vw, dow, stw, mask, mask_q, total, d_first, d_ffn, parts, att, attn, first, layer_held,
                normed, w2b, colb, lowb, slopeb,
                a_send, a_recv, b_send, b_recv, send, recv, vsend, vrecv_sem, asend, arecv, in_sem, w2_sem, col_sem, low_sem, slope_sem,
                swap_sems, attn_sems, out_sem):
    dp, blk = lax.axis_index("dp"), lax.axis_index("blk")
    z, x = dp // 2, dp % 2
    y, c = blk // 2, blk % 2
    core_dev, x_dev, y_dev = (dp, blk + 1 - 2 * c), (dp + 1 - 2 * x, blk), (dp, blk + 2 - 4 * y)
    cross_dev = (dp + 1 - 2 * x, blk + 1 - 2 * c)
    up_dev, down_dev = ((dp + 2) % 8, blk), ((dp + 6) % 8, blk)
    rounds = 24
    rows, width = tokens.shape
    dim = width // HEADS
    n_attn = WR // (2 * dim)

    ff = normed.shape[1]
    n_ff = ff // FC
    n_o, n_q = width // FC, 3 * width // FC

    def piece2(j):
        return [pltpu.make_async_copy(w2_in.at[pl.ds(j * FC, FC)], w2b.at[j % PIECES], w2_sem.at[j % PIECES]),
                pltpu.make_async_copy(low_ffn_in.at[:, pl.ds(j * FC, FC)], lowb.at[j % PIECES], low_sem.at[j % PIECES])]

    def pre_place(q):
        half = n_ff // 2
        return ((q + 1) % 2 + x * (2 * (q % 2) - 1)) * half + q // 2

    def piece_slope(q):
        return pltpu.make_async_copy(slope_in.at[:, pl.ds(pre_place(q) * FC, FC)], slopeb.at[q % PIECES], slope_sem.at[q % PIECES])

    def piece_col(q, ref, j):
        return pltpu.make_async_copy(ref.at[:, pl.ds(j * FC, FC)], colb.at[q % PIECES], col_sem.at[q % PIECES])

    def start_col(q):
        def go(ref, low, high, where=None):
            def start():
                piece_col(q, ref, q - low if where is None else where(q)).start()
            if isinstance(q, int):
                if low <= q < high:
                    start()
            else:
                pl.when((q >= low) & (q < high))(start)
        go(w1_in, 0, n_ff, pre_place)
        go(wo_in, n_ff, n_ff + n_o)
        go(wq_in, n_ff + n_o, n_ff + n_o + n_q)

    early = [pltpu.make_async_copy(qw_in, qw, in_sem.at[0]), pltpu.make_async_copy(kw_in, kw, in_sem.at[1]),
             pltpu.make_async_copy(vw_in, vw, in_sem.at[2])]
    normed_load = pltpu.make_async_copy(normed_in, normed, in_sem.at[3])
    layer_copy = pltpu.make_async_copy(layer_held, layer_out, in_sem.at[4])
    grad_copy = pltpu.make_async_copy(d_first, grad_tok, in_sem.at[5])
    first_load = pltpu.make_async_copy(first_in, first, in_sem.at[6])
    attn_load = pltpu.make_async_copy(attn_in, attn, in_sem.at[7])
    att_load = pltpu.make_async_copy(att_in, att, in_sem.at[8])

    bar = pltpu.get_barrier_semaphore()
    z_devs = [((dp + 2 * k) % 8, blk) for k in range(1, 4)]
    for dev in [core_dev, x_dev, y_dev, cross_dev] + z_devs:
        pl.semaphore_signal(bar, inc=1, device_id=dev, device_id_type=MESH)
    def remote(src, dst, ssem, rsem, dev):
        return pltpu.make_async_remote_copy(src, dst, ssem, rsem, device_id=dev, device_id_type=MESH)

    def window_rows(kind):
        src, dst, dev, k = {"cross": (0, 2, y_dev, 0), "own": (0, 1, core_dev, 1), "relay": (2, 1, core_dev, 2)}[kind]
        copies = [remote(stw.at[src], stw.at[dst], asend.at[k], arecv.at[k], dev)]
        if kind == "own":
            copies.append(remote(dow.at[src], dow.at[dst], asend.at[3], arecv.at[3], dev))
        return copies

    def window_piece(kind, i):
        src, dst, dev, k = {"cross": (0, 2, y_dev, 4), "relay": (2, 1, core_dev, 4 + HEADS // 2)}[kind]
        cols = pl.ds(pl.multiple_of(i * 2 * dim, 2 * dim), 2 * dim)
        return remote(dow.at[src, :, cols], dow.at[dst, :, cols], asend.at[k + i], arecv.at[k + i], dev)

    def rows_of(ref, g, who, core):
        if g < 4:
            return ref.at[:, who, :, core, g]
        if g in (6, 7):
            return ref.at[:, :, g % 2, core, 0]
        return ref.at[:, g % 2, :, core, 0]

    a_own = [a2] * 4 + [a1] * 2 + [ao] * 2 + [aq] * 2
    a_far = [None] * 4 + [a1x] * 2 + [aoy] * 2 + [aqx] * 2

    def a_load(g, t):
        sems = (a_send.at[g, t], a_recv.at[g, t])
        if t == 0:
            return pltpu.make_async_copy(rows_of(a_own[g], g, x, c), am.at[g, 0], a_recv.at[g, 0])
        if t == 1:
            return remote(rows_of(a_own[g], g, x, 1 - c), am.at[g, 1], *sems, core_dev)
        if g < 4 or (g >= 8 and t == 3):
            return remote(rows_of(a_own[g], g, 1 - x, c if t == 2 else 1 - c), am.at[g, t], *sems, x_dev if t == 2 else cross_dev)
        if t == 2:
            part = rows_of(a_far[g], g, x, c) if g < 8 else aqx.at[:, g % 2]
            return pltpu.make_async_copy(part, am.at[g, 2], a_recv.at[g, 2])
        return remote(rows_of(a_far[g], g, x, 1 - c), am.at[g, 3], *sems, core_dev)

    def cot_load(b, t):
        part = (cot if t < 2 else cot_x).at[:, pl.ds(b * WR, WR)]
        if t % 2 == 0:
            return pltpu.make_async_copy(part, bm.at[b, t], b_recv.at[b, t])
        return remote(part, bm.at[b, t], b_send.at[b, t], b_recv.at[b, t], core_dev)

    def local(g, t):
        return t == 0 or (t == 2 and g >= 4)

    def a_arrive(g):
        for t in range(4):
            if local(g, t):
                a_load(g, t).wait()
            else:
                a_load(g, t).wait_recv()

    def b_to_core(b, t):
        return remote(bm.at[b, t], bm.at[b, t + 1], b_send.at[b, t + 1], b_recv.at[b, t + 1], core_dev)

    def b_far(b, src, dev):
        return remote(src, bm.at[b, 2], b_send.at[b, 2], b_recv.at[b, 2], dev)

    def pre_far(k):
        return b_far(2 + k, pre_other.at[k], x_dev)

    def attn_far(k):
        cols = pl.ds(k * 2 * dim, 2 * dim)
        return remote(attn_other.at[:, cols], bm.at[6, 2, :, cols], attn_sems.at[0, k], attn_sems.at[1, k], y_dev)

    def proj_block(who, k):
        return jnp.where(who == 0, k + k // 2, jnp.where(k == 0, 4, 3 * k - 1))

    def proj_far(k):
        return b_far(7 + k, dpj.at[proj_block(1 - x, k)], x_dev)

    for b in range(2):
        cot_load(b, 0).start()
    for g in range(4):
        a_load(g, 0).start()
    normed_load.start()
    for j in range(PIECES):
        for cp in piece2(j):
            cp.start()
    for b in range(2):
        cot_load(b, 2).start()
    for j in range(PIECES):
        start_col(j)
        piece_slope(j).start()
    for g in range(4, 10):
        a_load(g, 0).start()
        a_load(g, 2).start()
    for cp in early + [first_load, attn_load, att_load]:
        cp.start()

    vec[...] = jnp.zeros_like(vec)
    total[...] = jnp.zeros_like(total)
    parts[...] = jnp.zeros_like(parts)
    q_spots = blk * rows + lax.broadcasted_iota(jnp.int32, (1, rows), 1)
    k_spots = (blk - 2) * rows + lax.broadcasted_iota(jnp.int32, (3 * rows, 1), 0)
    mask[...] = jnp.where((k_spots >= sequence_starts(lens, q_spots)) & (k_spots <= q_spots), 0.0, -1e30)
    q_spots = (blk + 1) * rows + lax.broadcasted_iota(jnp.int32, (1, 2 * rows), 1)
    k_spots = blk * rows + lax.broadcasted_iota(jnp.int32, (rows, 1), 0)
    mask_q[...] = jnp.where(k_spots >= sequence_starts(lens, q_spots), 0.0, -1e30)

    pl.semaphore_wait(bar, 7)
    for g in range(4):
        for t in (2, 3, 1):
            a_load(g, t).start()
        if g < 2:
            cot_load(g, 1).start()
            cot_load(g, 3).start()
    for g in range(4, 10):
        a_load(g, 1).start()
        if g < 8:
            a_load(g, 3).start()

    def is_out(r):
        return (r >= 20) & (r < 22)

    def proj_turn(r):
        return jnp.where(r < 20, (r - 16) // 2, 2)

    def place(r):
        q = r % 2
        g = jnp.where(r < 8, r // 2, jnp.where(r < 16, 4 + q, jnp.where(is_out(r), 6 + q, 8 + q)))
        b = jnp.where(r < 8, q, jnp.where(r < 16, 2 + (r - 8) // 2, jnp.where(is_out(r), 6, 7 + proj_turn(r))))
        return g, b

    def turned_axes(r):
        is_o = is_out(r)
        here = jnp.where(is_o, x, y)
        sum_dev = (jnp.where(is_o, x_dev[0], y_dev[0]), jnp.where(is_o, x_dev[1], y_dev[1]))
        swap_dev = (jnp.where(is_o, y_dev[0], x_dev[0]), jnp.where(is_o, y_dev[1], x_dev[1]))
        return here, sum_dev, swap_dev

    def multiply(r):
        g, b = place(r)
        res = None
        for t in range(4):
            term = dot32(am[g, t].reshape(8 * ROWS, tok), bm[b, t])
            res = term if res is None else res + term
        prod[r % KEEP] = res.reshape(4, 2, ROWS, WR)

    S1, SR, SL, SZR, SZL, SZY = range(6)

    def from_slot(r):
        return jnp.where(is_out(r), RECV + r % 2, r % RECV)

    def message(src, dst, kind, which):
        def make(r):
            slot = from_slot(r)
            return remote(src.at[r % SEND], dst.at[slot], send.at[kind, r % SEND], recv.at[kind, slot], turned_axes(r)[which])
        return make

    step1, stepz = message(s1, r1, S1, 1), message(szy, rzy, SZY, 1)

    def put(step, ref, r, value):
        @pl.when(r >= SEND)
        def _():
            step(r - SEND).wait_send()

        ref[r % SEND] = value.astype(BF16)
        step(r).start()

    def chain(src, dst, kind, r, lo, hi, dev):
        return remote(src.at[r % SEND, lo:hi], dst.at[r % RECV, lo:hi], send.at[kind, r % SEND], recv.at[kind, r % RECV], dev)

    def chain_hop(hop, r, src, dst, kind_r, kind_l, term):
        slot, rslot = r % SEND, r % RECV

        @pl.when(z == hop)
        def _():
            if hop > 0:
                chain(src[0], dst[0], kind_r, r, hop - 1, 3, up_dev).wait_recv()

            @pl.when(r >= SEND)
            def _():
                chain(src[0], dst[0], kind_r, r - SEND, hop, 3, up_dev).wait_send()

            for d in range(hop + 1, 4):
                value = term(r, d)
                if hop > 0:
                    value = value + dst[0][rslot, d - 1].astype(F32)
                src[0][slot, d - 1] = value.astype(BF16)
            chain(src[0], dst[0], kind_r, r, hop, 3, up_dev).start()

        @pl.when(z == 3 - hop)
        def _():
            if hop > 0:
                chain(src[1], dst[1], kind_l, r, 0, 4 - hop, down_dev).wait_recv()

            @pl.when(r >= SEND)
            def _():
                chain(src[1], dst[1], kind_l, r - SEND, 0, 3 - hop, down_dev).wait_send()

            for d in range(0, 3 - hop):
                value = term(r, d)
                if hop > 0:
                    value = value + dst[1][rslot, d].astype(F32)
                src[1][slot, d] = value.astype(BF16)
            chain(src[1], dst[1], kind_l, r, 0, 3 - hop, down_dev).start()

    def chain_last(r, src, dst, kind_r, kind_l, total_ref):
        rslot = r % RECV
        for at in range(4):
            @pl.when(z == at)
            def _():
                if at == 3:
                    chain(src[0], dst[0], kind_r, r, 2, 3, up_dev).wait_recv()
                if at == 0:
                    chain(src[1], dst[1], kind_l, r, 0, 1, down_dev).wait_recv()
                value = None
                if at > 0:
                    value = dst[0][rslot, at - 1].astype(F32)
                if at < 3:
                    down = dst[1][rslot, at].astype(F32)
                    value = down if value is None else value + down
                total_ref[...] = value

    def chain_drain(r, src, dst, kind_r, kind_l):
        for hop in range(3):
            @pl.when(z == hop)
            def _():
                chain(src[0], dst[0], kind_r, r, hop, 3, up_dev).wait_send()

            @pl.when(z == 3 - hop)
            def _():
                chain(src[1], dst[1], kind_l, r, 0, 3 - hop, down_dev).wait_send()

    def z_term(r, d):
        return prod[r % KEEP, d, :, :, WY:WR]

    def t_term(r, d):
        return prod[r % KEEP, d, turned_axes(r)[0], :, 0:WY]

    zsrc, zdst = (szr, szl), (rzr, rzl)
    csrc, cdst = (sr, sl), (rr, rl)

    def y0(r):
        multiply(r)
        put(step1, s1, r, prod[r % KEEP, :, 1 - turned_axes(r)[0], :, 0:WY])

    def y1(r):
        step1(r).wait_recv()
        here = turned_axes(r)[0]
        prod[r % KEEP, :, here, :, 0:WY] = prod[r % KEEP, :, here, :, 0:WY] + r1[from_slot(r)].astype(F32)
        chain_hop(0, r, csrc, cdst, SR, SL, t_term)

    def y2(r):
        chain_hop(1, r, csrc, cdst, SR, SL, t_term)

    def y3(r):
        chain_hop(2, r, csrc, cdst, SR, SL, t_term)

    def y4(r):
        chain_last(r, csrc, cdst, SR, SL, out.at[r, :, 0:WY])
        out[r, :, 0:WY] = out[r, :, 0:WY] + prod[r % KEEP, z, turned_axes(r)[0], :, 0:WY]

    def z0(r):
        chain_hop(0, r, zsrc, zdst, SZR, SZL, z_term)

    def z1(r):
        chain_hop(1, r, zsrc, zdst, SZR, SZL, z_term)

    def z2(r):
        chain_hop(2, r, zsrc, zdst, SZR, SZL, z_term)

    def z3(r):
        here = turned_axes(r)[0]
        chain_last(r, zsrc, zdst, SZR, SZL, kz)
        kz[...] = kz[...] + prod[r % KEEP, z, :, :, WY:WR]
        put(stepz, szy, r, kz[1 - here])
        kzy[r % KEEP] = kz[here]

    def z4(r):
        stepz(r).wait_recv()
        out[r, :, WY:WR] = kzy[r % KEEP] + rzy[from_slot(r)].astype(F32)

    def swapping(r):
        return r >= 8

    def mine(r):
        return (r % 2) == jnp.where(is_out(r), y, x)

    def swap_slot(r):
        return (r - 8) // 2

    def swap0(r):
        @pl.when(swapping(r) & ~mine(r))
        def _():
            k = swap_slot(r)
            sswap[k] = out[r].astype(BF16)
            step_swap(r).start()

        @pl.when(~swapping(r) | mine(r))
        def _():
            share(r)

    def swap1(r):
        @pl.when(swapping(r) & mine(r))
        def _():
            k = swap_slot(r)
            step_swap(r).wait_recv()
            swapped[k] = rswap[k].astype(F32)
            share_far(r)

    def step_swap(r):
        k = swap_slot(r)
        return remote(sswap.at[k], rswap.at[k], send_swap(k), recv_swap(k), turned_axes(r)[2])

    def send_swap(k):
        return swap_sems.at[0, k]

    def recv_swap(k):
        return swap_sems.at[1, k]

    def cols_at(start):
        return pl.ds(pl.multiple_of(start, WR), WR)

    def share_out(r, src, who):
        def go(here, place_of):
            @pl.when(here)
            def _():
                pltpu.make_async_copy(src, place_of(), out_sem.at[0]).start()

        go(r < 8, lambda: out2.at[pl.ds(pl.multiple_of(r // 2 * ROWS, ROWS), ROWS), cols_at(r % 2 * WR)])
        go((r >= 8) & (r < 16), lambda: out1.at[:, cols_at(who * (ff // 2) + (r - 8) // 2 * WR)])
        go(is_out(r), lambda: outo.at[:, cols_at(who * WR)])
        go((r >= 16) & ~is_out(r), lambda: outq.at[:, cols_at(proj_block(who, proj_turn(r)) * WR)])

    def share(r):
        share_out(r, out.at[r], jnp.where(is_out(r), y, x))

    def share_far(r):
        share_out(r, swapped.at[swap_slot(r)], 1 - jnp.where(is_out(r), y, x))

    def drain(r):
        step1(r).wait_send()
        stepz(r).wait_send()
        chain_drain(r, csrc, cdst, SR, SL)
        chain_drain(r, zsrc, zdst, SZR, SZL)

    v = vec.shape[0]
    h1, h2, h3 = v // 2, v // 4, v // 8
    o1 = c * h1
    o2 = o1 + x * h2
    o3 = o2 + y * h3
    base = h1 + h2 + h3

    def vstep(i):
        if i == 0:
            return [remote(vec.at[pl.ds((1 - c) * h1, h1)], vrecv.at[pl.ds(0, h1)], vsend.at[0], vrecv_sem.at[0], core_dev)]
        if i == 1:
            return [remote(vown.at[pl.ds(o1 + (1 - x) * h2, h2)], vrecv.at[pl.ds(h1, h2)], vsend.at[1], vrecv_sem.at[1], x_dev)]
        if i == 2:
            return [remote(vown.at[pl.ds(o2 + (1 - y) * h3, h3)], vrecv.at[pl.ds(h1 + h2, h3)], vsend.at[2], vrecv_sem.at[2], y_dev)]
        if i == 3:
            return [remote(vown.at[pl.ds(o3, h3)], vrecv.at[pl.ds(base + z * h3, h3)], vsend.at[3 + k], vrecv_sem.at[3 + k],
                           z_devs[k - 1]) for k in range(1, 4)]
        if i == 4:
            return [remote(vout.at[pl.ds(o3, h3)], vout.at[pl.ds(o3, h3)], vsend.at[7], vrecv_sem.at[7], y_dev)]
        if i == 5:
            return [remote(vout.at[pl.ds(o2, h2)], vout.at[pl.ds(o2, h2)], vsend.at[8], vrecv_sem.at[8], x_dev)]
        return [remote(vout.at[pl.ds(o1, h1)], vout.at[pl.ds(o1, h1)], vsend.at[9], vrecv_sem.at[9], core_dev)]

    def vector_step(i):
        if i > 0:
            for cp in vstep(i - 1):
                cp.wait_recv()
        if i == 1:
            vown[pl.ds(o1, h1)] = vec[pl.ds(o1, h1)] + vrecv[0:h1]
        if i == 2:
            vown[pl.ds(o2, h2)] = vown[pl.ds(o2, h2)] + vrecv[h1:h1 + h2]
        if i == 3:
            vown[pl.ds(o3, h3)] = vown[pl.ds(o3, h3)] + vrecv[h1 + h2:base]
            vrecv[pl.ds(base + z * h3, h3)] = vown[pl.ds(o3, h3)]
        if i == 4:
            total = vrecv[base:base + h3]
            for k in range(1, 4):
                total = total + vrecv[base + k * h3:base + (k + 1) * h3]
            vout[pl.ds(o3, h3)] = total
        if i < 7:
            for cp in vstep(i):
                cp.start()

    def rows_arrive():
        for cp in early:
            cp.wait()

    def cross_arrive():
        @pl.when(y == 0)
        def _():
            for cp in window_rows("cross"):
                cp.wait_recv()

        @pl.when((y == 0) & (c == 0))
        def _():
            for cp in window_rows("relay"):
                cp.start()

    def others_arrive():
        @pl.when(c == 0)
        def _():
            for cp in window_rows("own"):
                cp.wait_recv()

        @pl.when((y == 0) & (c == 1))
        def _():
            for cp in window_rows("relay"):
                cp.wait_recv()

    def cross_send(i):
        @pl.when(y == 1)
        def _():
            window_piece("cross", i).start()

    def cross_relay(i):
        @pl.when(y == 0)
        def _():
            window_piece("cross", i).wait_recv()

        @pl.when((y == 0) & (c == 0))
        def _():
            window_piece("relay", i).start()

    def windows_drain():
        @pl.when(y == 1)
        def _():
            for cp in window_rows("cross"):
                cp.wait_send()
            for i in range(HEADS // 2):
                window_piece("cross", i).wait_send()

        @pl.when(c == 1)
        def _():
            for cp in window_rows("own"):
                cp.wait_send()

        @pl.when((y == 0) & (c == 0))
        def _():
            for cp in window_rows("relay"):
                cp.wait_send()
            for i in range(HEADS // 2):
                window_piece("relay", i).wait_send()

    lower = lax.broadcasted_iota(jnp.int32, (1, 2 * dim), 1) < dim

    def one_head(values, sub):
        return jnp.where(lower if sub == 0 else ~lower, values, jnp.zeros_like(values))

    def both_heads(terms):
        return jnp.where(lower, terms[0], terms[1])

    def weights_of(i, sub, k1, v1, qj, q2, d2, bias):
        log_total = stw[qj, pl.ds(2 * i + sub, 1)]
        delta = stw[qj, pl.ds(HEADS + 2 * i + sub, 1)]
        probs = jnp.exp(dot_nt(k1, q2) + bias - log_total)
        return probs.astype(BF16), (probs * (dot_nt(v1, d2) - delta)).astype(BF16)

    def add(total_sum, term):
        return term if total_sum is None else total_sum + term

    def attend_near(i):
        cols = pl.ds(pl.multiple_of(i * 2 * dim, 2 * dim), 2 * dim)
        part_cols = pl.ds(pl.multiple_of(i % 4 * 2 * dim, 2 * dim), 2 * dim)

        def blocks(lowest):
            q2, d2 = qw[0, :, cols], dow[0, :, cols]
            dq, dk, dv = None, [None, None], [None, None]
            for kj in range(lowest, 3):
                k2, v2 = kw[kj, :, cols], vw[kj, :, cols]
                for sub in range(2):
                    k1 = one_head(k2, sub)
                    low_p, low_s = weights_of(i, sub, k1, one_head(v2, sub), 0, q2, d2, mask[kj * rows:(kj + 1) * rows])
                    dq = add(dq, dot_tn(k1, low_s))
                    if kj == 2:
                        dk[sub], dv[sub] = dot32(low_s, q2), dot32(low_p, d2)
            dpj[i // 4, :, part_cols] = (dq.T * (dim ** -0.5)).astype(BF16)
            d_ffn[:, cols] = both_heads(dk)
            d_ffn[:, pl.ds(pl.multiple_of(width + i * 2 * dim, 2 * dim), 2 * dim)] = both_heads(dv)

        for number in range(3):
            pl.when(blk == number if number < 2 else blk >= 2)(functools.partial(blocks, 2 - number))

    def attend_far(i):
        cols = pl.ds(pl.multiple_of(i * 2 * dim, 2 * dim), 2 * dim)
        part_cols = pl.ds(pl.multiple_of(i % 4 * 2 * dim, 2 * dim), 2 * dim)

        @pl.when((y == 0) & (c == 1))
        def _():
            window_piece("relay", i).wait_recv()

        def blocks(count):
            k2, v2 = kw[2, :, cols], vw[2, :, cols]
            dk, dv = [None, None], [None, None]
            for sub in range(2):
                k1, v1 = one_head(k2, sub), one_head(v2, sub)
                for qj in range(1, count + 1):
                    q2, d2 = qw[qj, :, cols], dow[qj, :, cols]
                    low_p, low_s = weights_of(i, sub, k1, v1, qj, q2, d2, mask_q[:, (qj - 1) * rows:qj * rows])
                    dk[sub], dv[sub] = add(dk[sub], dot32(low_s, q2)), add(dv[sub], dot32(low_p, d2))
            dk_sum, dv_sum = d_ffn[:, cols], d_ffn[:, pl.ds(pl.multiple_of(width + i * 2 * dim, 2 * dim), 2 * dim)]
            if count > 0:
                dk_sum, dv_sum = dk_sum + both_heads(dk), dv_sum + both_heads(dv)
            dpj[2 + i // 4, :, part_cols] = dk_sum.astype(BF16)
            dpj[4 + i // 4, :, part_cols] = dv_sum.astype(BF16)

        for number in range(3):
            pl.when(blk == 3 - number if number < 2 else blk <= 1)(functools.partial(blocks, number))

    V_IN_GAIN, V_IN_BIAS, V_QV, V_OUT, V_PA_GAIN, V_PA_BIAS, V_MID_GAIN, V_MID_BIAS, V_FC2 = (
        k * (width // 128) for k in (0, 1, 2, 4, 5, 6, 7, 8, 9))
    V_FC1 = 10 * (width // 128)
    V_FFN_GAIN = V_FC1 + ff // 128
    V_FFN_BIAS = V_FFN_GAIN + ff // 128
    V_HEADS = V_FFN_BIAS + ff // 128

    def put_row(first_row, row):
        for k in range(row.shape[1] // 128):
            vec[first_row + k:first_row + k + 1, :] = row[:, k * 128:(k + 1) * 128]

    def put_row_at(first_row, j, row):
        for k in range(FC // 128):
            vec[pl.ds(first_row + j * (FC // 128) + k, 1), :] = row[:, k * 128:(k + 1) * 128]

    def chunk_cols(j):
        return pl.ds(pl.multiple_of(j * FC, FC), FC)

    def ffn_first(j):
        cols = chunk_cols(j)
        for cp in piece2(j):
            cp.wait()
        weights = w2b[j % PIECES]
        total[...] = total[...] + dot32(lowb[j % PIECES], weights)
        grad = dot_nt(bm[0, 0], weights[:, 0:WR]) + dot_nt(bm[1, 0], weights[:, WR:])
        unit = normed[:, cols].astype(F32)
        d_ffn[:, cols] = grad
        put_row_at(V_FFN_GAIN, j, jnp.sum(grad * unit, axis=0, keepdims=True))
        put_row_at(V_FFN_BIAS, j, jnp.sum(grad, axis=0, keepdims=True))
        grad = grad * ffn_gain[:, cols]
        parts[0] = parts[0] + lane_sums(grad)
        parts[1] = parts[1] + lane_sums(grad * unit)

        @pl.when(j + PIECES < n_ff)
        def _():
            for cp in piece2(j + PIECES):
                cp.start()

    def ffn_between():
        layer_held[...] = (first[...] + total[...] + fc2_bias[...]).astype(BF16)
        layer_copy.start()
        total[...] = jnp.zeros_like(total)
        parts[2] = jnp.broadcast_to(jnp.sum(parts[0], axis=-1, keepdims=True) * (1.0 / ff), parts.shape[1:])
        parts[3] = jnp.broadcast_to(jnp.sum(parts[1], axis=-1, keepdims=True) * (1.0 / ff), parts.shape[1:])

    def ffn_second(q):
        j = pre_place(q)
        k = q // 2
        cols = chunk_cols(j)
        piece_col(q, w1_in, j).wait()
        piece_slope(q).wait()
        grad = d_ffn[:, cols] * ffn_gain[:, cols]
        grad = scale_ffn[:, 0:1] * (grad - parts[2][:, 0:1] - normed[:, cols].astype(F32) * parts[3][:, 0:1])
        low = (grad * slopeb[q % PIECES].astype(F32)).astype(BF16)
        put_row_at(V_FC1, j, jnp.sum(low.astype(F32), axis=0, keepdims=True))
        total[...] = total[...] + dot_nt(low, colb[q % PIECES])

        @pl.when(q % 2 == 0)
        def _():
            pre_other[k] = low
            pre_far(k).start()

        @pl.when(q % 2 == 1)
        def _():
            bm[2 + k, 0] = low
            b_to_core(2 + k, 0).start()

        @pl.when(q + PIECES < n_ff)
        def _():
            piece_slope(q + PIECES).start()

        start_col(q + PIECES)

    def unit_rows(values):
        centered = values - jnp.mean(values, axis=-1, keepdims=True)
        scale = lax.rsqrt(jnp.mean(centered * centered, axis=-1, keepdims=True) + 1e-05)
        return centered * scale, scale

    def norm_back(grad, values, gain_row, gain_at, bias_at):
        unit, scale = unit_rows(values)
        put_row(gain_at, jnp.sum(grad * unit, axis=0, keepdims=True))
        put_row(bias_at, jnp.sum(grad, axis=0, keepdims=True))
        grad = grad * gain_row
        return scale * (grad - jnp.mean(grad, axis=-1, keepdims=True) - unit * jnp.mean(grad * unit, axis=-1, keepdims=True))

    def middle_first():
        d_out = jnp.concatenate([bm[0, 0], bm[1, 0]], axis=1).astype(F32)
        put_row(V_FC2, jnp.sum(d_out, axis=0, keepdims=True))
        d_first[...] = d_out + norm_back(total[...], first[...], mid_gain[...], V_MID_GAIN, V_MID_BIAS)
        low = norm_back(d_first[...], attn[...], pa_gain[...], V_PA_GAIN, V_PA_BIAS).astype(BF16)
        for who in range(2):
            @pl.when(y == who)
            def _():
                bm[6, 0] = low[:, who * WR:(who + 1) * WR]
                attn_other[...] = low[:, (1 - who) * WR:(2 - who) * WR]

        b_to_core(6, 0).start()
        put_row(V_OUT, jnp.sum(low.astype(F32), axis=0, keepdims=True))

    def middle_second():
        for k in range(n_o):
            piece_col(n_ff + k, wo_in, k).wait()
        for who in range(2):
            @pl.when(y == who)
            def _():
                total[...] = (dot_nt(bm[6, 0], colb[(n_ff + who) % PIECES]) + dot_nt(attn_other[...], colb[(n_ff + 1 - who) % PIECES]))

        for k in range(n_o):
            start_col(n_ff + k + PIECES)
        attended = att[...]
        low = (total[...] * head_row(head_scale, width)).astype(BF16)
        dow[0] = low
        both = low.astype(F32) * attended
        high = both.astype(BF16)
        rest = (both - high.astype(F32)).astype(BF16)
        head_of = lax.broadcasted_iota(jnp.int32, (HEADS, width), 1) // dim
        pick = jnp.where(head_of == lax.broadcasted_iota(jnp.int32, (HEADS, width), 0), 1.0, 0.0).astype(BF16)
        by_column = jnp.broadcast_to(jnp.sum(total[...] * attended, axis=0, keepdims=True), (8, width))
        high_sum = by_column.astype(BF16)
        rest_sum = (by_column - high_sum.astype(F32)).astype(BF16)
        by_head = dot_nt(high_sum, pick) + dot_nt(rest_sum, pick)
        vec[V_HEADS:V_HEADS + 1, 0:HEADS] = by_head[0:1]
        stw[0, 0:HEADS] = lse[...]
        stw[0, HEADS:2 * HEADS] = dot_nt(pick, high) + dot_nt(pick, rest)

        @pl.when(y == 1)
        def _():
            for cp in window_rows("cross"):
                cp.start()

        @pl.when(c == 1)
        def _():
            for cp in window_rows("own"):
                cp.start()

    def proj_out(blocks):
        for who, k in blocks:
            @pl.when(x == who)
            def _():
                bm[7 + k, 0] = dpj[((0, 1, 3), (4, 2, 5))[who][k]]
                b_to_core(7 + k, 0).start()

            @pl.when(x != who)
            def _():
                proj_far(k).start()

    def input_first():
        base_q = n_ff + n_o
        for k in range(n_q):
            piece_col(base_q + k, wq_in, k).wait()
            term = dot_nt(dpj[k], colb[(base_q + k) % PIECES])
            total[...] = term if k == 0 else total[...] + term
            start_col(base_q + k + PIECES)

    def input_second():
        grad = norm_back(total[...], tokens[...].astype(F32), gain[...], V_IN_GAIN, V_IN_BIAS)
        d_first[...] = d_first[...] + grad
        grad_copy.start()
        for k, block in enumerate((0, 1, 4, 5)):
            put_row(V_QV + k * (WR // 128), jnp.sum(dpj[block].astype(F32), axis=0, keepdims=True))

    n_pairs = HEADS // 2
    after = MIDDLE + n_pairs + FAR
    plan = sorted(list(zip(LAG_Y, (y0, y1, y2, y3, y4))) + list(zip(LAG_Z, (z0, z1, z2, z3, z4)))
                  + list(zip(LAG_SWAP, (swap0, swap1))), key=lambda item: -item[0])
    last = max(LAG_Y + LAG_Z + LAG_SWAP)

    def relay(b):
        b_far(b, pre_other.at[0], x_dev).wait_recv()
        b_to_core(b, 2).start()

    def attn_relay():
        for k in range(n_attn):
            attn_far(k).wait_recv()
        b_to_core(6, 2).start()

    def b_arrive(b):
        b_to_core(b, 0).wait_recv()
        b_to_core(b, 2).wait_recv()

    def at_slot(s, number, work):
        @pl.when(s == number)
        def _():
            work()

    def sent_drain():
        windows_drain()
        for g in range(10):
            for t in range(1, 4):
                if not local(g, t):
                    a_load(g, t).wait_send()
        for b in range(2):
            cot_load(b, 1).wait_send()
            cot_load(b, 3).wait_send()
        for b in range(2, 10):
            b_to_core(b, 0).wait_send()
            b_to_core(b, 2).wait_send()
            if b != 6:
                b_far(b, pre_other.at[0], x_dev).wait_send()
        for k in range(n_attn):
            attn_far(k).wait_send()

    def slot_step(s, carry):
        at_slot(s, 0, lambda: [cot_load(b, 0).wait() for b in range(2)])
        at_slot(s, 0, normed_load.wait)
        for u in range(3):
            j = 3 * s + u

            @pl.when(j < n_ff)
            def _():
                ffn_first(j)

        at_slot(s, 2, first_load.wait)
        at_slot(s, 2, ffn_between)
        for u in range(3):
            j = 3 * (s - 3) + u

            @pl.when((j >= 0) & (j < n_ff))
            def _():
                ffn_second(j)

        at_slot(s, MIDDLE + 6, lambda: [a_load(g, 3).start() for g in (8, 9)])
        at_slot(s, MIDDLE, attn_load.wait)
        at_slot(s, MIDDLE, att_load.wait)
        at_slot(s, MIDDLE, middle_first)
        at_slot(s, MIDDLE, middle_second)
        at_slot(s, MIDDLE, rows_arrive)

        def relay_blocks(low, high, first_round, ahead):
            k = s + ahead - FIRST - first_round

            @pl.when((k >= 0) & (k < 2 * (high - low)) & (k % 2 == 0))
            def _():
                relay(low + k // 2)

        def arrive_blocks(low, high, first_round):
            k = s - FIRST - first_round

            @pl.when((k >= 0) & (k < 2 * (high - low)) & (k % 2 == 0))
            def _():
                b_arrive(low + k // 2)

        at_slot(s, FIRST, lambda: [[cot_load(b, 1).wait_recv(), cot_load(b, 2).wait(), cot_load(b, 3).wait_recv()] for b in range(2)])
        for g in range(4):
            at_slot(s, FIRST + 2 * g, functools.partial(a_arrive, g))
        for g in range(4, 10):
            at_slot(s, FIRST + (7, 19, 15)[(g - 4) // 2], functools.partial(a_arrive, g))
        relay_blocks(2, 6, 8, 1)
        at_slot(s, FIRST + 19, attn_relay)
        relay_blocks(7, 9, 16, 1)
        relay_blocks(9, 10, 22, 1)
        arrive_blocks(2, 6, 8)
        arrive_blocks(6, 7, 20)
        arrive_blocks(7, 9, 16)
        arrive_blocks(9, 10, 22)

        at_slot(s, FIRST + rounds + 3, sent_drain)
        for lag, work in plan:
            r = s - lag - FIRST

            @pl.when((r >= 0) & (r < rounds))
            def _():
                work(r)

        i = s - MIDDLE

        @pl.when((i >= 0) & (i < n_pairs))
        def _():
            cross_send(i)

        @pl.when((i >= 1) & (i < n_pairs + 1))
        def _():
            attend_near(i - 1)

        at_slot(s, MIDDLE + FAR - 1, cross_arrive)
        at_slot(s, MIDDLE + FAR, others_arrive)

        @pl.when((i >= FAR - 1) & (i < n_pairs + FAR - 1))
        def _():
            cross_relay(i - (FAR - 1))

        @pl.when((i >= FAR) & (i < n_pairs + FAR))
        def _():
            attend_far(i - FAR)

        for k in range(n_attn):
            at_slot(s, FIRST + 12 + k, attn_far(k).start)
        at_slot(s, MIDDLE + 4, lambda: proj_out([(0, 0)]))
        at_slot(s, MIDDLE + FAR + 3, lambda: proj_out([(1, 0), (1, 1)]))
        at_slot(s, MIDDLE + 8, lambda: proj_out([(0, 1)]))
        at_slot(s, after - 1, lambda: proj_out([(0, 2), (1, 2)]))
        at_slot(s, after - 1, input_first)
        at_slot(s, after, input_second)
        for i in range(8):
            @pl.when(s == after + 2 * i + (2 if i > 3 else 0))
            def _():
                vector_step(i)

        return carry

    lax.fori_loop(0, FIRST + rounds + last, slot_step, 0)
    lax.fori_loop(rounds - SEND, rounds, lambda r, carry: (drain(r), carry)[1], 0)

    def swap_drain(r, carry):
        @pl.when(~mine(r))
        def _():
            step_swap(r).wait_send()

        return carry

    lax.fori_loop(8, rounds, swap_drain, 0)
    for i in range(7):
        for cp in vstep(i):
            cp.wait_send()

    layer_copy.wait()
    grad_copy.wait()

    def share_wait(r, carry):
        pltpu.make_async_copy(out.at[0], out2.at[pl.ds(0, ROWS), pl.ds(0, WR)], out_sem.at[0]).wait()
        return carry

    lax.fori_loop(0, rounds, share_wait, 0)


def blocks_first(turned):
    return turned.reshape(4, 2, 2, 2, turned.shape[0] // 32 // ROWS, ROWS, turned.shape[1])


def finish_kernel(n_big, rows_of, *refs):
    n_vec = len(rows_of)
    n_in = n_big + 1
    big = refs[:n_in]
    out_big, out_vec = refs[n_in:n_in + n_big], refs[n_in + n_big:n_in + n_big + n_vec]
    out_heads = refs[n_in + n_big + n_vec]
    held, in_sem, out_sem = refs[n_in + n_big + n_vec + 1:-2], refs[-2], refs[-1]
    loads = [pltpu.make_async_copy(src, dst, in_sem.at[k]) for k, (src, dst) in enumerate(zip(big, held))]
    for cp in loads:
        cp.start()
    stores = [[pltpu.make_async_copy(src, dst, out_sem.at[k])] for k, (src, dst) in enumerate(zip(held, out_big))]
    stores.append([pltpu.make_async_copy(held[-1].at[pl.ds(first, count)], dst, out_sem.at[n_big + k])
                   for k, ((first, count), dst) in enumerate(zip(rows_of, out_vec))])
    for load, group in zip(loads, stores):
        load.wait()
        for cp in group:
            cp.start()
    at = sum(rows_of[-1])
    out_heads[...] = held[-1][at:at + 1, 0:HEADS]
    for group in stores:
        for cp in group:
            cp.wait()


def finish(layer_out, grad_tokens, out2, out1, outo, outq, flat, sizes):
    big = (layer_out, grad_tokens, out2, out1, outo, outq)
    rows_of, at = [], 0
    for size in sizes:
        rows_of.append((at, size // 128))
        at += size // 128
    hbm, vmem = pl.BlockSpec(memory_space=pl.ANY), pl.BlockSpec(memory_space=pltpu.VMEM)
    res = pl.pallas_call(
        functools.partial(finish_kernel, len(big), tuple(rows_of)),
        out_shape=[jax.ShapeDtypeStruct(item.shape, item.dtype) for item in big]
        + [jax.ShapeDtypeStruct((count, 128), F32) for _, count in rows_of] + [jax.ShapeDtypeStruct((1, HEADS), F32)],
        in_specs=[hbm] * (len(big) + 1),
        out_specs=[hbm] * (len(big) + len(rows_of)) + [vmem],
        scratch_shapes=[pltpu.VMEM(item.shape, item.dtype) for item in big + (flat,)]
        + [pltpu.SemaphoreType.DMA((len(big) + 1,)), pltpu.SemaphoreType.DMA((len(big) + len(rows_of),))],
    )(*big, flat)
    layer_out, grad_tokens, out2, out1, outo, outq = res[:6]
    ln1g, ln1b, qv, bo, pag, pab, ln2g, ln2b, c2, c1, lnfg, lnfb = (item.reshape(-1) for item in res[6:-1])
    return (layer_out, grad_tokens, ln1g, ln1b, outq, qv, res[-1].reshape(-1), outo, bo, pag, pab, ln2g, ln2b, out1, c1, lnfg, lnfb,
            out2, c2)


def fast_shards(
    tokens, lengths, ln1_gain, ln1_bias, w_qkv, qv_bias, head_scale, w_out, out_bias, lnpa_gain, lnpa_bias,
    ln2_gain, ln2_bias, w_fc1, fc1_bias, lnf_gain, lnf_bias, w_fc2, fc2_bias, cotangent,
):
    tok, width = tokens.shape
    ff = w_fc1.shape[1]
    (low_in_t, q_win, k_win, v_win, att, lse, scaled_t, attn, first, low_mid_t, normed, slope, scale_ffn, low_ffn, low_ffn_t,
     cot_x, low_in_x, low_mid_x, scaled_y) = forward(
        lengths, tokens, ln1_gain, ln1_bias, w_qkv, qv_bias, head_scale, w_out, out_bias, lnpa_gain, lnpa_bias, ln2_gain, ln2_bias,
        w_fc1, fc1_bias, lnf_gain, lnf_bias, cotangent)
    rounds = 24
    hbm, vmem, smem = (pl.BlockSpec(memory_space=space) for space in (pl.ANY, pltpu.VMEM, pltpu.SMEM))
    msgs = [(4, ROWS, WY), (3, ROWS, WY), (3, ROWS, WY), (3, 2, ROWS, WZ), (3, 2, ROWS, WZ), (ROWS, WZ)]
    n_swap = 8
    sizes = (width, width, 2 * width) + (width,) * 6 + (ff, ff, ff)
    v = -(-(sum(sizes) + 128) // 8192) * 64
    dma, shape = pltpu.SemaphoreType.DMA, jax.ShapeDtypeStruct
    f32s = [(KEEP, 4, 2, ROWS, WR), (2, ROWS, WZ), (KEEP, ROWS, WZ), (rounds, ROWS, WR), (n_swap, ROWS, WR),
            (v, 128), (v, 128), (v // 2 + v // 4 + v // 8 * 5, 128)]
    windows = [pltpu.VMEM((3, tok, width), BF16)] * 4 + [pltpu.VMEM((3, 2 * HEADS, tok), F32)]
    more = [(3 * tok, tok), (tok, 2 * tok), (tok, width), (tok, width), (tok, ff), (4, tok, 128), (tok, width), (tok, width), (tok, width)]
    out2, out1, outo, outq, flat, grad_tokens, layer_out = pl.pallas_call(
        functools.partial(back_kernel, tok),
        out_shape=[shape((ff // 32, width), F32), shape((width // 32, ff), F32), shape((width // 32, width), F32),
                   shape((width // 32, 3 * width), F32), shape((v, 128), F32), shape((tok, width), F32), shape((tok, width), BF16)],
        in_specs=[hbm] * 9 + [smem] + [hbm] * 3 + [vmem] + [hbm] * 3 + [vmem] * 6 + [smem, vmem] + [hbm] * 7,
        out_specs=[hbm] * 4 + [vmem] + [hbm] * 2,
        scratch_shapes=[pltpu.VMEM((10, 4, 4, 2, ROWS, tok), BF16), pltpu.VMEM((10, 4, tok, WR), BF16), pltpu.VMEM((4, tok, WR), BF16),
                        pltpu.VMEM((tok, WR), BF16), pltpu.VMEM((6, tok, WR), BF16)]
        + [pltpu.VMEM((SEND,) + m, BF16) for m in msgs] + [pltpu.VMEM((n_swap, ROWS, WR), BF16)]
        + [pltpu.VMEM((RECV + (2 if m[0] in (4, ROWS) else 0),) + m, BF16) for m in msgs] + [pltpu.VMEM((n_swap, ROWS, WR), BF16)]
        + [pltpu.VMEM(m, F32) for m in f32s] + windows + [pltpu.VMEM(m, F32) for m in more]
        + [pltpu.VMEM((tok, width), BF16), pltpu.VMEM((tok, ff), BF16), pltpu.VMEM((PIECES, FC, width), BF16), pltpu.VMEM((PIECES, width, FC), BF16),
           pltpu.VMEM((PIECES, tok, FC), BF16), pltpu.VMEM((PIECES, tok, FC), BF16),
           dma((10, 4)), dma((10, 4)), dma((10, 4)), dma((10, 4)), dma((6, SEND)), dma((6, RECV + 2)), dma((10,)), dma((10,)), dma((4 + HEADS,)), dma((4 + HEADS,)),
           dma((9,)), dma((PIECES,)), dma((PIECES,)), dma((PIECES,)), dma((PIECES,)), dma((2, n_swap)), dma((2, WR * HEADS // (2 * width))), dma((1,))],
        compiler_params=pltpu.CompilerParams(collective_id=0, has_side_effects=True, vmem_limit_bytes=63 << 20),
        cost_estimate=pl.CostEstimate(flops=30 << 30, bytes_accessed=50 << 20, transcendentals=4 << 20),
    )(blocks_first(low_ffn_t), blocks_first(low_mid_t), blocks_first(low_mid_x), blocks_first(scaled_t), blocks_first(scaled_y),
      blocks_first(low_in_t.reshape(width, tok)), low_in_x.reshape(4, 2, 2, ROWS, tok), cotangent, cot_x, lengths, q_win, k_win, v_win, lse, att, attn, first, scale_ffn, tokens,
      ln1_gain[None], lnpa_gain[None], ln2_gain[None], lnf_gain[None], head_scale[None], fc2_bias[None],
      normed, slope, low_ffn, w_fc2, w_fc1, w_out, w_qkv)
    return finish(layer_out, grad_tokens, out2, out1, outo, outq, flat, sizes)


def shards(
    tokens,
    lengths,
    ln1_gain,
    ln1_bias,
    w_qkv,
    qv_bias,
    head_scale,
    w_out,
    out_bias,
    lnpa_gain,
    lnpa_bias,
    ln2_gain,
    ln2_bias,
    w_fc1,
    fc1_bias,
    lnf_gain,
    lnf_bias,
    w_fc2,
    fc2_bias,
    cotangent,
):
    row_count, width = tokens.shape
    head_dim = width // HEADS
    factor = head_dim ** (-0.5)
    group = row_count * lax.axis_size("blk")
    own_start = lax.axis_index("blk") * row_count
    seq_ends = jnp.cumsum(lengths[0])
    positions = jnp.arange(group, dtype=jnp.int32)
    labels = jnp.sum((positions[:, None] >= seq_ends[None, :]).astype(jnp.int32), axis=1)
    q_labels = lax.dynamic_slice_in_dim(labels, own_start, row_count, 0)
    q_spots = own_start + jnp.arange(row_count, dtype=jnp.int32)
    inputs = tokens.astype(jnp.float32)
    normed_in, ln1_back = jax.vjp(norm_rows, inputs, ln1_gain, ln1_bias)
    low_in = normed_in.astype(jnp.bfloat16)
    projected = jnp.dot(low_in, w_qkv, preferred_element_type=jnp.float32)
    queries = (projected[:, :width] + qv_bias[:width]).astype(jnp.bfloat16)
    key_rows = projected[:, width : 2 * width].astype(jnp.bfloat16)
    value_rows = (projected[:, 2 * width :] + qv_bias[width:]).astype(jnp.bfloat16)
    query_heads = queries.reshape(row_count, HEADS, head_dim)

    def scored(key_block, start):
        count = key_block.shape[0]
        key_heads = key_block.reshape(count, HEADS, head_dim)
        raw_scores = (
            jnp.einsum("qhd,khd->hqk", query_heads, key_heads, preferred_element_type=jnp.float32)
            * factor
        )
        k_labels = lax.dynamic_slice_in_dim(labels, start, count, 0)
        k_spots = start + jnp.arange(count, dtype=jnp.int32)
        visible = (k_labels[None, :] == q_labels[:, None]) & (k_spots[None, :] <= q_spots[:, None])
        return (raw_scores, visible[None], key_heads)

    def by_blocks(step_fn, carry, pieces):
        count = pieces[0].shape[0]
        unit = max(1, 1024 // row_count) * row_count
        step = count if count <= unit else math.gcd(count, unit)

        def inner(block_index, state):
            offset = block_index * step
            sub_pieces = tuple((lax.dynamic_slice_in_dim(item, offset, step, 0) for item in pieces))
            return step_fn(state, sub_pieces, offset)

        return lax.fori_loop(0, count // step, inner, carry)

    def max_step(carry, pieces, start):
        top_score, totals = carry
        raw_scores, visible, key_heads = scored(pieces[0], start)
        raw_scores = jnp.where(visible, raw_scores, -1e30)
        new_top = jnp.maximum(top_score, jnp.max(raw_scores, axis=-1))
        totals = totals * jnp.exp(top_score - new_top) + jnp.sum(
            jnp.where(visible, jnp.exp(raw_scores - new_top[..., None]), 0.0), axis=-1
        )
        return (new_top, totals)

    start_top = jnp.full((HEADS, row_count), -1e30, jnp.float32)
    start_total = jnp.zeros((HEADS, row_count), jnp.float32)
    top_score, totals = by_blocks(
        max_step, (start_top, start_total), (lax.all_gather(key_rows, "blk", axis=0, tiled=True),)
    )
    log_total = top_score + jnp.log(totals)

    def value_step(carry, pieces, start):
        weighted, leftover = carry
        raw_scores, visible, key_heads = scored(pieces[0], start)
        value_heads = pieces[1].reshape(pieces[1].shape[0], HEADS, head_dim)
        probs = jnp.where(visible, jnp.exp(raw_scores - log_total[..., None]), 0.0)
        low_probs = probs.astype(jnp.bfloat16)
        rest_probs = (probs - low_probs.astype(jnp.float32)).astype(jnp.bfloat16)
        weighted = weighted + jnp.einsum(
            "hqk,khd->qhd", low_probs, value_heads, preferred_element_type=jnp.float32
        )
        leftover = leftover + jnp.einsum(
            "hqk,khd->qhd", rest_probs, value_heads, preferred_element_type=jnp.float32
        )
        return (weighted, leftover)

    empty_heads = jnp.zeros((row_count, HEADS, head_dim), jnp.float32)
    weighted, leftover = by_blocks(
        value_step,
        (empty_heads, empty_heads),
        (
            lax.all_gather(key_rows, "blk", axis=0, tiled=True),
            lax.all_gather(value_rows, "blk", axis=0, tiled=True),
        ),
    )
    attended = weighted.reshape(row_count, width)
    head_gain = jnp.repeat(head_scale, head_dim)
    scaled = (attended * head_gain).astype(jnp.bfloat16)
    attn_out = jnp.dot(scaled, w_out, preferred_element_type=jnp.float32) + out_bias
    branch, pa_back = jax.vjp(norm_rows, attn_out, lnpa_gain, lnpa_bias)
    first_sum = inputs + branch
    normed_mid, ln2_back = jax.vjp(norm_rows, first_sum, ln2_gain, ln2_bias)
    low_mid = normed_mid.astype(jnp.bfloat16)
    pre_act = jnp.dot(low_mid, w_fc1, preferred_element_type=jnp.float32) + fc1_bias
    activated, gelu_back = jax.vjp(gelu_exact, pre_act)
    ffn_normed, lnf_back = jax.vjp(norm_rows, activated, lnf_gain, lnf_bias)
    low_ffn = ffn_normed.astype(jnp.bfloat16)
    layer_out = (
        first_sum + jnp.dot(low_ffn, w_fc2, preferred_element_type=jnp.float32) + fc2_bias
    ).astype(jnp.bfloat16)
    d_output = cotangent.astype(jnp.float32)
    grad_w2 = over_rows(low_ffn, cotangent)
    grad_c2 = jnp.sum(d_output, axis=0)
    d_ffn = over_cols(cotangent, w_fc2)
    d_active, grad_lnf_gain, grad_lnf_bias = lnf_back(d_ffn)
    (d_pre,) = gelu_back(d_active)
    low_pre = d_pre.astype(jnp.bfloat16)
    grad_w1 = over_rows(low_mid, low_pre)
    grad_c1 = jnp.sum(low_pre.astype(jnp.float32), axis=0)
    d_mid = over_cols(low_pre, w_fc1)
    d_first_norm, grad_ln2_gain, grad_ln2_bias = ln2_back(d_mid)
    d_first = d_output + d_first_norm
    d_attn, grad_pa_gain, grad_pa_bias = pa_back(d_first)
    low_attn = d_attn.astype(jnp.bfloat16)
    grad_bo = jnp.sum(low_attn.astype(jnp.float32), axis=0)
    grad_wo = over_rows(scaled, low_attn)
    d_scaled = over_cols(low_attn, w_out)
    grad_hs = jnp.sum((d_scaled * attended).reshape(row_count, HEADS, head_dim), axis=(0, 2))
    d_attended = (d_scaled * head_gain).astype(jnp.bfloat16)
    d_heads = d_attended.reshape(row_count, HEADS, head_dim)
    delta_rows = jnp.sum(d_heads.astype(jnp.float32) * (weighted + leftover), axis=-1)
    delta = delta_rows.T

    def back_step(carry, pieces, start):
        count = pieces[0].shape[0]
        raw_scores, visible, key_heads = scored(pieces[0], start)
        value_heads = pieces[1].reshape(count, HEADS, head_dim)
        probs = jnp.where(visible, jnp.exp(raw_scores - log_total[..., None]), 0.0)
        d_probs = jnp.einsum(
            "qhd,khd->hqk", d_heads, value_heads, preferred_element_type=jnp.float32
        )
        d_scores = (probs * (d_probs - delta[..., None])).astype(jnp.bfloat16)
        d_query = (
            carry[0]
            + jnp.einsum("hqk,khd->qhd", d_scores, key_heads, preferred_element_type=jnp.float32)
            * factor
        )
        key_grad, value_grad = (carry[1], carry[2])
        low_probs = probs.astype(jnp.bfloat16)
        d_value = jnp.einsum(
            "hqk,qhd->khd", low_probs, d_heads, preferred_element_type=jnp.float32
        ).reshape(count, width)
        d_key = (
            jnp.einsum("hqk,qhd->khd", d_scores, query_heads, preferred_element_type=jnp.float32)
            * factor
        ).reshape(count, width)
        key_grad = lax.dynamic_update_slice_in_dim(
            key_grad, lax.dynamic_slice_in_dim(key_grad, start, count, 0) + d_key, start, 0
        )
        value_grad = lax.dynamic_update_slice_in_dim(
            value_grad, lax.dynamic_slice_in_dim(value_grad, start, count, 0) + d_value, start, 0
        )
        return (d_query, key_grad, value_grad)

    empty_group = jnp.zeros((group, width), jnp.float32)
    start_carry = (empty_heads, empty_group, empty_group)
    results = by_blocks(
        back_step,
        start_carry,
        (
            lax.all_gather(key_rows, "blk", axis=0, tiled=True),
            lax.all_gather(value_rows, "blk", axis=0, tiled=True),
        ),
    )
    d_query = results[0]
    own_keys, own_values = (
        lax.psum_scatter(
            results[1].astype(jnp.bfloat16), "blk", scatter_dimension=0, tiled=True
        ).astype(jnp.float32),
        lax.psum_scatter(
            results[2].astype(jnp.bfloat16), "blk", scatter_dimension=0, tiled=True
        ).astype(jnp.float32),
    )
    low_q = d_query.reshape(row_count, width).astype(jnp.bfloat16)
    low_k = own_keys.astype(jnp.bfloat16)
    low_v = own_values.astype(jnp.bfloat16)
    d_projected = jnp.concatenate([low_q, low_k, low_v], axis=1)
    grad_wqkv = over_rows(low_in, d_projected)
    grad_qv = jnp.concatenate(
        [jnp.sum(low_q.astype(jnp.float32), axis=0), jnp.sum(low_v.astype(jnp.float32), axis=0)]
    )
    d_in = over_cols(d_projected, w_qkv)
    d_in_norm, grad_ln1_gain, grad_ln1_bias = ln1_back(d_in)
    grad_tokens = d_first + d_in_norm
    share_wqkv, share_wo, share_w1, share_w2 = (
        lax.psum_scatter(grad_wqkv, ("dp", "blk"), scatter_dimension=0, tiled=True),
        lax.psum_scatter(grad_wo, ("dp", "blk"), scatter_dimension=0, tiled=True),
        lax.psum_scatter(grad_w1, ("dp", "blk"), scatter_dimension=0, tiled=True),
        lax.psum_scatter(grad_w2, ("dp", "blk"), scatter_dimension=0, tiled=True),
    )
    summed = lax.psum(
        (
            grad_ln1_gain,
            grad_ln1_bias,
            grad_qv,
            grad_hs,
            grad_bo,
            grad_pa_gain,
            grad_pa_bias,
            grad_ln2_gain,
            grad_ln2_bias,
            grad_c1,
            grad_lnf_gain,
            grad_lnf_bias,
            grad_c2,
        ),
        ("dp", "blk"),
    )
    return (
        layer_out,
        grad_tokens,
        summed[0],
        summed[1],
        share_wqkv,
        summed[2],
        summed[3],
        share_wo,
        summed[4],
        summed[5],
        summed[6],
        summed[7],
        summed[8],
        share_w1,
        summed[9],
        summed[10],
        summed[11],
        share_w2,
        summed[12],
    )


def solution(mesh):
    in_specs = (
        P(("dp", "blk"), None),
        P("dp", None),
        P(),
        P(),
        P(),
        P(),
        P(),
        P(),
        P(),
        P(),
        P(),
        P(),
        P(),
        P(),
        P(),
        P(),
        P(),
        P(),
        P(),
        P(("dp", "blk"), None),
    )
    out_specs = (
        P(("dp", "blk"), None),
        P(("dp", "blk"), None),
        P(),
        P(),
        P(("dp", "blk"), None),
        P(),
        P(),
        P(("dp", "blk"), None),
        P(),
        P(),
        P(),
        P(),
        P(),
        P(("dp", "blk"), None),
        P(),
        P(),
        P(),
        P(("dp", "blk"), None),
        P(),
    )
    body = fast_shards if dict(mesh.shape) == {"dp": 8, "blk": 4} else shards
    return jax.shard_map(body, mesh=mesh, in_specs=in_specs, out_specs=out_specs, check_vma=False)
```
